32 devices in a mesh: dp: 8 (over y, x, core), fsdp: 4 (over z).
Axes of the slice: x: 2, y: 2, z: 4, core: 2. Of those that a mesh axis runs over, the one named last changes fastest.
Arguments:
- layer_input: bfloat16 [32, 1024, 1024], P(('dp', 'fsdp')), may hold values from -6 to 6
- qkv_weight: bfloat16 [1024, 3072], P('fsdp'), may hold values from -0.1875 to 0.1875
- query_value_bias: bfloat16 [2, 1024], P(None, 'fsdp'), may hold values from -1.796875 to 1.796875
- out_weight: bfloat16 [1024, 1024], P('fsdp'), may hold values from -0.1875 to 0.1875
- out_bias: bfloat16 [1024], P('fsdp'), may hold values from -3 to 3
- up_weight: bfloat16 [1024, 4096], P('fsdp'), may hold values from -0.1875 to 0.1875
- up_bias: bfloat16 [4096], P('fsdp'), may hold values from -3 to 3
- down_weight: bfloat16 [4096, 1024], P('fsdp'), may hold values from -0.09375 to 0.09375
- down_bias: bfloat16 [1024], P('fsdp'), may hold values from -3 to 3
- norm_gain: bfloat16 [4, 1024], P(None, 'fsdp'), may hold values from 0.5 to 1.5
- norm_shift: bfloat16 [4, 1024], P(None, 'fsdp'), may hold values from -1.1953125 to 1.1953125
- doc_lengths: int32 [32, 8], P(('dp', 'fsdp')), may hold values from 0 to 1024, as said below
- cotangent: bfloat16 [32, 1024, 1024], P(('dp', 'fsdp')), may hold values from -6 to 6
Outputs:
- layer_out: bfloat16 [32, 1024, 1024], P(('dp', 'fsdp'))
- grad_input: float32 [32, 1024, 1024], P(('dp', 'fsdp'))
- qkv_grad: float32 [1024, 3072], P('fsdp')
- query_value_grad: float32 [2, 1024], P(None, 'fsdp')
- out_weight_grad: float32 [1024, 1024], P('fsdp')
- out_bias_grad: float32 [1024], P('fsdp')
- up_weight_grad: float32 [1024, 4096], P('fsdp')
- up_bias_grad: float32 [4096], P('fsdp')
- down_weight_grad: float32 [4096, 1024], P('fsdp')
- down_bias_grad: float32 [1024], P('fsdp')
- gain_grad: float32 [4, 1024], P(None, 'fsdp')
- shift_grad: float32 [4, 1024], P(None, 'fsdp')
The draws below stay inside these ranges and needn't reach their ends.
Inputs may be any that keep to these rules, and one draw needn't show every extreme that they name: `doc_lengths`: each row's lengths sum to between 512 and 1024; a zero marks an unused slot; in every draw some row holds a single document of 1024 tokens.
All inputs are finite; a program needn't handle non-finite values.
Results may differ from the reference program's by a relative error of at most 0.012.
Values may be sent and summed in bfloat16 or wider, within the bound.
No kernel may reach another device: no remote copies, remote signals or barrier semaphores. Data moves between devices by JAX's collectives and lax.ppermute only.
A program may use at most 256 MiB of HBM per device.

```python
import math
import jax
import jax.numpy as jnp
from jax import lax

D = 1024
HEADS = 16
HEAD_DIM = 64
FF = 4096
SEQ = 1024
DOCS = 8
ROWS = 32


def draw_doc_lengths(key, part):
    key = jax.random.fold_in(key, 11)
    key_count, key_level, key_length, key_full = jax.random.split(key, 4)
    row_fill = jax.random.randint(key_count, (ROWS, 1), SEQ // 2, SEQ + 1).astype(jnp.int32)
    level = jax.random.randint(key_level, (ROWS, DOCS), 0, 5).astype(jnp.int32)
    ceiling = jnp.maximum(jnp.right_shift(jnp.full((ROWS, DOCS), SEQ, jnp.int32), level), 1)
    drawn = 1 + jax.random.randint(key_length, (ROWS, DOCS), 0, 1 << 30).astype(jnp.int32) % ceiling
    doc_ends = jnp.minimum(jnp.cumsum(drawn, axis=1).astype(jnp.int32), row_fill)
    column = jnp.arange(DOCS, dtype=jnp.int32)[None, :]
    doc_ends = jnp.where(column == DOCS - 1, row_fill, doc_ends)
    doc_starts = jnp.concatenate([jnp.zeros((ROWS, 1), jnp.int32), doc_ends[:, :-1]], axis=1)
    lengths = doc_ends - doc_starts
    full_row = jax.random.randint(key_full, (), 0, ROWS)
    single = jnp.where(column == 0, SEQ, 0).astype(jnp.int32)
    row_ids = jnp.arange(ROWS, dtype=jnp.int32)[:, None]
    return jnp.where(row_ids == full_row, single, lengths).astype(jnp.int32)


def strengthened(values, rng, source, target, shards_of, factor):
    owner, partner = [(jnp.arange(values.shape[position]) // (values.shape[position] // shards_of)).reshape([-1 if axis == position else 1 for axis in range(values.ndim)]) for position in (source, target)]
    chosen = jax.random.permutation(rng, shards_of)[partner]
    strong = (owner == chosen) | (owner == (partner + shards_of // 2) % shards_of)
    return jnp.where(strong, factor * values, values)


def block_scale(own_key, dims, shards, smallest, top_value):
    loudness, own = 1.0, jax.random.fold_in(own_key, 6)
    for position, shards_of in shards:
        heights = jnp.exp(jax.random.uniform(jax.random.fold_in(own, position), (shards_of,), jnp.float32, smallest / len(shards), top_value / len(shards)))
        loudness = loudness * jnp.repeat(heights, dims[position] // shards_of).reshape([-1 if axis == position else 1 for axis in range(len(dims))])
    return loudness


def noise(stream_key, extent, scale, most, shards=(), held_as=jnp.bfloat16):
    values = scale * jax.random.normal(stream_key, extent, jnp.float32)
    if shards:
        values = values * block_scale(stream_key, extent, shards, -0.22, 0.18)
    return jnp.clip(values, -most, most).astype(held_as)


def gaussian_with(rng, extent, scale, bound, cuts, heavy, kind=jnp.bfloat16):
    values = scale * jax.random.normal(rng, extent, jnp.float32)
    if cuts:
        values = values * block_scale(rng, extent, cuts, -0.22, 0.18)
    return jnp.clip(strengthened(values, jax.random.fold_in(rng, 3), *heavy), -bound, bound).astype(kind)


def setup_inputs(seed: int = 0) -> dict:
    arg_keys = jax.random.split(jax.random.key(seed), 14)
    layer_input = noise(arg_keys[0], (ROWS, SEQ, D), 1.0, 6.0, ((0, 32),))
    qkv_weight = noise(arg_keys[1], (D, 3 * D), D ** -0.5, 0.1875, ((0, 4),))
    query_value_bias = noise(arg_keys[2], (2, D), 0.3, 1.796875, ((1, 4),))
    out_weight = noise(arg_keys[3], (D, D), D ** -0.5, 0.1875, ((0, 4),))
    out_bias = noise(arg_keys[4], (D,), 0.5, 3.0, ((0, 4),))
    up_weight = noise(arg_keys[5], (D, FF), D ** -0.5, 0.1875, ((0, 4),))
    up_bias = noise(arg_keys[6], (FF,), 0.5, 3.0, ((0, 4),))
    down_weight = noise(arg_keys[7], (FF, D), FF ** -0.5, 0.09375, ((0, 4),))
    down_bias = noise(arg_keys[8], (D,), 0.5, 3.0, ((0, 4),))
    norm_gain = jnp.clip(1.0 + 0.1 * jax.random.normal(arg_keys[9], (4, D), jnp.float32), 0.5, 1.5).astype(jnp.bfloat16)
    norm_shift = noise(arg_keys[10], (4, D), 0.2, 1.1953125, ((1, 4),))
    doc_lengths = draw_doc_lengths(jax.random.fold_in(arg_keys[13], 71), 0)
    cotangent = gaussian_with(arg_keys[12], (ROWS, SEQ, D), 1.0, 6.0, ((0, 32),), (0, 2, 32, 2.75))
    return {"layer_input": layer_input, "qkv_weight": qkv_weight, "query_value_bias": query_value_bias, "out_weight": out_weight, "out_bias": out_bias, "up_weight": up_weight, "up_bias": up_bias, "down_weight": down_weight, "down_bias": down_bias, "norm_gain": norm_gain, "norm_shift": norm_shift, "doc_lengths": doc_lengths, "cotangent": cotangent}


@jax.custom_vjp
def low(v):
    return lax.optimization_barrier(v.astype(jnp.bfloat16)).astype(jnp.float32)

@jax.custom_vjp
def low_back(v):
    return v

def low_keep(v):
    return (low(v), None)

def low_pass(kept, grad):
    return (grad,)

def back_keep(v):
    return (v, None)

def back_low(kept, grad):
    return (low(grad),)
low.defvjp(low_keep, low_pass)
low_back.defvjp(back_keep, back_low)
relax_alpha = 32.0
norm_eps = 1e-05
highest = lax.Precision.HIGHEST

def product(left, right):
    return jnp.dot(left, right, precision=highest, preferred_element_type=jnp.float32)

def normalize(values, gain, shift):
    centre = values - lax.optimization_barrier(jnp.mean(values, axis=-1, keepdims=True))
    spread = lax.optimization_barrier(jnp.mean(centre * centre, axis=-1, keepdims=True))
    return centre * lax.rsqrt(spread + norm_eps) * gain + shift

def gelu_tanh(values):
    return jax.nn.gelu(values, approximate=True)

def document_ids(lengths, length):
    doc_ends = jnp.cumsum(lengths).astype(jnp.int32)
    positions = jnp.arange(length, dtype=jnp.int32)
    doc_index = lax.optimization_barrier(jnp.sum((positions[:, None] >= doc_ends[None, :]).astype(jnp.int32), axis=1)).astype(jnp.int32)
    return (doc_index, positions < doc_ends[-1])

def attend_block(query_block, offset, keys, values, doc_index):
    block_rows = query_block.shape[0]
    raw_scores = low_back(jnp.einsum('qhd,khd->hqk', query_block, keys, precision=highest))
    score_scale = 1.0 / (relax_alpha * math.sqrt(query_block.shape[-1]))
    query_pos = offset + jnp.arange(block_rows, dtype=jnp.int32)
    key_pos = jnp.arange(keys.shape[0], dtype=jnp.int32)
    query_docs = lax.dynamic_slice_in_dim(doc_index, offset, block_rows)
    allowed = (key_pos[None, :] <= query_pos[:, None]) & (query_docs[:, None] == doc_index[None, :])
    scores = jnp.where(allowed[None], raw_scores * score_scale, -1000000000.0)
    row_top = lax.optimization_barrier(jnp.max(scores, axis=-1, keepdims=True))
    exp_scores = jnp.exp(relax_alpha * (scores - row_top))
    attn_probs = exp_scores / lax.optimization_barrier(jnp.sum(exp_scores, axis=-1, keepdims=True))
    return jnp.einsum('hqk,khd->qhd', low(attn_probs), values, precision=highest)

def attention(queries, keys, values, doc_index):
    length = queries.shape[0]
    block_rows = min(512, length)
    block_count = length // block_rows
    blocks = queries.reshape(block_count, block_rows, queries.shape[1], queries.shape[2])
    offsets = jnp.arange(block_count, dtype=jnp.int32) * block_rows
    checked = jax.checkpoint(attend_block)
    result = lax.map(lambda element: checked(element[0], element[1], keys, values, doc_index), (blocks, offsets))
    return result.reshape(length, queries.shape[1] * queries.shape[2])

def layer(params, resid_in, doc_index):
    qkv_weight, query_value_bias, out_weight, out_bias, up_weight, up_bias, down_weight, down_bias, norm_gain, norm_shift = params
    length = resid_in.shape[0]
    normed_one = low(normalize(resid_in, norm_gain[0], norm_shift[0]))
    qkv_shift = jnp.concatenate([query_value_bias[0], jnp.zeros_like(query_value_bias[0]), query_value_bias[1]])
    packed = low(low_back(product(normed_one, qkv_weight) + qkv_shift))
    pieces = packed.reshape(length, 3, HEADS, HEAD_DIM)
    attended = attention(pieces[:, 0], pieces[:, 1], pieces[:, 2], doc_index)
    attended = low(low_back(attended))
    mixed_pre = low_back(product(attended, out_weight) + out_bias)
    resid_mid = resid_in + normalize(mixed_pre, norm_gain[1], norm_shift[1])
    normed_two = low(normalize(resid_mid, norm_gain[2], norm_shift[2]))
    hidden_pre = low_back(product(normed_two, up_weight) + up_bias)
    hidden_act = low(gelu_tanh(hidden_pre))
    ffn_pre = low_back(product(hidden_act, down_weight) + down_bias)
    return resid_mid + normalize(ffn_pre, norm_gain[3], norm_shift[3])

def reference(layer_input, qkv_weight, query_value_bias, out_weight, out_bias, up_weight, up_bias, down_weight, down_bias, norm_gain, norm_shift, doc_lengths, cotangent):
    params = tuple((arr.astype(jnp.float32) for arr in (qkv_weight, query_value_bias, out_weight, out_bias, up_weight, up_bias, down_weight, down_bias, norm_gain, norm_shift)))
    length = layer_input.shape[1]

    def row_step(running, element):
        row_input, lengths, row_cot = element
        doc_index, live_mask = document_ids(lengths, length)
        resid_in = row_input.astype(jnp.float32)
        result, pullback = jax.vjp(lambda weights, inputs: layer(weights, inputs, doc_index), params, resid_in)
        out_grad = row_cot.astype(jnp.float32) * live_mask[:, None].astype(jnp.float32)
        grad_params, grad_row = pullback(out_grad)
        running = jax.tree.map(jnp.add, running, grad_params)
        return (running, (result.astype(jnp.bfloat16), grad_row))
    blank_grads = jax.tree.map(jnp.zeros_like, params)
    summed, (outputs, grad_input) = lax.scan(row_step, blank_grads, (layer_input, doc_lengths, cotangent))
    return (outputs, grad_input, summed[0], summed[1], summed[2], summed[3], summed[4], summed[5], summed[6], summed[7], summed[8], summed[9])
```

```python
import functools
import math

import jax
import jax.numpy as jnp
from jax import lax
from jax.experimental import pallas as pl
from jax.experimental.pallas import tpu as pltpu
from jax.sharding import PartitionSpec as P

F32 = jnp.float32
BF = jnp.bfloat16
SDS = jax.ShapeDtypeStruct
HEAD_DIM = 64
PAIR = 2 * HEAD_DIM
EPS = 1e-05
MASKED = -1e30
QUERY_SCALE = math.log2(math.e) / math.sqrt(HEAD_DIM)
GRAD_SCALE = 1.0 / math.sqrt(HEAD_DIM)
BLOCK = 256
GELU_A = math.sqrt(2.0 / math.pi)
GELU_B = 0.044715 * GELU_A


def params(**more):
    return pltpu.CompilerParams(vmem_limit_bytes=60 * 1024 * 1024, **more)


def cost(flops, nbytes, trans=0):
    return pl.CostEstimate(flops=int(flops), bytes_accessed=int(nbytes), transcendentals=int(trans))


def dot_nn(a, b):
    return lax.dot_general(a, b, (((1,), (0,)), ((), ())), preferred_element_type=F32)


def dot_nt(a, b):
    return lax.dot_general(a, b, (((1,), (1,)), ((), ())), preferred_element_type=F32)


def dot_tn(a, b):
    return lax.dot_general(a, b, (((0,), (0,)), ((), ())), preferred_element_type=F32)


def centred(values):
    centre = values - jnp.mean(values, axis=-1, keepdims=True)
    rstd = lax.rsqrt(jnp.mean(centre * centre, axis=-1, keepdims=True) + EPS)
    return centre * rstd, rstd


def norm_back(grad, vhat, rstd, gain):
    e = grad * gain
    mean_e = jnp.mean(e, axis=-1, keepdims=True)
    mean_ev = jnp.mean(e * vhat, axis=-1, keepdims=True)
    return (e - mean_e - vhat * mean_ev) * rstd


def col_sum(values):
    return jnp.sum(values, axis=0, keepdims=True)


def qkv_kernel(x_ref, w_ref, bias_ref, gain_ref, shift_ref, normed_ref, packed_ref):
    step = pl.program_id(0)

    @pl.when(step == 0)
    def _():
        vhat, _ = centred(x_ref[...].astype(F32))
        normed_ref[...] = (vhat * gain_ref[...] + shift_ref[...]).astype(BF)

    out = dot_nn(normed_ref[...], w_ref[...]) + bias_ref[...]
    is_query = step < pl.num_programs(0) // 3
    packed_ref[...] = (out * jnp.where(is_query, QUERY_SCALE, 1.0)).astype(BF)


def qkv_forward(x, weight, bias, gain, shift):
    tokens, width = x.shape
    cols = weight.shape[1]
    bn = width // 2
    row = pl.BlockSpec((1, width), lambda j: (0, 0))
    full = pl.BlockSpec((tokens, width), lambda j: (0, 0))
    return pl.pallas_call(
        qkv_kernel,
        grid=(cols // bn,),
        in_specs=[
            full,
            pl.BlockSpec((width, bn), lambda j: (0, j)),
            pl.BlockSpec((1, bn), lambda j: (0, j)),
            row,
            row,
        ],
        out_specs=(full, pl.BlockSpec((tokens, bn), lambda j: (0, j))),
        out_shape=(SDS((tokens, width), BF), SDS((tokens, cols), BF)),
        compiler_params=params(),
        cost_estimate=cost(2 * tokens * width * cols, 2 * width * cols + 2 * tokens * cols),
        name="qkv_forward",
    )(x, weight, bias, gain, shift)


def out_kernel(att_ref, x_ref, w_ref, bias_ref, gain_ref, shift_ref, mixed_ref, mid_ref, two_ref):
    mixed = dot_nn(att_ref[...], w_ref[...]) + bias_ref[...]
    mixed_ref[...] = mixed
    vhat, _ = centred(mixed)
    mid = x_ref[...].astype(F32) + vhat * gain_ref[1:2, :] + shift_ref[1:2, :]
    mid_ref[...] = mid
    vhat, _ = centred(mid)
    two_ref[...] = (vhat * gain_ref[2:3, :] + shift_ref[2:3, :]).astype(BF)


def out_forward(attended, x, weight, bias, gain, shift):
    tokens, width = x.shape
    tok = pl.BlockSpec((BLOCK, width), lambda i: (i, 0))

    def whole(arr):
        return pl.BlockSpec(arr.shape, lambda i: (0, 0))

    return pl.pallas_call(
        out_kernel,
        grid=(tokens // BLOCK,),
        in_specs=[tok, tok, whole(weight), whole(bias), whole(gain), whole(shift)],
        out_specs=(tok, tok, tok),
        out_shape=(SDS((tokens, width), F32), SDS((tokens, width), F32), SDS((tokens, width), BF)),
        compiler_params=params(),
        cost_estimate=cost(2 * tokens * width * width, 16 * tokens * width),
        name="out_forward",
    )(attended, x, weight, bias, gain, shift)


def up_kernel(two_ref, w_ref, bias_ref, act_ref, slope_ref):
    a = dot_nn(two_ref[...], w_ref[...]) + bias_ref[...]
    sq = a * a
    t = jnp.tanh(a * (sq * GELU_B + GELU_A))
    half = 0.5 * t + 0.5
    act = a * half
    act_ref[...] = act.astype(BF)
    slope = half + act * ((1.0 - half) * (sq * (6.0 * GELU_B) + 2.0 * GELU_A))
    slope_ref[...] = slope.astype(BF)


def up_forward(two, weight, bias):
    tokens, width = two.shape
    cols = weight.shape[1]
    bn = 512
    blk = pl.BlockSpec((tokens, bn), lambda j: (0, j))
    return pl.pallas_call(
        up_kernel,
        grid=(cols // bn,),
        in_specs=[
            pl.BlockSpec((tokens, width), lambda j: (0, 0)),
            pl.BlockSpec((width, bn), lambda j: (0, j)),
            pl.BlockSpec((1, bn), lambda j: (0, j)),
        ],
        out_specs=(blk, blk),
        out_shape=(SDS((tokens, cols), BF), SDS((tokens, cols), BF)),
        compiler_params=params(),
        cost_estimate=cost(2 * tokens * width * cols, 2 * width * cols + 4 * tokens * cols),
        name="up_forward",
    )(two, weight, bias)


def down_kernel(
    act_ref, w_ref, bias_ref, mid_ref, cot_ref, live_ref, gain_ref, shift_ref, out_ref, grad_ref, sums_ref
):
    @pl.when(pl.program_id(0) == 0)
    def _():
        sums_ref[...] = jnp.zeros_like(sums_ref)

    ffn = dot_nn(act_ref[...], w_ref[...]) + bias_ref[...]
    vhat, rstd = centred(ffn)
    gain = gain_ref[3:4, :]
    out_ref[...] = (mid_ref[...] + vhat * gain + shift_ref[3:4, :]).astype(BF)
    grad = cot_ref[...].astype(F32) * live_ref[...]
    low = norm_back(grad, vhat, rstd, gain).astype(BF)
    grad_ref[...] = low
    sums_ref[0:1, :] += col_sum(grad * vhat)
    sums_ref[1:2, :] += col_sum(grad)
    sums_ref[2:3, :] += col_sum(low.astype(F32))


def down_forward(act, weight, bias, mid, cot, live, gain, shift):
    tokens, width = mid.shape
    cols = act.shape[1]
    tok = pl.BlockSpec((BLOCK, width), lambda i: (i, 0))

    def whole(arr):
        return pl.BlockSpec(arr.shape, lambda i: (0, 0))

    return pl.pallas_call(
        down_kernel,
        grid=(tokens // BLOCK,),
        in_specs=[
            pl.BlockSpec((BLOCK, cols), lambda i: (i, 0)),
            whole(weight),
            whole(bias),
            tok,
            tok,
            pl.BlockSpec((BLOCK, 1), lambda i: (i, 0)),
            whole(gain),
            whole(shift),
        ],
        out_specs=(tok, tok, pl.BlockSpec((8, width), lambda i: (0, 0))),
        out_shape=(SDS((tokens, width), BF), SDS((tokens, width), BF), SDS((8, width), F32)),
        compiler_params=params(),
        cost_estimate=cost(2 * tokens * width * cols, 2 * width * cols + 2 * tokens * cols),
        name="down_forward",
    )(act, weight, bias, mid, cot, live, gain, shift)


def hidden_kernel(grad_ref, w_ref, slope_ref, out_ref, sum_ref):
    low = (dot_nt(grad_ref[...], w_ref[...]) * slope_ref[...].astype(F32)).astype(BF)
    out_ref[...] = low
    sum_ref[...] = col_sum(low.astype(F32))


def hidden_backward(grad, weight, slope):
    tokens, width = grad.shape
    cols = weight.shape[0]
    bn = 512
    blk = pl.BlockSpec((tokens, bn), lambda j: (0, j))
    return pl.pallas_call(
        hidden_kernel,
        grid=(cols // bn,),
        in_specs=[
            pl.BlockSpec((tokens, width), lambda j: (0, 0)),
            pl.BlockSpec((bn, width), lambda j: (j, 0)),
            blk,
        ],
        out_specs=(blk, pl.BlockSpec((1, bn), lambda j: (0, j))),
        out_shape=(SDS((tokens, cols), BF), SDS((1, cols), F32)),
        compiler_params=params(),
        cost_estimate=cost(2 * tokens * width * cols, 2 * width * cols + 4 * tokens * cols),
        name="hidden_backward",
    )(grad, weight, slope)


def mid_kernel(
    gh_ref, up_ref, out_w_ref, mid_ref, mixed_ref, cot_ref, live_ref, gain_ref,
    gmid_ref, gmix_ref, gatt_ref, sums_ref,
):
    @pl.when(pl.program_id(0) == 0)
    def _():
        sums_ref[...] = jnp.zeros_like(sums_ref)

    grad = dot_nt(gh_ref[...], up_ref[...])
    vhat, rstd = centred(mid_ref[...])
    sums_ref[0:1, :] += col_sum(grad * vhat)
    sums_ref[1:2, :] += col_sum(grad)
    gmid = cot_ref[...].astype(F32) * live_ref[...] + norm_back(grad, vhat, rstd, gain_ref[2:3, :])
    gmid_ref[...] = gmid
    vhat, rstd = centred(mixed_ref[...])
    sums_ref[2:3, :] += col_sum(gmid * vhat)
    sums_ref[3:4, :] += col_sum(gmid)
    low = norm_back(gmid, vhat, rstd, gain_ref[1:2, :]).astype(BF)
    gmix_ref[...] = low
    sums_ref[4:5, :] += col_sum(low.astype(F32))
    gatt_ref[...] = dot_nt(low, out_w_ref[...]).astype(BF)


def mid_backward(gh, up, out_w, mid, mixed, cot, live, gain):
    tokens, width = mid.shape
    cols = gh.shape[1]
    tok = pl.BlockSpec((BLOCK, width), lambda i: (i, 0))

    def whole(arr):
        return pl.BlockSpec(arr.shape, lambda i: (0, 0))

    return pl.pallas_call(
        mid_kernel,
        grid=(tokens // BLOCK,),
        in_specs=[
            pl.BlockSpec((BLOCK, cols), lambda i: (i, 0)),
            whole(up),
            whole(out_w),
            tok,
            tok,
            tok,
            pl.BlockSpec((BLOCK, 1), lambda i: (i, 0)),
            whole(gain),
        ],
        out_specs=(tok, tok, tok, pl.BlockSpec((8, width), lambda i: (0, 0))),
        out_shape=(
            SDS((tokens, width), F32),
            SDS((tokens, width), BF),
            SDS((tokens, width), BF),
            SDS((8, width), F32),
        ),
        compiler_params=params(),
        cost_estimate=cost(2 * tokens * width * (cols + width), 2 * width * cols + 2 * tokens * cols),
        name="mid_backward",
    )(gh, up, out_w, mid, mixed, cot, live, gain)


def input_kernel(n_grads, *refs):
    grad_refs, (w_ref, x_ref, gmid_ref, gain_ref, out_ref, sums_ref) = refs[:n_grads], refs[n_grads:]

    @pl.when(pl.program_id(0) == 0)
    def _():
        sums_ref[...] = jnp.zeros_like(sums_ref)

    grads = jnp.concatenate([ref[...] for ref in grad_refs], axis=1)
    grad = dot_nt(grads, w_ref[...])
    vhat, rstd = centred(x_ref[...].astype(F32))
    sums_ref[0:1, :] += col_sum(grad * vhat)
    sums_ref[1:2, :] += col_sum(grad)
    out_ref[...] = gmid_ref[...] + norm_back(grad, vhat, rstd, gain_ref[0:1, :])


def input_backward(grads, weight, x, gmid, gain):
    tokens, width = x.shape
    tok = pl.BlockSpec((BLOCK, width), lambda i: (i, 0))

    def whole(arr):
        return pl.BlockSpec(arr.shape, lambda i: (0, 0))

    return pl.pallas_call(
        functools.partial(input_kernel, len(grads)),
        grid=(tokens // BLOCK,),
        in_specs=[pl.BlockSpec((BLOCK, g.shape[1]), lambda i: (i, 0)) for g in grads]
        + [whole(weight), tok, tok, whole(gain)],
        out_specs=(tok, pl.BlockSpec((8, width), lambda i: (0, 0))),
        out_shape=(SDS((tokens, width), F32), SDS((8, width), F32)),
        compiler_params=params(),
        cost_estimate=cost(6 * tokens * width * width, 6 * width * width + 14 * tokens * width),
        name="input_backward",
    )(*grads, weight, x, gmid, gain)


def fill_bias(bias, start_ref):
    length = bias.shape[0]
    for j in range(length // BLOCK):
        key = lax.broadcasted_iota(jnp.int32, (BLOCK, length), 0) + j * BLOCK
        query = lax.broadcasted_iota(jnp.int32, (BLOCK, length), 1)
        allowed = (key <= query) & (key >= start_ref[...])
        bias[j * BLOCK : (j + 1) * BLOCK, :] = jnp.where(allowed, 0.0, MASKED)


def one_head(low, arr, head):
    zero = jnp.zeros_like(arr)
    return jnp.where(low, arr, zero) if head == 0 else jnp.where(low, zero, arr)


def attend_kernel(q_ref, k_ref, v_ref, start_ref, out_ref, lse_ref, bias):
    length = q_ref.shape[0]

    @pl.when(pl.program_id(0) == 0)
    def _():
        fill_bias(bias, start_ref)

    low = lax.broadcasted_iota(jnp.int32, (1, PAIR), 1) < HEAD_DIM
    low_rows = lax.broadcasted_iota(jnp.int32, (PAIR, 1), 0) < HEAD_DIM
    keys = k_ref[...]
    values = jnp.concatenate([v_ref[...], jnp.ones((length, PAIR), BF)], axis=1)
    for i in range(length // BLOCK):
        reach = (i + 1) * BLOCK
        sl = slice(i * BLOCK, reach)
        queries = q_ref[sl, :]
        parts = []
        for head in range(2):
            scores = dot_nt(keys[:reach], one_head(low, queries, head)) + bias[:reach, sl]
            top = jnp.max(scores, axis=0, keepdims=True)
            probs = jnp.exp2(scores - top).astype(BF)
            mixed = dot_tn(values[:reach], probs)
            total = mixed[PAIR : PAIR + 1]
            parts.append(mixed[:PAIR] / total)
            lse_ref[0, head : head + 1, sl] = top + jnp.log2(total)
        out_ref[sl, :] = jnp.where(low_rows, parts[0], parts[1]).T.astype(BF)


def attend(packed, start_row):
    length = packed.shape[0]
    pairs = packed.shape[1] // (3 * PAIR)

    def blk(offset):
        return pl.BlockSpec((length, PAIR), lambda h: (0, offset + h))

    return pl.pallas_call(
        attend_kernel,
        grid=(pairs,),
        in_specs=[blk(0), blk(pairs), blk(2 * pairs), pl.BlockSpec((1, length), lambda h: (0, 0))],
        out_specs=(blk(0), pl.BlockSpec((1, 2, length), lambda h: (h, 0, 0))),
        out_shape=(SDS((length, PAIR * pairs), BF), SDS((pairs, 2, length), F32)),
        scratch_shapes=[pltpu.VMEM((length, length), F32)],
        compiler_params=params(),
        cost_estimate=cost(8 * pairs * length * length * PAIR, 8 * length * pairs * PAIR),
        name="attend",
    )(packed, packed, packed, start_row)


def attend_back_kernel(
    q_ref, k_ref, v_ref, g_ref, o_ref, lse_ref, start_ref, gq_ref, gk_ref, gv_ref, sq_ref, sv_ref, bias, acc
):
    length = q_ref.shape[0]

    @pl.when(pl.program_id(0) == 0)
    def _():
        fill_bias(bias, start_ref)

    low = lax.broadcasted_iota(jnp.int32, (1, PAIR), 1) < HEAD_DIM
    queries, grads = q_ref[...], g_ref[...]
    q_of = [one_head(low, queries, head) for head in range(2)]
    g_of = [one_head(low, grads, head) for head in range(2)]
    inner = (grads.astype(F32) * o_ref[...].astype(F32)).T
    inner_of = [col_sum(inner[:HEAD_DIM]), col_sum(inner[HEAD_DIM:])]
    sum_v = jnp.zeros((1, PAIR), F32)
    for j in range(length // BLOCK):
        first = j * BLOCK
        sl = slice(first, first + BLOCK)
        keys, values = k_ref[sl, :], v_ref[sl, :]
        gk = gv = gq = 0.0
        for head in range(2):
            scores = dot_nt(keys, q_of[head][first:]) + bias[sl, first:]
            probs = jnp.exp2(scores - lse_ref[0, head : head + 1, first:])
            gprobs = dot_nt(values, g_of[head][first:])
            gscores = (probs * (gprobs - inner_of[head][:, first:]) * GRAD_SCALE).astype(BF)
            gv = gv + dot_nn(probs.astype(BF), g_of[head][first:])
            gk = gk + dot_nn(gscores, q_of[head][first:])
            gq = gq + dot_tn(gscores, one_head(low, keys, head))
        low_v = gv.astype(BF)
        gv_ref[sl, :] = low_v
        gk_ref[sl, :] = (gk * (1.0 / QUERY_SCALE)).astype(BF)
        sum_v = sum_v + col_sum(low_v.astype(F32))
        if j == 0:
            acc[...] = gq
        else:
            acc[first:, :] += gq
    low_q = acc[...].astype(BF)
    gq_ref[...] = low_q
    sq_ref[...] = col_sum(low_q.astype(F32))
    sv_ref[...] = sum_v


def attend_back(packed, grads, attended, lse, start_row, part, parts):
    length = packed.shape[0]
    total = packed.shape[1] // (3 * PAIR)
    pairs = total // parts
    skip = part * pairs

    def blk(offset):
        return pl.BlockSpec((length, PAIR), lambda h: (0, offset + h))

    row = pl.BlockSpec((1, PAIR), lambda h: (0, h))
    grad = SDS((length, PAIR * pairs), BF)
    sums = SDS((1, PAIR * pairs), F32)
    return pl.pallas_call(
        attend_back_kernel,
        grid=(pairs,),
        in_specs=[
            blk(skip),
            blk(total + skip),
            blk(2 * total + skip),
            blk(skip),
            blk(skip),
            pl.BlockSpec((1, 2, length), lambda h: (skip + h, 0, 0)),
            pl.BlockSpec((1, length), lambda h: (0, 0)),
        ],
        out_specs=(blk(0), blk(0), blk(0), row, row),
        out_shape=(grad, grad, grad, sums, sums),
        scratch_shapes=[pltpu.VMEM((length, length), F32), pltpu.VMEM((length, PAIR), F32)],
        compiler_params=params(),
        cost_estimate=cost(20 * pairs * length * length * PAIR, 16 * length * pairs * PAIR),
        name="attend_back",
    )(packed, packed, packed, grads, attended, lse, start_row)


def swap(arr, axis, mask):
    size = lax.axis_size(axis)
    return lax.ppermute(arr, axis, [(i, i ^ mask) for i in range(size)])


def after(first, then):
    return lax.optimization_barrier((first, then))


def shard_swaps(piece):
    return [swap(piece, "fsdp", k) for k in range(1, lax.axis_size("fsdp"))]


def plane_swaps(got, order):
    first, second = order
    own = jnp.stack(got)
    two = jnp.concatenate([own, swap(own, "dp", first)])
    four = swap(two, "dp", second)
    return [
        ((0, first), two),
        ((second, second ^ first), four),
        ((1, 1 ^ first), swap(two, "dp", 1)),
        ((1 ^ second, 1 ^ second ^ first), swap(four, "dp", 1)),
    ]


def place_kernel(layout, masks, shards, n_own, idx_ref, *refs):
    n_out = len(layout)
    owns = refs[:n_own]
    slots = refs[n_own : n_own + len(masks)]
    outs = refs[n_own + len(masks) : -1]
    sems = refs[-1]
    dp, z = idx_ref[0], idx_ref[1]
    copies = []

    def start(src, dst):
        copy = pltpu.make_async_copy(src, dst, sems.at[len(copies)])
        copy.start()
        copies.append(copy)

    for o in range(n_out):
        rows = owns[o].shape[0]
        start(owns[o], outs[o].at[pl.ds(pl.multiple_of(z * rows, rows), rows), :])
    for pair, ref in zip(masks, slots):
        for which, mask in enumerate(pair):
            for k in range(1, shards):
                at = which * (shards - 1) + k - 1
                for o, (c0, c1) in enumerate(layout):
                    shard_rows = owns[o].shape[0]
                    rows = ref.shape[1]
                    dst = pl.multiple_of((z ^ k) * shard_rows + (dp ^ mask) * rows, rows)
                    src = ref.at[at] if n_out == 1 else ref.at[at, :, c0:c1]
                    start(src, outs[o].at[pl.ds(dst, rows), :])
    for copy in copies:
        copy.wait()


def place(idx, owns, flow, layout, shards):
    masks = [m for m, _ in flow]
    slots = [a for _, a in flow]
    any_spec = pl.BlockSpec(memory_space=pl.ANY)
    n_copies = len(owns) * (1 + 2 * (shards - 1) * len(slots))
    outs = tuple(SDS((o.shape[0] * shards, o.shape[1]), BF) for o in owns)
    nbytes = sum(2 * 2 * math.prod(o.shape) for o in outs)
    return pl.pallas_call(
        functools.partial(place_kernel, layout, masks, shards, len(owns)),
        in_specs=[pl.BlockSpec(memory_space=pltpu.SMEM)] + [any_spec] * (len(owns) + len(slots)),
        out_specs=(pl.BlockSpec(memory_space=pltpu.VMEM),) * len(owns),
        out_shape=outs,
        scratch_shapes=[pltpu.SemaphoreType.DMA((n_copies,))],
        compiler_params=params(),
        cost_estimate=cost(0, nbytes),
        name="place",
    )(idx, *owns, *slots)


def split_down(refs, zz):
    (wide,) = refs
    rows, cols = wide.shape[0] // 4, wide.shape[1] // 2
    part = wide[zz * rows : (zz + 1) * rows]
    return part[:, :cols], part[:, cols:]


def split_up(refs, zz):
    (wide,) = refs
    rows = wide.shape[0] // 8
    return wide[2 * zz * rows : (2 * zz + 1) * rows], wide[(2 * zz + 1) * rows : (2 * zz + 2) * rows]


def split_rows(refs, zz):
    rows = refs[0].shape[0] // 4
    return (jnp.concatenate([r[zz * rows : (zz + 1) * rows] for r in refs], axis=1),)


def grad_kernel(keep, groups, split, first, idx_ref, *refs):
    step = pl.program_id(0)
    z = idx_ref[1]
    at, dots = 0, []
    for n_left, n_right in groups:
        left = [r[...] for r in refs[at : at + n_left]]
        right = [r[...] for r in refs[at + n_left : at + n_left + n_right]]
        at += n_left + n_right
        left = left[0] if n_left == 1 else jnp.concatenate(left, axis=1)
        right = right[0] if n_right == 1 else jnp.concatenate(right, axis=1)
        dots.append(dot_tn(left, right))
    rest = refs[at:]
    if not keep:
        for zz in range(4):
            for f, part in enumerate(split(dots, zz)):
                rest[0][0, zz ^ z, f] = part.astype(BF)
        return
    got_ref, outs = rest[0], rest[1:]
    for dst in range(4):

        @pl.when(step == dst)
        def _():
            for zz in range(4):
                slot = zz ^ z
                for f, part in enumerate(split(dots, zz)):
                    bit = dst // 2 if first[f] == 4 else dst % 2
                    low = (part + got_ref[0, slot, f].astype(F32)).astype(BF)
                    outs[2 * f + bit][0, slot] = low


def grad_call(name, idx, specs, args, groups, split, first, piece, flops, got=None):
    keep = got is not None
    flows, rows, cols = piece
    block = pl.BlockSpec((1, 4) + piece, lambda i, idx: (i, 0, 0, 0, 0))
    half = (1, 4, rows, cols)
    if keep:
        maps = {
            4: (lambda i, idx: (jnp.minimum(i, 1), 0, 0, 0), lambda i, idx: (jnp.maximum(i - 2, 0), 0, 0, 0)),
            2: (lambda i, idx: (i // 2, 0, 0, 0), lambda i, idx: (i // 2, 0, 0, 0)),
        }
        specs = specs + [block]
        args = args + [got]
        out_specs = tuple(pl.BlockSpec(half, m) for mask in first for m in maps[mask])
        out_shape = (SDS((2, 4, rows, cols), BF),) * (2 * flows)
    else:
        out_specs = block
        out_shape = SDS((4, 4) + piece, BF)
    return pl.pallas_call(
        functools.partial(grad_kernel, keep, groups, split, first),
        grid_spec=pltpu.PrefetchScalarGridSpec(
            num_scalar_prefetch=1, grid=(4,), in_specs=specs, out_specs=out_specs
        ),
        out_shape=out_shape,
        compiler_params=params(),
        cost_estimate=cost(flops, flops // 400),
        name=name + ("_keep" if keep else "_send"),
    )(idx, *args)


def chip_of(i, idx):
    return (idx[0] // 2) ^ (3 - i)


def core_of(keep, idx):
    return idx[0] & 1 if keep else (idx[0] & 1) ^ 1


def grad_down(idx, act, grad, got=None):
    tokens, width = grad.shape
    keep = got is not None
    rows = act.shape[1] // 32

    def block(zz):
        return pl.BlockSpec(
            (tokens, rows), lambda i, idx: (0, zz * 8 + chip_of(i, idx) * 2 + core_of(keep, idx))
        )

    specs = [block(0), block(1), block(2), block(3), pl.BlockSpec((tokens, width), lambda i, idx: (0, 0))]
    args = [act, act, act, act, grad]
    flops = act.shape[1] * width * tokens
    piece = (2, rows, width // 2)
    return grad_call(
        "grad_down", idx, specs, args, [(4, 1)], split_down, (4, 2), piece, flops, got
    )


def grad_up(idx, two, grad, got=None):
    tokens, width = two.shape
    keep = got is not None
    cols = grad.shape[1] // 8
    specs = [
        pl.BlockSpec((tokens, width), lambda i, idx: (0, 0)),
        pl.BlockSpec((tokens, cols), lambda i, idx: (0, chip_of(i, idx) * 2 + core_of(keep, idx))),
    ]
    flops = grad.shape[1] * width * tokens
    piece = (2, width // 8, cols)
    return grad_call("grad_up", idx, specs, [two, grad], [(1, 1)], split_up, (4, 2), piece, flops, got)


def grad_heads(idx, first, one, gq, gk, gv, att=None, gmix=None, got=None):
    tokens, width = one.shape
    keep = got is not None
    rows = width // 8

    def left(zz):
        return pl.BlockSpec((tokens, rows), lambda i, idx: (0, zz * 2 + core_of(keep, idx)))

    def right(cols):
        return pl.BlockSpec((tokens, cols), lambda i, idx: (0, chip_of(i, idx)))

    lefts = [left(0), left(1), left(2), left(3)]
    specs, args, groups = lefts + [right(PAIR)] * 3, [one] * 4 + [gq, gk, gv], [(4, 3)]
    cols = 3 * PAIR
    if att is not None:
        specs, args, groups = specs + lefts + [right(width // 4)], args + [att] * 4 + [gmix], groups + [(4, 1)]
        cols += width // 4
    piece = (1, rows, cols)
    flops = 4 * tokens * width * cols
    return grad_call("grad_heads", idx, specs, args, groups, split_rows, (first,), piece, flops, got)


def add_low(a, b):
    return (a.astype(F32) + b.astype(F32)).astype(BF)


def add_wide(a, b):
    return a.astype(F32) + b.astype(F32)


def plane_first(parts, first):
    return [swap(parts[2 * f], "dp", mask) for f, mask in enumerate(first)]


def plane_second(parts, got, first):
    send = [add_low(parts[2 * f + 1][0], got[f][0]) for f in range(len(first))]
    keep = [add_low(parts[2 * f + 1][1], got[f][1]) for f in range(len(first))]
    return keep, [swap(s, "dp", 6 - mask) for s, mask in zip(send, first)]


def across(keep, got):
    both = jnp.stack([add_wide(k, g) for k, g in zip(keep, got)], axis=1)
    back = swap(both[1::2].astype(BF), "fsdp", 1)
    both = add_wide(both[0::2], back)
    back = swap(both[1].astype(BF), "fsdp", 2)
    return add_low(both[0], back)


def spread(piece, first):
    second = 6 - first
    two = jnp.stack([piece, swap(piece, "dp", first)])
    four = swap(two, "dp", second)
    return [
        ((0, first), two),
        ((second, 6), four),
        ((1, 1 ^ first), swap(two, "dp", 1)),
        ((1 ^ second, 7), swap(four, "dp", 1)),
    ]


def place_down(dp, piece, outs):
    (out,) = outs
    rows, cols = piece.shape[1], piece.shape[2]
    at = pl.ds(pl.multiple_of(dp * rows, rows), rows)
    out[at, :cols] = piece[0].astype(F32)
    out[at, cols:] = piece[1].astype(F32)


def place_up(dp, piece, outs):
    (out,) = outs
    rows, cols = piece.shape[1], piece.shape[2]
    at = pl.ds(pl.multiple_of(dp * cols, cols), cols)
    out[:rows, at] = piece[0].astype(F32)
    out[rows:, at] = piece[1].astype(F32)


def place_heads(half, dp, piece, outs):
    rows = piece.shape[1]
    chip, core = dp // 2, dp % 2
    at_rows = pl.ds(pl.multiple_of(core * rows, rows), rows)
    width = outs[0].shape[1] // 3
    for part in range(3):
        at = pl.multiple_of(part * width + half * (width // 2) + chip * PAIR, PAIR)
        outs[0][at_rows, pl.ds(at, PAIR)] = piece[0, :, part * PAIR : (part + 1) * PAIR].astype(F32)
    if half == 0:
        cols = width // 4
        at = pl.multiple_of(chip * cols, cols)
        outs[1][at_rows, pl.ds(at, cols)] = piece[0, :, 3 * PAIR :].astype(F32)


def finish_kernel(placers, masks, idx_ref, *refs):
    n_in = sum(len(m) for m in masks)
    ins, outs = list(refs[:n_in]), refs[n_in:]
    for placer, pairs in zip(placers, masks):
        for pair in pairs:
            ref = ins.pop(0)
            for which, mask in enumerate(pair):
                placer(idx_ref[0] ^ mask, ref[which], outs)


def finish(name, idx, placers, pieces, shapes):
    masks = [[m for m, _ in p] for p in pieces]
    arrays = [a for p in pieces for _, a in p]
    vmem = pl.BlockSpec(memory_space=pltpu.VMEM)
    return pl.pallas_call(
        functools.partial(finish_kernel, placers, masks),
        in_specs=[pl.BlockSpec(memory_space=pltpu.SMEM)] + [vmem] * len(arrays),
        out_specs=(vmem,) * len(shapes),
        out_shape=tuple(SDS(s, F32) for s in shapes),
        compiler_params=params(),
        cost_estimate=cost(0, sum(6 * math.prod(s) for s in shapes)),
        name=name,
    )(idx, *arrays)


def segment_starts(lengths, length):
    ends = jnp.cumsum(lengths)
    positions = jnp.arange(length, dtype=jnp.int32)
    begun = jnp.where(ends[None, :] <= positions[:, None], ends[None, :], 0)
    return jnp.max(begun, axis=1).astype(jnp.int32), positions < ends[-1]


def eighth(shard):
    rows = shard.shape[0] // 8
    return lax.dynamic_slice_in_dim(shard, lax.axis_index("dp") * rows, rows, axis=0)


SMALL_ROWS = 16


def pack_small(qv_bias, out_bias, up_bias, down_bias, gain, shift):
    flat = [a.reshape(-1) for a in (qv_bias, out_bias, up_bias, down_bias, gain, shift)]
    return jnp.concatenate(flat)


def unpack_small(shards):
    count, total = shards.shape
    unit = total // SMALL_ROWS
    sizes = ((2, unit), (1, unit), (1, 4 * unit), (1, unit), (4, unit), (4, unit))
    out, at = [], 0
    for lead, cols in sizes:
        block = shards[:, at : at + lead * cols].reshape(count, lead, cols)
        out.append(jnp.swapaxes(block, 0, 1).reshape(lead, count * cols))
        at += lead * cols
    return out


def by_shard(rows, count):
    flat = []
    for arr in rows:
        lead, cols = arr.shape
        flat.append(
            jnp.swapaxes(arr.reshape(lead, count, cols // count), 0, 1).reshape(count, -1)
        )
    return jnp.concatenate(flat, axis=1)


def gather_small(own, got):
    z = lax.axis_index("fsdp")
    slots = jnp.stack([own] + got)
    low, high = z % 2, z // 2
    slots = jnp.where(low == 0, slots, slots[jnp.array([1, 0, 3, 2])])
    return jnp.where(high == 0, slots, slots[jnp.array([2, 3, 0, 1])])


def on_device(
    layer_input,
    qkv_weight,
    query_value_bias,
    out_weight,
    out_bias,
    up_weight,
    up_bias,
    down_weight,
    down_bias,
    norm_gain,
    norm_shift,
    doc_lengths,
    cotangent,
):
    _, tokens, width = layer_input.shape
    shards = lax.axis_size("fsdp")
    halves = shards == 4 and lax.axis_size("dp") == 8
    idx = jnp.stack([lax.axis_index("dp"), lax.axis_index("fsdp")]).astype(jnp.int32)
    x = layer_input[0]
    cot = cotangent[0]
    start, live = segment_starts(doc_lengths[0], tokens)
    start_row = start[None, :]
    live_col = live.astype(F32)[:, None]
    small_own = pack_small(query_value_bias, out_bias, up_bias, down_bias, norm_gain, norm_shift)
    if halves:
        piece = eighth(qkv_weight)
        cols = piece.shape[1]
        extra = small_own.reshape(piece.shape[0], -1)
        got_q = shard_swaps(jnp.concatenate([piece, extra], axis=1))
        piece_u = jnp.concatenate([eighth(out_weight), eighth(up_weight)], axis=1)
        got_q, piece_u = after(got_q, piece_u)
        small = gather_small(small_own, [g[:, cols:].reshape(-1) for g in got_q])
        flow_q = plane_swaps([g[:, :cols] for g in got_q], (4, 2))
        got_u = shard_swaps(piece_u)
        got_u, piece_d = after(got_u, eighth(down_weight))
        got_d = shard_swaps(piece_d)
        (w_qkv,) = place(idx, [qkv_weight], flow_q, [(0, cols)], shards)
        flow_u = plane_swaps(got_u, (4, 2))
        w_out, w_up = place(
            idx, [out_weight, up_weight], flow_u, [(0, width), (width, piece_u.shape[1])], shards
        )
        flow_d = plane_swaps(got_d, (2, 4))
        (w_down,) = place(idx, [down_weight], flow_d, [(0, width)], shards)
    else:
        small = lax.all_gather(small_own, "fsdp", axis=0)
        w_qkv = lax.all_gather(qkv_weight, "fsdp", axis=0, tiled=True)
        w_out = lax.all_gather(out_weight, "fsdp", axis=0, tiled=True)
        w_up = lax.all_gather(up_weight, "fsdp", axis=0, tiled=True)
        w_down = lax.all_gather(down_weight, "fsdp", axis=0, tiled=True)
    qv_b, out_b, up_b, down_b, gain, shift = unpack_small(small.astype(F32))
    qkv_b = jnp.concatenate([qv_b[0:1], jnp.zeros((1, width), F32), qv_b[1:2]], axis=1)

    normed_one, packed = qkv_forward(x, w_qkv, qkv_b, gain[0:1], shift[0:1])
    attended, lse = attend(packed, start_row)
    mixed, mid, two = out_forward(attended, x, w_out, out_b, gain, shift)
    act, slope = up_forward(two, w_up, up_b)
    layer_out, gffn, sums3 = down_forward(act, w_down, down_b, mid, cot, live_col, gain, shift)

    both = (4, 2)
    if halves:
        send = grad_down(idx, act, gffn)
        got_down = swap(send, "dp", 1)
        _, gffn = after(send, gffn)
    ghid, up_sum = hidden_backward(gffn, w_down, slope)
    if halves:
        got_down, act, ghid = lax.optimization_barrier((got_down, act, ghid))
        down_parts = grad_down(idx, act, gffn, got_down)
        down_got = plane_first(down_parts, both)
        down_parts, ghid = after(down_parts, ghid)
        send = grad_up(idx, two, ghid)
        got_up = swap(send, "dp", 1)
        _, ghid = after(send, ghid)
    gmid, gmix, gatt, sums21 = mid_backward(ghid, w_up, w_out, mid, mixed, cot, live_col, gain)
    if halves:
        down_got, gatt = after(down_got, gatt)
        down_keep, down_got = plane_second(down_parts, down_got, both)
        got_up, ghid = after(got_up, ghid)
        up_parts = grad_up(idx, two, ghid, got_up)
        up_got = plane_first(up_parts, both)
        up_parts, down_keep, gatt = lax.optimization_barrier((up_parts, down_keep, gatt))
    gq0, gk0, gv0, sq0, sv0 = attend_back(packed, gatt, attended, lse, start_row, 0, 2)
    if halves:
        send = grad_heads(idx, 4, normed_one, gq0, gk0, gv0, attended, gmix)
        got_heads = swap(send, "dp", 1)
        up_got, down_got, send, gatt = lax.optimization_barrier((up_got, down_got, send, gatt))
        up_keep, up_got = plane_second(up_parts, up_got, both)
        down_piece = across(down_keep, down_got)
    gq1, gk1, gv1, sq1, sv1 = attend_back(packed, gatt, attended, lse, start_row, 1, 2)
    if halves:
        got_heads, gq1 = after(got_heads, gq1)
        heads_parts = grad_heads(idx, 4, normed_one, gq0, gk0, gv0, attended, gmix, got_heads)
        heads_got = plane_first(heads_parts, (4,))
        send = grad_heads(idx, 2, normed_one, gq1, gk1, gv1)
        got_last = swap(send, "dp", 1)
        up_piece = across(up_keep, up_got)
        down_all = spread(down_piece, 4)
        last_parts = grad_heads(idx, 2, normed_one, gq1, gk1, gv1, got=got_last)
        last_got = plane_first(last_parts, (2,))
        last_parts, gq1 = after(last_parts, gq1)
    grad_input, sums0 = input_backward([gq0, gq1, gk0, gk1, gv0, gv1], w_qkv, x, gmid, gain)
    small_grads = by_shard(
        [
            jnp.concatenate([jnp.concatenate([sq0, sq1], axis=1), jnp.concatenate([sv0, sv1], axis=1)]),
            sums21[4:5],
            up_sum,
            sums3[2:3],
            jnp.concatenate([sums0[0:1], sums21[2:3], sums21[0:1], sums3[0:1]]),
            jnp.concatenate([sums0[1:2], sums21[3:4], sums21[1:2], sums3[1:2]]),
        ],
        shards,
    )
    if halves:
        heads_keep, heads_got = plane_second(heads_parts, heads_got, (4,))
        up_all = spread(up_piece, 2)
        last_keep, last_got = plane_second(last_parts, last_got, (2,))
        heads_piece = across(heads_keep, heads_got)
        last_piece = across(last_keep, last_got)
        tail = small_grads.reshape(-1, width // 8)
        for mask in (1, 2, 4):
            tail = tail + swap(tail, "dp", mask)
        for mask in (1, 2):
            tail = tail + swap(tail, "fsdp", mask)
        small_sum = lax.dynamic_index_in_dim(
            tail.reshape(small_grads.shape), lax.axis_index("fsdp"), 0, keepdims=False
        )
        heads_all = spread(heads_piece, 4)
        last_all = spread(last_piece, 2)
        (down_grad,) = finish("finish_down", idx, [place_down], [down_all], [down_weight.shape])
        (up_grad,) = finish("finish_up", idx, [place_up], [up_all], [up_weight.shape])
        qkv_grad, out_grad = finish(
            "finish_heads",
            idx,
            [functools.partial(place_heads, 0), functools.partial(place_heads, 1)],
            [heads_all, last_all],
            [qkv_weight.shape, out_weight.shape],
        )
    else:
        gpacked = jnp.concatenate([gq0, gq1, gk0, gk1, gv0, gv1], axis=1)

        def reduced(left, right):
            grad = dot_tn(left, right)
            return lax.psum(lax.psum_scatter(grad, "fsdp", scatter_dimension=0, tiled=True), "dp")

        qkv_grad = reduced(normed_one, gpacked)
        out_grad = reduced(attended, gmix)
        up_grad = reduced(two, ghid)
        down_grad = reduced(act, gffn)
        small_sum = lax.dynamic_index_in_dim(
            lax.psum(small_grads, ("dp", "fsdp")), lax.axis_index("fsdp"), 0, keepdims=False
        )
    qv_g, outb_g, upb_g, downb_g, gain_g, shift_g = unpack_small(small_sum[None])
    return (
        layer_out[None],
        grad_input[None],
        qkv_grad,
        qv_g,
        out_grad,
        outb_g[0],
        up_grad,
        upb_g[0],
        down_grad,
        downb_g[0],
        gain_g,
        shift_g,
    )


def solution(mesh):
    rows = P(("dp", "fsdp"), None, None)
    split = P("fsdp", None)
    placed = (
        rows,
        split,
        P(None, "fsdp"),
        split,
        P("fsdp"),
        split,
        P("fsdp"),
        split,
        P("fsdp"),
        P(None, "fsdp"),
        P(None, "fsdp"),
        P(("dp", "fsdp"), None),
        rows,
    )
    return jax.shard_map(
        on_device,
        mesh=mesh,
        in_specs=placed,
        out_specs=(
            rows,
            rows,
            split,
            P(None, "fsdp"),
            split,
            P("fsdp"),
            split,
            P("fsdp"),
            split,
            P("fsdp"),
            P(None, "fsdp"),
            P(None, "fsdp"),
        ),
        check_vma=False,
    )
```

```python
import functools
import math

import jax
import jax.numpy as jnp
from jax import lax
from jax.experimental import pallas as pl
from jax.experimental.pallas import tpu as pltpu
from jax.sharding import PartitionSpec as P

F32 = jnp.float32
BF = jnp.bfloat16
SDS = jax.ShapeDtypeStruct
HEAD_DIM = 64
PAIR = 2 * HEAD_DIM
EPS = 1e-05
MASKED = -1e30
QUERY_SCALE = math.log2(math.e) / math.sqrt(HEAD_DIM)
GRAD_SCALE = 1.0 / math.sqrt(HEAD_DIM)
BLOCK = 256
GELU_A = math.sqrt(2.0 / math.pi)
GELU_B = 0.044715 * GELU_A


def params(**more):
    return pltpu.CompilerParams(vmem_limit_bytes=60 * 1024 * 1024, **more)


def cost(flops, nbytes, trans=0):
    return pl.CostEstimate(flops=int(flops) // 1, bytes_accessed=int(nbytes) // 1, transcendentals=int(trans))


def dot_nn(a, b):
    return lax.dot_general(a, b, (((1,), (0,)), ((), ())), preferred_element_type=F32)


def dot_nt(a, b):
    return lax.dot_general(a, b, (((1,), (1,)), ((), ())), preferred_element_type=F32)


def dot_tn(a, b):
    return lax.dot_general(a, b, (((0,), (0,)), ((), ())), preferred_element_type=F32)


def centred(values):
    centre = values - jnp.mean(values, axis=-1, keepdims=True)
    rstd = lax.rsqrt(jnp.mean(centre * centre, axis=-1, keepdims=True) + EPS)
    return centre * rstd, rstd


def norm_back(grad, vhat, rstd, gain):
    e = grad * gain
    mean_e = jnp.mean(e, axis=-1, keepdims=True)
    mean_ev = jnp.mean(e * vhat, axis=-1, keepdims=True)
    return (e - mean_e - vhat * mean_ev) * rstd


def col_sum(values):
    return jnp.sum(values, axis=0, keepdims=True)


def piece_copies(spec, idx_ref, own_refs, slot_refs, places, sems):
    own_spec, slot_spec = spec
    dp, z = idx_ref[0], idx_ref[1]
    copies = []

    def add(group, src, dst):
        copies.append((group, pltpu.make_async_copy(src, dst, sems.at[len(copies)])))

    for o, first, cols, group in own_spec:
        rows = own_refs[o].shape[0]
        dst = places[o].at[pl.ds(pl.multiple_of(z * rows, rows), rows), first : first + cols]
        add(group, own_refs[o].at[:, first : first + cols], dst)
    for (pair, parts), ref in zip(slot_spec, slot_refs):
        rows = ref.shape[1]
        others = ref.shape[0] // 2
        for which, mask in enumerate(pair):
            for k in range(1, others + 1):
                at = which * others + k - 1
                for o, there, here, cols, group in parts:
                    dst = pl.multiple_of((z ^ k) * own_refs[o].shape[0] + (dp ^ mask) * rows, rows)
                    add(
                        group,
                        ref.at[at, :, here : here + cols],
                        places[o].at[pl.ds(dst, rows), there : there + cols],
                    )
    return copies


def count_copies(spec, slots):
    own_spec, slot_spec = spec
    return len(own_spec) + sum(len(parts) * s.shape[0] for (_, parts), s in zip(slot_spec, slots))


def start_all(copies):
    for _, copy in copies:
        copy.start()


def wait_group(copies, group):
    for g, copy in copies:
        if g == group:
            copy.wait()


def whole_shapes(owns, shards):
    return [(o.shape[0] * shards, o.shape[1]) for o in owns]


ANY = pl.BlockSpec(memory_space=pl.ANY)
SMEM = pl.BlockSpec(memory_space=pltpu.SMEM)


def qkv_kernel(spec, n_slots, idx_ref, own_ref, *refs):
    slots = refs[:n_slots]
    x_ref, bias_ref, gain_ref, shift_ref, normed_ref, packed_ref, out_ref = refs[n_slots : n_slots + 7]
    weight, sems, out_sem = refs[n_slots + 7 :]
    step, steps = pl.program_id(0), pl.num_programs(0)
    copies = piece_copies(spec, idx_ref, [own_ref], slots, [weight], sems)
    bn = packed_ref.shape[1]

    @pl.when(step == 0)
    def _():
        start_all(copies)
        vhat, _ = centred(x_ref[...].astype(F32))
        normed_ref[...] = (vhat * gain_ref[...] + shift_ref[...]).astype(BF)
        wait_group(copies, 0)

    half = weight.shape[1] // 2

    @pl.when(step == half // bn)
    def _():
        wait_group(copies, 1)
        pltpu.make_async_copy(weight, out_ref, out_sem).start()

    block = weight[:, pl.ds(pl.multiple_of(step * bn, bn), bn)]
    out = dot_nn(normed_ref[...], block) + bias_ref[...]
    packed_ref[...] = (out * jnp.where(step < steps // 3, QUERY_SCALE, 1.0)).astype(BF)

    @pl.when(step == steps - 1)
    def _():
        pltpu.make_async_copy(weight, out_ref, out_sem).wait()


def qkv_forward(idx, own, spec, slots, shards, x, bias, gain, shift):
    tokens, width = x.shape
    ((rows, cols),) = whole_shapes([own], shards)
    bn = width // 2
    row = pl.BlockSpec((1, width), lambda j: (0, 0))
    full = pl.BlockSpec((tokens, width), lambda j: (0, 0))
    return pl.pallas_call(
        functools.partial(qkv_kernel, spec, len(slots)),
        grid=(cols // bn,),
        in_specs=[SMEM] + [ANY] * (1 + len(slots))
        + [full, pl.BlockSpec((1, bn), lambda j: (0, j)), row, row],
        out_specs=(full, pl.BlockSpec((tokens, bn), lambda j: (0, j)), ANY),
        out_shape=(SDS((tokens, width), BF), SDS((tokens, cols), BF), SDS((rows, cols), BF)),
        scratch_shapes=[
            pltpu.VMEM((rows, cols), BF),
            pltpu.SemaphoreType.DMA((count_copies(spec, slots),)),
            pltpu.SemaphoreType.DMA(()),
        ],
        compiler_params=params(),
        cost_estimate=cost(2 * tokens * width * cols, 2 * width * cols + 2 * tokens * cols),
        name="qkv_forward",
    )(idx, own, *slots, x, bias, gain, shift)


def gelu_and_slope(a):
    sq = a * a
    t = jnp.tanh(a * (sq * GELU_B + GELU_A))
    half = 0.5 * t + 0.5
    act = a * half
    slope = half + act * ((1.0 - half) * (sq * (6.0 * GELU_B) + 2.0 * GELU_A))
    return act.astype(BF), slope.astype(BF)


def up_kernel(spec, n_slots, first, idx_ref, own_out, own_up, *refs):
    slots = refs[:n_slots]
    att_ref, x_ref, outb_ref, upb_ref, gain_ref, shift_ref = refs[n_slots : n_slots + 6]
    mixed_ref, mid_ref, two_ref, act_ref, slope_ref, wout_ref, wup_ref = refs[n_slots + 6 : n_slots + 13]
    w_out, w_up, sems, out_sems = refs[n_slots + 13 :]
    step, steps = pl.program_id(0), pl.num_programs(0)
    copies = piece_copies(spec, idx_ref, [own_out, own_up], slots, [w_out, w_up], sems)
    saves = [
        pltpu.make_async_copy(w_out, wout_ref, out_sems.at[0]),
        pltpu.make_async_copy(w_up, wup_ref, out_sems.at[1]),
    ]

    @pl.when(step == 0)
    def _():
        start_all(copies)
        wait_group(copies, 0)
        saves[0].start()

    @pl.when(step == first)
    def _():
        wait_group(copies, 1)
        saves[1].start()

    @pl.when(step < first)
    def _():
        mixed = dot_nn(att_ref[...], w_out[...]) + outb_ref[...]
        mixed_ref[...] = mixed
        vhat, _ = centred(mixed)
        mid = x_ref[...].astype(F32) + vhat * gain_ref[1:2, :] + shift_ref[1:2, :]
        mid_ref[...] = mid
        vhat, _ = centred(mid)
        at = pl.ds(pl.multiple_of(step * BLOCK, BLOCK), BLOCK)
        two_ref[at, :] = (vhat * gain_ref[2:3, :] + shift_ref[2:3, :]).astype(BF)

    @pl.when(step >= first)
    def _():
        bn = act_ref.shape[1]
        at = pl.ds(pl.multiple_of((step - first) * bn, bn), bn)
        a = dot_nn(two_ref[...], w_up[:, at]) + upb_ref[...]
        act_ref[...], slope_ref[...] = gelu_and_slope(a)

    @pl.when(step == steps - 1)
    def _():
        saves[0].wait()
        saves[1].wait()


def up_forward(idx, owns, spec, slots, shards, attended, x, out_bias, up_bias, gain, shift):
    tokens, width = x.shape
    out_shape, up_shape = whole_shapes(owns, shards)
    cols = up_shape[1]
    bn = width // 2
    first = tokens // BLOCK
    tok = pl.BlockSpec((BLOCK, width), lambda i: (jnp.minimum(i, first - 1), 0))
    col = pl.BlockSpec((tokens, bn), lambda i: (0, jnp.maximum(i - first, 0)))

    def whole(arr):
        return pl.BlockSpec(arr.shape, lambda i: (0, 0))

    return pl.pallas_call(
        functools.partial(up_kernel, spec, len(slots), first),
        grid=(first + cols // bn,),
        in_specs=[SMEM] + [ANY] * (2 + len(slots))
        + [
            tok,
            tok,
            whole(out_bias),
            pl.BlockSpec((1, bn), lambda i: (0, jnp.maximum(i - first, 0))),
            whole(gain),
            whole(shift),
        ],
        out_specs=(tok, tok, pl.BlockSpec((tokens, width), lambda i: (0, 0)), col, col, ANY, ANY),
        out_shape=(
            SDS((tokens, width), F32),
            SDS((tokens, width), F32),
            SDS((tokens, width), BF),
            SDS((tokens, cols), BF),
            SDS((tokens, cols), BF),
            SDS(out_shape, BF),
            SDS(up_shape, BF),
        ),
        scratch_shapes=[
            pltpu.VMEM(out_shape, BF),
            pltpu.VMEM(up_shape, BF),
            pltpu.SemaphoreType.DMA((count_copies(spec, slots),)),
            pltpu.SemaphoreType.DMA((2,)),
        ],
        compiler_params=params(),
        cost_estimate=cost(2 * tokens * width * (cols + width), 2 * width * cols + 4 * tokens * cols),
        name="up_forward",
    )(idx, *owns, *slots, attended, x, out_bias, up_bias, gain, shift)


def down_kernel(spec, n_slots, first, idx_ref, own_ref, *refs):
    slots = refs[:n_slots]
    act_ref, slope_ref, bias_ref, mid_ref, cot_ref, live_ref, gain_ref, shift_ref = refs[n_slots : n_slots + 8]
    out_ref, grad_ref, sums_ref, hid_ref, hsum_ref, weight, sems = refs[n_slots + 8 :]
    step = pl.program_id(0)
    copies = piece_copies(spec, idx_ref, [own_ref], slots, [weight], sems)

    @pl.when(step == 0)
    def _():
        start_all(copies)
        sums_ref[...] = jnp.zeros_like(sums_ref)
        wait_group(copies, 0)

    @pl.when(step < first)
    def _():
        ffn = dot_nn(act_ref[...], weight[...]) + bias_ref[...]
        vhat, rstd = centred(ffn)
        gain = gain_ref[3:4, :]
        out_ref[...] = (mid_ref[...] + vhat * gain + shift_ref[3:4, :]).astype(BF)
        grad = cot_ref[...].astype(F32) * live_ref[...]
        low = norm_back(grad, vhat, rstd, gain).astype(BF)
        grad_ref[pl.ds(pl.multiple_of(step * BLOCK, BLOCK), BLOCK), :] = low
        sums_ref[0:1, :] += col_sum(grad * vhat)
        sums_ref[1:2, :] += col_sum(grad)
        sums_ref[2:3, :] += col_sum(low.astype(F32))

    @pl.when(step >= first)
    def _():
        bn = hid_ref.shape[1]
        at = pl.ds(pl.multiple_of((step - first) * bn, bn), bn)
        low = (dot_nt(grad_ref[...], weight[at, :]) * slope_ref[...].astype(F32)).astype(BF)
        hid_ref[...] = low
        hsum_ref[...] = col_sum(low.astype(F32))


def down_both(idx, own, spec, slots, shards, act, slope, bias, mid, cot, live, gain, shift):
    tokens, width = mid.shape
    (shape,) = whole_shapes([own], shards)
    cols = shape[0]
    bn = width // 2
    first = tokens // BLOCK

    def at(i):
        return jnp.minimum(i, first - 1)

    tok = pl.BlockSpec((BLOCK, width), lambda i: (at(i), 0))
    col = pl.BlockSpec((tokens, bn), lambda i: (0, jnp.maximum(i - first, 0)))

    def whole(arr):
        return pl.BlockSpec(arr.shape, lambda i: (0, 0))

    return pl.pallas_call(
        functools.partial(down_kernel, spec, len(slots), first),
        grid=(first + cols // bn,),
        in_specs=[SMEM] + [ANY] * (1 + len(slots))
        + [
            pl.BlockSpec((BLOCK, cols), lambda i: (at(i), 0)),
            col,
            whole(bias),
            tok,
            tok,
            pl.BlockSpec((BLOCK, 1), lambda i: (at(i), 0)),
            whole(gain),
            whole(shift),
        ],
        out_specs=(
            tok,
            pl.BlockSpec((tokens, width), lambda i: (0, 0)),
            pl.BlockSpec((8, width), lambda i: (0, 0)),
            col,
            pl.BlockSpec((1, bn), lambda i: (0, jnp.maximum(i - first, 0))),
        ),
        out_shape=(
            SDS((tokens, width), BF),
            SDS((tokens, width), BF),
            SDS((8, width), F32),
            SDS((tokens, cols), BF),
            SDS((1, cols), F32),
        ),
        scratch_shapes=[pltpu.VMEM(shape, BF), pltpu.SemaphoreType.DMA((count_copies(spec, slots),))],
        compiler_params=params(),
        cost_estimate=cost(4 * tokens * width * cols, 2 * width * cols + 6 * tokens * cols),
        name="down_both",
    )(idx, own, *slots, act, slope, bias, mid, cot, live, gain, shift)


def mid_kernel(
    gh_ref, up_ref, out_w_ref, mid_ref, mixed_ref, cot_ref, live_ref, gain_ref,
    gmid_ref, gmix_ref, gatt_ref, sums_ref,
):
    @pl.when(pl.program_id(0) == 0)
    def _():
        sums_ref[...] = jnp.zeros_like(sums_ref)

    grad = dot_nt(gh_ref[...], up_ref[...])
    vhat, rstd = centred(mid_ref[...])
    sums_ref[0:1, :] += col_sum(grad * vhat)
    sums_ref[1:2, :] += col_sum(grad)
    gmid = cot_ref[...].astype(F32) * live_ref[...] + norm_back(grad, vhat, rstd, gain_ref[2:3, :])
    gmid_ref[...] = gmid
    vhat, rstd = centred(mixed_ref[...])
    sums_ref[2:3, :] += col_sum(gmid * vhat)
    sums_ref[3:4, :] += col_sum(gmid)
    low = norm_back(gmid, vhat, rstd, gain_ref[1:2, :]).astype(BF)
    gmix_ref[...] = low
    sums_ref[4:5, :] += col_sum(low.astype(F32))
    gatt_ref[...] = dot_nt(low, out_w_ref[...]).astype(BF)


def mid_backward(gh, up, out_w, mid, mixed, cot, live, gain):
    tokens, width = mid.shape
    cols = gh.shape[1]
    tok = pl.BlockSpec((BLOCK, width), lambda i: (i, 0))

    def whole(arr):
        return pl.BlockSpec(arr.shape, lambda i: (0, 0))

    return pl.pallas_call(
        mid_kernel,
        grid=(tokens // BLOCK,),
        in_specs=[
            pl.BlockSpec((BLOCK, cols), lambda i: (i, 0)),
            whole(up),
            whole(out_w),
            tok,
            tok,
            tok,
            pl.BlockSpec((BLOCK, 1), lambda i: (i, 0)),
            whole(gain),
        ],
        out_specs=(tok, tok, tok, pl.BlockSpec((8, width), lambda i: (0, 0))),
        out_shape=(
            SDS((tokens, width), F32),
            SDS((tokens, width), BF),
            SDS((tokens, width), BF),
            SDS((8, width), F32),
        ),
        compiler_params=params(),
        cost_estimate=cost(2 * tokens * width * (cols + width), 2 * width * cols + 2 * tokens * cols),
        name="mid_backward",
    )(gh, up, out_w, mid, mixed, cot, live, gain)


def input_kernel(n_grads, n_into, *refs):
    grad_refs, (w_ref, x_ref, gmid_ref, gain_ref) = refs[:n_grads], refs[n_grads : n_grads + 4]
    out_ref, sums_ref = refs[n_grads + 4 + n_into :]

    @pl.when(pl.program_id(0) == 0)
    def _():
        sums_ref[...] = jnp.zeros_like(sums_ref)

    grads = jnp.concatenate([ref[...] for ref in grad_refs], axis=1)
    grad = dot_nt(grads, w_ref[...])
    vhat, rstd = centred(x_ref[...].astype(F32))
    sums_ref[0:1, :] += col_sum(grad * vhat)
    sums_ref[1:2, :] += col_sum(grad)
    out_ref[...] = gmid_ref[...] + norm_back(grad, vhat, rstd, gain_ref[0:1, :])


def input_backward(grads, weight, x, gmid, gain, first, count, into=None):
    tokens, width = x.shape
    tok = pl.BlockSpec((BLOCK, width), lambda i: (first + i, 0))

    def whole(arr):
        return pl.BlockSpec(arr.shape, lambda i: (0, 0))

    in_specs = [pl.BlockSpec((BLOCK, g.shape[1]), lambda i: (first + i, 0)) for g in grads]
    in_specs += [whole(weight), tok, tok, whole(gain)]
    args = [*grads, weight, x, gmid, gain]
    aliases = {}
    if into is not None:
        aliases = {len(args): 0}
        in_specs.append(pl.BlockSpec(memory_space=pl.ANY))
        args.append(into)
    return pl.pallas_call(
        functools.partial(input_kernel, len(grads), len(aliases)),
        grid=(count,),
        in_specs=in_specs,
        out_specs=(tok, pl.BlockSpec((8, width), lambda i: (0, 0))),
        out_shape=(SDS((tokens, width), F32), SDS((8, width), F32)),
        input_output_aliases=aliases,
        compiler_params=params(),
        cost_estimate=cost(6 * count * BLOCK * width * width, 6 * width * width),
        name="input_backward",
    )(*args)


def fill_bias(bias, start_ref):
    length = bias.shape[0]
    for j in range(length // BLOCK):
        key = lax.broadcasted_iota(jnp.int32, (BLOCK, length), 0) + j * BLOCK
        query = lax.broadcasted_iota(jnp.int32, (BLOCK, length), 1)
        allowed = (key <= query) & (key >= start_ref[...])
        bias[j * BLOCK : (j + 1) * BLOCK, :] = jnp.where(allowed, 0.0, MASKED)


def one_head(low, arr, head):
    zero = jnp.zeros_like(arr)
    return jnp.where(low, arr, zero) if head == 0 else jnp.where(low, zero, arr)


def attend_kernel(q_ref, k_ref, v_ref, start_ref, out_ref, lse_ref, bias):
    length = q_ref.shape[0]

    @pl.when(pl.program_id(0) == 0)
    def _():
        fill_bias(bias, start_ref)

    low = lax.broadcasted_iota(jnp.int32, (1, PAIR), 1) < HEAD_DIM
    low_rows = lax.broadcasted_iota(jnp.int32, (PAIR, 1), 0) < HEAD_DIM
    keys = k_ref[...]
    values = jnp.concatenate([v_ref[...], jnp.ones((length, PAIR), BF)], axis=1)
    for i in range(length // BLOCK):
        reach = (i + 1) * BLOCK
        sl = slice(i * BLOCK, reach)
        queries = q_ref[sl, :]
        parts = []
        for head in range(2):
            scores = dot_nt(keys[:reach], one_head(low, queries, head)) + bias[:reach, sl]
            top = jnp.max(scores, axis=0, keepdims=True)
            probs = jnp.exp2(scores - top).astype(BF)
            mixed = dot_tn(values[:reach], probs)
            total = mixed[PAIR : PAIR + 1]
            parts.append(mixed[:PAIR] / total)
            lse_ref[0, head : head + 1, sl] = top + jnp.log2(total)
        out_ref[sl, :] = jnp.where(low_rows, parts[0], parts[1]).T.astype(BF)


def attend(packed, start_row):
    length = packed.shape[0]
    pairs = packed.shape[1] // (3 * PAIR)

    def blk(offset):
        return pl.BlockSpec((length, PAIR), lambda h: (0, offset + h))

    return pl.pallas_call(
        attend_kernel,
        grid=(pairs,),
        in_specs=[blk(0), blk(pairs), blk(2 * pairs), pl.BlockSpec((1, length), lambda h: (0, 0))],
        out_specs=(blk(0), pl.BlockSpec((1, 2, length), lambda h: (h, 0, 0))),
        out_shape=(SDS((length, PAIR * pairs), BF), SDS((pairs, 2, length), F32)),
        scratch_shapes=[pltpu.VMEM((length, length), F32)],
        compiler_params=params(),
        cost_estimate=cost(8 * pairs * length * length * PAIR, 8 * length * pairs * PAIR),
        name="attend",
    )(packed, packed, packed, start_row)


def attend_back_kernel(
    q_ref, k_ref, v_ref, g_ref, o_ref, lse_ref, start_ref, gq_ref, gk_ref, gv_ref, sq_ref, sv_ref, bias, acc
):
    length = q_ref.shape[0]

    @pl.when(pl.program_id(0) == 0)
    def _():
        fill_bias(bias, start_ref)

    low = lax.broadcasted_iota(jnp.int32, (1, PAIR), 1) < HEAD_DIM
    queries, grads = q_ref[...], g_ref[...]
    q_of = [one_head(low, queries, head) for head in range(2)]
    g_of = [one_head(low, grads, head) for head in range(2)]
    inner = (grads.astype(F32) * o_ref[...].astype(F32)).T
    inner_of = [col_sum(inner[:HEAD_DIM]), col_sum(inner[HEAD_DIM:])]
    sum_v = jnp.zeros((1, PAIR), F32)
    for j in range(length // BLOCK):
        first = j * BLOCK
        sl = slice(first, first + BLOCK)
        keys, values = k_ref[sl, :], v_ref[sl, :]
        gk = gv = gq = 0.0
        for head in range(2):
            scores = dot_nt(keys, q_of[head][first:]) + bias[sl, first:]
            probs = jnp.exp2(scores - lse_ref[0, head : head + 1, first:])
            gprobs = dot_nt(values, g_of[head][first:])
            gscores = (probs * (gprobs - inner_of[head][:, first:]) * GRAD_SCALE).astype(BF)
            gv = gv + dot_nn(probs.astype(BF), g_of[head][first:])
            gk = gk + dot_nn(gscores, q_of[head][first:])
            gq = gq + dot_tn(gscores, one_head(low, keys, head))
        low_v = gv.astype(BF)
        gv_ref[sl, :] = low_v
        gk_ref[sl, :] = (gk * (1.0 / QUERY_SCALE)).astype(BF)
        sum_v = sum_v + col_sum(low_v.astype(F32))
        if j == 0:
            acc[...] = gq
        else:
            acc[first:, :] += gq
    low_q = acc[...].astype(BF)
    gq_ref[...] = low_q
    sq_ref[...] = col_sum(low_q.astype(F32))
    sv_ref[...] = sum_v


def attend_back(packed, grads, attended, lse, start_row, first, count, columns, into=None):
    length = packed.shape[0]
    total = packed.shape[1] // (3 * PAIR)

    def blk(offset):
        return pl.BlockSpec((length, PAIR), lambda h: (0, offset + h))

    row = pl.BlockSpec((1, PAIR), lambda h: (0, columns + h))
    out = blk(columns)
    grad = SDS((length, PAIR * total // 2), BF)
    sums = SDS((1, PAIR * total // 2), F32)
    in_specs = [
        blk(first),
        blk(total + first),
        blk(2 * total + first),
        blk(first),
        blk(first),
        pl.BlockSpec((1, 2, length), lambda h: (first + h, 0, 0)),
        pl.BlockSpec((1, length), lambda h: (0, 0)),
    ]
    args = [packed, packed, packed, grads, attended, lse, start_row]
    kernel, aliases = attend_back_kernel, {}
    if into is not None:
        in_specs = in_specs + [pl.BlockSpec(memory_space=pl.ANY)] * len(into)
        aliases = {len(args) + i: i for i in range(len(into))}
        args = args + list(into)

        def kernel(*refs):
            attend_back_kernel(*refs[:7], *refs[7 + len(into) :])

    return pl.pallas_call(
        kernel,
        grid=(count,),
        in_specs=in_specs,
        out_specs=(out, out, out, row, row),
        out_shape=(grad, grad, grad, sums, sums),
        input_output_aliases=aliases,
        scratch_shapes=[pltpu.VMEM((length, length), F32), pltpu.VMEM((length, PAIR), F32)],
        compiler_params=params(),
        cost_estimate=cost(20 * count * length * length * PAIR, 16 * length * count * PAIR),
        name="attend_back",
    )(*args)


def swap(arr, axis, mask):
    size = lax.axis_size(axis)
    return lax.ppermute(arr, axis, [(i, i ^ mask) for i in range(size)])


def after(first, then):
    return lax.optimization_barrier((first, then))


def shard_swaps(piece):
    return [swap(piece, "fsdp", k) for k in range(1, lax.axis_size("fsdp"))]


PLANE_MASKS = [
    (0, 4), (2, 6), (1, 5), (3, 7),
    (0, 2), (4, 6), (1, 3), (5, 7),
]


def plane_slots(two, four):
    return [a for t, f in zip(two, four) for a in (t, f, swap(t, "dp", 1), swap(f, "dp", 1))]


def plane_spec(parts):
    return [(pair, parts[i // 4]) for i, pair in enumerate(PLANE_MASKS)]


def split_down(wide, zz):
    rows, cols = wide.shape[0] // 4, wide.shape[1] // 2
    part = wide[zz * rows : (zz + 1) * rows]
    return part[:, :cols], part[:, cols:]


def split_up(wide, zz):
    rows = wide.shape[0] // 8
    return wide[2 * zz * rows : (2 * zz + 1) * rows], wide[(2 * zz + 1) * rows : (2 * zz + 2) * rows]


def side_by_side(refs):
    blocks = [r[...] for r in refs]
    return blocks[0] if len(blocks) == 1 else jnp.concatenate(blocks, axis=1)


def emit(keep, wide, split, z, chip, rest):
    if not keep:
        for zz in range(4):
            for f, part in enumerate(split(wide, zz)):
                rest[0][0, 0, zz ^ z, f] = part.astype(BF)
        return
    got_ref, outs = rest[0], rest[1:]
    for dst in range(4):

        @pl.when(chip == dst)
        def _():
            for zz in range(4):
                slot = zz ^ z
                for f, part in enumerate(split(wide, zz)):
                    bit = dst // 2 if f == 0 else dst % 2
                    low = (part + got_ref[0, 0, slot, f].astype(F32)).astype(BF)
                    outs[2 * f + bit][0, 0, slot] = low


def grad_kernel(keep, jobs, idx_ref, *refs):
    step, z = pl.program_id(0), idx_ref[1]
    at = 0
    n_in = sum(n for groups, _ in jobs for group in groups for n in group)
    rest = refs[n_in:]
    for number, (groups, split) in enumerate(jobs):
        blocks = []
        for n_left, n_right in groups:
            blocks.append((refs[at : at + n_left], refs[at + n_left : at + n_left + n_right]))
            at += n_left + n_right

        @pl.when(step // 4 == number)
        def _():
            dots = [dot_tn(side_by_side(left), side_by_side(right)) for left, right in blocks]
            wide = dots[0] if len(dots) == 1 else jnp.concatenate(dots, axis=1)
            emit(keep, wide, split, z, step % 4, rest)


def grad_call(name, idx, specs, args, jobs, piece, flops, got=None):
    keep = got is not None
    n_jobs = len(jobs)
    rows, cols = piece
    block = pl.BlockSpec((1, 1, 4, 2, rows, cols), lambda i, idx: (i % 4, i // 4, 0, 0, 0, 0))
    half = (1, 1, 4, rows, cols)
    if keep:
        along_y = (
            lambda i, idx: (jnp.minimum(i % 4, 1), i // 4, 0, 0, 0),
            lambda i, idx: (jnp.maximum(i % 4 - 2, 0), i // 4, 0, 0, 0),
        )
        along_x = (lambda i, idx: (i % 4 // 2, i // 4, 0, 0, 0),) * 2
        specs = specs + [block]
        args = args + [got]
        out_specs = tuple(pl.BlockSpec(half, m) for m in along_y + along_x)
        out_shape = (SDS((2, n_jobs, 4, rows, cols), BF),) * 4
    else:
        out_specs = block
        out_shape = SDS((4, n_jobs, 4, 2, rows, cols), BF)
    return pl.pallas_call(
        functools.partial(grad_kernel, keep, jobs),
        grid_spec=pltpu.PrefetchScalarGridSpec(
            num_scalar_prefetch=1, grid=(4 * n_jobs,), in_specs=specs, out_specs=out_specs
        ),
        out_shape=out_shape,
        compiler_params=params(),
        cost_estimate=cost(flops, flops // 400),
        name=name + ("_keep" if keep else "_send"),
    )(idx, *args)


def chip_of(i, idx):
    return (idx[0] // 2) ^ (3 - i)


def core_of(keep, idx):
    return idx[0] & 1 if keep else (idx[0] & 1) ^ 1


def grad_down(idx, act, gffn, got=None):
    tokens, width = gffn.shape
    keep = got is not None
    rows = act.shape[1] // 32

    def act_spec(zz):
        def at(i, idx):
            return (0, zz * 8 + chip_of(i, idx) * 2 + core_of(keep, idx))

        return pl.BlockSpec((tokens, rows), at)

    specs = [act_spec(0), act_spec(1), act_spec(2), act_spec(3)]
    specs += [pl.BlockSpec((tokens, width), lambda i, idx: (0, 0))]
    args = [act, act, act, act, gffn]
    flops = act.shape[1] * width * tokens
    jobs = [([(4, 1)], split_down)]
    return grad_call("grad_down", idx, specs, args, jobs, (rows, width // 2), flops, got)


def grad_up(idx, two, ghid, got=None):
    tokens, width = two.shape
    keep = got is not None
    cols = ghid.shape[1] // 8
    specs = [
        pl.BlockSpec((tokens, width), lambda i, idx: (0, 0)),
        pl.BlockSpec((tokens, cols), lambda i, idx: (0, chip_of(i, idx) * 2 + core_of(keep, idx))),
    ]
    flops = ghid.shape[1] * width * tokens
    jobs = [([(1, 1)], split_up)]
    return grad_call("grad_up", idx, specs, [two, ghid], jobs, (width // 8, cols), flops, got)


def grad_heads(idx, one, gq, gk, gv, att=None, gmix=None, got=None):
    tokens, width = one.shape
    keep = got is not None
    rows = width // 8

    def left(zz):
        return pl.BlockSpec((tokens, rows), lambda i, idx: (0, zz * 2 + core_of(keep, idx)))

    def right(cols):
        return pl.BlockSpec((tokens, cols), lambda i, idx: (0, chip_of(i, idx)))

    lefts = [left(0), left(1), left(2), left(3)]
    specs, args, groups = lefts + [right(PAIR)] * 3, [one] * 4 + [gq, gk, gv], [(4, 3)]
    cols = 3 * PAIR
    if att is not None:
        specs, args, groups = specs + lefts + [right(width // 4)], args + [att] * 4 + [gmix], groups + [(4, 1)]
        cols += width // 4
    flops = 4 * tokens * width * cols
    return grad_call("grad_heads", idx, specs, args, [(groups, split_up)], (rows // 2, cols), flops, got)


def add_low(a, b):
    return (a.astype(F32) + b.astype(F32)).astype(BF)


def add_wide(a, b):
    return a.astype(F32) + b.astype(F32)


def plane_first(parts):
    return [swap(parts[2 * f], "dp", mask) for f, mask in enumerate((4, 2))]


def plane_adds(parts, got):
    send = [add_low(parts[2 * f + 1][0], got[f][0]) for f in range(2)]
    keep = [add_low(parts[2 * f + 1][1], got[f][1]) for f in range(2)]
    return keep, send


def plane_second(parts, got):
    keep, send = plane_adds(parts, got)
    return keep, [swap(s, "dp", mask) for s, mask in zip(send, (2, 4))]


def across_first(keep, got):
    both = jnp.stack([add_wide(k, g) for k, g in zip(keep, got)], axis=2)
    return both[:, 0::2].astype(BF), swap(both[:, 1::2].astype(BF), "fsdp", 1)


def across_second(both, got):
    return add_low(both[:, 0], got[:, 0]), swap(add_low(both[:, 1], got[:, 1]), "fsdp", 2)


def spread_first(piece, first):
    return jnp.stack([piece, swap(piece, "dp", first)])


def spread_second(two, first):
    return swap(two, "dp", 6 - first)


def spread_core(two, four, first):
    second = 6 - first
    return [
        ((0, first), two),
        ((second, 6), four),
        ((1, 1 ^ first), swap(two, "dp", 1)),
        ((1 ^ second, 7), swap(four, "dp", 1)),
    ]


def place_down(dp, piece, outs):
    rows, cols = piece.shape[1], piece.shape[2]
    at = pl.ds(pl.multiple_of(dp * rows, rows), rows)
    outs[1][at, :cols] = piece[0].astype(F32)
    outs[1][at, cols:] = piece[1].astype(F32)


def place_up(dp, piece, outs):
    rows, cols = piece.shape[1], piece.shape[2]
    at = pl.ds(pl.multiple_of(dp * cols, cols), cols)
    outs[0][:rows, at] = piece[0].astype(F32)
    outs[0][rows:, at] = piece[1].astype(F32)


def place_heads(half, dp, piece, outs):
    rows = piece.shape[1]
    width = outs[0].shape[1] // 3
    chip, core = dp // 2, dp % 2
    for flow in range(2):
        at_rows = pl.ds(pl.multiple_of((core * 2 + flow) * rows, rows), rows)
        part_of = piece[flow].astype(F32)
        for part in range(3):
            at = pl.multiple_of(part * width + half * (width // 2) + chip * PAIR, PAIR)
            outs[0][at_rows, pl.ds(at, PAIR)] = part_of[:, part * PAIR : (part + 1) * PAIR]
        if half == 0:
            cols = width // 4
            at = pl.multiple_of(chip * cols, cols)
            outs[1][at_rows, pl.ds(at, cols)] = part_of[:, 3 * PAIR :]


def finish_kernel(placers, masks, idx_ref, *refs):
    ins, outs = list(refs[: sum(map(len, masks))]), refs[sum(map(len, masks)) :]
    for placer, pairs in zip(placers, masks):
        for pair in pairs:
            ref = ins.pop(0)
            for which, mask in enumerate(pair):
                placer(idx_ref[0] ^ mask, ref[which], outs)


def finish(name, idx, placers, flows, shapes):
    masks = [[m for m, _ in flow] for flow in flows]
    arrays = [a for flow in flows for _, a in flow]
    vmem = pl.BlockSpec(memory_space=pltpu.VMEM)
    return pl.pallas_call(
        functools.partial(finish_kernel, placers, masks),
        in_specs=[SMEM] + [vmem] * len(arrays),
        out_specs=(vmem,) * len(shapes),
        out_shape=tuple(SDS(s, F32) for s in shapes),
        compiler_params=params(),
        cost_estimate=cost(0, sum(6 * math.prod(s) for s in shapes)),
        name=name,
    )(idx, *arrays)


def segment_starts(lengths, length):
    ends = jnp.cumsum(lengths)
    positions = jnp.arange(length, dtype=jnp.int32)
    begun = jnp.where(ends[None, :] <= positions[:, None], ends[None, :], 0)
    return jnp.max(begun, axis=1).astype(jnp.int32), positions < ends[-1]


def eighth(shard):
    rows = shard.shape[0] // 8
    return lax.dynamic_slice_in_dim(shard, lax.axis_index("dp") * rows, rows, axis=0)


SMALL_ROWS = 16


def pack_small(qv_bias, out_bias, up_bias, down_bias, gain, shift):
    flat = [a.reshape(-1) for a in (qv_bias, out_bias, up_bias, down_bias, gain, shift)]
    return jnp.concatenate(flat)


def unpack_small(shards):
    count, total = shards.shape
    unit = total // SMALL_ROWS
    sizes = ((2, unit), (1, unit), (1, 4 * unit), (1, unit), (4, unit), (4, unit))
    out, at = [], 0
    for lead, cols in sizes:
        block = shards[:, at : at + lead * cols].reshape(count, lead, cols)
        out.append(jnp.swapaxes(block, 0, 1).reshape(lead, count * cols))
        at += lead * cols
    return out


def by_shard(rows, count):
    flat = []
    for arr in rows:
        lead, cols = arr.shape
        flat.append(
            jnp.swapaxes(arr.reshape(lead, count, cols // count), 0, 1).reshape(count, -1)
        )
    return jnp.concatenate(flat, axis=1)


def gather_small(own, got):
    z = lax.axis_index("fsdp")
    slots = jnp.stack([own] + got)
    low, high = z % 2, z // 2
    slots = jnp.where(low == 0, slots, slots[jnp.array([1, 0, 3, 2])])
    return jnp.where(high == 0, slots, slots[jnp.array([2, 3, 0, 1])])


def on_device(
    layer_input,
    qkv_weight,
    query_value_bias,
    out_weight,
    out_bias,
    up_weight,
    up_bias,
    down_weight,
    down_bias,
    norm_gain,
    norm_shift,
    doc_lengths,
    cotangent,
):
    _, tokens, width = layer_input.shape
    shards = lax.axis_size("fsdp")
    halves = shards == 4 and lax.axis_size("dp") == 8
    idx = jnp.stack([lax.axis_index("dp"), lax.axis_index("fsdp")]).astype(jnp.int32)
    x = layer_input[0]
    cot = cotangent[0]
    start, live = segment_starts(doc_lengths[0], tokens)
    start_row = start[None, :]
    live_col = live.astype(F32)[:, None]
    small_own = pack_small(query_value_bias, out_bias, up_bias, down_bias, norm_gain, norm_shift)
    tie = lax.optimization_barrier
    both = (4, 2)
    if halves:
        piece = eighth(qkv_weight)
        cols = piece.shape[1]
        extra = small_own.reshape(piece.shape[0], -1)
        got = shard_swaps(jnp.concatenate([piece, extra], axis=1))
        small = gather_small(small_own, [g[:, cols:].reshape(-1) for g in got])
        half_q = cols // 2
        q_own = [jnp.stack([g[:, :half_q] for g in got]), jnp.stack([g[:, half_q:cols] for g in got])]
        q_own, piece = after(q_own, jnp.concatenate([eighth(out_weight), eighth(up_weight)], axis=1))
        q_got = [swap(o, "dp", m) for o, m in zip(q_own, both)]
        got_u = shard_swaps(piece)
        q_two = [jnp.concatenate([o, g]) for o, g in zip(q_own, q_got)]
        q_four = [swap(t, "dp", 6 - m) for t, m in zip(q_two, both)]
        slots_q = plane_slots(q_two, q_four)
        q_four, got_u = after(q_four, got_u)
        half_u = piece.shape[1] // 2
        u_own = [jnp.stack([g[:, :half_u] for g in got_u]), jnp.stack([g[:, half_u:] for g in got_u])]
        u_own, piece = after(u_own, eighth(down_weight))
        u_got = [swap(o, "dp", m) for o, m in zip(u_own, both)]
        got_d = shard_swaps(piece)
        own_q, own_u, own_d, at, count = qkv_weight, [out_weight, up_weight], down_weight, idx, shards
    else:
        small = lax.all_gather(small_own, "fsdp", axis=0)
        own_q = lax.all_gather(qkv_weight, "fsdp", axis=0, tiled=True)
        own_u = [
            lax.all_gather(out_weight, "fsdp", axis=0, tiled=True),
            lax.all_gather(up_weight, "fsdp", axis=0, tiled=True),
        ]
        own_d = lax.all_gather(down_weight, "fsdp", axis=0, tiled=True)
        half_q, half_u, at, count = own_q.shape[1] // 2, 0, jnp.zeros_like(idx), 1
        slots_q = slots_u = slots_d = []
    qv_b, out_b, up_b, down_b, gain, shift = unpack_small(small.astype(F32))
    qkv_b = jnp.concatenate([qv_b[0:1], jnp.zeros((1, width), F32), qv_b[1:2]], axis=1)

    spec = (
        [(0, 0, half_q, 0), (0, half_q, half_q, 1)],
        plane_spec([[(0, 0, 0, half_q, 0)], [(0, half_q, 0, half_q, 1)]]) if halves else [],
    )
    normed_one, packed, w_qkv = qkv_forward(
        at, own_q, spec, slots_q, count, x, qkv_b, gain[0:1], shift[0:1]
    )
    if halves:
        packed, u_got, got_d = tie((packed, u_got, got_d))
        u_two = [jnp.concatenate([o, g]) for o, g in zip(u_own, u_got)]
        u_four = [swap(t, "dp", 6 - m) for t, m in zip(u_two, both)]
        half_d = width // 2
        d_own = [jnp.stack([g[:, :half_d] for g in got_d]), jnp.stack([g[:, half_d:] for g in got_d])]
        d_got = [swap(o, "dp", m) for o, m in zip(d_own, both)]
        u_two, d_own, packed = tie((u_two, d_own, packed))
    attended, lse = attend(packed, start_row)
    if halves:
        attended, u_four, d_got = tie((attended, u_four, d_got))
        slots_u = plane_slots(u_two, u_four)
        d_two = [jnp.concatenate([o, g]) for o, g in zip(d_own, d_got)]
        d_four = [swap(t, "dp", 6 - m) for t, m in zip(d_two, both)]
    up_cols = own_u[1].shape[1]
    rest = half_u - width
    spec = (
        [(0, 0, width, 0), (1, 0, up_cols, 1)],
        plane_spec([[(0, 0, 0, width, 0), (1, 0, width, rest, 1)], [(1, rest, 0, half_u, 1)]])
        if halves
        else [],
    )
    mixed, mid, two, act, slope, w_out, w_up = up_forward(
        at, own_u, spec, slots_u, count, attended, x, out_b, up_b, gain, shift
    )
    if halves:
        act, d_four = after(act, d_four)
        slots_d = plane_slots(d_two, d_four)
    half = width // 2
    spec = ([(0, 0, width, 0)], plane_spec([[(0, 0, 0, half, 0)], [(0, half, 0, half, 0)]]) if halves else [])
    layer_out, gffn, sums3, ghid, up_sum = down_both(
        at, own_d, spec, slots_d, count, act, slope, down_b, mid, cot, live_col, gain, shift
    )

    if halves:
        send = grad_down(idx, act, gffn)
        got_down = swap(send, "dp", 1)
        send, ghid = after(send, ghid)
        send = grad_up(idx, two, ghid)
        got_up = swap(send, "dp", 1)
        send, got_down, act = tie((send, got_down, act))
        down_parts = grad_down(idx, act, gffn, got_down)
        down_got = plane_first(down_parts)
        down_parts, ghid = after(down_parts, ghid)
    gmid, gmix, gatt, sums21 = mid_backward(ghid, w_up, w_out, mid, mixed, cot, live_col, gain)
    if halves:
        down_got, got_up, gmix = tie((down_got, got_up, gmix))
        down_keep, down_got = plane_second(down_parts, down_got)
        ghid, down_keep = after(ghid, down_keep)
        up_parts = grad_up(idx, two, ghid, got_up)
        up_got = plane_first(up_parts)
        up_parts, gatt = after(up_parts, gatt)
    pairs = width // PAIR
    back = functools.partial(attend_back, packed)
    gq0, gk0, gv0, sq0, sv0 = back(gatt, attended, lse, start_row, 0, pairs // 2, 0)
    if halves:
        gq0, gmix = after(gq0, gmix)
        send = grad_heads(idx, normed_one, gq0, gk0, gv0, attended, gmix)
        got_heads = swap(send, "dp", 1)
        up_got, send, gatt = tie((up_got, send, gatt))
        up_keep, up_got = plane_second(up_parts, up_got)
        up_keep, gatt = after(up_keep, gatt)
    gq1, gk1, gv1, sq1, sv1 = back(gatt, attended, lse, start_row, pairs // 2, pairs // 2, 0)
    if halves:
        down_got, up_got, gq1 = tie((down_got, up_got, gq1))
        keep = [jnp.concatenate(pair) for pair in zip(down_keep, up_keep)]
        got = [jnp.concatenate(pair) for pair in zip(down_got, up_got)]
        ffn_total, ffn_got = across_first(keep, got)
        ffn_total, gq1 = after(ffn_total, gq1)
        send = grad_heads(idx, normed_one, gq1, gk1, gv1)
        got_last = swap(send, "dp", 1)
        send, got_heads, gq0 = tie((send, got_heads, gq0))
        heads_parts = grad_heads(idx, normed_one, gq0, gk0, gv0, attended, gmix, got_heads)
        heads_got = plane_first(heads_parts)
        heads_parts, got_last, gq1, ffn_got = tie((heads_parts, got_last, gq1, ffn_got))
        ffn_total, ffn_got = across_second(ffn_total, ffn_got)
        ffn_total, gq1 = after(ffn_total, gq1)
        last_parts = grad_heads(idx, normed_one, gq1, gk1, gv1, got=got_last)
        last_got = plane_first(last_parts)
        last_parts, heads_got, gq1 = tie((last_parts, heads_got, gq1))
        heads_keep, heads_got = plane_second(heads_parts, heads_got)
        heads_keep, gq1 = after(heads_keep, gq1)
    grads = [gq0, gq1, gk0, gk1, gv0, gv1]
    blocks = tokens // BLOCK
    grad_input, sums0 = input_backward(grads, w_qkv, x, gmid, gain, 0, blocks // 2)
    if halves:
        sums0, heads_got, last_got, ffn_got = tie((sums0, heads_got, last_got, ffn_got))
        last_keep, last_got = plane_second(last_parts, last_got)
        heads_total, heads_got = across_first(heads_keep, heads_got)
        ffn_piece = add_low(ffn_total, ffn_got)
        last_keep, heads_total, ffn_piece, grad_input = tie((last_keep, heads_total, ffn_piece, grad_input))
    grad_input, sums0_rest = input_backward(
        grads, w_qkv, x, gmid, gain, blocks // 2, blocks // 2, grad_input
    )
    if halves:
        sums0_rest, last_got, heads_got = tie((sums0_rest, last_got, heads_got))
    sums0 = sums0 + sums0_rest
    small_grads = by_shard(
        [
            jnp.concatenate([jnp.concatenate([sq0, sq1], axis=1), jnp.concatenate([sv0, sv1], axis=1)]),
            sums21[4:5],
            up_sum,
            sums3[2:3],
            jnp.concatenate([sums0[0:1], sums21[2:3], sums21[0:1], sums3[0:1]]),
            jnp.concatenate([sums0[1:2], sums21[3:4], sums21[1:2], sums3[1:2]]),
        ],
        shards,
    )
    if halves:
        last_total, last_got = across_first(last_keep, last_got)
        heads_total, heads_got = across_second(heads_total, heads_got)
        ffn_piece, last_total = after(ffn_piece, last_total)
        down_two = spread_first(ffn_piece[0], 4)
        up_two = spread_first(ffn_piece[1], 2)
        tail = small_grads.reshape(-1, width // 8)
        tail_got = swap(tail, "dp", 1)

        last_total, last_got, heads_got, tail_got, down_two, up_two = tie(
            (last_total, last_got, heads_got, tail_got, down_two, up_two)
        )
        last_total, last_got = across_second(last_total, last_got)
        heads_two = spread_first(add_low(heads_total, heads_got)[0], 4)
        down_four = spread_second(down_two, 4)
        up_four = spread_second(up_two, 2)
        tail = tail + tail_got
        tail_got = swap(tail, "dp", 2)

        last_total, last_got, heads_two, tail_got = tie((last_total, last_got, heads_two, tail_got))
        last_two = spread_first(add_low(last_total, last_got)[0], 2)
        heads_four = spread_second(heads_two, 4)
        tail = tail + tail_got
        tail_got = swap(tail, "dp", 4)

        last_two, heads_four, tail_got, down_four, up_four = tie(
            (last_two, heads_four, tail_got, down_four, up_four)
        )
        last_four = spread_second(last_two, 2)
        tail = tail + tail_got
        tail_got = swap(tail, "fsdp", 1)
        heads_all = spread_core(heads_two, heads_four, 4)
        down_all = spread_core(down_two, down_four, 4)
        up_all = spread_core(up_two, up_four, 2)
        up_grad, down_grad = finish(
            "finish_ffn", idx, [place_down, place_up], [down_all, up_all], [up_weight.shape, down_weight.shape]
        )

        last_four, tail_got, up_grad = tie((last_four, tail_got, up_grad))
        tail = tail + tail_got
        tail_got = swap(tail, "fsdp", 2)
        last_all = spread_core(last_two, last_four, 2)
        tail = tail + tail_got
        small_sum = lax.dynamic_index_in_dim(
            tail.reshape(small_grads.shape), lax.axis_index("fsdp"), 0, keepdims=False
        )
        qkv_grad, out_grad = finish(
            "finish_heads",
            idx,
            [functools.partial(place_heads, 0), functools.partial(place_heads, 1)],
            [heads_all, last_all],
            [qkv_weight.shape, out_weight.shape],
        )
    else:
        gpacked = jnp.concatenate([gq0, gq1, gk0, gk1, gv0, gv1], axis=1)

        def reduced(left, right):
            grad = dot_tn(left, right)
            return lax.psum(lax.psum_scatter(grad, "fsdp", scatter_dimension=0, tiled=True), "dp")

        qkv_grad = reduced(normed_one, gpacked)
        out_grad = reduced(attended, gmix)
        up_grad = reduced(two, ghid)
        down_grad = reduced(act, gffn)
        small_sum = lax.dynamic_index_in_dim(
            lax.psum(small_grads, ("dp", "fsdp")), lax.axis_index("fsdp"), 0, keepdims=False
        )
    qv_g, outb_g, upb_g, downb_g, gain_g, shift_g = unpack_small(small_sum[None])
    return (
        layer_out[None],
        grad_input[None],
        qkv_grad,
        qv_g,
        out_grad,
        outb_g[0],
        up_grad,
        upb_g[0],
        down_grad,
        downb_g[0],
        gain_g,
        shift_g,
    )


def solution(mesh):
    rows = P(("dp", "fsdp"), None, None)
    split = P("fsdp", None)
    placed = (
        rows,
        split,
        P(None, "fsdp"),
        split,
        P("fsdp"),
        split,
        P("fsdp"),
        split,
        P("fsdp"),
        P(None, "fsdp"),
        P(None, "fsdp"),
        P(("dp", "fsdp"), None),
        rows,
    )
    return jax.shard_map(
        on_device,
        mesh=mesh,
        in_specs=placed,
        out_specs=(
            rows,
            rows,
            split,
            P(None, "fsdp"),
            split,
            P("fsdp"),
            split,
            P("fsdp"),
            split,
            P("fsdp"),
            P(None, "fsdp"),
            P(None, "fsdp"),
        ),
        check_vma=False,
    )
```

```python
import functools
import math

import jax
import jax.numpy as jnp
from jax import lax
from jax.experimental import pallas as pl
from jax.experimental.pallas import tpu as pltpu
from jax.sharding import PartitionSpec as P

F32 = jnp.float32
BF = jnp.bfloat16
SDS = jax.ShapeDtypeStruct
HEAD_DIM = 64
PAIR = 2 * HEAD_DIM
EPS = 1e-05
MASKED = -1e30
QUERY_SCALE = math.log2(math.e) / math.sqrt(HEAD_DIM)
GRAD_SCALE = 1.0 / math.sqrt(HEAD_DIM)
BLOCK = 256
UP_COLS = 1024
HIDDEN_COLS = 1024
GELU_A = math.sqrt(2.0 / math.pi)
GELU_B = 0.044715 * GELU_A


def params(**more):
    return pltpu.CompilerParams(vmem_limit_bytes=60 * 1024 * 1024, **more)


def cost(flops, nbytes, trans=0):
    return pl.CostEstimate(flops=int(flops) // 1, bytes_accessed=int(nbytes) // 1, transcendentals=int(trans))


def dot_nn(a, b):
    return lax.dot_general(a, b, (((1,), (0,)), ((), ())), preferred_element_type=F32)


def dot_nt(a, b):
    return lax.dot_general(a, b, (((1,), (1,)), ((), ())), preferred_element_type=F32)


def dot_tn(a, b):
    return lax.dot_general(a, b, (((0,), (0,)), ((), ())), preferred_element_type=F32)


def centred(values):
    centre = values - jnp.mean(values, axis=-1, keepdims=True)
    rstd = lax.rsqrt(jnp.mean(centre * centre, axis=-1, keepdims=True) + EPS)
    return centre * rstd, rstd


def norm_back(grad, vhat, rstd, gain):
    e = grad * gain
    mean_e = jnp.mean(e, axis=-1, keepdims=True)
    mean_ev = jnp.mean(e * vhat, axis=-1, keepdims=True)
    return (e - mean_e - vhat * mean_ev) * rstd


def col_sum(values):
    return jnp.sum(values, axis=0, keepdims=True)


def piece_copies(spec, idx_ref, own_refs, slot_refs, places, sems):
    own_spec, slot_spec = spec
    dp, z = idx_ref[0], idx_ref[1]
    copies = []

    def add(group, src, dst):
        copies.append((group, pltpu.make_async_copy(src, dst, sems.at[len(copies)])))

    for o, first, cols, group in own_spec:
        rows = own_refs[o].shape[0]
        dst = places[o].at[pl.ds(pl.multiple_of(z * rows, rows), rows), first : first + cols]
        add(group, own_refs[o].at[:, first : first + cols], dst)
    for (pair, parts), ref in zip(slot_spec, slot_refs):
        rows = ref.shape[1]
        others = ref.shape[0] // 2
        for which, mask in enumerate(pair):
            for k in range(1, others + 1):
                at = which * others + k - 1
                for o, there, here, cols, group in parts:
                    dst = pl.multiple_of((z ^ k) * own_refs[o].shape[0] + (dp ^ mask) * rows, rows)
                    add(
                        group,
                        ref.at[at, :, here : here + cols],
                        places[o].at[pl.ds(dst, rows), there : there + cols],
                    )
    return copies


def count_copies(spec, slots):
    own_spec, slot_spec = spec
    return len(own_spec) + sum(len(parts) * s.shape[0] for (_, parts), s in zip(slot_spec, slots))


def start_all(copies):
    for _, copy in copies:
        copy.start()


def wait_group(copies, group):
    for g, copy in copies:
        if g == group:
            copy.wait()


def whole_shapes(owns, shards):
    return [(o.shape[0] * shards, o.shape[1]) for o in owns]


ANY = pl.BlockSpec(memory_space=pl.ANY)
SMEM = pl.BlockSpec(memory_space=pltpu.SMEM)


def qkv_kernel(spec, n_slots, idx_ref, own_ref, *refs):
    slots = refs[:n_slots]
    x_ref, bias_ref, gain_ref, shift_ref, normed_ref, packed_ref, out_ref = refs[n_slots : n_slots + 7]
    weight, sems, out_sem = refs[n_slots + 7 :]
    step, steps = pl.program_id(0), pl.num_programs(0)
    copies = piece_copies(spec, idx_ref, [own_ref], slots, [weight], sems)
    bn = packed_ref.shape[1]

    @pl.when(step == 0)
    def _():
        start_all(copies)
        vhat, _ = centred(x_ref[...].astype(F32))
        normed_ref[...] = (vhat * gain_ref[...] + shift_ref[...]).astype(BF)
        wait_group(copies, 0)

    half = weight.shape[1] // 2

    @pl.when(step == half // bn)
    def _():
        wait_group(copies, 1)
        pltpu.make_async_copy(weight, out_ref, out_sem).start()

    block = weight[:, pl.ds(pl.multiple_of(step * bn, bn), bn)]
    out = dot_nn(normed_ref[...], block) + bias_ref[...]
    packed_ref[...] = (out * jnp.where(step < steps // 3, QUERY_SCALE, 1.0)).astype(BF)

    @pl.when(step == steps - 1)
    def _():
        pltpu.make_async_copy(weight, out_ref, out_sem).wait()


def qkv_forward(idx, own, spec, slots, shards, x, bias, gain, shift):
    tokens, width = x.shape
    ((rows, cols),) = whole_shapes([own], shards)
    bn = width // 2
    row = pl.BlockSpec((1, width), lambda j: (0, 0))
    full = pl.BlockSpec((tokens, width), lambda j: (0, 0))
    return pl.pallas_call(
        functools.partial(qkv_kernel, spec, len(slots)),
        grid=(cols // bn,),
        in_specs=[SMEM] + [ANY] * (1 + len(slots))
        + [full, pl.BlockSpec((1, bn), lambda j: (0, j)), row, row],
        out_specs=(full, pl.BlockSpec((tokens, bn), lambda j: (0, j)), ANY),
        out_shape=(SDS((tokens, width), BF), SDS((tokens, cols), BF), SDS((rows, cols), BF)),
        scratch_shapes=[
            pltpu.VMEM((rows, cols), BF),
            pltpu.SemaphoreType.DMA((count_copies(spec, slots),)),
            pltpu.SemaphoreType.DMA(()),
        ],
        compiler_params=params(),
        cost_estimate=cost(2 * tokens * width * cols, 2 * width * cols + 2 * tokens * cols),
        name="qkv_forward",
    )(idx, own, *slots, x, bias, gain, shift)


def gelu_and_slope(a):
    sq = a * a
    t = jnp.tanh(a * (sq * GELU_B + GELU_A))
    half = 0.5 * t + 0.5
    act = a * half
    slope = half + act * ((1.0 - half) * (sq * (6.0 * GELU_B) + 2.0 * GELU_A))
    return act.astype(BF), slope.astype(BF)


def out_kernel(spec, n_slots, idx_ref, own_ref, *refs):
    slots = refs[:n_slots]
    att_ref, x_ref, bias_ref, gain_ref, shift_ref = refs[n_slots : n_slots + 5]
    mixed_ref, mid_ref, two_ref, save_ref, weight, sems, save_sem = refs[n_slots + 5 :]
    step, steps = pl.program_id(0), pl.num_programs(0)
    copies = piece_copies(spec, idx_ref, [own_ref], slots, [weight], sems)
    save = pltpu.make_async_copy(weight, save_ref, save_sem)

    @pl.when(step == 0)
    def _():
        start_all(copies)
        wait_group(copies, 0)
        save.start()

    mixed = dot_nn(att_ref[...], weight[...]) + bias_ref[...]
    mixed_ref[...] = mixed
    vhat, _ = centred(mixed)
    mid = x_ref[...].astype(F32) + vhat * gain_ref[1:2, :] + shift_ref[1:2, :]
    mid_ref[...] = mid
    vhat, _ = centred(mid)
    two_ref[...] = (vhat * gain_ref[2:3, :] + shift_ref[2:3, :]).astype(BF)

    @pl.when(step == steps - 1)
    def _():
        save.wait()


def out_forward(idx, own, spec, slots, shards, attended, x, bias, gain, shift):
    tokens, width = x.shape
    (shape,) = whole_shapes([own], shards)
    tok = pl.BlockSpec((BLOCK, width), lambda i: (i, 0))

    def whole(arr):
        return pl.BlockSpec(arr.shape, lambda i: (0, 0))

    return pl.pallas_call(
        functools.partial(out_kernel, spec, len(slots)),
        grid=(tokens // BLOCK,),
        in_specs=[SMEM] + [ANY] * (1 + len(slots)) + [tok, tok, whole(bias), whole(gain), whole(shift)],
        out_specs=(tok, tok, tok, ANY),
        out_shape=(
            SDS((tokens, width), F32),
            SDS((tokens, width), F32),
            SDS((tokens, width), BF),
            SDS(shape, BF),
        ),
        scratch_shapes=[
            pltpu.VMEM(shape, BF),
            pltpu.SemaphoreType.DMA((count_copies(spec, slots),)),
            pltpu.SemaphoreType.DMA(()),
        ],
        compiler_params=params(),
        cost_estimate=cost(2 * tokens * width * width, 16 * tokens * width),
        name="out_forward",
    )(idx, own, *slots, attended, x, bias, gain, shift)


def up_kernel(spec, n_slots, idx_ref, own_ref, *refs):
    slots = refs[:n_slots]
    two_ref, bias_ref, act_ref, slope_ref, save_ref, weight, sems, save_sem = refs[n_slots:]
    step, steps = pl.program_id(0), pl.num_programs(0)
    copies = piece_copies(spec, idx_ref, [own_ref], slots, [weight], sems)
    save = pltpu.make_async_copy(weight, save_ref, save_sem)

    @pl.when(step == 0)
    def _():
        start_all(copies)
        wait_group(copies, 0)
        save.start()

    bn = act_ref.shape[1]
    at = pl.ds(pl.multiple_of(step * bn, bn), bn)
    a = dot_nn(two_ref[...], weight[:, at]) + bias_ref[...]
    act_ref[...], slope_ref[...] = gelu_and_slope(a)

    @pl.when(step == steps - 1)
    def _():
        save.wait()


def up_forward(idx, own, spec, slots, shards, two, bias):
    tokens, width = two.shape
    (shape,) = whole_shapes([own], shards)
    cols = shape[1]
    bn = UP_COLS
    col = pl.BlockSpec((tokens, bn), lambda i: (0, i))
    return pl.pallas_call(
        functools.partial(up_kernel, spec, len(slots)),
        grid=(cols // bn,),
        in_specs=[SMEM] + [ANY] * (1 + len(slots))
        + [pl.BlockSpec((tokens, width), lambda i: (0, 0)), pl.BlockSpec((1, bn), lambda i: (0, i))],
        out_specs=(col, col, ANY),
        out_shape=(SDS((tokens, cols), BF), SDS((tokens, cols), BF), SDS(shape, BF)),
        scratch_shapes=[
            pltpu.VMEM(shape, BF),
            pltpu.SemaphoreType.DMA((count_copies(spec, slots),)),
            pltpu.SemaphoreType.DMA(()),
        ],
        compiler_params=params(),
        cost_estimate=cost(2 * tokens * width * cols, 2 * width * cols + 4 * tokens * cols),
        name="up_forward",
    )(idx, own, *slots, two, bias)


def down_kernel(spec, n_slots, first, idx_ref, own_ref, *refs):
    slots = refs[:n_slots]
    act_ref, slope_ref, bias_ref, mid_ref, cot_ref, live_ref, gain_ref, shift_ref = refs[n_slots : n_slots + 8]
    out_ref, grad_ref, sums_ref, hid_ref, hsum_ref, weight, sems = refs[n_slots + 8 :]
    step = pl.program_id(0)
    copies = piece_copies(spec, idx_ref, [own_ref], slots, [weight], sems)

    @pl.when(step == 0)
    def _():
        start_all(copies)
        sums_ref[...] = jnp.zeros_like(sums_ref)
        wait_group(copies, 0)

    @pl.when(step < first)
    def _():
        ffn = dot_nn(act_ref[...], weight[...]) + bias_ref[...]
        vhat, rstd = centred(ffn)
        gain = gain_ref[3:4, :]
        out_ref[...] = (mid_ref[...] + vhat * gain + shift_ref[3:4, :]).astype(BF)
        grad = cot_ref[...].astype(F32) * live_ref[...]
        low = norm_back(grad, vhat, rstd, gain).astype(BF)
        grad_ref[pl.ds(pl.multiple_of(step * BLOCK, BLOCK), BLOCK), :] = low
        sums_ref[0:1, :] += col_sum(grad * vhat)
        sums_ref[1:2, :] += col_sum(grad)
        sums_ref[2:3, :] += col_sum(low.astype(F32))

    @pl.when(step >= first)
    def _():
        bn = hid_ref.shape[1]
        at = pl.ds(pl.multiple_of((step - first) * bn, bn), bn)
        low = (dot_nt(grad_ref[...], weight[at, :]) * slope_ref[...].astype(F32)).astype(BF)
        hid_ref[...] = low
        hsum_ref[...] = col_sum(low.astype(F32))


def down_both(idx, own, spec, slots, shards, act, slope, bias, mid, cot, live, gain, shift):
    tokens, width = mid.shape
    (shape,) = whole_shapes([own], shards)
    cols = shape[0]
    bn = HIDDEN_COLS
    first = tokens // BLOCK

    def at(i):
        return jnp.minimum(i, first - 1)

    tok = pl.BlockSpec((BLOCK, width), lambda i: (at(i), 0))
    col = pl.BlockSpec((tokens, bn), lambda i: (0, jnp.maximum(i - first, 0)))

    def whole(arr):
        return pl.BlockSpec(arr.shape, lambda i: (0, 0))

    return pl.pallas_call(
        functools.partial(down_kernel, spec, len(slots), first),
        grid=(first + cols // bn,),
        in_specs=[SMEM] + [ANY] * (1 + len(slots))
        + [
            pl.BlockSpec((BLOCK, cols), lambda i: (at(i), 0)),
            col,
            whole(bias),
            tok,
            tok,
            pl.BlockSpec((BLOCK, 1), lambda i: (at(i), 0)),
            whole(gain),
            whole(shift),
        ],
        out_specs=(
            tok,
            pl.BlockSpec((tokens, width), lambda i: (0, 0)),
            pl.BlockSpec((8, width), lambda i: (0, 0)),
            col,
            pl.BlockSpec((1, bn), lambda i: (0, jnp.maximum(i - first, 0))),
        ),
        out_shape=(
            SDS((tokens, width), BF),
            SDS((tokens, width), BF),
            SDS((8, width), F32),
            SDS((tokens, cols), BF),
            SDS((1, cols), F32),
        ),
        scratch_shapes=[pltpu.VMEM(shape, BF), pltpu.SemaphoreType.DMA((count_copies(spec, slots),))],
        compiler_params=params(),
        cost_estimate=cost(4 * tokens * width * cols, 2 * width * cols + 6 * tokens * cols),
        name="down_both",
    )(idx, own, *slots, act, slope, bias, mid, cot, live, gain, shift)


def mid_kernel(
    gh_ref, up_ref, out_w_ref, mid_ref, mixed_ref, cot_ref, live_ref, gain_ref,
    gmid_ref, gmix_ref, gatt_ref, sums_ref,
):
    @pl.when(pl.program_id(0) == 0)
    def _():
        sums_ref[...] = jnp.zeros_like(sums_ref)

    grad = dot_nt(gh_ref[...], up_ref[...])
    vhat, rstd = centred(mid_ref[...])
    sums_ref[0:1, :] += col_sum(grad * vhat)
    sums_ref[1:2, :] += col_sum(grad)
    gmid = cot_ref[...].astype(F32) * live_ref[...] + norm_back(grad, vhat, rstd, gain_ref[2:3, :])
    gmid_ref[...] = gmid
    vhat, rstd = centred(mixed_ref[...])
    sums_ref[2:3, :] += col_sum(gmid * vhat)
    sums_ref[3:4, :] += col_sum(gmid)
    low = norm_back(gmid, vhat, rstd, gain_ref[1:2, :]).astype(BF)
    gmix_ref[...] = low
    sums_ref[4:5, :] += col_sum(low.astype(F32))
    gatt_ref[...] = dot_nt(low, out_w_ref[...]).astype(BF)


def mid_backward(gh, up, out_w, mid, mixed, cot, live, gain):
    tokens, width = mid.shape
    cols = gh.shape[1]
    tok = pl.BlockSpec((BLOCK, width), lambda i: (i, 0))

    def whole(arr):
        return pl.BlockSpec(arr.shape, lambda i: (0, 0))

    return pl.pallas_call(
        mid_kernel,
        grid=(tokens // BLOCK,),
        in_specs=[
            pl.BlockSpec((BLOCK, cols), lambda i: (i, 0)),
            whole(up),
            whole(out_w),
            tok,
            tok,
            tok,
            pl.BlockSpec((BLOCK, 1), lambda i: (i, 0)),
            whole(gain),
        ],
        out_specs=(tok, tok, tok, pl.BlockSpec((8, width), lambda i: (0, 0))),
        out_shape=(
            SDS((tokens, width), F32),
            SDS((tokens, width), BF),
            SDS((tokens, width), BF),
            SDS((8, width), F32),
        ),
        compiler_params=params(),
        cost_estimate=cost(2 * tokens * width * (cols + width), 2 * width * cols + 2 * tokens * cols),
        name="mid_backward",
    )(gh, up, out_w, mid, mixed, cot, live, gain)


def input_kernel(n_grads, n_into, *refs):
    grad_refs, (w_ref, x_ref, gmid_ref, gain_ref) = refs[:n_grads], refs[n_grads : n_grads + 4]
    out_ref, sums_ref = refs[n_grads + 4 + n_into :]

    @pl.when(pl.program_id(0) == 0)
    def _():
        sums_ref[...] = jnp.zeros_like(sums_ref)

    grads = jnp.concatenate([ref[...] for ref in grad_refs], axis=1)
    grad = dot_nt(grads, w_ref[...])
    vhat, rstd = centred(x_ref[...].astype(F32))
    sums_ref[0:1, :] += col_sum(grad * vhat)
    sums_ref[1:2, :] += col_sum(grad)
    out_ref[...] = gmid_ref[...] + norm_back(grad, vhat, rstd, gain_ref[0:1, :])


def input_backward(grads, weight, x, gmid, gain, first, count, into=None):
    tokens, width = x.shape
    tok = pl.BlockSpec((BLOCK, width), lambda i: (first + i, 0))

    def whole(arr):
        return pl.BlockSpec(arr.shape, lambda i: (0, 0))

    in_specs = [pl.BlockSpec((BLOCK, g.shape[1]), lambda i: (first + i, 0)) for g in grads]
    in_specs += [whole(weight), tok, tok, whole(gain)]
    args = [*grads, weight, x, gmid, gain]
    aliases = {}
    if into is not None:
        aliases = {len(args): 0}
        in_specs.append(pl.BlockSpec(memory_space=pl.ANY))
        args.append(into)
    return pl.pallas_call(
        functools.partial(input_kernel, len(grads), len(aliases)),
        grid=(count,),
        in_specs=in_specs,
        out_specs=(tok, pl.BlockSpec((8, width), lambda i: (0, 0))),
        out_shape=(SDS((tokens, width), F32), SDS((8, width), F32)),
        input_output_aliases=aliases,
        compiler_params=params(),
        cost_estimate=cost(6 * count * BLOCK * width * width, 6 * width * width),
        name="input_backward",
    )(*args)


def fill_bias(bias, start_ref):
    length = bias.shape[0]
    for j in range(length // BLOCK):
        key = lax.broadcasted_iota(jnp.int32, (BLOCK, length), 0) + j * BLOCK
        query = lax.broadcasted_iota(jnp.int32, (BLOCK, length), 1)
        allowed = (key <= query) & (key >= start_ref[...])
        bias[j * BLOCK : (j + 1) * BLOCK, :] = jnp.where(allowed, 0.0, MASKED)


def one_head(low, arr, head):
    zero = jnp.zeros_like(arr)
    return jnp.where(low, arr, zero) if head == 0 else jnp.where(low, zero, arr)


def attend_kernel(q_ref, k_ref, v_ref, start_ref, out_ref, lse_ref, bias):
    length = q_ref.shape[0]

    @pl.when(pl.program_id(0) == 0)
    def _():
        fill_bias(bias, start_ref)

    low = lax.broadcasted_iota(jnp.int32, (1, PAIR), 1) < HEAD_DIM
    low_rows = lax.broadcasted_iota(jnp.int32, (PAIR, 1), 0) < HEAD_DIM
    keys = k_ref[...]
    values = jnp.concatenate([v_ref[...], jnp.ones((length, PAIR), BF)], axis=1)
    for i in range(length // BLOCK):
        reach = (i + 1) * BLOCK
        sl = slice(i * BLOCK, reach)
        queries = q_ref[sl, :]
        parts = []
        for head in range(2):
            scores = dot_nt(keys[:reach], one_head(low, queries, head)) + bias[:reach, sl]
            top = jnp.max(scores, axis=0, keepdims=True)
            probs = jnp.exp2(scores - top).astype(BF)
            mixed = dot_tn(values[:reach], probs)
            total = mixed[PAIR : PAIR + 1]
            parts.append(mixed[:PAIR] / total)
            lse_ref[0, head : head + 1, sl] = top + jnp.log2(total)
        out_ref[sl, :] = jnp.where(low_rows, parts[0], parts[1]).T.astype(BF)


def attend(packed, start_row, first, count, into=None):
    length = packed.shape[0]
    pairs = packed.shape[1] // (3 * PAIR)

    def blk(offset):
        return pl.BlockSpec((length, PAIR), lambda h: (0, offset + first + h))

    in_specs = [blk(0), blk(pairs), blk(2 * pairs), pl.BlockSpec((1, length), lambda h: (0, 0))]
    args = [packed, packed, packed, start_row]
    kernel, aliases = attend_kernel, {}
    if into is not None:
        in_specs = in_specs + [ANY] * len(into)
        aliases = {len(args) + i: i for i in range(len(into))}
        args = args + list(into)

        def kernel(*refs):
            attend_kernel(*refs[:4], *refs[4 + len(into) :])

    return pl.pallas_call(
        kernel,
        grid=(count,),
        in_specs=in_specs,
        out_specs=(blk(0), pl.BlockSpec((1, 2, length), lambda h: (first + h, 0, 0))),
        out_shape=(SDS((length, PAIR * pairs), BF), SDS((pairs, 2, length), F32)),
        input_output_aliases=aliases,
        scratch_shapes=[pltpu.VMEM((length, length), F32)],
        compiler_params=params(),
        cost_estimate=cost(8 * count * length * length * PAIR, 8 * length * count * PAIR),
        name="attend",
    )(*args)


def attend_back_kernel(
    q_ref, k_ref, v_ref, g_ref, o_ref, lse_ref, start_ref, gq_ref, gk_ref, gv_ref, sq_ref, sv_ref, bias, acc
):
    length = q_ref.shape[0]

    @pl.when(pl.program_id(0) == 0)
    def _():
        fill_bias(bias, start_ref)

    low = lax.broadcasted_iota(jnp.int32, (1, PAIR), 1) < HEAD_DIM
    queries, grads = q_ref[...], g_ref[...]
    q_of = [one_head(low, queries, head) for head in range(2)]
    g_of = [one_head(low, grads, head) for head in range(2)]
    inner = (grads.astype(F32) * o_ref[...].astype(F32)).T
    inner_of = [col_sum(inner[:HEAD_DIM]), col_sum(inner[HEAD_DIM:])]
    sum_v = jnp.zeros((1, PAIR), F32)
    for j in range(length // BLOCK):
        first = j * BLOCK
        sl = slice(first, first + BLOCK)
        keys, values = k_ref[sl, :], v_ref[sl, :]
        gk = gv = gq = 0.0
        for head in range(2):
            scores = dot_nt(keys, q_of[head][first:]) + bias[sl, first:]
            probs = jnp.exp2(scores - lse_ref[0, head : head + 1, first:])
            gprobs = dot_nt(values, g_of[head][first:])
            gscores = (probs * (gprobs - inner_of[head][:, first:]) * GRAD_SCALE).astype(BF)
            gv = gv + dot_nn(probs.astype(BF), g_of[head][first:])
            gk = gk + dot_nn(gscores, q_of[head][first:])
            gq = gq + dot_tn(gscores, one_head(low, keys, head))
        low_v = gv.astype(BF)
        gv_ref[sl, :] = low_v
        gk_ref[sl, :] = (gk * (1.0 / QUERY_SCALE)).astype(BF)
        sum_v = sum_v + col_sum(low_v.astype(F32))
        if j == 0:
            acc[...] = gq
        else:
            acc[first:, :] += gq
    low_q = acc[...].astype(BF)
    gq_ref[...] = low_q
    sq_ref[...] = col_sum(low_q.astype(F32))
    sv_ref[...] = sum_v


def attend_back(packed, grads, attended, lse, start_row, first, count, columns, into=None):
    length = packed.shape[0]
    total = packed.shape[1] // (3 * PAIR)

    def blk(offset):
        return pl.BlockSpec((length, PAIR), lambda h: (0, offset + h))

    row = pl.BlockSpec((1, PAIR), lambda h: (0, columns + h))
    out = blk(columns)
    grad = SDS((length, PAIR * total // 2), BF)
    sums = SDS((1, PAIR * total // 2), F32)
    in_specs = [
        blk(first),
        blk(total + first),
        blk(2 * total + first),
        blk(first),
        blk(first),
        pl.BlockSpec((1, 2, length), lambda h: (first + h, 0, 0)),
        pl.BlockSpec((1, length), lambda h: (0, 0)),
    ]
    args = [packed, packed, packed, grads, attended, lse, start_row]
    kernel, aliases = attend_back_kernel, {}
    if into is not None:
        in_specs = in_specs + [pl.BlockSpec(memory_space=pl.ANY)] * len(into)
        aliases = {len(args) + i: i for i in range(len(into))}
        args = args + list(into)

        def kernel(*refs):
            attend_back_kernel(*refs[:7], *refs[7 + len(into) :])

    return pl.pallas_call(
        kernel,
        grid=(count,),
        in_specs=in_specs,
        out_specs=(out, out, out, row, row),
        out_shape=(grad, grad, grad, sums, sums),
        input_output_aliases=aliases,
        scratch_shapes=[pltpu.VMEM((length, length), F32), pltpu.VMEM((length, PAIR), F32)],
        compiler_params=params(),
        cost_estimate=cost(20 * count * length * length * PAIR, 16 * length * count * PAIR),
        name="attend_back",
    )(*args)


def swap(arr, axis, mask):
    size = lax.axis_size(axis)
    return lax.ppermute(arr, axis, [(i, i ^ mask) for i in range(size)])


def after(first, then):
    return lax.optimization_barrier((first, then))


def shard_swaps(piece):
    return [swap(piece, "fsdp", k) for k in range(1, lax.axis_size("fsdp"))]


def shard_pair(piece, got):
    return swap(jnp.stack([piece, got]), "fsdp", 1)


def shard_slots(got, pair):
    return [pair[0], got, pair[1]]


PLANE_MASKS = [
    (0, 4), (2, 6), (1, 5), (3, 7),
    (0, 2), (4, 6), (1, 3), (5, 7),
]


def plane_slots(two, four):
    return [a for t, f in zip(two, four) for a in (t, f, swap(t, "dp", 1), swap(f, "dp", 1))]


def plane_spec(parts):
    return [(pair, parts[i // 4]) for i, pair in enumerate(PLANE_MASKS)]


def split_down(wide, zz):
    rows, cols = wide.shape[0] // 4, wide.shape[1] // 2
    part = wide[zz * rows : (zz + 1) * rows]
    return part[:, :cols], part[:, cols:]


def split_up(wide, zz):
    rows = wide.shape[0] // 8
    return wide[2 * zz * rows : (2 * zz + 1) * rows], wide[(2 * zz + 1) * rows : (2 * zz + 2) * rows]


def side_by_side(refs):
    blocks = [r[...] for r in refs]
    return blocks[0] if len(blocks) == 1 else jnp.concatenate(blocks, axis=1)


def emit(keep, direct, wide, split, z, chip, rest):
    if not keep:
        for zz in range(4):
            for f, part in enumerate(split(wide, zz)):
                rest[0][0, 0, zz ^ z, f] = part.astype(BF)
        return
    got_ref, outs = rest[0], rest[1:]
    for dst in range(4):

        @pl.when(chip == dst)
        def _():
            for zz in range(4):
                slot = zz ^ z
                for f, part in enumerate(split(wide, zz)):
                    low = (part + got_ref[0, 0, slot, f].astype(F32)).astype(BF)
                    if direct:
                        outs[dst][0, slot, f] = low
                    else:
                        bit = dst // 2 if f == 0 else dst % 2
                        outs[2 * f + bit][0, 0, slot] = low


def grad_kernel(keep, direct, jobs, idx_ref, *refs):
    step, z = pl.program_id(0), idx_ref[1]
    at = 0
    n_in = sum(n for groups, _ in jobs for group in groups for n in group)
    rest = refs[n_in:]
    for number, (groups, split) in enumerate(jobs):
        blocks = []
        for n_left, n_right in groups:
            blocks.append((refs[at : at + n_left], refs[at + n_left : at + n_left + n_right]))
            at += n_left + n_right

        @pl.when(step // 4 == number)
        def _():
            dots = [dot_tn(side_by_side(left), side_by_side(right)) for left, right in blocks]
            wide = dots[0] if len(dots) == 1 else jnp.concatenate(dots, axis=1)
            emit(keep, direct, wide, split, z, step % 4, rest)


def grad_call(name, idx, specs, args, jobs, piece, flops, got=None, direct=True):
    keep = got is not None
    n_jobs = len(jobs)
    rows, cols = piece
    block = pl.BlockSpec((1, 1, 4, 2, rows, cols), lambda i, idx: (i % 4, i // 4, 0, 0, 0, 0))
    half = (1, 1, 4, rows, cols)
    if keep and direct:
        specs = specs + [block]
        args = args + [got]
        out_specs = (pl.BlockSpec((1, 4, 2, rows, cols), lambda i, idx: (0, 0, 0, 0, 0)),) * 4
        out_shape = (SDS((1, 4, 2, rows, cols), BF),) * 4
    elif keep:
        along_y = (
            lambda i, idx: (jnp.minimum(i % 4, 1), i // 4, 0, 0, 0),
            lambda i, idx: (jnp.maximum(i % 4 - 2, 0), i // 4, 0, 0, 0),
        )
        along_x = (lambda i, idx: (i % 4 // 2, i // 4, 0, 0, 0),) * 2
        specs = specs + [block]
        args = args + [got]
        out_specs = tuple(pl.BlockSpec(half, m) for m in along_y + along_x)
        out_shape = (SDS((2, n_jobs, 4, rows, cols), BF),) * 4
    else:
        out_specs = block
        out_shape = SDS((4, n_jobs, 4, 2, rows, cols), BF)
    return pl.pallas_call(
        functools.partial(grad_kernel, keep, direct, jobs),
        grid_spec=pltpu.PrefetchScalarGridSpec(
            num_scalar_prefetch=1, grid=(4 * n_jobs,), in_specs=specs, out_specs=out_specs
        ),
        out_shape=out_shape,
        compiler_params=params(),
        cost_estimate=cost(flops, flops // 400),
        name=name + ("_keep" if keep else "_send"),
    )(idx, *args)


def chip_of(i, idx):
    return (idx[0] // 2) ^ (3 - i)


def core_of(keep, idx):
    return idx[0] & 1 if keep else (idx[0] & 1) ^ 1


def grad_down(idx, act, gffn, got=None):
    tokens, width = gffn.shape
    keep = got is not None
    rows = act.shape[1] // 32

    def act_spec(zz):
        def at(i, idx):
            return (0, zz * 8 + chip_of(i, idx) * 2 + core_of(keep, idx))

        return pl.BlockSpec((tokens, rows), at)

    specs = [act_spec(0), act_spec(1), act_spec(2), act_spec(3)]
    specs += [pl.BlockSpec((tokens, width), lambda i, idx: (0, 0))]
    args = [act, act, act, act, gffn]
    flops = act.shape[1] * width * tokens
    jobs = [([(4, 1)], split_down)]
    return grad_call("grad_down", idx, specs, args, jobs, (rows, width // 2), flops, got)


def grad_up(idx, two, ghid, got=None):
    tokens, width = two.shape
    keep = got is not None
    cols = ghid.shape[1] // 8
    specs = [
        pl.BlockSpec((tokens, width), lambda i, idx: (0, 0)),
        pl.BlockSpec((tokens, cols), lambda i, idx: (0, chip_of(i, idx) * 2 + core_of(keep, idx))),
    ]
    flops = ghid.shape[1] * width * tokens
    jobs = [([(1, 1)], split_up)]
    return grad_call("grad_up", idx, specs, [two, ghid], jobs, (width // 8, cols), flops, got)


def grad_heads(idx, one, gq, gk, gv, att=None, gmix=None, got=None):
    tokens, width = one.shape
    keep = got is not None
    rows = width // 8

    def left(zz):
        return pl.BlockSpec((tokens, rows), lambda i, idx: (0, zz * 2 + core_of(keep, idx)))

    def right(cols):
        return pl.BlockSpec((tokens, cols), lambda i, idx: (0, chip_of(i, idx)))

    lefts = [left(0), left(1), left(2), left(3)]
    specs, args, groups = lefts + [right(PAIR)] * 3, [one] * 4 + [gq, gk, gv], [(4, 3)]
    cols = 3 * PAIR
    if att is not None:
        specs, args, groups = specs + lefts + [right(width // 4)], args + [att] * 4 + [gmix], groups + [(4, 1)]
        cols += width // 4
    flops = 4 * tokens * width * cols
    return grad_call("grad_heads", idx, specs, args, [(groups, split_up)], (rows // 2, cols), flops, got, False)


def add_low(a, b):
    return (a.astype(F32) + b.astype(F32)).astype(BF)


def add_wide(a, b):
    return a.astype(F32) + b.astype(F32)


def plane_first(parts):
    return [swap(parts[2 * f], "dp", mask) for f, mask in enumerate((4, 2))]


def plane_adds(parts, got):
    send = [add_low(parts[2 * f + 1][0], got[f][0]) for f in range(2)]
    keep = [add_low(parts[2 * f + 1][1], got[f][1]) for f in range(2)]
    return keep, send


def plane_second(parts, got):
    keep, send = plane_adds(parts, got)
    return keep, [swap(s, "dp", mask) for s, mask in zip(send, (2, 4))]


def plane_direct(parts):
    return [swap(part, "dp", mask) for part, mask in zip(parts, (6, 4, 2))]


def plane_total(parts, got):
    return add_wide(parts[3], got[0]) + add_wide(got[1], got[2])


def across_first(both):
    return both[:, 0::2].astype(BF), both[:, 1::2].astype(BF)


def spread(piece):
    four = jnp.stack([piece] + [swap(piece, "dp", mask) for mask in (2, 4, 6)])
    return four


def spread_core(four):
    return [((0, 2, 4, 6), four), ((1, 3, 5, 7), swap(four, "dp", 1))]


def place_ffn(dp, piece, outs):
    up_grad, down_grad = outs
    rows, cols = piece.shape[2], piece.shape[3]
    at = pl.ds(pl.multiple_of(dp * rows, rows), rows)
    down_grad[at, :cols] = piece[0, 0].astype(F32)
    down_grad[at, cols:] = piece[0, 1].astype(F32)
    at = pl.ds(pl.multiple_of(dp * cols, cols), cols)
    up_grad[:rows, at] = piece[1, 0].astype(F32)
    up_grad[rows:, at] = piece[1, 1].astype(F32)


def place_heads(dp, piece, outs):
    qkv_grad, out_grad = outs
    width = out_grad.shape[1]
    rows, cols = out_grad.shape[0] // 2, width // 4
    chip, core = dp // 2, dp % 2
    at_rows = pl.ds(pl.multiple_of(core * rows, rows), rows)
    part_of = piece[:rows].astype(F32)
    for half, skip in ((0, 0), (1, 3 * PAIR + cols)):
        for part in range(3):
            at = pl.multiple_of(part * width + half * (width // 2) + chip * PAIR, PAIR)
            here = skip + part * PAIR
            qkv_grad[at_rows, pl.ds(at, PAIR)] = part_of[:, here : here + PAIR]
    at = pl.multiple_of(chip * cols, cols)
    out_grad[at_rows, pl.ds(at, cols)] = part_of[:, 3 * PAIR : 3 * PAIR + cols]


def finish_kernel(placer, masks, idx_ref, *refs):
    ins, outs = refs[: len(masks)], refs[len(masks) :]
    for group, ref in zip(masks, ins):
        for which, mask in enumerate(group):
            placer(idx_ref[0] ^ mask, ref[which], outs)


def finish(name, idx, placer, flow, shapes):
    masks = [m for m, _ in flow]
    arrays = [a for _, a in flow]
    vmem = pl.BlockSpec(memory_space=pltpu.VMEM)
    return pl.pallas_call(
        functools.partial(finish_kernel, placer, masks),
        in_specs=[SMEM] + [vmem] * len(arrays),
        out_specs=(vmem,) * len(shapes),
        out_shape=tuple(SDS(s, F32) for s in shapes),
        compiler_params=params(),
        cost_estimate=cost(0, sum(6 * math.prod(s) for s in shapes)),
        name=name,
    )(idx, *arrays)


def segment_starts(lengths, length):
    ends = jnp.cumsum(lengths)
    positions = jnp.arange(length, dtype=jnp.int32)
    begun = jnp.where(ends[None, :] <= positions[:, None], ends[None, :], 0)
    return jnp.max(begun, axis=1).astype(jnp.int32), positions < ends[-1]


def eighth(shard):
    rows = shard.shape[0] // 8
    return lax.dynamic_slice_in_dim(shard, lax.axis_index("dp") * rows, rows, axis=0)


SMALL_ROWS = 16


def pack_small(qv_bias, out_bias, up_bias, down_bias, gain, shift):
    flat = [a.reshape(-1) for a in (qv_bias, out_bias, up_bias, down_bias, gain, shift)]
    return jnp.concatenate(flat)


def unpack_small(shards):
    count, total = shards.shape
    unit = total // SMALL_ROWS
    sizes = ((2, unit), (1, unit), (1, 4 * unit), (1, unit), (4, unit), (4, unit))
    out, at = [], 0
    for lead, cols in sizes:
        block = shards[:, at : at + lead * cols].reshape(count, lead, cols)
        out.append(jnp.swapaxes(block, 0, 1).reshape(lead, count * cols))
        at += lead * cols
    return out


def by_shard(rows, count):
    flat = []
    for arr in rows:
        lead, cols = arr.shape
        flat.append(
            jnp.swapaxes(arr.reshape(lead, count, cols // count), 0, 1).reshape(count, -1)
        )
    return jnp.concatenate(flat, axis=1)


def gather_small(own, got):
    z = lax.axis_index("fsdp")
    slots = jnp.stack([own] + got)
    low, high = z % 2, z // 2
    slots = jnp.where(low == 0, slots, slots[jnp.array([1, 0, 3, 2])])
    return jnp.where(high == 0, slots, slots[jnp.array([2, 3, 0, 1])])


def on_device(
    layer_input,
    qkv_weight,
    query_value_bias,
    out_weight,
    out_bias,
    up_weight,
    up_bias,
    down_weight,
    down_bias,
    norm_gain,
    norm_shift,
    doc_lengths,
    cotangent,
):
    _, tokens, width = layer_input.shape
    shards = lax.axis_size("fsdp")
    halves = shards == 4 and lax.axis_size("dp") == 8
    idx = jnp.stack([lax.axis_index("dp"), lax.axis_index("fsdp")]).astype(jnp.int32)
    x = layer_input[0]
    cot = cotangent[0]
    start, live = segment_starts(doc_lengths[0], tokens)
    start_row = start[None, :]
    live_col = live.astype(F32)[:, None]
    small_own = pack_small(query_value_bias, out_bias, up_bias, down_bias, norm_gain, norm_shift)
    tie = lax.optimization_barrier
    both = (4, 2)
    if halves:
        piece = eighth(qkv_weight)
        cols = piece.shape[1]
        extra = small_own.reshape(piece.shape[0], -1)
        got = shard_swaps(jnp.concatenate([piece, extra], axis=1))
        small = gather_small(small_own, [g[:, cols:].reshape(-1) for g in got])
        half_q = cols // 2
        q_own = [jnp.stack([g[:, :half_q] for g in got]), jnp.stack([g[:, half_q:cols] for g in got])]
        q_own, piece_u = after(q_own, jnp.concatenate([eighth(out_weight), eighth(up_weight)], axis=1))
        q_got = [swap(o, "dp", m) for o, m in zip(q_own, both)]
        got_u = swap(piece_u, "fsdp", 2)
        q_two = [jnp.concatenate([o, g]) for o, g in zip(q_own, q_got)]
        q_four = [swap(t, "dp", 6 - m) for t, m in zip(q_two, both)]
        slots_q = plane_slots(q_two, q_four)
        q_four, got_u = after(q_four, got_u)
        half_u = piece_u.shape[1] // 2
        pair_u = shard_pair(piece_u, got_u)
        own_q, own_u, own_d, at, count = qkv_weight, [out_weight, up_weight], down_weight, idx, shards
    else:
        small = lax.all_gather(small_own, "fsdp", axis=0)
        own_q = lax.all_gather(qkv_weight, "fsdp", axis=0, tiled=True)
        own_u = [
            lax.all_gather(out_weight, "fsdp", axis=0, tiled=True),
            lax.all_gather(up_weight, "fsdp", axis=0, tiled=True),
        ]
        own_d = lax.all_gather(down_weight, "fsdp", axis=0, tiled=True)
        half_q, half_u, at, count = own_q.shape[1] // 2, 0, jnp.zeros_like(idx), 1
        slots_q = slots_u = slots_d = []
    qv_b, out_b, up_b, down_b, gain, shift = unpack_small(small.astype(F32))
    qkv_b = jnp.concatenate([qv_b[0:1], jnp.zeros((1, width), F32), qv_b[1:2]], axis=1)

    spec = (
        [(0, 0, half_q, 0), (0, half_q, half_q, 1)],
        plane_spec([[(0, 0, 0, half_q, 0)], [(0, half_q, 0, half_q, 1)]]) if halves else [],
    )
    normed_one, packed, w_qkv = qkv_forward(
        at, own_q, spec, slots_q, count, x, qkv_b, gain[0:1], shift[0:1]
    )
    if halves:
        packed, pair_u = after(packed, pair_u)
        slots = shard_slots(got_u, pair_u)
        u_own = [jnp.stack([g[:, :half_u] for g in slots]), jnp.stack([g[:, half_u:] for g in slots])]
        u_got = [swap(o, "dp", m) for o, m in zip(u_own, both)]
        u_own, piece_d = after(u_own, eighth(down_weight))
        got_d = swap(piece_d, "fsdp", 2)
        u_own, packed = after(u_own, packed)
    pairs = width // PAIR
    part = attend(packed, start_row, 0, pairs // 2)
    if halves:
        part, u_got, got_d = tie((part, u_got, got_d))
        u_two = [jnp.concatenate([o, g]) for o, g in zip(u_own, u_got)]
        u_four = [swap(t, "dp", 6 - m) for t, m in zip(u_two, both)]
        u_two, got_d, packed = tie((u_two, got_d, packed))
        pair_d = shard_pair(piece_d, got_d)
    attended, lse = attend(packed, start_row, pairs // 2, pairs // 2, part)
    if halves:
        attended, u_four, pair_d = tie((attended, u_four, pair_d))
        slots_u = plane_slots(u_two, u_four)
        slots = shard_slots(got_d, pair_d)
        half_d = width // 2
        d_own = [jnp.stack([g[:, :half_d] for g in slots]), jnp.stack([g[:, half_d:] for g in slots])]
        d_got = [swap(o, "dp", m) for o, m in zip(d_own, both)]
    spec = ([(0, 0, width, 0)], plane_spec([[(0, 0, 0, width, 0)], []])[:4] if halves else [])
    mixed, mid, two, w_out = out_forward(
        at, own_u[0], spec, slots_u[:4], count, attended, x, out_b, gain, shift
    )
    if halves:
        two, d_got = after(two, d_got)
        d_two = [jnp.concatenate([o, g]) for o, g in zip(d_own, d_got)]
        d_four = [swap(t, "dp", 6 - m) for t, m in zip(d_two, both)]
        two, d_two = after(two, d_two)
    up_cols = own_u[1].shape[1]
    rest = half_u - width
    spec = (
        [(0, 0, up_cols, 0)],
        plane_spec([[(0, 0, width, rest, 0)], [(0, rest, 0, half_u, 0)]]) if halves else [],
    )
    act, slope, w_up = up_forward(at, own_u[1], spec, slots_u, count, two, up_b)
    if halves:
        act, d_four = after(act, d_four)
        slots_d = plane_slots(d_two, d_four)
    half = width // 2
    spec = ([(0, 0, width, 0)], plane_spec([[(0, 0, 0, half, 0)], [(0, half, 0, half, 0)]]) if halves else [])
    layer_out, gffn, sums3, ghid, up_sum = down_both(
        at, own_d, spec, slots_d, count, act, slope, down_b, mid, cot, live_col, gain, shift
    )

    if halves:
        send = grad_down(idx, act, gffn)
        got_down = swap(send, "dp", 1)
        send, ghid = after(send, ghid)
        send = grad_up(idx, two, ghid)
        got_up = swap(send, "dp", 1)
        send, got_down, act = tie((send, got_down, act))
        down_parts = grad_down(idx, act, gffn, got_down)
        down_got = plane_direct(down_parts)
        down_parts, ghid = after(down_parts, ghid)
    gmid, gmix, gatt, sums21 = mid_backward(ghid, w_up, w_out, mid, mixed, cot, live_col, gain)
    if halves:
        got_up, ghid, gmix, down_got[1:] = tie((got_up, ghid, gmix, down_got[1:]))
        up_parts = grad_up(idx, two, ghid, got_up)
        up_got = plane_direct(up_parts)
        up_parts, gatt = after(up_parts, gatt)
    back = functools.partial(attend_back, packed)
    gq0, gk0, gv0, sq0, sv0 = back(gatt, attended, lse, start_row, 0, pairs // 2, 0)
    if halves:
        gq0, gmix, down_got[0] = tie((gq0, gmix, down_got[0]))
        send = grad_heads(idx, normed_one, gq0, gk0, gv0, attended, gmix)
        got_heads = swap(send, "dp", 1)
        send, gatt, up_got[1:] = tie((send, gatt, up_got[1:]))
    gq1, gk1, gv1, sq1, sv1 = back(gatt, attended, lse, start_row, pairs // 2, pairs // 2, 0)
    if halves:
        up_got[0], gq1 = after(up_got[0], gq1)
        total = jnp.concatenate([plane_total(down_parts, down_got), plane_total(up_parts, up_got)])
        ffn_keep, ffn_send = across_first(total)
        ffn_got = swap(ffn_send, "fsdp", 1)
        ffn_keep, ffn_send, gq1 = tie((ffn_keep, ffn_send, gq1))
        send = grad_heads(idx, normed_one, gq1, gk1, gv1)
        got_last = swap(send, "dp", 1)
        send, got_heads, gq0 = tie((send, got_heads, gq0))
        heads_parts = grad_heads(idx, normed_one, gq0, gk0, gv0, attended, gmix, got_heads)
        heads_got = plane_first(heads_parts)
        heads_parts, got_last, gq1 = tie((heads_parts, got_last, gq1))
        last_parts = grad_heads(idx, normed_one, gq1, gk1, gv1, got=got_last)
        last_got = plane_first(last_parts)
        last_parts, ffn_got, gq1 = tie((last_parts, ffn_got, gq1))
        ffn_send = [add_low(ffn_keep[w, 1], ffn_got[w, 1]) for w in range(2)]
        ffn_keep = add_low(ffn_keep[:, 0], ffn_got[:, 0])
        down_got = swap(ffn_send[0], "fsdp", 2)
        ffn_send, gq1 = after(ffn_send, gq1)
    grads = [gq0, gq1, gk0, gk1, gv0, gv1]
    blocks = tokens // BLOCK
    grad_input, sums0 = input_backward(grads, w_qkv, x, gmid, gain, 0, blocks // 2)
    if halves:
        sums0, heads_got, last_got, down_got, up_send = tie(
            (sums0, heads_got, last_got, down_got, ffn_send[1])
        )
        up_got = swap(up_send, "fsdp", 2)
        heads_keep, heads_send = plane_adds(heads_parts, heads_got)
        last_keep, last_send = plane_adds(last_parts, last_got)
        heads_send = [jnp.concatenate(pair, axis=-1) for pair in zip(heads_send, last_send)]
        heads_got = [swap(part, "dp", mask) for part, mask in zip(heads_send, (2, 4))]
        heads_send, grad_input = after(heads_send, grad_input)
    grad_input, sums0_rest = input_backward(
        grads, w_qkv, x, gmid, gain, blocks // 2, blocks // 2, grad_input
    )
    if halves:
        sums0_rest, heads_got, up_got = tie((sums0_rest, heads_got, up_got))
    sums0 = sums0 + sums0_rest
    small_grads = by_shard(
        [
            jnp.concatenate([jnp.concatenate([sq0, sq1], axis=1), jnp.concatenate([sv0, sv1], axis=1)]),
            sums21[4:5],
            up_sum,
            sums3[2:3],
            jnp.concatenate([sums0[0:1], sums21[2:3], sums21[0:1], sums3[0:1]]),
            jnp.concatenate([sums0[1:2], sums21[3:4], sums21[1:2], sums3[1:2]]),
        ],
        shards,
    )
    if halves:
        keep = [jnp.concatenate(pair, axis=-1) for pair in zip(heads_keep, last_keep)]
        total = jnp.stack([add_wide(k, g) for k, g in zip(keep, heads_got)], axis=2)
        keep, send = across_first(total)
        tail = small_grads.reshape(-1, width)
        more = tail.shape[0]
        got = swap(jnp.concatenate([send.reshape(-1, width), tail.astype(BF)]), "fsdp", 1)
        keep, up_got = after(keep, up_got)
        ffn_four = spread(add_low(ffn_keep, jnp.stack([down_got, up_got])))

        keep, got = tie((keep, got))
        tail = tail + got[-more:].astype(F32)
        got = got[:-more].reshape(keep.shape)
        send = add_low(keep[:, 1], got[:, 1])
        keep = add_low(keep[:, 0], got[:, 0])[0]
        got = swap(jnp.concatenate([send.reshape(-1, width), tail.astype(BF)]), "fsdp", 2)

        keep, got, ffn_four = tie((keep, got, ffn_four))
        tail = (tail + got[-more:].astype(F32)).astype(BF)
        piece = add_low(keep.reshape(-1, width), got[:-more])
        piece = jnp.concatenate([piece, tail])
        heads_got = [swap(piece, "dp", mask) for mask in (2, 4, 6)]
        ffn_all = spread_core(ffn_four)
        up_grad, down_grad = finish(
            "finish_ffn", idx, place_ffn, ffn_all, [up_weight.shape, down_weight.shape]
        )

        up_grad, heads_got = after(up_grad, heads_got)
        heads_four = jnp.stack([piece] + heads_got)
        heads_all = spread_core(heads_four)
        heads_core = heads_all[1][1]
        heads_all = [heads_all[0], (heads_all[1][0], heads_core)]
        tail = jnp.sum(heads_four[:, -more:].astype(F32), axis=0) + jnp.sum(
            heads_core[:, -more:].astype(F32), axis=0
        )
        small_sum = lax.dynamic_index_in_dim(
            tail.reshape(small_grads.shape), lax.axis_index("fsdp"), 0, keepdims=False
        )
        qkv_grad, out_grad = finish(
            "finish_heads", idx, place_heads, heads_all, [qkv_weight.shape, out_weight.shape]
        )
    else:
        gpacked = jnp.concatenate([gq0, gq1, gk0, gk1, gv0, gv1], axis=1)

        def reduced(left, right):
            grad = dot_tn(left, right)
            return lax.psum(lax.psum_scatter(grad, "fsdp", scatter_dimension=0, tiled=True), "dp")

        qkv_grad = reduced(normed_one, gpacked)
        out_grad = reduced(attended, gmix)
        up_grad = reduced(two, ghid)
        down_grad = reduced(act, gffn)
        small_sum = lax.dynamic_index_in_dim(
            lax.psum(small_grads, ("dp", "fsdp")), lax.axis_index("fsdp"), 0, keepdims=False
        )
    qv_g, outb_g, upb_g, downb_g, gain_g, shift_g = unpack_small(small_sum[None])
    return (
        layer_out[None],
        grad_input[None],
        qkv_grad,
        qv_g,
        out_grad,
        outb_g[0],
        up_grad,
        upb_g[0],
        down_grad,
        downb_g[0],
        gain_g,
        shift_g,
    )


def solution(mesh):
    rows = P(("dp", "fsdp"), None, None)
    split = P("fsdp", None)
    placed = (
        rows,
        split,
        P(None, "fsdp"),
        split,
        P("fsdp"),
        split,
        P("fsdp"),
        split,
        P("fsdp"),
        P(None, "fsdp"),
        P(None, "fsdp"),
        P(("dp", "fsdp"), None),
        rows,
    )
    return jax.shard_map(
        on_device,
        mesh=mesh,
        in_specs=placed,
        out_specs=(
            rows,
            rows,
            split,
            P(None, "fsdp"),
            split,
            P("fsdp"),
            split,
            P("fsdp"),
            split,
            P("fsdp"),
            P(None, "fsdp"),
            P(None, "fsdp"),
        ),
        check_vma=False,
    )
```

```python
import functools
import math

import jax
import jax.numpy as jnp
from jax import lax
from jax.experimental import pallas as pl
from jax.experimental.pallas import tpu as pltpu
from jax.sharding import PartitionSpec as P

F32 = jnp.float32
BF = jnp.bfloat16
SDS = jax.ShapeDtypeStruct
HEAD_DIM = 64
PAIR = 2 * HEAD_DIM
EPS = 1e-05
MASKED = -1e30
QUERY_SCALE = math.log2(math.e) / math.sqrt(HEAD_DIM)
GRAD_SCALE = 1.0 / math.sqrt(HEAD_DIM)
BLOCK = 256
UP_COLS = 1024
HIDDEN_COLS = 1024
GELU_A = math.sqrt(2.0 / math.pi)
GELU_B = 0.044715 * GELU_A


def params(**more):
    return pltpu.CompilerParams(vmem_limit_bytes=60 * 1024 * 1024, **more)


def cost(flops, nbytes, trans=0):
    return pl.CostEstimate(flops=int(flops) // 1, bytes_accessed=int(nbytes) // 1, transcendentals=int(trans))


def dot_nn(a, b):
    return lax.dot_general(a, b, (((1,), (0,)), ((), ())), preferred_element_type=F32)


def dot_nt(a, b):
    return lax.dot_general(a, b, (((1,), (1,)), ((), ())), preferred_element_type=F32)


def dot_tn(a, b):
    return lax.dot_general(a, b, (((0,), (0,)), ((), ())), preferred_element_type=F32)


def centred(values):
    centre = values - jnp.mean(values, axis=-1, keepdims=True)
    rstd = lax.rsqrt(jnp.mean(centre * centre, axis=-1, keepdims=True) + EPS)
    return centre * rstd, rstd


def norm_back(grad, vhat, rstd, gain):
    e = grad * gain
    mean_e = jnp.mean(e, axis=-1, keepdims=True)
    mean_ev = jnp.mean(e * vhat, axis=-1, keepdims=True)
    return (e - mean_e - vhat * mean_ev) * rstd


def col_sum(values):
    return jnp.sum(values, axis=0, keepdims=True)


def piece_copies(spec, idx_ref, own_refs, slot_refs, places, sems):
    own_spec, slot_spec = spec
    dp, z = idx_ref[0], idx_ref[1]
    copies = []

    def add(group, src, dst):
        copies.append((group, pltpu.make_async_copy(src, dst, sems.at[len(copies)])))

    for o, first, cols, group in own_spec:
        rows = own_refs[o].shape[0]
        dst = places[o].at[pl.ds(pl.multiple_of(z * rows, rows), rows), first : first + cols]
        add(group, own_refs[o].at[:, first : first + cols], dst)
    for (pair, parts), ref in zip(slot_spec, slot_refs):
        rows = ref.shape[1]
        others = ref.shape[0] // 2
        for which, mask in enumerate(pair):
            for k in range(1, others + 1):
                at = which * others + k - 1
                for o, there, here, cols, group in parts:
                    group = k if group is None else group
                    dst = pl.multiple_of((z ^ k) * own_refs[o].shape[0] + (dp ^ mask) * rows, rows)
                    add(
                        group,
                        ref.at[at, :, here : here + cols],
                        places[o].at[pl.ds(dst, rows), there : there + cols],
                    )
    return copies


def count_copies(spec, slots):
    own_spec, slot_spec = spec
    return len(own_spec) + sum(len(parts) * s.shape[0] for (_, parts), s in zip(slot_spec, slots))


def start_all(copies):
    for _, copy in copies:
        copy.start()


def wait_group(copies, group):
    for g, copy in copies:
        if g == group:
            copy.wait()


def whole_shapes(owns, shards):
    return [(o.shape[0] * shards, o.shape[1]) for o in owns]


ANY = pl.BlockSpec(memory_space=pl.ANY)
SMEM = pl.BlockSpec(memory_space=pltpu.SMEM)


def qkv_kernel(spec, n_slots, idx_ref, own_ref, *refs):
    slots = refs[:n_slots]
    x_ref, bias_ref, gain_ref, shift_ref, normed_ref, packed_ref, out_ref = refs[n_slots : n_slots + 7]
    weight, sems, out_sem = refs[n_slots + 7 :]
    step, steps = pl.program_id(0), pl.num_programs(0)
    copies = piece_copies(spec, idx_ref, [own_ref], slots, [weight], sems)
    bn = packed_ref.shape[1]

    @pl.when(step == 0)
    def _():
        start_all(copies)
        vhat, _ = centred(x_ref[...].astype(F32))
        normed_ref[...] = (vhat * gain_ref[...] + shift_ref[...]).astype(BF)
        wait_group(copies, 0)

    half = weight.shape[1] // 2

    @pl.when(step == half // bn)
    def _():
        wait_group(copies, 1)
        pltpu.make_async_copy(weight, out_ref, out_sem).start()

    block = weight[:, pl.ds(pl.multiple_of(step * bn, bn), bn)]
    out = dot_nn(normed_ref[...], block) + bias_ref[...]
    packed_ref[...] = (out * jnp.where(step < steps // 3, QUERY_SCALE, 1.0)).astype(BF)

    @pl.when(step == steps - 1)
    def _():
        pltpu.make_async_copy(weight, out_ref, out_sem).wait()


def qkv_forward(idx, own, spec, slots, shards, x, bias, gain, shift):
    tokens, width = x.shape
    ((rows, cols),) = whole_shapes([own], shards)
    bn = width // 2
    row = pl.BlockSpec((1, width), lambda j: (0, 0))
    full = pl.BlockSpec((tokens, width), lambda j: (0, 0))
    return pl.pallas_call(
        functools.partial(qkv_kernel, spec, len(slots)),
        grid=(cols // bn,),
        in_specs=[SMEM] + [ANY] * (1 + len(slots))
        + [full, pl.BlockSpec((1, bn), lambda j: (0, j)), row, row],
        out_specs=(full, pl.BlockSpec((tokens, bn), lambda j: (0, j)), ANY),
        out_shape=(SDS((tokens, width), BF), SDS((tokens, cols), BF), SDS((rows, cols), BF)),
        scratch_shapes=[
            pltpu.VMEM((rows, cols), BF),
            pltpu.SemaphoreType.DMA((count_copies(spec, slots),)),
            pltpu.SemaphoreType.DMA(()),
        ],
        compiler_params=params(),
        cost_estimate=cost(2 * tokens * width * cols, 2 * width * cols + 2 * tokens * cols),
        name="qkv_forward",
    )(idx, own, *slots, x, bias, gain, shift)


def gelu_and_slope(a):
    sq = a * a
    t = jnp.tanh(a * (sq * GELU_B + GELU_A))
    half = 0.5 * t + 0.5
    act = a * half
    slope = half + act * ((1.0 - half) * (sq * (6.0 * GELU_B) + 2.0 * GELU_A))
    return act.astype(BF), slope.astype(BF)


def out_kernel(spec, n_slots, idx_ref, own_ref, *refs):
    slots = refs[:n_slots]
    att_ref, x_ref, bias_ref, gain_ref, shift_ref = refs[n_slots : n_slots + 5]
    mixed_ref, mid_ref, two_ref, save_ref, weight, sems, save_sem = refs[n_slots + 5 :]
    step, steps = pl.program_id(0), pl.num_programs(0)
    copies = piece_copies(spec, idx_ref, [own_ref], slots, [weight], sems)
    save = pltpu.make_async_copy(weight, save_ref, save_sem)

    @pl.when(step == 0)
    def _():
        start_all(copies)
        wait_group(copies, 0)
        save.start()

    mixed = dot_nn(att_ref[...], weight[...]) + bias_ref[...]
    mixed_ref[...] = mixed
    vhat, _ = centred(mixed)
    mid = x_ref[...].astype(F32) + vhat * gain_ref[1:2, :] + shift_ref[1:2, :]
    mid_ref[...] = mid
    vhat, _ = centred(mid)
    two_ref[...] = (vhat * gain_ref[2:3, :] + shift_ref[2:3, :]).astype(BF)

    @pl.when(step == steps - 1)
    def _():
        save.wait()


def out_forward(idx, own, spec, slots, shards, attended, x, bias, gain, shift):
    tokens, width = x.shape
    (shape,) = whole_shapes([own], shards)
    tok = pl.BlockSpec((BLOCK, width), lambda i: (i, 0))

    def whole(arr):
        return pl.BlockSpec(arr.shape, lambda i: (0, 0))

    return pl.pallas_call(
        functools.partial(out_kernel, spec, len(slots)),
        grid=(tokens // BLOCK,),
        in_specs=[SMEM] + [ANY] * (1 + len(slots)) + [tok, tok, whole(bias), whole(gain), whole(shift)],
        out_specs=(tok, tok, tok, ANY),
        out_shape=(
            SDS((tokens, width), F32),
            SDS((tokens, width), F32),
            SDS((tokens, width), BF),
            SDS(shape, BF),
        ),
        scratch_shapes=[
            pltpu.VMEM(shape, BF),
            pltpu.SemaphoreType.DMA((count_copies(spec, slots),)),
            pltpu.SemaphoreType.DMA(()),
        ],
        compiler_params=params(),
        cost_estimate=cost(2 * tokens * width * width, 16 * tokens * width),
        name="out_forward",
    )(idx, own, *slots, attended, x, bias, gain, shift)


def up_kernel(spec, n_slots, idx_ref, own_ref, *refs):
    slots = refs[:n_slots]
    two_ref, bias_ref, act_ref, slope_ref, save_ref, weight, sems, save_sems = refs[n_slots:]
    step = pl.program_id(0)
    copies = piece_copies(spec, idx_ref, [own_ref], slots, [weight], sems)
    bn = act_ref.shape[1]
    blocks = weight.shape[1] // bn

    def save(j):
        cols = slice(j * bn, (j + 1) * bn)
        return pltpu.make_async_copy(weight.at[:, cols], save_ref.at[:, cols], save_sems.at[j])

    @pl.when(step == 0)
    def _():
        start_all(copies)

    for j in range(blocks):

        @pl.when(step == j)
        def _():
            wait_group(copies, j)
            save(j).start()

    at = pl.ds(pl.multiple_of(step * bn, bn), bn)
    a = dot_nn(two_ref[...], weight[:, at]) + bias_ref[...]
    act_ref[...], slope_ref[...] = gelu_and_slope(a)

    @pl.when(step == blocks - 1)
    def _():
        for j in range(blocks):
            save(j).wait()


def up_forward(idx, own, spec, slots, shards, two, bias):
    tokens, width = two.shape
    (shape,) = whole_shapes([own], shards)
    cols = shape[1]
    bn = UP_COLS
    col = pl.BlockSpec((tokens, bn), lambda i: (0, i))
    return pl.pallas_call(
        functools.partial(up_kernel, spec, len(slots)),
        grid=(cols // bn,),
        in_specs=[SMEM] + [ANY] * (1 + len(slots))
        + [pl.BlockSpec((tokens, width), lambda i: (0, 0)), pl.BlockSpec((1, bn), lambda i: (0, i))],
        out_specs=(col, col, ANY),
        out_shape=(SDS((tokens, cols), BF), SDS((tokens, cols), BF), SDS(shape, BF)),
        scratch_shapes=[
            pltpu.VMEM(shape, BF),
            pltpu.SemaphoreType.DMA((count_copies(spec, slots),)),
            pltpu.SemaphoreType.DMA((cols // bn,)),
        ],
        compiler_params=params(),
        cost_estimate=cost(2 * tokens * width * cols, 2 * width * cols + 4 * tokens * cols),
        name="up_forward",
    )(idx, own, *slots, two, bias)


def down_kernel(spec, n_slots, first, idx_ref, own_ref, *refs):
    slots = refs[:n_slots]
    act_ref, slope_ref, bias_ref, mid_ref, cot_ref, live_ref, gain_ref, shift_ref = refs[n_slots : n_slots + 8]
    out_ref, grad_ref, sums_ref, hid_ref, hsum_ref, weight, sems = refs[n_slots + 8 :]
    step = pl.program_id(0)
    copies = piece_copies(spec, idx_ref, [own_ref], slots, [weight], sems)

    @pl.when(step == 0)
    def _():
        start_all(copies)
        sums_ref[...] = jnp.zeros_like(sums_ref)

    rows = own_ref.shape[0]

    @pl.when(step < first)
    def _():
        ffn = jnp.broadcast_to(bias_ref[...], out_ref.shape)
        for k in range(weight.shape[0] // rows):

            @pl.when(step == 0)
            def _():
                wait_group(copies, k)

            part = pl.ds(pl.multiple_of((idx_ref[1] ^ k) * rows, rows), rows)
            ffn = ffn + dot_nn(act_ref[:, part], weight[part, :])
        vhat, rstd = centred(ffn)
        gain = gain_ref[3:4, :]
        out_ref[...] = (mid_ref[...] + vhat * gain + shift_ref[3:4, :]).astype(BF)
        grad = cot_ref[...].astype(F32) * live_ref[...]
        low = norm_back(grad, vhat, rstd, gain).astype(BF)
        grad_ref[pl.ds(pl.multiple_of(step * BLOCK, BLOCK), BLOCK), :] = low
        sums_ref[0:1, :] += col_sum(grad * vhat)
        sums_ref[1:2, :] += col_sum(grad)
        sums_ref[2:3, :] += col_sum(low.astype(F32))

    @pl.when(step >= first)
    def _():
        bn = hid_ref.shape[1]
        at = pl.ds(pl.multiple_of((step - first) * bn, bn), bn)
        low = (dot_nt(grad_ref[...], weight[at, :]) * slope_ref[...].astype(F32)).astype(BF)
        hid_ref[...] = low
        hsum_ref[...] = col_sum(low.astype(F32))


def down_both(idx, own, spec, slots, shards, act, slope, bias, mid, cot, live, gain, shift):
    tokens, width = mid.shape
    (shape,) = whole_shapes([own], shards)
    cols = shape[0]
    bn = HIDDEN_COLS
    first = tokens // BLOCK

    def at(i):
        return jnp.minimum(i, first - 1)

    tok = pl.BlockSpec((BLOCK, width), lambda i: (at(i), 0))
    col = pl.BlockSpec((tokens, bn), lambda i: (0, jnp.maximum(i - first, 0)))

    def whole(arr):
        return pl.BlockSpec(arr.shape, lambda i: (0, 0))

    return pl.pallas_call(
        functools.partial(down_kernel, spec, len(slots), first),
        grid=(first + cols // bn,),
        in_specs=[SMEM] + [ANY] * (1 + len(slots))
        + [
            pl.BlockSpec((BLOCK, cols), lambda i: (at(i), 0)),
            col,
            whole(bias),
            tok,
            tok,
            pl.BlockSpec((BLOCK, 1), lambda i: (at(i), 0)),
            whole(gain),
            whole(shift),
        ],
        out_specs=(
            tok,
            pl.BlockSpec((tokens, width), lambda i: (0, 0)),
            pl.BlockSpec((8, width), lambda i: (0, 0)),
            col,
            pl.BlockSpec((1, bn), lambda i: (0, jnp.maximum(i - first, 0))),
        ),
        out_shape=(
            SDS((tokens, width), BF),
            SDS((tokens, width), BF),
            SDS((8, width), F32),
            SDS((tokens, cols), BF),
            SDS((1, cols), F32),
        ),
        scratch_shapes=[pltpu.VMEM(shape, BF), pltpu.SemaphoreType.DMA((count_copies(spec, slots),))],
        compiler_params=params(),
        cost_estimate=cost(4 * tokens * width * cols, 2 * width * cols + 6 * tokens * cols),
        name="down_both",
    )(idx, own, *slots, act, slope, bias, mid, cot, live, gain, shift)


def column_loads(src, dst, sems):
    n = dst.shape[1] // sems.shape[0]
    cols = [slice(j * n, (j + 1) * n) for j in range(sems.shape[0])]
    return [(pltpu.make_async_copy(src.at[:, c], dst.at[:, c], sems.at[j]), c) for j, c in enumerate(cols)]


def mid_kernel(
    gh_ref, up_ref, out_w_ref, mid_ref, mixed_ref, cot_ref, live_ref, gain_ref,
    gmid_ref, gmix_ref, gatt_ref, sums_ref, weight, sems,
):
    load = column_loads(up_ref, weight, sems)

    @pl.when(pl.program_id(0) == 0)
    def _():
        for copy, _ in load:
            copy.start()
        sums_ref[...] = jnp.zeros_like(sums_ref)

    grad = 0.0
    for copy, cols in load:

        @pl.when(pl.program_id(0) == 0)
        def _():
            copy.wait()

        grad = grad + dot_nt(gh_ref[:, cols], weight[:, cols])
    vhat, rstd = centred(mid_ref[...])
    sums_ref[0:1, :] += col_sum(grad * vhat)
    sums_ref[1:2, :] += col_sum(grad)
    gmid = cot_ref[...].astype(F32) * live_ref[...] + norm_back(grad, vhat, rstd, gain_ref[2:3, :])
    gmid_ref[...] = gmid
    vhat, rstd = centred(mixed_ref[...])
    sums_ref[2:3, :] += col_sum(gmid * vhat)
    sums_ref[3:4, :] += col_sum(gmid)
    low = norm_back(gmid, vhat, rstd, gain_ref[1:2, :]).astype(BF)
    gmix_ref[...] = low
    sums_ref[4:5, :] += col_sum(low.astype(F32))
    gatt_ref[...] = dot_nt(low, out_w_ref[...]).astype(BF)


def mid_backward(gh, up, out_w, mid, mixed, cot, live, gain):
    tokens, width = mid.shape
    cols = gh.shape[1]
    tok = pl.BlockSpec((BLOCK, width), lambda i: (i, 0))

    def whole(arr):
        return pl.BlockSpec(arr.shape, lambda i: (0, 0))

    return pl.pallas_call(
        mid_kernel,
        grid=(tokens // BLOCK,),
        in_specs=[
            pl.BlockSpec((BLOCK, cols), lambda i: (i, 0)),
            ANY,
            whole(out_w),
            tok,
            tok,
            tok,
            pl.BlockSpec((BLOCK, 1), lambda i: (i, 0)),
            whole(gain),
        ],
        out_specs=(tok, tok, tok, pl.BlockSpec((8, width), lambda i: (0, 0))),
        out_shape=(
            SDS((tokens, width), F32),
            SDS((tokens, width), BF),
            SDS((tokens, width), BF),
            SDS((8, width), F32),
        ),
        scratch_shapes=[pltpu.VMEM(up.shape, BF), pltpu.SemaphoreType.DMA((4,))],
        compiler_params=params(),
        cost_estimate=cost(2 * tokens * width * (cols + width), 2 * width * cols + 2 * tokens * cols),
        name="mid_backward",
    )(gh, up, out_w, mid, mixed, cot, live, gain)


def input_kernel(n_grads, n_into, *refs):
    grad_refs, (w_ref, x_ref, gmid_ref, gain_ref) = refs[:n_grads], refs[n_grads : n_grads + 4]
    out_ref, sums_ref, weight, sems = refs[n_grads + 4 + n_into :]
    load = column_loads(w_ref, weight, sems)

    @pl.when(pl.program_id(0) == 0)
    def _():
        for copy, _ in load:
            copy.start()
        sums_ref[...] = jnp.zeros_like(sums_ref)

    grad = 0.0
    for ref, (copy, cols) in zip(grad_refs, load):

        @pl.when(pl.program_id(0) == 0)
        def _():
            copy.wait()

        grad = grad + dot_nt(ref[...], weight[:, cols])
    vhat, rstd = centred(x_ref[...].astype(F32))
    sums_ref[0:1, :] += col_sum(grad * vhat)
    sums_ref[1:2, :] += col_sum(grad)
    out_ref[...] = gmid_ref[...] + norm_back(grad, vhat, rstd, gain_ref[0:1, :])


def input_backward(grads, weight, x, gmid, gain, first, count, into=None):
    tokens, width = x.shape
    tok = pl.BlockSpec((BLOCK, width), lambda i: (first + i, 0))

    def whole(arr):
        return pl.BlockSpec(arr.shape, lambda i: (0, 0))

    in_specs = [pl.BlockSpec((BLOCK, g.shape[1]), lambda i: (first + i, 0)) for g in grads]
    in_specs += [ANY, tok, tok, whole(gain)]
    args = [*grads, weight, x, gmid, gain]
    aliases = {}
    if into is not None:
        aliases = {len(args): 0}
        in_specs.append(pl.BlockSpec(memory_space=pl.ANY))
        args.append(into)
    return pl.pallas_call(
        functools.partial(input_kernel, len(grads), len(aliases)),
        grid=(count,),
        in_specs=in_specs,
        out_specs=(tok, pl.BlockSpec((8, width), lambda i: (0, 0))),
        out_shape=(SDS((tokens, width), F32), SDS((8, width), F32)),
        input_output_aliases=aliases,
        scratch_shapes=[pltpu.VMEM(weight.shape, BF), pltpu.SemaphoreType.DMA((len(grads),))],
        compiler_params=params(),
        cost_estimate=cost(6 * count * BLOCK * width * width, 6 * width * width),
        name="input_backward",
    )(*args)


def fill_bias(bias, start_ref):
    length = bias.shape[0]
    for j in range(length // BLOCK):
        key = lax.broadcasted_iota(jnp.int32, (BLOCK, length), 0) + j * BLOCK
        query = lax.broadcasted_iota(jnp.int32, (BLOCK, length), 1)
        allowed = (key <= query) & (key >= start_ref[...])
        bias[j * BLOCK : (j + 1) * BLOCK, :] = jnp.where(allowed, 0.0, MASKED)


def one_head(low, arr, head):
    zero = jnp.zeros_like(arr)
    return jnp.where(low, arr, zero) if head == 0 else jnp.where(low, zero, arr)


def attend_kernel(q_ref, k_ref, v_ref, start_ref, out_ref, lse_ref, bias):
    length = q_ref.shape[0]

    @pl.when(pl.program_id(0) == 0)
    def _():
        fill_bias(bias, start_ref)

    low = lax.broadcasted_iota(jnp.int32, (1, PAIR), 1) < HEAD_DIM
    low_rows = lax.broadcasted_iota(jnp.int32, (PAIR, 1), 0) < HEAD_DIM
    keys = k_ref[...]
    values = jnp.concatenate([v_ref[...], jnp.ones((length, PAIR), BF)], axis=1)
    for i in range(length // BLOCK):
        reach = (i + 1) * BLOCK
        sl = slice(i * BLOCK, reach)
        queries = q_ref[sl, :]
        parts = []
        for head in range(2):
            scores = dot_nt(keys[:reach], one_head(low, queries, head)) + bias[:reach, sl]
            top = jnp.max(scores, axis=0, keepdims=True)
            probs = jnp.exp2(scores - top).astype(BF)
            mixed = dot_tn(values[:reach], probs)
            total = mixed[PAIR : PAIR + 1]
            parts.append(mixed[:PAIR] / total)
            lse_ref[0, head : head + 1, sl] = top + jnp.log2(total)
        out_ref[sl, :] = jnp.where(low_rows, parts[0], parts[1]).T.astype(BF)


def attend(packed, start_row, first, count, into=None):
    length = packed.shape[0]
    pairs = packed.shape[1] // (3 * PAIR)

    def blk(offset):
        return pl.BlockSpec((length, PAIR), lambda h: (0, offset + first + h))

    in_specs = [blk(0), blk(pairs), blk(2 * pairs), pl.BlockSpec((1, length), lambda h: (0, 0))]
    args = [packed, packed, packed, start_row]
    kernel, aliases = attend_kernel, {}
    if into is not None:
        in_specs = in_specs + [ANY] * len(into)
        aliases = {len(args) + i: i for i in range(len(into))}
        args = args + list(into)

        def kernel(*refs):
            attend_kernel(*refs[:4], *refs[4 + len(into) :])

    return pl.pallas_call(
        kernel,
        grid=(count,),
        in_specs=in_specs,
        out_specs=(blk(0), pl.BlockSpec((1, 2, length), lambda h: (first + h, 0, 0))),
        out_shape=(SDS((length, PAIR * pairs), BF), SDS((pairs, 2, length), F32)),
        input_output_aliases=aliases,
        scratch_shapes=[pltpu.VMEM((length, length), F32)],
        compiler_params=params(),
        cost_estimate=cost(8 * count * length * length * PAIR, 8 * length * count * PAIR),
        name="attend",
    )(*args)


def attend_back_kernel(
    q_ref, k_ref, v_ref, g_ref, o_ref, lse_ref, start_ref, gq_ref, gk_ref, gv_ref, sq_ref, sv_ref, bias, acc
):
    length = q_ref.shape[0]

    @pl.when(pl.program_id(0) == 0)
    def _():
        fill_bias(bias, start_ref)

    low = lax.broadcasted_iota(jnp.int32, (1, PAIR), 1) < HEAD_DIM
    queries, grads = q_ref[...], g_ref[...]
    q_of = [one_head(low, queries, head) for head in range(2)]
    g_of = [one_head(low, grads, head) for head in range(2)]
    inner = (grads.astype(F32) * o_ref[...].astype(F32)).T
    inner_of = [col_sum(inner[:HEAD_DIM]), col_sum(inner[HEAD_DIM:])]
    sum_v = jnp.zeros((1, PAIR), F32)
    for j in range(length // BLOCK):
        first = j * BLOCK
        sl = slice(first, first + BLOCK)
        keys, values = k_ref[sl, :], v_ref[sl, :]
        gk = gv = gq = 0.0
        for head in range(2):
            scores = dot_nt(keys, q_of[head][first:]) + bias[sl, first:]
            probs = jnp.exp2(scores - lse_ref[0, head : head + 1, first:])
            gprobs = dot_nt(values, g_of[head][first:])
            gscores = (probs * (gprobs - inner_of[head][:, first:]) * GRAD_SCALE).astype(BF)
            gv = gv + dot_nn(probs.astype(BF), g_of[head][first:])
            gk = gk + dot_nn(gscores, q_of[head][first:])
            gq = gq + dot_tn(gscores, one_head(low, keys, head))
        low_v = gv.astype(BF)
        gv_ref[sl, :] = low_v
        gk_ref[sl, :] = (gk * (1.0 / QUERY_SCALE)).astype(BF)
        sum_v = sum_v + col_sum(low_v.astype(F32))
        if j == 0:
            acc[...] = gq
        else:
            acc[first:, :] += gq
    low_q = acc[...].astype(BF)
    gq_ref[...] = low_q
    sq_ref[...] = col_sum(low_q.astype(F32))
    sv_ref[...] = sum_v


def attend_back(packed, grads, attended, lse, start_row, first, count, columns, into=None):
    length = packed.shape[0]
    total = packed.shape[1] // (3 * PAIR)

    def blk(offset):
        return pl.BlockSpec((length, PAIR), lambda h: (0, offset + h))

    row = pl.BlockSpec((1, PAIR), lambda h: (0, columns + h))
    out = blk(columns)
    grad = SDS((length, PAIR * total // 2), BF)
    sums = SDS((1, PAIR * total // 2), F32)
    in_specs = [
        blk(first),
        blk(total + first),
        blk(2 * total + first),
        blk(first),
        blk(first),
        pl.BlockSpec((1, 2, length), lambda h: (first + h, 0, 0)),
        pl.BlockSpec((1, length), lambda h: (0, 0)),
    ]
    args = [packed, packed, packed, grads, attended, lse, start_row]
    kernel, aliases = attend_back_kernel, {}
    if into is not None:
        in_specs = in_specs + [pl.BlockSpec(memory_space=pl.ANY)] * len(into)
        aliases = {len(args) + i: i for i in range(len(into))}
        args = args + list(into)

        def kernel(*refs):
            attend_back_kernel(*refs[:7], *refs[7 + len(into) :])

    return pl.pallas_call(
        kernel,
        grid=(count,),
        in_specs=in_specs,
        out_specs=(out, out, out, row, row),
        out_shape=(grad, grad, grad, sums, sums),
        input_output_aliases=aliases,
        scratch_shapes=[pltpu.VMEM((length, length), F32), pltpu.VMEM((length, PAIR), F32)],
        compiler_params=params(),
        cost_estimate=cost(20 * count * length * length * PAIR, 16 * length * count * PAIR),
        name="attend_back",
    )(*args)


def swap(arr, axis, mask):
    size = lax.axis_size(axis)
    return lax.ppermute(arr, axis, [(i, i ^ mask) for i in range(size)])


def after(first, then):
    return lax.optimization_barrier((first, then))


def shard_swaps(piece):
    return [swap(piece, "fsdp", k) for k in range(1, lax.axis_size("fsdp"))]


def shard_pair(piece, got):
    return swap(jnp.stack([piece, got]), "fsdp", 1)


def shard_slots(got, pair):
    return [pair[0], got, pair[1]]


PLANE_MASKS = [
    (0, 4), (2, 6), (1, 5), (3, 7),
    (0, 2), (4, 6), (1, 3), (5, 7),
]


def plane_slots(two, four):
    return [a for t, f in zip(two, four) for a in (t, f, swap(t, "dp", 1), swap(f, "dp", 1))]


def plane_spec(parts):
    return [(pair, parts[i // 4]) for i, pair in enumerate(PLANE_MASKS)]


def split_down(wide, zz):
    rows, cols = wide.shape[0] // 4, wide.shape[1] // 2
    part = wide[zz * rows : (zz + 1) * rows]
    return part[:, :cols], part[:, cols:]


def split_up(wide, zz):
    rows = wide.shape[0] // 8
    return wide[2 * zz * rows : (2 * zz + 1) * rows], wide[(2 * zz + 1) * rows : (2 * zz + 2) * rows]


def side_by_side(refs):
    blocks = [r[...] for r in refs]
    return blocks[0] if len(blocks) == 1 else jnp.concatenate(blocks, axis=1)


def emit(keep, direct, wide, split, z, chip, rest):
    if not keep:
        for zz in range(4):
            for f, part in enumerate(split(wide, zz)):
                rest[0][0, 0, zz ^ z, f] = part.astype(BF)
        return
    got_ref, outs = rest[0], rest[1:]
    for dst in range(4):

        @pl.when(chip == dst)
        def _():
            for zz in range(4):
                slot = zz ^ z
                for f, part in enumerate(split(wide, zz)):
                    low = (part + got_ref[0, 0, slot, f].astype(F32)).astype(BF)
                    if direct:
                        outs[dst][0, slot, f] = low
                    else:
                        bit = dst // 2 if f == 0 else dst % 2
                        outs[2 * f + bit][0, 0, slot] = low


def grad_kernel(keep, direct, jobs, idx_ref, *refs):
    step, z = pl.program_id(0), idx_ref[1]
    at = 0
    n_in = sum(n for groups, _ in jobs for group in groups for n in group)
    rest = refs[n_in:]
    for number, (groups, split) in enumerate(jobs):
        blocks = []
        for n_left, n_right in groups:
            blocks.append((refs[at : at + n_left], refs[at + n_left : at + n_left + n_right]))
            at += n_left + n_right

        @pl.when(step // 4 == number)
        def _():
            dots = [dot_tn(side_by_side(left), side_by_side(right)) for left, right in blocks]
            wide = dots[0] if len(dots) == 1 else jnp.concatenate(dots, axis=1)
            emit(keep, direct, wide, split, z, step % 4, rest)


def grad_call(name, idx, specs, args, jobs, piece, flops, got=None, direct=True):
    keep = got is not None
    n_jobs = len(jobs)
    rows, cols = piece
    block = pl.BlockSpec((1, 1, 4, 2, rows, cols), lambda i, idx: (i % 4, i // 4, 0, 0, 0, 0))
    half = (1, 1, 4, rows, cols)
    if keep and direct:
        specs = specs + [block]
        args = args + [got]
        out_specs = (pl.BlockSpec((1, 4, 2, rows, cols), lambda i, idx: (0, 0, 0, 0, 0)),) * 4
        out_shape = (SDS((1, 4, 2, rows, cols), BF),) * 4
    elif keep:
        along_y = (
            lambda i, idx: (jnp.minimum(i % 4, 1), i // 4, 0, 0, 0),
            lambda i, idx: (jnp.maximum(i % 4 - 2, 0), i // 4, 0, 0, 0),
        )
        along_x = (lambda i, idx: (i % 4 // 2, i // 4, 0, 0, 0),) * 2
        specs = specs + [block]
        args = args + [got]
        out_specs = tuple(pl.BlockSpec(half, m) for m in along_y + along_x)
        out_shape = (SDS((2, n_jobs, 4, rows, cols), BF),) * 4
    else:
        out_specs = block
        out_shape = SDS((4, n_jobs, 4, 2, rows, cols), BF)
    return pl.pallas_call(
        functools.partial(grad_kernel, keep, direct, jobs),
        grid_spec=pltpu.PrefetchScalarGridSpec(
            num_scalar_prefetch=1, grid=(4 * n_jobs,), in_specs=specs, out_specs=out_specs
        ),
        out_shape=out_shape,
        compiler_params=params(),
        cost_estimate=cost(flops, flops // 400),
        name=name + ("_keep" if keep else "_send"),
    )(idx, *args)


def chip_of(i, idx):
    return (idx[0] // 2) ^ (3 - i)


def core_of(keep, idx):
    return idx[0] & 1 if keep else (idx[0] & 1) ^ 1


def grad_down(idx, act, gffn, got=None):
    tokens, width = gffn.shape
    keep = got is not None
    rows = act.shape[1] // 32

    def act_spec(zz):
        def at(i, idx):
            return (0, zz * 8 + chip_of(i, idx) * 2 + core_of(keep, idx))

        return pl.BlockSpec((tokens, rows), at)

    specs = [act_spec(0), act_spec(1), act_spec(2), act_spec(3)]
    specs += [pl.BlockSpec((tokens, width), lambda i, idx: (0, 0))]
    args = [act, act, act, act, gffn]
    flops = act.shape[1] * width * tokens
    jobs = [([(4, 1)], split_down)]
    return grad_call("grad_down", idx, specs, args, jobs, (rows, width // 2), flops, got)


def grad_up(idx, two, ghid, got=None):
    tokens, width = two.shape
    keep = got is not None
    cols = ghid.shape[1] // 8
    specs = [
        pl.BlockSpec((tokens, width), lambda i, idx: (0, 0)),
        pl.BlockSpec((tokens, cols), lambda i, idx: (0, chip_of(i, idx) * 2 + core_of(keep, idx))),
    ]
    flops = ghid.shape[1] * width * tokens
    jobs = [([(1, 1)], split_up)]
    return grad_call("grad_up", idx, specs, [two, ghid], jobs, (width // 8, cols), flops, got)


def grad_heads(idx, one, gq, gk, gv, att=None, gmix=None, got=None):
    tokens, width = one.shape
    keep = got is not None
    rows = width // 8

    def left(zz):
        return pl.BlockSpec((tokens, rows), lambda i, idx: (0, zz * 2 + core_of(keep, idx)))

    def right(cols):
        return pl.BlockSpec((tokens, cols), lambda i, idx: (0, chip_of(i, idx)))

    lefts = [left(0), left(1), left(2), left(3)]
    specs, args, groups = lefts + [right(PAIR)] * 3, [one] * 4 + [gq, gk, gv], [(4, 3)]
    cols = 3 * PAIR
    if att is not None:
        specs, args, groups = specs + lefts + [right(width // 4)], args + [att] * 4 + [gmix], groups + [(4, 1)]
        cols += width // 4
    flops = 4 * tokens * width * cols
    return grad_call("grad_heads", idx, specs, args, [(groups, split_up)], (rows // 2, cols), flops, got, False)


def add_low(a, b):
    return (a.astype(F32) + b.astype(F32)).astype(BF)


def add_wide(a, b):
    return a.astype(F32) + b.astype(F32)


def plane_first(parts):
    return [swap(parts[2 * f], "dp", mask) for f, mask in enumerate((4, 2))]


def plane_adds(parts, got):
    send = [add_low(parts[2 * f + 1][0], got[f][0]) for f in range(2)]
    keep = [add_low(parts[2 * f + 1][1], got[f][1]) for f in range(2)]
    return keep, send


def plane_second(parts, got):
    keep, send = plane_adds(parts, got)
    return keep, [swap(s, "dp", mask) for s, mask in zip(send, (2, 4))]


def plane_direct(parts):
    return [swap(part, "dp", mask) for part, mask in zip(parts, (6, 4, 2))]


def plane_total(parts, got):
    return add_wide(parts[3], got[0]) + add_wide(got[1], got[2])


def flows_total(keep, got):
    return jnp.stack([add_wide(k, g) for k, g in zip(keep, got)], axis=2)


def across_first(both):
    return both[:, 0::2].astype(BF), both[:, 1::2].astype(BF)


def spread(piece):
    four = jnp.stack([piece] + [swap(piece, "dp", mask) for mask in (2, 4, 6)])
    return four


def spread_core(four):
    return [((0, 2, 4, 6), four), ((1, 3, 5, 7), swap(four, "dp", 1))]


def place_ffn(dp, piece, outs):
    up_grad, down_grad = outs
    rows, cols = piece.shape[2], piece.shape[3]
    at = pl.ds(pl.multiple_of(dp * rows, rows), rows)
    down_grad[at, :cols] = piece[0, 0].astype(F32)
    down_grad[at, cols:] = piece[0, 1].astype(F32)
    at = pl.ds(pl.multiple_of(dp * cols, cols), cols)
    up_grad[:rows, at] = piece[1, 0].astype(F32)
    up_grad[rows:, at] = piece[1, 1].astype(F32)


def place_heads(dp, piece, outs):
    qkv_grad, out_grad = outs
    width = out_grad.shape[1]
    rows, cols = out_grad.shape[0] // 2, width // 4
    chip, core = dp // 2, dp % 2
    at_rows = pl.ds(pl.multiple_of(core * rows, rows), rows)
    part_of = piece[:rows].astype(F32)
    for half, skip in ((0, 0), (1, 3 * PAIR + cols)):
        for part in range(3):
            at = pl.multiple_of(part * width + half * (width // 2) + chip * PAIR, PAIR)
            here = skip + part * PAIR
            qkv_grad[at_rows, pl.ds(at, PAIR)] = part_of[:, here : here + PAIR]
    at = pl.multiple_of(chip * cols, cols)
    out_grad[at_rows, pl.ds(at, cols)] = part_of[:, 3 * PAIR : 3 * PAIR + cols]


def finish_kernel(placer, masks, idx_ref, *refs):
    ins, outs = refs[: len(masks)], refs[len(masks) :]
    for group, ref in zip(masks, ins):
        for which, mask in enumerate(group):
            placer(idx_ref[0] ^ mask, ref[which], outs)


def finish(name, idx, placer, flow, shapes):
    masks = [m for m, _ in flow]
    arrays = [a for _, a in flow]
    vmem = pl.BlockSpec(memory_space=pltpu.VMEM)
    return pl.pallas_call(
        functools.partial(finish_kernel, placer, masks),
        in_specs=[SMEM] + [vmem] * len(arrays),
        out_specs=(vmem,) * len(shapes),
        out_shape=tuple(SDS(s, F32) for s in shapes),
        compiler_params=params(),
        cost_estimate=cost(0, sum(6 * math.prod(s) for s in shapes)),
        name=name,
    )(idx, *arrays)


def segment_starts(lengths, length):
    ends = jnp.cumsum(lengths)
    positions = jnp.arange(length, dtype=jnp.int32)
    begun = jnp.where(ends[None, :] <= positions[:, None], ends[None, :], 0)
    return jnp.max(begun, axis=1).astype(jnp.int32), positions < ends[-1]


def by_block(there, here, cols):
    parts = []
    while cols:
        n = min(cols, UP_COLS - there % UP_COLS)
        parts.append((0, there, here, n, there // UP_COLS))
        there, here, cols = there + n, here + n, cols - n
    return parts


def eighth(shard):
    rows = shard.shape[0] // 8
    return lax.dynamic_slice_in_dim(shard, lax.axis_index("dp") * rows, rows, axis=0)


SMALL_ROWS = 16


def pack_small(qv_bias, out_bias, up_bias, down_bias, gain, shift):
    flat = [a.reshape(-1) for a in (qv_bias, out_bias, up_bias, down_bias, gain, shift)]
    return jnp.concatenate(flat)


def unpack_small(shards):
    count, total = shards.shape
    unit = total // SMALL_ROWS
    sizes = ((2, unit), (1, unit), (1, 4 * unit), (1, unit), (4, unit), (4, unit))
    out, at = [], 0
    for lead, cols in sizes:
        block = shards[:, at : at + lead * cols].reshape(count, lead, cols)
        out.append(jnp.swapaxes(block, 0, 1).reshape(lead, count * cols))
        at += lead * cols
    return out


def by_shard(rows, count):
    flat = []
    for arr in rows:
        lead, cols = arr.shape
        flat.append(
            jnp.swapaxes(arr.reshape(lead, count, cols // count), 0, 1).reshape(count, -1)
        )
    return jnp.concatenate(flat, axis=1)


def gather_small(own, got):
    z = lax.axis_index("fsdp")
    slots = jnp.stack([own] + got)
    low, high = z % 2, z // 2
    slots = jnp.where(low == 0, slots, slots[jnp.array([1, 0, 3, 2])])
    return jnp.where(high == 0, slots, slots[jnp.array([2, 3, 0, 1])])


def on_device(
    layer_input,
    qkv_weight,
    query_value_bias,
    out_weight,
    out_bias,
    up_weight,
    up_bias,
    down_weight,
    down_bias,
    norm_gain,
    norm_shift,
    doc_lengths,
    cotangent,
):
    _, tokens, width = layer_input.shape
    shards = lax.axis_size("fsdp")
    halves = shards == 4 and lax.axis_size("dp") == 8
    idx = jnp.stack([lax.axis_index("dp"), lax.axis_index("fsdp")]).astype(jnp.int32)
    x = layer_input[0]
    cot = cotangent[0]
    start, live = segment_starts(doc_lengths[0], tokens)
    start_row = start[None, :]
    live_col = live.astype(F32)[:, None]
    small_own = pack_small(query_value_bias, out_bias, up_bias, down_bias, norm_gain, norm_shift)
    tie = lax.optimization_barrier
    both = (4, 2)
    if halves:
        piece = eighth(qkv_weight)
        cols = piece.shape[1]
        extra = small_own.reshape(piece.shape[0], -1)
        got = shard_swaps(jnp.concatenate([piece, extra], axis=1))
        small = gather_small(small_own, [g[:, cols:].reshape(-1) for g in got])
        half_q = cols // 2
        q_own = [jnp.stack([g[:, :half_q] for g in got]), jnp.stack([g[:, half_q:cols] for g in got])]
        q_own, piece_u = after(q_own, jnp.concatenate([eighth(out_weight), eighth(up_weight)], axis=1))
        q_got = [swap(o, "dp", m) for o, m in zip(q_own, both)]
        got_u = swap(piece_u, "fsdp", 2)
        q_two = [jnp.concatenate([o, g]) for o, g in zip(q_own, q_got)]
        q_four = [swap(t, "dp", 6 - m) for t, m in zip(q_two, both)]
        slots_q = plane_slots(q_two, q_four)
        q_four, got_u = after(q_four, got_u)
        half_u = piece_u.shape[1] // 2
        pair_u = shard_pair(piece_u, got_u)
        own_q, own_u, own_d, at, count = qkv_weight, [out_weight, up_weight], down_weight, idx, shards
    else:
        small = lax.all_gather(small_own, "fsdp", axis=0)
        own_q = lax.all_gather(qkv_weight, "fsdp", axis=0, tiled=True)
        own_u = [
            lax.all_gather(out_weight, "fsdp", axis=0, tiled=True),
            lax.all_gather(up_weight, "fsdp", axis=0, tiled=True),
        ]
        own_d = lax.all_gather(down_weight, "fsdp", axis=0, tiled=True)
        half_q, half_u, at, count = own_q.shape[1] // 2, 0, jnp.zeros_like(idx), 1
        slots_q = slots_u = slots_d = []
    qv_b, out_b, up_b, down_b, gain, shift = unpack_small(small.astype(F32))
    qkv_b = jnp.concatenate([qv_b[0:1], jnp.zeros((1, width), F32), qv_b[1:2]], axis=1)

    spec = (
        [(0, 0, half_q, 0), (0, half_q, half_q, 1)],
        plane_spec([[(0, 0, 0, half_q, 0)], [(0, half_q, 0, half_q, 1)]]) if halves else [],
    )
    normed_one, packed, w_qkv = qkv_forward(
        at, own_q, spec, slots_q, count, x, qkv_b, gain[0:1], shift[0:1]
    )
    if halves:
        packed, pair_u = after(packed, pair_u)
        slots = shard_slots(got_u, pair_u)
        u_own = [jnp.stack([g[:, :half_u] for g in slots]), jnp.stack([g[:, half_u:] for g in slots])]
        u_got = [swap(o, "dp", m) for o, m in zip(u_own, both)]
        u_own, piece_d = after(u_own, eighth(down_weight))
        got_d = swap(piece_d, "fsdp", 2)
        u_own, packed = after(u_own, packed)
    pairs = width // PAIR
    part = attend(packed, start_row, 0, pairs // 2)
    if halves:
        part, u_got, got_d = tie((part, u_got, got_d))
        u_two = [jnp.concatenate([o, g]) for o, g in zip(u_own, u_got)]
        u_four = [swap(t, "dp", 6 - m) for t, m in zip(u_two, both)]
        u_two, got_d, packed = tie((u_two, got_d, packed))
        pair_d = shard_pair(piece_d, got_d)
    attended, lse = attend(packed, start_row, pairs // 2, pairs // 2, part)
    if halves:
        attended, u_four, pair_d = tie((attended, u_four, pair_d))
        slots_u = plane_slots(u_two, u_four)
        slots = shard_slots(got_d, pair_d)
        half_d = width // 2
        d_own = [jnp.stack([g[:, :half_d] for g in slots]), jnp.stack([g[:, half_d:] for g in slots])]
        d_got = [swap(o, "dp", m) for o, m in zip(d_own, both)]
    spec = ([(0, 0, width, 0)], plane_spec([[(0, 0, 0, width, 0)], []])[:4] if halves else [])
    mixed, mid, two, w_out = out_forward(
        at, own_u[0], spec, slots_u[:4], count, attended, x, out_b, gain, shift
    )
    if halves:
        two, d_got = after(two, d_got)
        d_two = [jnp.concatenate([o, g]) for o, g in zip(d_own, d_got)]
        d_four = [swap(t, "dp", 6 - m) for t, m in zip(d_two, both)]
        two, d_two = after(two, d_two)
    up_cols = own_u[1].shape[1]
    rest = half_u - width
    spec = (
        [(o, there, n, group) for o, there, _, n, group in by_block(0, 0, up_cols)],
        plane_spec([by_block(0, width, rest), by_block(rest, 0, half_u)]) if halves else [],
    )
    act, slope, w_up = up_forward(at, own_u[1], spec, slots_u, count, two, up_b)
    if halves:
        act, d_four = after(act, d_four)
        slots_d = plane_slots(d_two, d_four)
    half = width // 2
    spec = ([(0, 0, width, 0)], plane_spec([[(0, 0, 0, half, None)], [(0, half, 0, half, None)]]) if halves else [])
    layer_out, gffn, sums3, ghid, up_sum = down_both(
        at, own_d, spec, slots_d, count, act, slope, down_b, mid, cot, live_col, gain, shift
    )

    if halves:
        send = grad_down(idx, act, gffn)
        got_down = swap(send, "dp", 1)
        send, ghid = after(send, ghid)
        send = grad_up(idx, two, ghid)
        got_up = swap(send, "dp", 1)
        send, got_down, act = tie((send, got_down, act))
        down_parts = grad_down(idx, act, gffn, got_down)
        down_got = plane_direct(down_parts)
        down_parts, ghid = after(down_parts, ghid)
    gmid, gmix, gatt, sums21 = mid_backward(ghid, w_up, w_out, mid, mixed, cot, live_col, gain)
    if halves:
        got_up, ghid, gmix, down_got[1:] = tie((got_up, ghid, gmix, down_got[1:]))
        up_parts = grad_up(idx, two, ghid, got_up)
        up_got = plane_direct(up_parts)
        up_parts, gatt = after(up_parts, gatt)
    back = functools.partial(attend_back, packed)
    gq0, gk0, gv0, sq0, sv0 = back(gatt, attended, lse, start_row, 0, pairs // 2, 0)
    if halves:
        gq0, gmix, down_got[0] = tie((gq0, gmix, down_got[0]))
        send = grad_heads(idx, normed_one, gq0, gk0, gv0, attended, gmix)
        got_heads = swap(send, "dp", 1)
        send, gatt, up_got[1:] = tie((send, gatt, up_got[1:]))
    gq1, gk1, gv1, sq1, sv1 = back(gatt, attended, lse, start_row, pairs // 2, pairs // 2, 0)
    if halves:
        up_got[0], gq1 = after(up_got[0], gq1)
        total = jnp.concatenate([plane_total(down_parts, down_got), plane_total(up_parts, up_got)])
        ffn_keep, ffn_send = across_first(total)
        ffn_got = swap(ffn_send, "fsdp", 1)
        ffn_keep, ffn_send, gq1 = tie((ffn_keep, ffn_send, gq1))
        send = grad_heads(idx, normed_one, gq1, gk1, gv1)
        got_last = swap(send, "dp", 1)
        send, got_heads, gq0 = tie((send, got_heads, gq0))
        heads_parts = grad_heads(idx, normed_one, gq0, gk0, gv0, attended, gmix, got_heads)
        heads_got = plane_first(heads_parts)
        heads_parts, got_last, gq1 = tie((heads_parts, got_last, gq1))
        last_parts = grad_heads(idx, normed_one, gq1, gk1, gv1, got=got_last)
        last_got = plane_first(last_parts)
        last_parts, ffn_got, gq1, heads_got = tie((last_parts, ffn_got, gq1, heads_got))
        heads_keep, heads_send = plane_adds(heads_parts, heads_got)
        heads_got = [swap(part, "dp", mask) for part, mask in zip(heads_send, (2, 4))]
        heads_send, gq1 = after(heads_send, gq1)
        ffn_send = [add_low(ffn_keep[w, 1], ffn_got[w, 1]) for w in range(2)]
        ffn_keep = add_low(ffn_keep[:, 0], ffn_got[:, 0])
        down_got = swap(ffn_send[0], "fsdp", 2)
        ffn_send, gq1 = after(ffn_send, gq1)
    grads = [gq0, gq1, gk0, gk1, gv0, gv1]
    blocks = tokens // BLOCK
    grad_input, sums0 = input_backward(grads, w_qkv, x, gmid, gain, 0, blocks // 2)
    if halves:
        sums0, heads_got, last_got, down_got, up_send = tie(
            (sums0, heads_got, last_got, down_got, ffn_send[1])
        )
        up_got = swap(up_send, "fsdp", 2)
        last_keep, last_send = plane_adds(last_parts, last_got)
        last_got = [swap(part, "dp", mask) for part, mask in zip(last_send, (2, 4))]
        heads_keep, send = across_first(flows_total(heads_keep, heads_got))
        heads_got = swap(send, "fsdp", 1)
        last_send, send, grad_input = tie((last_send, send, grad_input))
    grad_input, sums0_rest = input_backward(
        grads, w_qkv, x, gmid, gain, blocks // 2, blocks // 2, grad_input
    )
    if halves:
        sums0_rest, heads_got, last_got, up_got = tie((sums0_rest, heads_got, last_got, up_got))
    sums0 = sums0 + sums0_rest
    small_grads = by_shard(
        [
            jnp.concatenate([jnp.concatenate([sq0, sq1], axis=1), jnp.concatenate([sv0, sv1], axis=1)]),
            sums21[4:5],
            up_sum,
            sums3[2:3],
            jnp.concatenate([sums0[0:1], sums21[2:3], sums21[0:1], sums3[0:1]]),
            jnp.concatenate([sums0[1:2], sums21[3:4], sums21[1:2], sums3[1:2]]),
        ],
        shards,
    )
    if halves:
        lane = PAIR * 3
        more = -(-small_grads.size // (16 * lane)) * 16
        tail = jnp.pad(small_grads.reshape(-1), (0, more * lane - small_grads.size)).reshape(more, lane)
        last_keep, send = across_first(flows_total(last_keep, last_got))
        last_got = swap(jnp.concatenate([send.reshape(-1, lane), tail.astype(BF)]), "fsdp", 1)
        heads_send = add_low(heads_keep[:, 1], heads_got[:, 1])
        heads_keep = add_low(heads_keep[:, 0], heads_got[:, 0])[0]
        heads_got = swap(heads_send, "fsdp", 2)
        last_keep, up_got = after(last_keep, up_got)
        ffn_four = spread(add_low(ffn_keep, jnp.stack([down_got, up_got])))

        last_keep, last_got, heads_got = tie((last_keep, last_got, heads_got))
        tail = tail + last_got[-more:].astype(F32)
        last_got = last_got[:-more].reshape(last_keep.shape)
        send = add_low(last_keep[:, 1], last_got[:, 1])
        last_keep = add_low(last_keep[:, 0], last_got[:, 0])[0]
        last_got = swap(jnp.concatenate([send.reshape(-1, lane), tail.astype(BF)]), "fsdp", 2)

        last_keep, last_got, ffn_four = tie((last_keep, last_got, ffn_four))
        tail = (tail + last_got[-more:].astype(F32)).astype(BF)
        piece = jnp.concatenate(
            [
                add_low(heads_keep.reshape(-1, width - lane), heads_got.reshape(-1, width - lane)),
                add_low(last_keep.reshape(-1, lane), last_got[:-more]),
            ],
            axis=1,
        )
        tail = tail.reshape(-1)[: small_grads.size].reshape(-1, width)
        more = tail.shape[0]
        piece = jnp.concatenate([piece, tail])
        heads_got = [swap(piece, "dp", mask) for mask in (2, 4, 6)]
        ffn_all = spread_core(ffn_four)
        up_grad, down_grad = finish(
            "finish_ffn", idx, place_ffn, ffn_all, [up_weight.shape, down_weight.shape]
        )

        up_grad, heads_got = after(up_grad, heads_got)
        heads_four = jnp.stack([piece] + heads_got)
        heads_all = spread_core(heads_four)
        heads_core = heads_all[1][1]
        heads_all = [heads_all[0], (heads_all[1][0], heads_core)]
        tail = jnp.sum(heads_four[:, -more:].astype(F32), axis=0) + jnp.sum(
            heads_core[:, -more:].astype(F32), axis=0
        )
        small_sum = lax.dynamic_index_in_dim(
            tail.reshape(small_grads.shape), lax.axis_index("fsdp"), 0, keepdims=False
        )
        qkv_grad, out_grad = finish(
            "finish_heads", idx, place_heads, heads_all, [qkv_weight.shape, out_weight.shape]
        )
    else:
        gpacked = jnp.concatenate([gq0, gq1, gk0, gk1, gv0, gv1], axis=1)

        def reduced(left, right):
            grad = dot_tn(left, right)
            return lax.psum(lax.psum_scatter(grad, "fsdp", scatter_dimension=0, tiled=True), "dp")

        qkv_grad = reduced(normed_one, gpacked)
        out_grad = reduced(attended, gmix)
        up_grad = reduced(two, ghid)
        down_grad = reduced(act, gffn)
        small_sum = lax.dynamic_index_in_dim(
            lax.psum(small_grads, ("dp", "fsdp")), lax.axis_index("fsdp"), 0, keepdims=False
        )
    qv_g, outb_g, upb_g, downb_g, gain_g, shift_g = unpack_small(small_sum[None])
    return (
        layer_out[None],
        grad_input[None],
        qkv_grad,
        qv_g,
        out_grad,
        outb_g[0],
        up_grad,
        upb_g[0],
        down_grad,
        downb_g[0],
        gain_g,
        shift_g,
    )


def solution(mesh):
    rows = P(("dp", "fsdp"), None, None)
    split = P("fsdp", None)
    placed = (
        rows,
        split,
        P(None, "fsdp"),
        split,
        P("fsdp"),
        split,
        P("fsdp"),
        split,
        P("fsdp"),
        P(None, "fsdp"),
        P(None, "fsdp"),
        P(("dp", "fsdp"), None),
        rows,
    )
    return jax.shard_map(
        on_device,
        mesh=mesh,
        in_specs=placed,
        out_specs=(
            rows,
            rows,
            split,
            P(None, "fsdp"),
            split,
            P("fsdp"),
            split,
            P("fsdp"),
            split,
            P("fsdp"),
            P(None, "fsdp"),
            P(None, "fsdp"),
        ),
        check_vma=False,
    )
```

```python
import functools
import math

import jax
import jax.numpy as jnp
from jax import lax
from jax.experimental import pallas as pl
from jax.experimental.pallas import tpu as pltpu
from jax.sharding import PartitionSpec as P

F32 = jnp.float32
BF = jnp.bfloat16
SDS = jax.ShapeDtypeStruct
HEAD_DIM = 64
PAIR = 2 * HEAD_DIM
EPS = 1e-05
MASKED = -1e30
QUERY_SCALE = math.log2(math.e) / math.sqrt(HEAD_DIM)
GRAD_SCALE = 1.0 / math.sqrt(HEAD_DIM)
BLOCK = 256
UP_COLS = 1024
HIDDEN_COLS = 1024
GELU_A = math.sqrt(2.0 / math.pi)
GELU_B = 0.044715 * GELU_A


def params(**more):
    return pltpu.CompilerParams(vmem_limit_bytes=60 * 1024 * 1024, **more)


def cost(flops, nbytes, trans=0):
    return pl.CostEstimate(flops=int(flops) // 1, bytes_accessed=int(nbytes) // 1, transcendentals=int(trans))


def dot_nn(a, b):
    return lax.dot_general(a, b, (((1,), (0,)), ((), ())), preferred_element_type=F32)


def dot_nt(a, b):
    return lax.dot_general(a, b, (((1,), (1,)), ((), ())), preferred_element_type=F32)


def dot_tn(a, b):
    return lax.dot_general(a, b, (((0,), (0,)), ((), ())), preferred_element_type=F32)


def centred(values):
    centre = values - jnp.mean(values, axis=-1, keepdims=True)
    rstd = lax.rsqrt(jnp.mean(centre * centre, axis=-1, keepdims=True) + EPS)
    return centre * rstd, rstd


def norm_back(grad, vhat, rstd, gain):
    e = grad * gain
    mean_e = jnp.mean(e, axis=-1, keepdims=True)
    mean_ev = jnp.mean(e * vhat, axis=-1, keepdims=True)
    return (e - mean_e - vhat * mean_ev) * rstd


def col_sum(values):
    return jnp.sum(values, axis=0, keepdims=True)


def piece_copies(spec, idx_ref, own_refs, slot_refs, places, sems):
    own_spec, slot_spec = spec
    dp, z = idx_ref[0], idx_ref[1]
    copies = []

    def add(group, src, dst):
        copies.append((group, pltpu.make_async_copy(src, dst, sems.at[len(copies)])))

    for o, first, cols, group in own_spec:
        rows = own_refs[o].shape[0]
        dst = places[o].at[pl.ds(pl.multiple_of(z * rows, rows), rows), first : first + cols]
        add(group, own_refs[o].at[:, first : first + cols], dst)
    for (pair, parts), ref in zip(slot_spec, slot_refs):
        rows = ref.shape[1]
        others = ref.shape[0] // 2
        for which, mask in enumerate(pair):
            for k in range(1, others + 1):
                at = which * others + k - 1
                for o, there, here, cols, group in parts:
                    dst = pl.multiple_of((z ^ k) * own_refs[o].shape[0] + (dp ^ mask) * rows, rows)
                    add(
                        group,
                        ref.at[at, :, here : here + cols],
                        places[o].at[pl.ds(dst, rows), there : there + cols],
                    )
    return copies


def count_copies(spec, slots):
    own_spec, slot_spec = spec
    return len(own_spec) + sum(len(parts) * s.shape[0] for (_, parts), s in zip(slot_spec, slots))


def start_all(copies):
    for _, copy in copies:
        copy.start()


def wait_group(copies, group):
    for g, copy in copies:
        if g == group:
            copy.wait()


def whole_shapes(owns, shards):
    return [(o.shape[0] * shards, o.shape[1]) for o in owns]


ANY = pl.BlockSpec(memory_space=pl.ANY)
SMEM = pl.BlockSpec(memory_space=pltpu.SMEM)


def qkv_kernel(spec, n_slots, idx_ref, own_ref, *refs):
    slots = refs[:n_slots]
    x_ref, bias_ref, gain_ref, shift_ref, normed_ref, packed_ref, out_ref = refs[n_slots : n_slots + 7]
    weight, sems, out_sem = refs[n_slots + 7 :]
    step, steps = pl.program_id(0), pl.num_programs(0)
    copies = piece_copies(spec, idx_ref, [own_ref], slots, [weight], sems)
    bn = packed_ref.shape[1]

    @pl.when(step == 0)
    def _():
        start_all(copies)
        vhat, _ = centred(x_ref[...].astype(F32))
        normed_ref[...] = (vhat * gain_ref[...] + shift_ref[...]).astype(BF)
        wait_group(copies, 0)

    half = weight.shape[1] // 2

    @pl.when(step == half // bn)
    def _():
        wait_group(copies, 1)
        pltpu.make_async_copy(weight, out_ref, out_sem).start()

    block = weight[:, pl.ds(pl.multiple_of(step * bn, bn), bn)]
    out = dot_nn(normed_ref[...], block) + bias_ref[...]
    packed_ref[...] = (out * jnp.where(step < steps // 3, QUERY_SCALE, 1.0)).astype(BF)

    @pl.when(step == steps - 1)
    def _():
        pltpu.make_async_copy(weight, out_ref, out_sem).wait()


def qkv_forward(idx, own, spec, slots, shards, x, bias, gain, shift):
    tokens, width = x.shape
    ((rows, cols),) = whole_shapes([own], shards)
    bn = width // 2
    row = pl.BlockSpec((1, width), lambda j: (0, 0))
    full = pl.BlockSpec((tokens, width), lambda j: (0, 0))
    return pl.pallas_call(
        functools.partial(qkv_kernel, spec, len(slots)),
        grid=(cols // bn,),
        in_specs=[SMEM] + [ANY] * (1 + len(slots))
        + [full, pl.BlockSpec((1, bn), lambda j: (0, j)), row, row],
        out_specs=(full, pl.BlockSpec((tokens, bn), lambda j: (0, j)), ANY),
        out_shape=(SDS((tokens, width), BF), SDS((tokens, cols), BF), SDS((rows, cols), BF)),
        scratch_shapes=[
            pltpu.VMEM((rows, cols), BF),
            pltpu.SemaphoreType.DMA((count_copies(spec, slots),)),
            pltpu.SemaphoreType.DMA(()),
        ],
        compiler_params=params(),
        cost_estimate=cost(2 * tokens * width * cols, 2 * width * cols + 2 * tokens * cols),
        name="qkv_forward",
    )(idx, own, *slots, x, bias, gain, shift)


def gelu_and_slope(a):
    sq = a * a
    t = jnp.tanh(a * (sq * GELU_B + GELU_A))
    half = 0.5 * t + 0.5
    act = a * half
    slope = half + act * ((1.0 - half) * (sq * (6.0 * GELU_B) + 2.0 * GELU_A))
    return act.astype(BF), slope.astype(BF)


def out_kernel(spec, n_slots, idx_ref, own_ref, *refs):
    slots = refs[:n_slots]
    att_ref, x_ref, bias_ref, gain_ref, shift_ref = refs[n_slots : n_slots + 5]
    mixed_ref, mid_ref, two_ref, save_ref, weight, sems, save_sem = refs[n_slots + 5 :]
    step, steps = pl.program_id(0), pl.num_programs(0)
    copies = piece_copies(spec, idx_ref, [own_ref], slots, [weight], sems)
    save = pltpu.make_async_copy(weight, save_ref, save_sem)

    @pl.when(step == 0)
    def _():
        start_all(copies)
        wait_group(copies, 0)
        save.start()

    mixed = dot_nn(att_ref[...], weight[...]) + bias_ref[...]
    mixed_ref[...] = mixed
    vhat, _ = centred(mixed)
    mid = x_ref[...].astype(F32) + vhat * gain_ref[1:2, :] + shift_ref[1:2, :]
    mid_ref[...] = mid
    vhat, _ = centred(mid)
    two_ref[...] = (vhat * gain_ref[2:3, :] + shift_ref[2:3, :]).astype(BF)

    @pl.when(step == steps - 1)
    def _():
        save.wait()


def out_forward(idx, own, spec, slots, shards, attended, x, bias, gain, shift):
    tokens, width = x.shape
    (shape,) = whole_shapes([own], shards)
    tok = pl.BlockSpec((BLOCK, width), lambda i: (i, 0))

    def whole(arr):
        return pl.BlockSpec(arr.shape, lambda i: (0, 0))

    return pl.pallas_call(
        functools.partial(out_kernel, spec, len(slots)),
        grid=(tokens // BLOCK,),
        in_specs=[SMEM] + [ANY] * (1 + len(slots)) + [tok, tok, whole(bias), whole(gain), whole(shift)],
        out_specs=(tok, tok, tok, ANY),
        out_shape=(
            SDS((tokens, width), F32),
            SDS((tokens, width), F32),
            SDS((tokens, width), BF),
            SDS(shape, BF),
        ),
        scratch_shapes=[
            pltpu.VMEM(shape, BF),
            pltpu.SemaphoreType.DMA((count_copies(spec, slots),)),
            pltpu.SemaphoreType.DMA(()),
        ],
        compiler_params=params(),
        cost_estimate=cost(2 * tokens * width * width, 16 * tokens * width),
        name="out_forward",
    )(idx, own, *slots, attended, x, bias, gain, shift)


def up_kernel(spec, n_slots, idx_ref, own_ref, *refs):
    slots = refs[:n_slots]
    two_ref, bias_ref, act_ref, slope_ref, save_ref, weight, sems, save_sem = refs[n_slots:]
    step, steps = pl.program_id(0), pl.num_programs(0)
    copies = piece_copies(spec, idx_ref, [own_ref], slots, [weight], sems)
    save = pltpu.make_async_copy(weight, save_ref, save_sem)

    @pl.when(step == 0)
    def _():
        start_all(copies)
        wait_group(copies, 0)
        save.start()

    bn = act_ref.shape[1]
    at = pl.ds(pl.multiple_of(step * bn, bn), bn)
    a = dot_nn(two_ref[...], weight[:, at]) + bias_ref[...]
    act_ref[...], slope_ref[...] = gelu_and_slope(a)

    @pl.when(step == steps - 1)
    def _():
        save.wait()


def up_forward(idx, own, spec, slots, shards, two, bias):
    tokens, width = two.shape
    (shape,) = whole_shapes([own], shards)
    cols = shape[1]
    bn = UP_COLS
    col = pl.BlockSpec((tokens, bn), lambda i: (0, i))
    return pl.pallas_call(
        functools.partial(up_kernel, spec, len(slots)),
        grid=(cols // bn,),
        in_specs=[SMEM] + [ANY] * (1 + len(slots))
        + [pl.BlockSpec((tokens, width), lambda i: (0, 0)), pl.BlockSpec((1, bn), lambda i: (0, i))],
        out_specs=(col, col, ANY),
        out_shape=(SDS((tokens, cols), BF), SDS((tokens, cols), BF), SDS(shape, BF)),
        scratch_shapes=[
            pltpu.VMEM(shape, BF),
            pltpu.SemaphoreType.DMA((count_copies(spec, slots),)),
            pltpu.SemaphoreType.DMA(()),
        ],
        compiler_params=params(),
        cost_estimate=cost(2 * tokens * width * cols, 2 * width * cols + 4 * tokens * cols),
        name="up_forward",
    )(idx, own, *slots, two, bias)


def down_kernel(spec, n_slots, first, idx_ref, own_ref, *refs):
    slots = refs[:n_slots]
    act_ref, slope_ref, bias_ref, mid_ref, cot_ref, live_ref, gain_ref, shift_ref = refs[n_slots : n_slots + 8]
    out_ref, grad_ref, sums_ref, hid_ref, hsum_ref, weight, sems = refs[n_slots + 8 :]
    step = pl.program_id(0)
    copies = piece_copies(spec, idx_ref, [own_ref], slots, [weight], sems)

    @pl.when(step == 0)
    def _():
        start_all(copies)
        sums_ref[...] = jnp.zeros_like(sums_ref)
        wait_group(copies, 0)

    @pl.when(step < first)
    def _():
        ffn = dot_nn(act_ref[...], weight[...]) + bias_ref[...]
        vhat, rstd = centred(ffn)
        gain = gain_ref[3:4, :]
        out_ref[...] = (mid_ref[...] + vhat * gain + shift_ref[3:4, :]).astype(BF)
        grad = cot_ref[...].astype(F32) * live_ref[...]
        low = norm_back(grad, vhat, rstd, gain).astype(BF)
        grad_ref[pl.ds(pl.multiple_of(step * BLOCK, BLOCK), BLOCK), :] = low
        sums_ref[0:1, :] += col_sum(grad * vhat)
        sums_ref[1:2, :] += col_sum(grad)
        sums_ref[2:3, :] += col_sum(low.astype(F32))

    @pl.when(step >= first)
    def _():
        bn = hid_ref.shape[1]
        at = pl.ds(pl.multiple_of((step - first) * bn, bn), bn)
        low = (dot_nt(grad_ref[...], weight[at, :]) * slope_ref[...].astype(F32)).astype(BF)
        hid_ref[...] = low
        hsum_ref[...] = col_sum(low.astype(F32))


def down_both(idx, own, spec, slots, shards, act, slope, bias, mid, cot, live, gain, shift):
    tokens, width = mid.shape
    (shape,) = whole_shapes([own], shards)
    cols = shape[0]
    bn = HIDDEN_COLS
    first = tokens // BLOCK

    def at(i):
        return jnp.minimum(i, first - 1)

    tok = pl.BlockSpec((BLOCK, width), lambda i: (at(i), 0))
    col = pl.BlockSpec((tokens, bn), lambda i: (0, jnp.maximum(i - first, 0)))

    def whole(arr):
        return pl.BlockSpec(arr.shape, lambda i: (0, 0))

    return pl.pallas_call(
        functools.partial(down_kernel, spec, len(slots), first),
        grid=(first + cols // bn,),
        in_specs=[SMEM] + [ANY] * (1 + len(slots))
        + [
            pl.BlockSpec((BLOCK, cols), lambda i: (at(i), 0)),
            col,
            whole(bias),
            tok,
            tok,
            pl.BlockSpec((BLOCK, 1), lambda i: (at(i), 0)),
            whole(gain),
            whole(shift),
        ],
        out_specs=(
            tok,
            pl.BlockSpec((tokens, width), lambda i: (0, 0)),
            pl.BlockSpec((8, width), lambda i: (0, 0)),
            col,
            pl.BlockSpec((1, bn), lambda i: (0, jnp.maximum(i - first, 0))),
        ),
        out_shape=(
            SDS((tokens, width), BF),
            SDS((tokens, width), BF),
            SDS((8, width), F32),
            SDS((tokens, cols), BF),
            SDS((1, cols), F32),
        ),
        scratch_shapes=[pltpu.VMEM(shape, BF), pltpu.SemaphoreType.DMA((count_copies(spec, slots),))],
        compiler_params=params(),
        cost_estimate=cost(4 * tokens * width * cols, 2 * width * cols + 6 * tokens * cols),
        name="down_both",
    )(idx, own, *slots, act, slope, bias, mid, cot, live, gain, shift)


def mid_kernel(
    gh_ref, up_ref, out_w_ref, mid_ref, mixed_ref, cot_ref, live_ref, gain_ref,
    gmid_ref, gmix_ref, gatt_ref, sums_ref,
):
    @pl.when(pl.program_id(0) == 0)
    def _():
        sums_ref[...] = jnp.zeros_like(sums_ref)

    grad = dot_nt(gh_ref[...], up_ref[...])
    vhat, rstd = centred(mid_ref[...])
    sums_ref[0:1, :] += col_sum(grad * vhat)
    sums_ref[1:2, :] += col_sum(grad)
    gmid = cot_ref[...].astype(F32) * live_ref[...] + norm_back(grad, vhat, rstd, gain_ref[2:3, :])
    gmid_ref[...] = gmid
    vhat, rstd = centred(mixed_ref[...])
    sums_ref[2:3, :] += col_sum(gmid * vhat)
    sums_ref[3:4, :] += col_sum(gmid)
    low = norm_back(gmid, vhat, rstd, gain_ref[1:2, :]).astype(BF)
    gmix_ref[...] = low
    sums_ref[4:5, :] += col_sum(low.astype(F32))
    gatt_ref[...] = dot_nt(low, out_w_ref[...]).astype(BF)


def mid_backward(gh, up, out_w, mid, mixed, cot, live, gain):
    tokens, width = mid.shape
    cols = gh.shape[1]
    tok = pl.BlockSpec((BLOCK, width), lambda i: (i, 0))

    def whole(arr):
        return pl.BlockSpec(arr.shape, lambda i: (0, 0))

    return pl.pallas_call(
        mid_kernel,
        grid=(tokens // BLOCK,),
        in_specs=[
            pl.BlockSpec((BLOCK, cols), lambda i: (i, 0)),
            whole(up),
            whole(out_w),
            tok,
            tok,
            tok,
            pl.BlockSpec((BLOCK, 1), lambda i: (i, 0)),
            whole(gain),
        ],
        out_specs=(tok, tok, tok, pl.BlockSpec((8, width), lambda i: (0, 0))),
        out_shape=(
            SDS((tokens, width), F32),
            SDS((tokens, width), BF),
            SDS((tokens, width), BF),
            SDS((8, width), F32),
        ),
        compiler_params=params(),
        cost_estimate=cost(2 * tokens * width * (cols + width), 2 * width * cols + 2 * tokens * cols),
        name="mid_backward",
    )(gh, up, out_w, mid, mixed, cot, live, gain)


def input_kernel(n_grads, n_into, *refs):
    grad_refs, (w_ref, x_ref, gmid_ref, gain_ref) = refs[:n_grads], refs[n_grads : n_grads + 4]
    out_ref, sums_ref = refs[n_grads + 4 + n_into :]

    @pl.when(pl.program_id(0) == 0)
    def _():
        sums_ref[...] = jnp.zeros_like(sums_ref)

    grads = jnp.concatenate([ref[...] for ref in grad_refs], axis=1)
    grad = dot_nt(grads, w_ref[...])
    vhat, rstd = centred(x_ref[...].astype(F32))
    sums_ref[0:1, :] += col_sum(grad * vhat)
    sums_ref[1:2, :] += col_sum(grad)
    out_ref[...] = gmid_ref[...] + norm_back(grad, vhat, rstd, gain_ref[0:1, :])


def input_backward(grads, weight, x, gmid, gain, first, count, into=None):
    tokens, width = x.shape
    tok = pl.BlockSpec((BLOCK, width), lambda i: (first + i, 0))

    def whole(arr):
        return pl.BlockSpec(arr.shape, lambda i: (0, 0))

    in_specs = [pl.BlockSpec((BLOCK, g.shape[1]), lambda i: (first + i, 0)) for g in grads]
    in_specs += [whole(weight), tok, tok, whole(gain)]
    args = [*grads, weight, x, gmid, gain]
    aliases = {}
    if into is not None:
        aliases = {len(args): 0}
        in_specs.append(pl.BlockSpec(memory_space=pl.ANY))
        args.append(into)
    return pl.pallas_call(
        functools.partial(input_kernel, len(grads), len(aliases)),
        grid=(count,),
        in_specs=in_specs,
        out_specs=(tok, pl.BlockSpec((8, width), lambda i: (0, 0))),
        out_shape=(SDS((tokens, width), F32), SDS((8, width), F32)),
        input_output_aliases=aliases,
        compiler_params=params(),
        cost_estimate=cost(6 * count * BLOCK * width * width, 6 * width * width),
        name="input_backward",
    )(*args)


def fill_bias(bias, start_ref):
    length = bias.shape[0]
    for j in range(length // BLOCK):
        key = lax.broadcasted_iota(jnp.int32, (BLOCK, length), 0) + j * BLOCK
        query = lax.broadcasted_iota(jnp.int32, (BLOCK, length), 1)
        allowed = (key <= query) & (key >= start_ref[...])
        bias[j * BLOCK : (j + 1) * BLOCK, :] = jnp.where(allowed, 0.0, MASKED)


def one_head(low, arr, head):
    zero = jnp.zeros_like(arr)
    return jnp.where(low, arr, zero) if head == 0 else jnp.where(low, zero, arr)


def attend_kernel(q_ref, k_ref, v_ref, start_ref, out_ref, lse_ref, bias):
    length = q_ref.shape[0]

    @pl.when(pl.program_id(0) == 0)
    def _():
        fill_bias(bias, start_ref)

    low = lax.broadcasted_iota(jnp.int32, (1, PAIR), 1) < HEAD_DIM
    low_rows = lax.broadcasted_iota(jnp.int32, (PAIR, 1), 0) < HEAD_DIM
    keys = k_ref[...]
    values = jnp.concatenate([v_ref[...], jnp.ones((length, PAIR), BF)], axis=1)
    for i in range(length // BLOCK):
        reach = (i + 1) * BLOCK
        sl = slice(i * BLOCK, reach)
        queries = q_ref[sl, :]
        parts = []
        for head in range(2):
            scores = dot_nt(keys[:reach], one_head(low, queries, head)) + bias[:reach, sl]
            top = jnp.max(scores, axis=0, keepdims=True)
            probs = jnp.exp2(scores - top).astype(BF)
            mixed = dot_tn(values[:reach], probs)
            total = mixed[PAIR : PAIR + 1]
            parts.append(mixed[:PAIR] / total)
            lse_ref[0, head : head + 1, sl] = top + jnp.log2(total)
        out_ref[sl, :] = jnp.where(low_rows, parts[0], parts[1]).T.astype(BF)


def attend(packed, start_row, first, count, into=None):
    length = packed.shape[0]
    pairs = packed.shape[1] // (3 * PAIR)

    def blk(offset):
        return pl.BlockSpec((length, PAIR), lambda h: (0, offset + first + h))

    in_specs = [blk(0), blk(pairs), blk(2 * pairs), pl.BlockSpec((1, length), lambda h: (0, 0))]
    args = [packed, packed, packed, start_row]
    kernel, aliases = attend_kernel, {}
    if into is not None:
        in_specs = in_specs + [ANY] * len(into)
        aliases = {len(args) + i: i for i in range(len(into))}
        args = args + list(into)

        def kernel(*refs):
            attend_kernel(*refs[:4], *refs[4 + len(into) :])

    return pl.pallas_call(
        kernel,
        grid=(count,),
        in_specs=in_specs,
        out_specs=(blk(0), pl.BlockSpec((1, 2, length), lambda h: (first + h, 0, 0))),
        out_shape=(SDS((length, PAIR * pairs), BF), SDS((pairs, 2, length), F32)),
        input_output_aliases=aliases,
        scratch_shapes=[pltpu.VMEM((length, length), F32)],
        compiler_params=params(),
        cost_estimate=cost(8 * count * length * length * PAIR, 8 * length * count * PAIR),
        name="attend",
    )(*args)


def share_out(wide, idx_ref, send_ref, own_ref):
    core, z = idx_ref[0] & 1, idx_ref[1]
    rows = wide.shape[0] // 8
    for zz in range(4):
        for ref, c in ((send_ref, core ^ 1), (own_ref, core)):
            at = pl.ds(pl.multiple_of((2 * zz + c) * rows, rows), rows)
            part = wide[at, :].astype(BF)
            ref[0, 0, zz ^ z, 0] = part[: rows // 2]
            ref[0, 0, zz ^ z, 1] = part[rows // 2 :]


def attend_back_kernel(shared, *refs):
    if shared:
        idx_ref, one_ref, refs = refs[0], refs[1], refs[2:]
        send_ref, own_ref, wide = refs[12], refs[13], refs[16]
        refs = refs[:12] + refs[14:16]
    q_ref, k_ref, v_ref, g_ref, o_ref, lse_ref, start_ref = refs[:7]
    gq_ref, gk_ref, gv_ref, sq_ref, sv_ref, bias, acc = refs[7:]
    length = q_ref.shape[0]

    @pl.when(pl.program_id(0) == 0)
    def _():
        fill_bias(bias, start_ref)

    low = lax.broadcasted_iota(jnp.int32, (1, PAIR), 1) < HEAD_DIM
    queries, grads = q_ref[...], g_ref[...]
    q_of = [one_head(low, queries, head) for head in range(2)]
    g_of = [one_head(low, grads, head) for head in range(2)]
    inner = (grads.astype(F32) * o_ref[...].astype(F32)).T
    inner_of = [col_sum(inner[:HEAD_DIM]), col_sum(inner[HEAD_DIM:])]
    sum_v = jnp.zeros((1, PAIR), F32)
    for j in range(length // BLOCK):
        first = j * BLOCK
        sl = slice(first, first + BLOCK)
        keys, values = k_ref[sl, :], v_ref[sl, :]
        gk = gv = gq = 0.0
        for head in range(2):
            scores = dot_nt(keys, q_of[head][first:]) + bias[sl, first:]
            probs = jnp.exp2(scores - lse_ref[0, head : head + 1, first:])
            gprobs = dot_nt(values, g_of[head][first:])
            gscores = (probs * (gprobs - inner_of[head][:, first:]) * GRAD_SCALE).astype(BF)
            gv = gv + dot_nn(probs.astype(BF), g_of[head][first:])
            gk = gk + dot_nn(gscores, q_of[head][first:])
            gq = gq + dot_tn(gscores, one_head(low, keys, head))
        low_v = gv.astype(BF)
        gv_ref[sl, :] = low_v
        gk_ref[sl, :] = (gk * (1.0 / QUERY_SCALE)).astype(BF)
        sum_v = sum_v + col_sum(low_v.astype(F32))
        if j == 0:
            acc[...] = gq
        else:
            acc[first:, :] += gq
    low_q = acc[...].astype(BF)
    gq_ref[...] = low_q
    sq_ref[...] = col_sum(low_q.astype(F32))
    sv_ref[...] = sum_v
    if shared:
        grads = jnp.concatenate([low_q, gk_ref[...], gv_ref[...]], axis=1)
        wide[...] = dot_tn(one_ref[...], grads)
        share_out(wide, idx_ref, send_ref, own_ref)


def attend_back(packed, grads, attended, lse, start_row, part, parts, idx=None, one=None):
    length = packed.shape[0]
    total = packed.shape[1] // (3 * PAIR)
    count = total // parts
    first = part * count
    shared = one is not None

    def blk(offset):
        return pl.BlockSpec((length, PAIR), lambda h, *_: (0, offset + h))

    row = pl.BlockSpec((1, PAIR), lambda h, *_: (0, h))
    grad = SDS((length, PAIR * count), BF)
    sums = SDS((1, PAIR * count), F32)
    in_specs = [
        blk(first),
        blk(total + first),
        blk(2 * total + first),
        blk(first),
        blk(first),
        pl.BlockSpec((1, 2, length), lambda h, *_: (first + h, 0, 0)),
        pl.BlockSpec((1, length), lambda h, *_: (0, 0)),
    ]
    args = [packed, packed, packed, grads, attended, lse, start_row]
    out_specs = [blk(0), blk(0), blk(0), row, row]
    out_shape = [grad, grad, grad, sums, sums]
    scratch = [pltpu.VMEM((length, length), F32), pltpu.VMEM((length, PAIR), F32)]
    if shared:
        width = one.shape[1]
        piece = (4, 2, width // 16, 3 * PAIR)
        block = pl.BlockSpec((1, 1) + piece, lambda h, idx: (3 ^ h ^ (idx[0] // 2), 0, 0, 0, 0, 0))
        in_specs = [pl.BlockSpec(one.shape, lambda h, *_: (0, 0))] + in_specs
        args = [idx, one] + args
        out_specs = out_specs + [block, block]
        out_shape = out_shape + [SDS((4, 1) + piece, BF)] * 2
        scratch = scratch + [pltpu.VMEM((width, 3 * PAIR), F32)]
    return pl.pallas_call(
        functools.partial(attend_back_kernel, shared),
        grid_spec=pltpu.PrefetchScalarGridSpec(
            num_scalar_prefetch=int(shared),
            grid=(count,),
            in_specs=in_specs,
            out_specs=tuple(out_specs),
            scratch_shapes=scratch,
        ),
        out_shape=tuple(out_shape),
        compiler_params=params(),
        cost_estimate=cost(20 * count * length * length * PAIR, 16 * length * count * PAIR),
        name="attend_back",
    )(*args)


def swap(arr, axis, mask):
    size = lax.axis_size(axis)
    return lax.ppermute(arr, axis, [(i, i ^ mask) for i in range(size)])


def after(first, then):
    return lax.optimization_barrier((first, then))


def shard_swaps(piece):
    return [swap(piece, "fsdp", k) for k in range(1, lax.axis_size("fsdp"))]


def shard_pair(piece, got):
    return swap(jnp.stack([piece, got]), "fsdp", 1)


def shard_slots(got, pair):
    return [pair[0], got, pair[1]]


PLANE_MASKS = [
    (0, 4), (2, 6), (1, 5), (3, 7),
    (0, 2), (4, 6), (1, 3), (5, 7),
]


def plane_slots(two, four):
    return [a for t, f in zip(two, four) for a in (t, f, swap(t, "dp", 1), swap(f, "dp", 1))]


def plane_spec(parts):
    return [(pair, parts[i // 4]) for i, pair in enumerate(PLANE_MASKS)]


def split_down(wide, zz):
    rows, cols = wide.shape[0] // 4, wide.shape[1] // 2
    part = wide[zz * rows : (zz + 1) * rows]
    return part[:, :cols], part[:, cols:]


def split_up(wide, zz):
    rows = wide.shape[0] // 8
    return wide[2 * zz * rows : (2 * zz + 1) * rows], wide[(2 * zz + 1) * rows : (2 * zz + 2) * rows]


def side_by_side(refs):
    blocks = [r[...] for r in refs]
    return blocks[0] if len(blocks) == 1 else jnp.concatenate(blocks, axis=1)


def emit(keep, direct, wide, split, z, chip, rest):
    if not keep:
        for zz in range(4):
            for f, part in enumerate(split(wide, zz)):
                rest[0][0, 0, zz ^ z, f] = part.astype(BF)
        return
    got_ref, outs = rest[0], rest[1:]
    for dst in range(4):

        @pl.when(chip == dst)
        def _():
            for zz in range(4):
                slot = zz ^ z
                for f, part in enumerate(split(wide, zz)):
                    low = (part + got_ref[0, 0, slot, f].astype(F32)).astype(BF)
                    if direct:
                        outs[dst][0, slot, f] = low
                    else:
                        bit = dst // 2 if f == 0 else dst % 2
                        outs[2 * f + bit][0, 0, slot] = low


def grad_kernel(keep, direct, jobs, idx_ref, *refs):
    step, z = pl.program_id(0), idx_ref[1]
    at = 0
    n_in = sum(n for groups, _ in jobs for group in groups for n in group)
    rest = refs[n_in:]
    for number, (groups, split) in enumerate(jobs):
        blocks = []
        for n_left, n_right in groups:
            blocks.append((refs[at : at + n_left], refs[at + n_left : at + n_left + n_right]))
            at += n_left + n_right

        @pl.when(step // 4 == number)
        def _():
            dots = [dot_tn(side_by_side(left), side_by_side(right)) for left, right in blocks]
            wide = dots[0] if len(dots) == 1 else jnp.concatenate(dots, axis=1)
            emit(keep, direct, wide, split, z, step % 4, rest)


def grad_call(name, idx, specs, args, jobs, piece, flops, got=None, direct=True):
    keep = got is not None
    n_jobs = len(jobs)
    rows, cols = piece
    block = pl.BlockSpec((1, 1, 4, 2, rows, cols), lambda i, idx: (i % 4, i // 4, 0, 0, 0, 0))
    half = (1, 1, 4, rows, cols)
    if keep and direct:
        specs = specs + [block]
        args = args + [got]
        out_specs = (pl.BlockSpec((1, 4, 2, rows, cols), lambda i, idx: (0, 0, 0, 0, 0)),) * 4
        out_shape = (SDS((1, 4, 2, rows, cols), BF),) * 4
    elif keep:
        along_y = (
            lambda i, idx: (jnp.minimum(i % 4, 1), i // 4, 0, 0, 0),
            lambda i, idx: (jnp.maximum(i % 4 - 2, 0), i // 4, 0, 0, 0),
        )
        along_x = (lambda i, idx: (i % 4 // 2, i // 4, 0, 0, 0),) * 2
        specs = specs + [block]
        args = args + [got]
        out_specs = tuple(pl.BlockSpec(half, m) for m in along_y + along_x)
        out_shape = (SDS((2, n_jobs, 4, rows, cols), BF),) * 4
    else:
        out_specs = block
        out_shape = SDS((4, n_jobs, 4, 2, rows, cols), BF)
    return pl.pallas_call(
        functools.partial(grad_kernel, keep, direct, jobs),
        grid_spec=pltpu.PrefetchScalarGridSpec(
            num_scalar_prefetch=1, grid=(4 * n_jobs,), in_specs=specs, out_specs=out_specs
        ),
        out_shape=out_shape,
        compiler_params=params(),
        cost_estimate=cost(flops, flops // 400),
        name=name + ("_keep" if keep else "_send"),
    )(idx, *args)


def chip_of(i, idx):
    return (idx[0] // 2) ^ (3 - i)


def core_of(keep, idx):
    return idx[0] & 1 if keep else (idx[0] & 1) ^ 1


def grad_down(idx, act, gffn, got=None):
    tokens, width = gffn.shape
    keep = got is not None
    rows = act.shape[1] // 32

    def act_spec(zz):
        def at(i, idx):
            return (0, zz * 8 + chip_of(i, idx) * 2 + core_of(keep, idx))

        return pl.BlockSpec((tokens, rows), at)

    specs = [act_spec(0), act_spec(1), act_spec(2), act_spec(3)]
    specs += [pl.BlockSpec((tokens, width), lambda i, idx: (0, 0))]
    args = [act, act, act, act, gffn]
    flops = act.shape[1] * width * tokens
    jobs = [([(4, 1)], split_down)]
    return grad_call("grad_down", idx, specs, args, jobs, (rows, width // 2), flops, got)


def grad_up(idx, two, ghid, got=None):
    tokens, width = two.shape
    keep = got is not None
    cols = ghid.shape[1] // 8
    specs = [
        pl.BlockSpec((tokens, width), lambda i, idx: (0, 0)),
        pl.BlockSpec((tokens, cols), lambda i, idx: (0, chip_of(i, idx) * 2 + core_of(keep, idx))),
    ]
    flops = ghid.shape[1] * width * tokens
    jobs = [([(1, 1)], split_up)]
    return grad_call("grad_up", idx, specs, [two, ghid], jobs, (width // 8, cols), flops, got)


def grad_out_kernel(idx_ref, att_ref, gmix_ref, send_ref, own_ref, wide):
    wide[...] = dot_tn(att_ref[...], gmix_ref[...])
    share_out(wide, idx_ref, send_ref, own_ref)


def grad_out(idx, att, gmix):
    tokens, width = att.shape
    cols = width // 4
    piece = (4, 2, width // 16, cols)
    block = pl.BlockSpec((1, 1) + piece, lambda i, idx: (i, 0, 0, 0, 0, 0))
    return pl.pallas_call(
        grad_out_kernel,
        grid_spec=pltpu.PrefetchScalarGridSpec(
            num_scalar_prefetch=1,
            grid=(4,),
            in_specs=[
                pl.BlockSpec((tokens, width), lambda i, idx: (0, 0)),
                pl.BlockSpec((tokens, cols), lambda i, idx: (0, chip_of(i, idx))),
            ],
            out_specs=(block, block),
            scratch_shapes=[pltpu.VMEM((width, cols), F32)],
        ),
        out_shape=(SDS((4, 1) + piece, BF),) * 2,
        compiler_params=params(),
        cost_estimate=cost(2 * tokens * width * width, 8 * tokens * width),
        name="grad_out",
    )(idx, att, gmix)


def head_sums_kernel(n, *refs):
    owns, gots, outs = refs[:n], refs[n : 2 * n], refs[2 * n :]
    for dst in range(4):

        @pl.when(pl.program_id(0) == dst)
        def _():
            for f in range(2):
                parts = [o[0, 0, :, f].astype(F32) + g[0, 0, :, f].astype(F32) for o, g in zip(owns, gots)]
                bit = dst // 2 if f == 0 else dst % 2
                outs[2 * f + bit][0, 0] = jnp.concatenate(parts, axis=-1).astype(BF)


def head_sums(owns, gots):
    _, _, slots, _, rows, _ = owns[0].shape
    cols = sum(o.shape[-1] for o in owns)
    half = (1, 1, slots, rows, cols)
    along_y = (lambda i: (jnp.minimum(i, 1), 0, 0, 0, 0), lambda i: (jnp.maximum(i - 2, 0), 0, 0, 0, 0))
    along_x = (lambda i: (i // 2, 0, 0, 0, 0),) * 2
    return pl.pallas_call(
        functools.partial(head_sums_kernel, len(owns)),
        grid=(4,),
        in_specs=[pl.BlockSpec((1,) + a.shape[1:], lambda i: (i, 0, 0, 0, 0, 0)) for a in owns + gots],
        out_specs=tuple(pl.BlockSpec(half, m) for m in along_y + along_x),
        out_shape=(SDS((2, 1, slots, rows, cols), BF),) * 4,
        compiler_params=params(),
        cost_estimate=cost(0, 48 * slots * rows * cols),
        name="head_sums",
    )(*owns, *gots)


def add_low(a, b):
    return (a.astype(F32) + b.astype(F32)).astype(BF)


def add_wide(a, b):
    return a.astype(F32) + b.astype(F32)


def plane_first(parts):
    return [swap(parts[2 * f], "dp", mask) for f, mask in enumerate((4, 2))]


def plane_adds(parts, got):
    send = [add_low(parts[2 * f + 1][0], got[f][0]) for f in range(2)]
    keep = [add_low(parts[2 * f + 1][1], got[f][1]) for f in range(2)]
    return keep, send


def plane_second(parts, got):
    keep, send = plane_adds(parts, got)
    return keep, [swap(s, "dp", mask) for s, mask in zip(send, (2, 4))]


def plane_direct(parts):
    return [swap(part, "dp", mask) for part, mask in zip(parts, (6, 4, 2))]


def plane_total(parts, got):
    return add_wide(parts[3], got[0]) + add_wide(got[1], got[2])


def across_first(both):
    return both[:, 0::2].astype(BF), both[:, 1::2].astype(BF)


def spread(piece):
    four = jnp.stack([piece] + [swap(piece, "dp", mask) for mask in (2, 4, 6)])
    return four


def spread_core(four):
    return [((0, 2, 4, 6), four), ((1, 3, 5, 7), swap(four, "dp", 1))]


def place_ffn(dp, piece, outs):
    up_grad, down_grad = outs
    rows, cols = piece.shape[2], piece.shape[3]
    at = pl.ds(pl.multiple_of(dp * rows, rows), rows)
    down_grad[at, :cols] = piece[0, 0].astype(F32)
    down_grad[at, cols:] = piece[0, 1].astype(F32)
    at = pl.ds(pl.multiple_of(dp * cols, cols), cols)
    up_grad[:rows, at] = piece[1, 0].astype(F32)
    up_grad[rows:, at] = piece[1, 1].astype(F32)


def place_heads(dp, piece, outs):
    qkv_grad, out_grad = outs
    width = out_grad.shape[1]
    rows, cols = out_grad.shape[0] // 2, width // 4
    chip, core = dp // 2, dp % 2
    at_rows = pl.ds(pl.multiple_of(core * rows, rows), rows)
    part_of = piece[:rows].astype(F32)
    for half, skip in ((0, 0), (1, 3 * PAIR + cols)):
        for part in range(3):
            at = pl.multiple_of(part * width + half * (width // 2) + chip * PAIR, PAIR)
            here = skip + part * PAIR
            qkv_grad[at_rows, pl.ds(at, PAIR)] = part_of[:, here : here + PAIR]
    at = pl.multiple_of(chip * cols, cols)
    out_grad[at_rows, pl.ds(at, cols)] = part_of[:, 3 * PAIR : 3 * PAIR + cols]


def finish_kernel(placer, masks, idx_ref, *refs):
    ins, outs = refs[: len(masks)], refs[len(masks) :]
    for group, ref in zip(masks, ins):
        for which, mask in enumerate(group):
            placer(idx_ref[0] ^ mask, ref[which], outs)


def finish(name, idx, placer, flow, shapes):
    masks = [m for m, _ in flow]
    arrays = [a for _, a in flow]
    vmem = pl.BlockSpec(memory_space=pltpu.VMEM)
    return pl.pallas_call(
        functools.partial(finish_kernel, placer, masks),
        in_specs=[SMEM] + [vmem] * len(arrays),
        out_specs=(vmem,) * len(shapes),
        out_shape=tuple(SDS(s, F32) for s in shapes),
        compiler_params=params(),
        cost_estimate=cost(0, sum(6 * math.prod(s) for s in shapes)),
        name=name,
    )(idx, *arrays)


def segment_starts(lengths, length):
    ends = jnp.cumsum(lengths)
    positions = jnp.arange(length, dtype=jnp.int32)
    begun = jnp.where(ends[None, :] <= positions[:, None], ends[None, :], 0)
    return jnp.max(begun, axis=1).astype(jnp.int32), positions < ends[-1]


def eighth(shard):
    rows = shard.shape[0] // 8
    return lax.dynamic_slice_in_dim(shard, lax.axis_index("dp") * rows, rows, axis=0)


SMALL_ROWS = 16


def pack_small(qv_bias, out_bias, up_bias, down_bias, gain, shift):
    flat = [a.reshape(-1) for a in (qv_bias, out_bias, up_bias, down_bias, gain, shift)]
    return jnp.concatenate(flat)


def unpack_small(shards):
    count, total = shards.shape
    unit = total // SMALL_ROWS
    sizes = ((2, unit), (1, unit), (1, 4 * unit), (1, unit), (4, unit), (4, unit))
    out, at = [], 0
    for lead, cols in sizes:
        block = shards[:, at : at + lead * cols].reshape(count, lead, cols)
        out.append(jnp.swapaxes(block, 0, 1).reshape(lead, count * cols))
        at += lead * cols
    return out


def by_shard(rows, count):
    flat = []
    for arr in rows:
        lead, cols = arr.shape
        flat.append(
            jnp.swapaxes(arr.reshape(lead, count, cols // count), 0, 1).reshape(count, -1)
        )
    return jnp.concatenate(flat, axis=1)


def gather_small(own, got):
    z = lax.axis_index("fsdp")
    slots = jnp.stack([own] + got)
    low, high = z % 2, z // 2
    slots = jnp.where(low == 0, slots, slots[jnp.array([1, 0, 3, 2])])
    return jnp.where(high == 0, slots, slots[jnp.array([2, 3, 0, 1])])


def on_device(
    layer_input,
    qkv_weight,
    query_value_bias,
    out_weight,
    out_bias,
    up_weight,
    up_bias,
    down_weight,
    down_bias,
    norm_gain,
    norm_shift,
    doc_lengths,
    cotangent,
):
    _, tokens, width = layer_input.shape
    shards = lax.axis_size("fsdp")
    halves = shards == 4 and lax.axis_size("dp") == 8
    idx = jnp.stack([lax.axis_index("dp"), lax.axis_index("fsdp")]).astype(jnp.int32)
    x = layer_input[0]
    cot = cotangent[0]
    start, live = segment_starts(doc_lengths[0], tokens)
    start_row = start[None, :]
    live_col = live.astype(F32)[:, None]
    small_own = pack_small(query_value_bias, out_bias, up_bias, down_bias, norm_gain, norm_shift)
    tie = lax.optimization_barrier
    both = (4, 2)
    if halves:
        piece = eighth(qkv_weight)
        cols = piece.shape[1]
        extra = small_own.reshape(piece.shape[0], -1)
        got = shard_swaps(jnp.concatenate([piece, extra], axis=1))
        small = gather_small(small_own, [g[:, cols:].reshape(-1) for g in got])
        half_q = cols // 2
        q_own = [jnp.stack([g[:, :half_q] for g in got]), jnp.stack([g[:, half_q:cols] for g in got])]
        q_own, piece_u = after(q_own, jnp.concatenate([eighth(out_weight), eighth(up_weight)], axis=1))
        q_got = [swap(o, "dp", m) for o, m in zip(q_own, both)]
        got_u = swap(piece_u, "fsdp", 2)
        q_two = [jnp.concatenate([o, g]) for o, g in zip(q_own, q_got)]
        q_four = [swap(t, "dp", 6 - m) for t, m in zip(q_two, both)]
        slots_q = plane_slots(q_two, q_four)
        q_four, got_u = after(q_four, got_u)
        half_u = piece_u.shape[1] // 2
        pair_u = shard_pair(piece_u, got_u)
        own_q, own_u, own_d, at, count = qkv_weight, [out_weight, up_weight], down_weight, idx, shards
    else:
        small = lax.all_gather(small_own, "fsdp", axis=0)
        own_q = lax.all_gather(qkv_weight, "fsdp", axis=0, tiled=True)
        own_u = [
            lax.all_gather(out_weight, "fsdp", axis=0, tiled=True),
            lax.all_gather(up_weight, "fsdp", axis=0, tiled=True),
        ]
        own_d = lax.all_gather(down_weight, "fsdp", axis=0, tiled=True)
        half_q, half_u, at, count = own_q.shape[1] // 2, 0, jnp.zeros_like(idx), 1
        slots_q = slots_u = slots_d = []
    qv_b, out_b, up_b, down_b, gain, shift = unpack_small(small.astype(F32))
    qkv_b = jnp.concatenate([qv_b[0:1], jnp.zeros((1, width), F32), qv_b[1:2]], axis=1)

    spec = (
        [(0, 0, half_q, 0), (0, half_q, half_q, 1)],
        plane_spec([[(0, 0, 0, half_q, 0)], [(0, half_q, 0, half_q, 1)]]) if halves else [],
    )
    normed_one, packed, w_qkv = qkv_forward(
        at, own_q, spec, slots_q, count, x, qkv_b, gain[0:1], shift[0:1]
    )
    if halves:
        packed, pair_u = after(packed, pair_u)
        slots = shard_slots(got_u, pair_u)
        u_own = [jnp.stack([g[:, :half_u] for g in slots]), jnp.stack([g[:, half_u:] for g in slots])]
        u_got = [swap(o, "dp", m) for o, m in zip(u_own, both)]
        u_own, piece_d = after(u_own, eighth(down_weight))
        got_d = swap(piece_d, "fsdp", 2)
        u_own, packed = after(u_own, packed)
    pairs = width // PAIR
    part = attend(packed, start_row, 0, pairs // 2)
    if halves:
        part, u_got, got_d = tie((part, u_got, got_d))
        u_two = [jnp.concatenate([o, g]) for o, g in zip(u_own, u_got)]
        u_four = [swap(t, "dp", 6 - m) for t, m in zip(u_two, both)]
        u_two, got_d, packed = tie((u_two, got_d, packed))
        pair_d = shard_pair(piece_d, got_d)
    attended, lse = attend(packed, start_row, pairs // 2, pairs // 2, part)
    if halves:
        attended, u_four, pair_d = tie((attended, u_four, pair_d))
        slots_u = plane_slots(u_two, u_four)
        slots = shard_slots(got_d, pair_d)
        half_d = width // 2
        d_own = [jnp.stack([g[:, :half_d] for g in slots]), jnp.stack([g[:, half_d:] for g in slots])]
        d_got = [swap(o, "dp", m) for o, m in zip(d_own, both)]
    spec = ([(0, 0, width, 0)], plane_spec([[(0, 0, 0, width, 0)], []])[:4] if halves else [])
    mixed, mid, two, w_out = out_forward(
        at, own_u[0], spec, slots_u[:4], count, attended, x, out_b, gain, shift
    )
    if halves:
        two, d_got = after(two, d_got)
        d_two = [jnp.concatenate([o, g]) for o, g in zip(d_own, d_got)]
        d_four = [swap(t, "dp", 6 - m) for t, m in zip(d_two, both)]
        two, d_two = after(two, d_two)
    up_cols = own_u[1].shape[1]
    rest = half_u - width
    spec = (
        [(0, 0, up_cols, 0)],
        plane_spec([[(0, 0, width, rest, 0)], [(0, rest, 0, half_u, 0)]]) if halves else [],
    )
    act, slope, w_up = up_forward(at, own_u[1], spec, slots_u, count, two, up_b)
    if halves:
        act, d_four = after(act, d_four)
        slots_d = plane_slots(d_two, d_four)
    half = width // 2
    spec = ([(0, 0, width, 0)], plane_spec([[(0, 0, 0, half, 0)], [(0, half, 0, half, 0)]]) if halves else [])
    layer_out, gffn, sums3, ghid, up_sum = down_both(
        at, own_d, spec, slots_d, count, act, slope, down_b, mid, cot, live_col, gain, shift
    )

    if halves:
        send = grad_down(idx, act, gffn)
        got_down = swap(send, "dp", 1)
        send, ghid = after(send, ghid)
        send = grad_up(idx, two, ghid)
        got_up = swap(send, "dp", 1)
        send, got_down, act = tie((send, got_down, act))
        down_parts = grad_down(idx, act, gffn, got_down)
        down_got = plane_direct(down_parts)
        down_parts, ghid = after(down_parts, ghid)
    gmid, gmix, gatt, sums21 = mid_backward(ghid, w_up, w_out, mid, mixed, cot, live_col, gain)
    if halves:
        got_up, ghid, gmix, down_got[1:] = tie((got_up, ghid, gmix, down_got[1:]))
        up_parts = grad_up(idx, two, ghid, got_up)
        up_got = plane_direct(up_parts)
        up_parts, gatt = after(up_parts, gatt)
    back = functools.partial(attend_back, packed)
    share = (idx, normed_one) if halves else ()
    gq0, gk0, gv0, sq0, sv0, *shared0 = back(gatt, attended, lse, start_row, 0, 2, *share)
    if halves:
        gq0, gmix, down_got[0] = tie((gq0, gmix, down_got[0]))
        got0 = swap(shared0[0], "dp", 1)
        out_send, out_own = grad_out(idx, attended, gmix)
        out_got = swap(out_send, "dp", 1)
        out_send, gatt, up_got[1:] = tie((out_send, gatt, up_got[1:]))
    gq1, gk1, gv1, sq1, sv1, *shared1 = back(gatt, attended, lse, start_row, 1, 2, *share)
    if halves:
        up_got[0], gq1 = after(up_got[0], gq1)
        got1 = swap(shared1[0], "dp", 1)
        total = jnp.concatenate([plane_total(down_parts, down_got), plane_total(up_parts, up_got)])
        ffn_keep, ffn_send = across_first(total)
        ffn_got = swap(ffn_send, "fsdp", 1)
        ffn_keep, ffn_send, gq1, got0, out_got, got1 = tie((ffn_keep, ffn_send, gq1, got0, out_got, got1))
        heads_parts = head_sums([shared0[1], out_own, shared1[1]], [got0, out_got, got1])
        heads_got = plane_first(heads_parts)
        _, _, gq1 = tie((heads_parts[0], heads_parts[2], gq1))
    grads = [gq0, gq1, gk0, gk1, gv0, gv1]
    grad_input, sums0 = input_backward(grads, w_qkv, x, gmid, gain, 0, tokens // BLOCK)
    if halves:
        sums0, heads_got, ffn_got = tie((sums0, heads_got, ffn_got))
        heads_keep, heads_send = plane_adds(heads_parts, heads_got)
        heads_got = [swap(part, "dp", mask) for part, mask in zip(heads_send, (2, 4))]
        ffn_send = add_low(ffn_keep[:, 1], ffn_got[:, 1])
        ffn_keep = add_low(ffn_keep[:, 0], ffn_got[:, 0])
        ffn_got = swap(ffn_send, "fsdp", 2)
    small_grads = by_shard(
        [
            jnp.concatenate([jnp.concatenate([sq0, sq1], axis=1), jnp.concatenate([sv0, sv1], axis=1)]),
            sums21[4:5],
            up_sum,
            sums3[2:3],
            jnp.concatenate([sums0[0:1], sums21[2:3], sums21[0:1], sums3[0:1]]),
            jnp.concatenate([sums0[1:2], sums21[3:4], sums21[1:2], sums3[1:2]]),
        ],
        shards,
    )
    if halves:
        total = jnp.stack([add_wide(k, g) for k, g in zip(heads_keep, heads_got)], axis=2)
        keep, send = across_first(total)
        tail = small_grads.reshape(-1, width)
        more = tail.shape[0]
        got = swap(jnp.concatenate([send.reshape(-1, width), tail.astype(BF)]), "fsdp", 1)
        keep, ffn_got = after(keep, ffn_got)
        ffn_four = spread(add_low(ffn_keep, ffn_got))

        keep, got = tie((keep, got))
        tail = tail + got[-more:].astype(F32)
        got = got[:-more].reshape(keep.shape)
        send = add_low(keep[:, 1], got[:, 1])
        keep = add_low(keep[:, 0], got[:, 0])[0]
        got = swap(jnp.concatenate([send.reshape(-1, width), tail.astype(BF)]), "fsdp", 2)

        keep, got, ffn_four = tie((keep, got, ffn_four))
        tail = (tail + got[-more:].astype(F32)).astype(BF)
        piece = add_low(keep.reshape(-1, width), got[:-more])
        piece = jnp.concatenate([piece, tail])
        heads_got = [swap(piece, "dp", mask) for mask in (2, 4, 6)]
        ffn_all = spread_core(ffn_four)
        up_grad, down_grad = finish(
            "finish_ffn", idx, place_ffn, ffn_all, [up_weight.shape, down_weight.shape]
        )

        up_grad, heads_got = after(up_grad, heads_got)
        heads_four = jnp.stack([piece] + heads_got)
        heads_all = spread_core(heads_four)
        heads_core = heads_all[1][1]
        heads_all = [heads_all[0], (heads_all[1][0], heads_core)]
        tail = jnp.sum(heads_four[:, -more:].astype(F32), axis=0) + jnp.sum(
            heads_core[:, -more:].astype(F32), axis=0
        )
        small_sum = lax.dynamic_index_in_dim(
            tail.reshape(small_grads.shape), lax.axis_index("fsdp"), 0, keepdims=False
        )
        qkv_grad, out_grad = finish(
            "finish_heads", idx, place_heads, heads_all, [qkv_weight.shape, out_weight.shape]
        )
    else:
        gpacked = jnp.concatenate([gq0, gq1, gk0, gk1, gv0, gv1], axis=1)

        def reduced(left, right):
            grad = dot_tn(left, right)
            return lax.psum(lax.psum_scatter(grad, "fsdp", scatter_dimension=0, tiled=True), "dp")

        qkv_grad = reduced(normed_one, gpacked)
        out_grad = reduced(attended, gmix)
        up_grad = reduced(two, ghid)
        down_grad = reduced(act, gffn)
        small_sum = lax.dynamic_index_in_dim(
            lax.psum(small_grads, ("dp", "fsdp")), lax.axis_index("fsdp"), 0, keepdims=False
        )
    qv_g, outb_g, upb_g, downb_g, gain_g, shift_g = unpack_small(small_sum[None])
    return (
        layer_out[None],
        grad_input[None],
        qkv_grad,
        qv_g,
        out_grad,
        outb_g[0],
        up_grad,
        upb_g[0],
        down_grad,
        downb_g[0],
        gain_g,
        shift_g,
    )


def solution(mesh):
    rows = P(("dp", "fsdp"), None, None)
    split = P("fsdp", None)
    placed = (
        rows,
        split,
        P(None, "fsdp"),
        split,
        P("fsdp"),
        split,
        P("fsdp"),
        split,
        P("fsdp"),
        P(None, "fsdp"),
        P(None, "fsdp"),
        P(("dp", "fsdp"), None),
        rows,
    )
    return jax.shard_map(
        on_device,
        mesh=mesh,
        in_specs=placed,
        out_specs=(
            rows,
            rows,
            split,
            P(None, "fsdp"),
            split,
            P("fsdp"),
            split,
            P("fsdp"),
            split,
            P("fsdp"),
            P(None, "fsdp"),
            P(None, "fsdp"),
        ),
        check_vma=False,
    )
```

```python
import functools
import math

import jax
import jax.numpy as jnp
from jax import lax
from jax.experimental import pallas as pl
from jax.experimental.pallas import tpu as pltpu
from jax.sharding import PartitionSpec as P

F32 = jnp.float32
BF = jnp.bfloat16
SDS = jax.ShapeDtypeStruct
HEAD_DIM = 64
PAIR = 2 * HEAD_DIM
EPS = 1e-05
MASKED = -1e30
QUERY_SCALE = math.log2(math.e) / math.sqrt(HEAD_DIM)
GRAD_SCALE = 1.0 / math.sqrt(HEAD_DIM)
BLOCK = 256
UP_COLS = 1024
HIDDEN_COLS = 1024
GELU_A = math.sqrt(2.0 / math.pi)
GELU_B = 0.044715 * GELU_A


def params(**more):
    return pltpu.CompilerParams(vmem_limit_bytes=60 * 1024 * 1024, **more)


def cost(flops, nbytes, trans=0):
    return pl.CostEstimate(flops=int(flops) // 1, bytes_accessed=int(nbytes) // 1, transcendentals=int(trans))


def dot_nn(a, b):
    return lax.dot_general(a, b, (((1,), (0,)), ((), ())), preferred_element_type=F32)


def dot_nt(a, b):
    return lax.dot_general(a, b, (((1,), (1,)), ((), ())), preferred_element_type=F32)


def dot_tn(a, b):
    return lax.dot_general(a, b, (((0,), (0,)), ((), ())), preferred_element_type=F32)


def centred(values):
    centre = values - jnp.mean(values, axis=-1, keepdims=True)
    rstd = lax.rsqrt(jnp.mean(centre * centre, axis=-1, keepdims=True) + EPS)
    return centre * rstd, rstd


def norm_back(grad, vhat, rstd, gain):
    e = grad * gain
    mean_e = jnp.mean(e, axis=-1, keepdims=True)
    mean_ev = jnp.mean(e * vhat, axis=-1, keepdims=True)
    return (e - mean_e - vhat * mean_ev) * rstd


def col_sum(values):
    return jnp.sum(values, axis=0, keepdims=True)


def piece_copies(spec, idx_ref, own_refs, slot_refs, places, sems):
    own_spec, slot_spec = spec
    dp, z = idx_ref[0], idx_ref[1]
    copies = []

    def add(group, src, dst):
        copies.append((group, pltpu.make_async_copy(src, dst, sems.at[len(copies)])))

    for o, first, cols, group in own_spec:
        rows = own_refs[o].shape[0]
        dst = places[o].at[pl.ds(pl.multiple_of(z * rows, rows), rows), first : first + cols]
        add(group, own_refs[o].at[:, first : first + cols], dst)
    for (pair, parts), ref in zip(slot_spec, slot_refs):
        rows = ref.shape[1]
        others = ref.shape[0] // 2
        for which, mask in enumerate(pair):
            for k in range(1, others + 1):
                at = which * others + k - 1
                for o, there, here, cols, group in parts:
                    dst = pl.multiple_of((z ^ k) * own_refs[o].shape[0] + (dp ^ mask) * rows, rows)
                    add(
                        group,
                        ref.at[at, :, here : here + cols],
                        places[o].at[pl.ds(dst, rows), there : there + cols],
                    )
    return copies


def count_copies(spec, slots):
    own_spec, slot_spec = spec
    return len(own_spec) + sum(len(parts) * s.shape[0] for (_, parts), s in zip(slot_spec, slots))


def start_all(copies):
    for _, copy in copies:
        copy.start()


def wait_group(copies, group):
    for g, copy in copies:
        if g == group:
            copy.wait()


def whole_shapes(owns, shards):
    return [(o.shape[0] * shards, o.shape[1]) for o in owns]


ANY = pl.BlockSpec(memory_space=pl.ANY)
SMEM = pl.BlockSpec(memory_space=pltpu.SMEM)


def qkv_kernel(spec, n_slots, idx_ref, own_ref, *refs):
    slots = refs[:n_slots]
    x_ref, bias_ref, gain_ref, shift_ref, normed_ref, packed_ref, out_ref = refs[n_slots : n_slots + 7]
    weight, sems, out_sem = refs[n_slots + 7 :]
    step, steps = pl.program_id(0), pl.num_programs(0)
    copies = piece_copies(spec, idx_ref, [own_ref], slots, [weight], sems)
    bn = packed_ref.shape[1]

    @pl.when(step == 0)
    def _():
        start_all(copies)
        vhat, _ = centred(x_ref[...].astype(F32))
        normed_ref[...] = (vhat * gain_ref[...] + shift_ref[...]).astype(BF)
        wait_group(copies, 0)

    half = weight.shape[1] // 2

    @pl.when(step == half // bn)
    def _():
        wait_group(copies, 1)
        pltpu.make_async_copy(weight, out_ref, out_sem).start()

    block = weight[:, pl.ds(pl.multiple_of(step * bn, bn), bn)]
    out = dot_nn(normed_ref[...], block) + bias_ref[...]
    packed_ref[...] = (out * jnp.where(step < steps // 3, QUERY_SCALE, 1.0)).astype(BF)

    @pl.when(step == steps - 1)
    def _():
        pltpu.make_async_copy(weight, out_ref, out_sem).wait()


def qkv_forward(idx, own, spec, slots, shards, x, bias, gain, shift):
    tokens, width = x.shape
    ((rows, cols),) = whole_shapes([own], shards)
    bn = width // 2
    row = pl.BlockSpec((1, width), lambda j: (0, 0))
    full = pl.BlockSpec((tokens, width), lambda j: (0, 0))
    return pl.pallas_call(
        functools.partial(qkv_kernel, spec, len(slots)),
        grid=(cols // bn,),
        in_specs=[SMEM] + [ANY] * (1 + len(slots))
        + [full, pl.BlockSpec((1, bn), lambda j: (0, j)), row, row],
        out_specs=(full, pl.BlockSpec((tokens, bn), lambda j: (0, j)), ANY),
        out_shape=(SDS((tokens, width), BF), SDS((tokens, cols), BF), SDS((rows, cols), BF)),
        scratch_shapes=[
            pltpu.VMEM((rows, cols), BF),
            pltpu.SemaphoreType.DMA((count_copies(spec, slots),)),
            pltpu.SemaphoreType.DMA(()),
        ],
        compiler_params=params(),
        cost_estimate=cost(2 * tokens * width * cols, 2 * width * cols + 2 * tokens * cols),
        name="qkv_forward",
    )(idx, own, *slots, x, bias, gain, shift)


def gelu_and_slope(a):
    sq = a * a
    t = jnp.tanh(a * (sq * GELU_B + GELU_A))
    half = 0.5 * t + 0.5
    act = a * half
    slope = half + act * ((1.0 - half) * (sq * (6.0 * GELU_B) + 2.0 * GELU_A))
    return act.astype(BF), slope.astype(BF)


def out_kernel(spec, n_slots, idx_ref, own_ref, *refs):
    slots = refs[:n_slots]
    att_ref, x_ref, bias_ref, gain_ref, shift_ref = refs[n_slots : n_slots + 5]
    mixed_ref, mid_ref, two_ref, save_ref, weight, sems, save_sem = refs[n_slots + 5 :]
    step, steps = pl.program_id(0), pl.num_programs(0)
    copies = piece_copies(spec, idx_ref, [own_ref], slots, [weight], sems)
    save = pltpu.make_async_copy(weight, save_ref, save_sem)

    @pl.when(step == 0)
    def _():
        start_all(copies)
        wait_group(copies, 0)
        save.start()

    mixed = dot_nn(att_ref[...], weight[...]) + bias_ref[...]
    mixed_ref[...] = mixed
    vhat, _ = centred(mixed)
    mid = x_ref[...].astype(F32) + vhat * gain_ref[1:2, :] + shift_ref[1:2, :]
    mid_ref[...] = mid
    vhat, _ = centred(mid)
    two_ref[...] = (vhat * gain_ref[2:3, :] + shift_ref[2:3, :]).astype(BF)

    @pl.when(step == steps - 1)
    def _():
        save.wait()


def out_forward(idx, own, spec, slots, shards, attended, x, bias, gain, shift):
    tokens, width = x.shape
    (shape,) = whole_shapes([own], shards)
    tok = pl.BlockSpec((BLOCK, width), lambda i: (i, 0))

    def whole(arr):
        return pl.BlockSpec(arr.shape, lambda i: (0, 0))

    return pl.pallas_call(
        functools.partial(out_kernel, spec, len(slots)),
        grid=(tokens // BLOCK,),
        in_specs=[SMEM] + [ANY] * (1 + len(slots)) + [tok, tok, whole(bias), whole(gain), whole(shift)],
        out_specs=(tok, tok, tok, ANY),
        out_shape=(
            SDS((tokens, width), F32),
            SDS((tokens, width), F32),
            SDS((tokens, width), BF),
            SDS(shape, BF),
        ),
        scratch_shapes=[
            pltpu.VMEM(shape, BF),
            pltpu.SemaphoreType.DMA((count_copies(spec, slots),)),
            pltpu.SemaphoreType.DMA(()),
        ],
        compiler_params=params(),
        cost_estimate=cost(2 * tokens * width * width, 16 * tokens * width),
        name="out_forward",
    )(idx, own, *slots, attended, x, bias, gain, shift)


def up_kernel(spec, n_slots, idx_ref, own_ref, *refs):
    slots = refs[:n_slots]
    two_ref, bias_ref, act_ref, slope_ref, save_ref, weight, sems, save_sem = refs[n_slots:]
    step, steps = pl.program_id(0), pl.num_programs(0)
    copies = piece_copies(spec, idx_ref, [own_ref], slots, [weight], sems)
    save = pltpu.make_async_copy(weight, save_ref, save_sem)

    @pl.when(step == 0)
    def _():
        start_all(copies)
        wait_group(copies, 0)
        save.start()

    bn = act_ref.shape[1]
    at = pl.ds(pl.multiple_of(step * bn, bn), bn)
    a = dot_nn(two_ref[...], weight[:, at]) + bias_ref[...]
    act_ref[...], slope_ref[...] = gelu_and_slope(a)

    @pl.when(step == steps - 1)
    def _():
        save.wait()


def up_forward(idx, own, spec, slots, shards, two, bias):
    tokens, width = two.shape
    (shape,) = whole_shapes([own], shards)
    cols = shape[1]
    bn = UP_COLS
    col = pl.BlockSpec((tokens, bn), lambda i: (0, i))
    return pl.pallas_call(
        functools.partial(up_kernel, spec, len(slots)),
        grid=(cols // bn,),
        in_specs=[SMEM] + [ANY] * (1 + len(slots))
        + [pl.BlockSpec((tokens, width), lambda i: (0, 0)), pl.BlockSpec((1, bn), lambda i: (0, i))],
        out_specs=(col, col, ANY),
        out_shape=(SDS((tokens, cols), BF), SDS((tokens, cols), BF), SDS(shape, BF)),
        scratch_shapes=[
            pltpu.VMEM(shape, BF),
            pltpu.SemaphoreType.DMA((count_copies(spec, slots),)),
            pltpu.SemaphoreType.DMA(()),
        ],
        compiler_params=params(),
        cost_estimate=cost(2 * tokens * width * cols, 2 * width * cols + 4 * tokens * cols),
        name="up_forward",
    )(idx, own, *slots, two, bias)


def down_kernel(spec, n_slots, first, idx_ref, own_ref, *refs):
    slots = refs[:n_slots]
    act_ref, slope_ref, bias_ref, mid_ref, cot_ref, live_ref, gain_ref, shift_ref = refs[n_slots : n_slots + 8]
    out_ref, grad_ref, sums_ref, hid_ref, hsum_ref, weight, sems = refs[n_slots + 8 :]
    step = pl.program_id(0)
    copies = piece_copies(spec, idx_ref, [own_ref], slots, [weight], sems)

    @pl.when(step == 0)
    def _():
        start_all(copies)
        sums_ref[...] = jnp.zeros_like(sums_ref)
        wait_group(copies, 0)

    @pl.when(step < first)
    def _():
        ffn = dot_nn(act_ref[...], weight[...]) + bias_ref[...]
        vhat, rstd = centred(ffn)
        gain = gain_ref[3:4, :]
        out_ref[...] = (mid_ref[...] + vhat * gain + shift_ref[3:4, :]).astype(BF)
        grad = cot_ref[...].astype(F32) * live_ref[...]
        low = norm_back(grad, vhat, rstd, gain).astype(BF)
        grad_ref[pl.ds(pl.multiple_of(step * BLOCK, BLOCK), BLOCK), :] = low
        sums_ref[0:1, :] += col_sum(grad * vhat)
        sums_ref[1:2, :] += col_sum(grad)
        sums_ref[2:3, :] += col_sum(low.astype(F32))

    @pl.when(step >= first)
    def _():
        bn = hid_ref.shape[1]
        at = pl.ds(pl.multiple_of((step - first) * bn, bn), bn)
        low = (dot_nt(grad_ref[...], weight[at, :]) * slope_ref[...].astype(F32)).astype(BF)
        hid_ref[...] = low
        hsum_ref[...] = col_sum(low.astype(F32))


def down_both(idx, own, spec, slots, shards, act, slope, bias, mid, cot, live, gain, shift):
    tokens, width = mid.shape
    (shape,) = whole_shapes([own], shards)
    cols = shape[0]
    bn = HIDDEN_COLS
    first = tokens // BLOCK

    def at(i):
        return jnp.minimum(i, first - 1)

    tok = pl.BlockSpec((BLOCK, width), lambda i: (at(i), 0))
    col = pl.BlockSpec((tokens, bn), lambda i: (0, jnp.maximum(i - first, 0)))

    def whole(arr):
        return pl.BlockSpec(arr.shape, lambda i: (0, 0))

    return pl.pallas_call(
        functools.partial(down_kernel, spec, len(slots), first),
        grid=(first + cols // bn,),
        in_specs=[SMEM] + [ANY] * (1 + len(slots))
        + [
            pl.BlockSpec((BLOCK, cols), lambda i: (at(i), 0)),
            col,
            whole(bias),
            tok,
            tok,
            pl.BlockSpec((BLOCK, 1), lambda i: (at(i), 0)),
            whole(gain),
            whole(shift),
        ],
        out_specs=(
            tok,
            pl.BlockSpec((tokens, width), lambda i: (0, 0)),
            pl.BlockSpec((8, width), lambda i: (0, 0)),
            col,
            pl.BlockSpec((1, bn), lambda i: (0, jnp.maximum(i - first, 0))),
        ),
        out_shape=(
            SDS((tokens, width), BF),
            SDS((tokens, width), BF),
            SDS((8, width), F32),
            SDS((tokens, cols), BF),
            SDS((1, cols), F32),
        ),
        scratch_shapes=[pltpu.VMEM(shape, BF), pltpu.SemaphoreType.DMA((count_copies(spec, slots),))],
        compiler_params=params(),
        cost_estimate=cost(4 * tokens * width * cols, 2 * width * cols + 6 * tokens * cols),
        name="down_both",
    )(idx, own, *slots, act, slope, bias, mid, cot, live, gain, shift)


def mid_kernel(
    gh_ref, up_ref, out_w_ref, mid_ref, mixed_ref, cot_ref, live_ref, gain_ref,
    gmid_ref, gmix_ref, gatt_ref, sums_ref,
):
    @pl.when(pl.program_id(0) == 0)
    def _():
        sums_ref[...] = jnp.zeros_like(sums_ref)

    grad = dot_nt(gh_ref[...], up_ref[...])
    vhat, rstd = centred(mid_ref[...])
    sums_ref[0:1, :] += col_sum(grad * vhat)
    sums_ref[1:2, :] += col_sum(grad)
    gmid = cot_ref[...].astype(F32) * live_ref[...] + norm_back(grad, vhat, rstd, gain_ref[2:3, :])
    gmid_ref[...] = gmid
    vhat, rstd = centred(mixed_ref[...])
    sums_ref[2:3, :] += col_sum(gmid * vhat)
    sums_ref[3:4, :] += col_sum(gmid)
    low = norm_back(gmid, vhat, rstd, gain_ref[1:2, :]).astype(BF)
    gmix_ref[...] = low
    sums_ref[4:5, :] += col_sum(low.astype(F32))
    gatt_ref[...] = dot_nt(low, out_w_ref[...]).astype(BF)


def mid_backward(gh, up, out_w, mid, mixed, cot, live, gain):
    tokens, width = mid.shape
    cols = gh.shape[1]
    tok = pl.BlockSpec((BLOCK, width), lambda i: (i, 0))

    def whole(arr):
        return pl.BlockSpec(arr.shape, lambda i: (0, 0))

    return pl.pallas_call(
        mid_kernel,
        grid=(tokens // BLOCK,),
        in_specs=[
            pl.BlockSpec((BLOCK, cols), lambda i: (i, 0)),
            whole(up),
            whole(out_w),
            tok,
            tok,
            tok,
            pl.BlockSpec((BLOCK, 1), lambda i: (i, 0)),
            whole(gain),
        ],
        out_specs=(tok, tok, tok, pl.BlockSpec((8, width), lambda i: (0, 0))),
        out_shape=(
            SDS((tokens, width), F32),
            SDS((tokens, width), BF),
            SDS((tokens, width), BF),
            SDS((8, width), F32),
        ),
        compiler_params=params(),
        cost_estimate=cost(2 * tokens * width * (cols + width), 2 * width * cols + 2 * tokens * cols),
        name="mid_backward",
    )(gh, up, out_w, mid, mixed, cot, live, gain)


def input_kernel(n_grads, n_into, *refs):
    grad_refs, (w_ref, x_ref, gmid_ref, gain_ref) = refs[:n_grads], refs[n_grads : n_grads + 4]
    out_ref, sums_ref = refs[n_grads + 4 + n_into :]

    @pl.when(pl.program_id(0) == 0)
    def _():
        sums_ref[...] = jnp.zeros_like(sums_ref)

    grads = jnp.concatenate([ref[...] for ref in grad_refs], axis=1)
    grad = dot_nt(grads, w_ref[...])
    vhat, rstd = centred(x_ref[...].astype(F32))
    sums_ref[0:1, :] += col_sum(grad * vhat)
    sums_ref[1:2, :] += col_sum(grad)
    out_ref[...] = gmid_ref[...] + norm_back(grad, vhat, rstd, gain_ref[0:1, :])


def input_backward(grads, weight, x, gmid, gain, first, count, into=None):
    tokens, width = x.shape
    tok = pl.BlockSpec((BLOCK, width), lambda i: (first + i, 0))

    def whole(arr):
        return pl.BlockSpec(arr.shape, lambda i: (0, 0))

    in_specs = [pl.BlockSpec((BLOCK, g.shape[1]), lambda i: (first + i, 0)) for g in grads]
    in_specs += [whole(weight), tok, tok, whole(gain)]
    args = [*grads, weight, x, gmid, gain]
    aliases = {}
    if into is not None:
        aliases = {len(args): 0}
        in_specs.append(pl.BlockSpec(memory_space=pl.ANY))
        args.append(into)
    return pl.pallas_call(
        functools.partial(input_kernel, len(grads), len(aliases)),
        grid=(count,),
        in_specs=in_specs,
        out_specs=(tok, pl.BlockSpec((8, width), lambda i: (0, 0))),
        out_shape=(SDS((tokens, width), F32), SDS((8, width), F32)),
        input_output_aliases=aliases,
        compiler_params=params(),
        cost_estimate=cost(6 * count * BLOCK * width * width, 6 * width * width),
        name="input_backward",
    )(*args)


def fill_bias(bias, start_ref):
    length = bias.shape[0]
    for j in range(length // BLOCK):
        key = lax.broadcasted_iota(jnp.int32, (BLOCK, length), 0) + j * BLOCK
        query = lax.broadcasted_iota(jnp.int32, (BLOCK, length), 1)
        allowed = (key <= query) & (key >= start_ref[...])
        bias[j * BLOCK : (j + 1) * BLOCK, :] = jnp.where(allowed, 0.0, MASKED)


def one_head(low, arr, head):
    zero = jnp.zeros_like(arr)
    return jnp.where(low, arr, zero) if head == 0 else jnp.where(low, zero, arr)


def attend_kernel(q_ref, k_ref, v_ref, start_ref, out_ref, lse_ref, bias):
    length = q_ref.shape[0]

    @pl.when(pl.program_id(0) == 0)
    def _():
        fill_bias(bias, start_ref)

    low = lax.broadcasted_iota(jnp.int32, (1, PAIR), 1) < HEAD_DIM
    low_rows = lax.broadcasted_iota(jnp.int32, (PAIR, 1), 0) < HEAD_DIM
    keys = k_ref[...]
    values = jnp.concatenate([v_ref[...], jnp.ones((length, PAIR), BF)], axis=1)
    for i in range(length // BLOCK):
        reach = (i + 1) * BLOCK
        sl = slice(i * BLOCK, reach)
        queries = q_ref[sl, :]
        parts = []
        for head in range(2):
            scores = dot_nt(keys[:reach], one_head(low, queries, head)) + bias[:reach, sl]
            top = jnp.max(scores, axis=0, keepdims=True)
            probs = jnp.exp2(scores - top).astype(BF)
            mixed = dot_tn(values[:reach], probs)
            total = mixed[PAIR : PAIR + 1]
            parts.append(mixed[:PAIR] / total)
            lse_ref[0, head : head + 1, sl] = top + jnp.log2(total)
        out_ref[sl, :] = jnp.where(low_rows, parts[0], parts[1]).T.astype(BF)


def attend(packed, start_row, first, count, into=None):
    length = packed.shape[0]
    pairs = packed.shape[1] // (3 * PAIR)

    def blk(offset):
        return pl.BlockSpec((length, PAIR), lambda h: (0, offset + first + h))

    in_specs = [blk(0), blk(pairs), blk(2 * pairs), pl.BlockSpec((1, length), lambda h: (0, 0))]
    args = [packed, packed, packed, start_row]
    kernel, aliases = attend_kernel, {}
    if into is not None:
        in_specs = in_specs + [ANY] * len(into)
        aliases = {len(args) + i: i for i in range(len(into))}
        args = args + list(into)

        def kernel(*refs):
            attend_kernel(*refs[:4], *refs[4 + len(into) :])

    return pl.pallas_call(
        kernel,
        grid=(count,),
        in_specs=in_specs,
        out_specs=(blk(0), pl.BlockSpec((1, 2, length), lambda h: (first + h, 0, 0))),
        out_shape=(SDS((length, PAIR * pairs), BF), SDS((pairs, 2, length), F32)),
        input_output_aliases=aliases,
        scratch_shapes=[pltpu.VMEM((length, length), F32)],
        compiler_params=params(),
        cost_estimate=cost(8 * count * length * length * PAIR, 8 * length * count * PAIR),
        name="attend",
    )(*args)


def share_out(wide, idx_ref, send_ref, own_ref):
    core, z = idx_ref[0] & 1, idx_ref[1]
    rows = wide.shape[0] // 8
    for zz in range(4):
        for ref, c in ((send_ref, core ^ 1), (own_ref, core)):
            at = pl.ds(pl.multiple_of((2 * zz + c) * rows, rows), rows)
            part = wide[at, :].astype(BF)
            ref[0, 0, zz ^ z, 0] = part[: rows // 2]
            ref[0, 0, zz ^ z, 1] = part[rows // 2 :]


def attend_back_kernel(shared, *refs):
    if shared:
        idx_ref, one_ref, refs = refs[0], refs[1], refs[2:]
        send_ref, own_ref, wide = refs[12], refs[13], refs[16]
        refs = refs[:12] + refs[14:16]
    q_ref, k_ref, v_ref, g_ref, o_ref, lse_ref, start_ref = refs[:7]
    gq_ref, gk_ref, gv_ref, sq_ref, sv_ref, bias, acc = refs[7:]
    length = q_ref.shape[0]

    @pl.when(pl.program_id(0) == 0)
    def _():
        fill_bias(bias, start_ref)

    low = lax.broadcasted_iota(jnp.int32, (1, PAIR), 1) < HEAD_DIM
    queries, grads = q_ref[...], g_ref[...]
    q_of = [one_head(low, queries, head) for head in range(2)]
    g_of = [one_head(low, grads, head) for head in range(2)]
    inner = (grads.astype(F32) * o_ref[...].astype(F32)).T
    inner_of = [col_sum(inner[:HEAD_DIM]), col_sum(inner[HEAD_DIM:])]
    sum_v = jnp.zeros((1, PAIR), F32)
    for j in range(length // BLOCK):
        first = j * BLOCK
        sl = slice(first, first + BLOCK)
        keys, values = k_ref[sl, :], v_ref[sl, :]
        gk = gv = gq = 0.0
        for head in range(2):
            scores = dot_nt(keys, q_of[head][first:]) + bias[sl, first:]
            probs = jnp.exp2(scores - lse_ref[0, head : head + 1, first:])
            gprobs = dot_nt(values, g_of[head][first:])
            gscores = (probs * (gprobs - inner_of[head][:, first:]) * GRAD_SCALE).astype(BF)
            gv = gv + dot_nn(probs.astype(BF), g_of[head][first:])
            gk = gk + dot_nn(gscores, q_of[head][first:])
            gq = gq + dot_tn(gscores, one_head(low, keys, head))
        low_v = gv.astype(BF)
        gv_ref[sl, :] = low_v
        gk_ref[sl, :] = (gk * (1.0 / QUERY_SCALE)).astype(BF)
        sum_v = sum_v + col_sum(low_v.astype(F32))
        if j == 0:
            acc[...] = gq
        else:
            acc[first:, :] += gq
    low_q = acc[...].astype(BF)
    gq_ref[...] = low_q
    sq_ref[...] = col_sum(low_q.astype(F32))
    sv_ref[...] = sum_v
    if shared:
        grads = jnp.concatenate([low_q, gk_ref[...], gv_ref[...]], axis=1)
        wide[...] = dot_tn(one_ref[...], grads)
        share_out(wide, idx_ref, send_ref, own_ref)


def attend_back(packed, grads, attended, lse, start_row, part, parts, idx=None, one=None):
    length = packed.shape[0]
    total = packed.shape[1] // (3 * PAIR)
    count = total // parts
    first = part * count
    shared = one is not None

    def blk(offset):
        return pl.BlockSpec((length, PAIR), lambda h, *_: (0, offset + h))

    row = pl.BlockSpec((1, PAIR), lambda h, *_: (0, h))
    grad = SDS((length, PAIR * count), BF)
    sums = SDS((1, PAIR * count), F32)
    in_specs = [
        blk(first),
        blk(total + first),
        blk(2 * total + first),
        blk(first),
        blk(first),
        pl.BlockSpec((1, 2, length), lambda h, *_: (first + h, 0, 0)),
        pl.BlockSpec((1, length), lambda h, *_: (0, 0)),
    ]
    args = [packed, packed, packed, grads, attended, lse, start_row]
    out_specs = [blk(0), blk(0), blk(0), row, row]
    out_shape = [grad, grad, grad, sums, sums]
    scratch = [pltpu.VMEM((length, length), F32), pltpu.VMEM((length, PAIR), F32)]
    if shared:
        width = one.shape[1]
        piece = (4, 2, width // 16, 3 * PAIR)
        block = pl.BlockSpec((1, 1) + piece, lambda h, idx: (3 ^ h ^ (idx[0] // 2), 0, 0, 0, 0, 0))
        in_specs = [pl.BlockSpec(one.shape, lambda h, *_: (0, 0))] + in_specs
        args = [idx, one] + args
        out_specs = out_specs + [block, block]
        out_shape = out_shape + [SDS((4, 1) + piece, BF)] * 2
        scratch = scratch + [pltpu.VMEM((width, 3 * PAIR), F32)]
    return pl.pallas_call(
        functools.partial(attend_back_kernel, shared),
        grid_spec=pltpu.PrefetchScalarGridSpec(
            num_scalar_prefetch=int(shared),
            grid=(count,),
            in_specs=in_specs,
            out_specs=tuple(out_specs),
            scratch_shapes=scratch,
        ),
        out_shape=tuple(out_shape),
        compiler_params=params(),
        cost_estimate=cost(20 * count * length * length * PAIR, 16 * length * count * PAIR),
        name="attend_back",
    )(*args)


def swap(arr, axis, mask):
    size = lax.axis_size(axis)
    return lax.ppermute(arr, axis, [(i, i ^ mask) for i in range(size)])


def after(first, then):
    return lax.optimization_barrier((first, then))


def shard_swaps(piece):
    return [swap(piece, "fsdp", k) for k in range(1, lax.axis_size("fsdp"))]


def shard_pair(piece, got):
    return swap(jnp.stack([piece, got]), "fsdp", 1)


def shard_slots(got, pair):
    return [pair[0], got, pair[1]]


PLANE_MASKS = [
    (0, 4), (2, 6), (1, 5), (3, 7),
    (0, 2), (4, 6), (1, 3), (5, 7),
]


def plane_slots(two, four):
    return [a for t, f in zip(two, four) for a in (t, f, swap(t, "dp", 1), swap(f, "dp", 1))]


def plane_spec(parts):
    return [(pair, parts[i // 4]) for i, pair in enumerate(PLANE_MASKS)]


def split_down(wide, zz):
    rows, cols = wide.shape[0] // 4, wide.shape[1] // 2
    part = wide[zz * rows : (zz + 1) * rows]
    return part[:, :cols], part[:, cols:]


def split_up(wide, zz):
    rows = wide.shape[0] // 8
    return wide[2 * zz * rows : (2 * zz + 1) * rows], wide[(2 * zz + 1) * rows : (2 * zz + 2) * rows]


def side_by_side(refs):
    blocks = [r[...] for r in refs]
    return blocks[0] if len(blocks) == 1 else jnp.concatenate(blocks, axis=1)


def emit(keep, direct, wide, split, z, chip, rest):
    if not keep:
        for zz in range(4):
            for f, part in enumerate(split(wide, zz)):
                rest[0][0, 0, zz ^ z, f] = part.astype(BF)
        return
    got_ref, outs = rest[0], rest[1:]
    for dst in range(4):

        @pl.when(chip == dst)
        def _():
            for zz in range(4):
                slot = zz ^ z
                for f, part in enumerate(split(wide, zz)):
                    low = (part + got_ref[0, 0, slot, f].astype(F32)).astype(BF)
                    if direct:
                        outs[dst][0, slot, f] = low
                    else:
                        bit = dst // 2 if f == 0 else dst % 2
                        outs[2 * f + bit][0, 0, slot] = low


def grad_kernel(keep, direct, jobs, idx_ref, *refs):
    step, z = pl.program_id(0), idx_ref[1]
    at = 0
    n_in = sum(n for groups, _ in jobs for group in groups for n in group)
    rest = refs[n_in:]
    for number, (groups, split) in enumerate(jobs):
        blocks = []
        for n_left, n_right in groups:
            blocks.append((refs[at : at + n_left], refs[at + n_left : at + n_left + n_right]))
            at += n_left + n_right

        @pl.when(step // 4 == number)
        def _():
            dots = [dot_tn(side_by_side(left), side_by_side(right)) for left, right in blocks]
            wide = dots[0] if len(dots) == 1 else jnp.concatenate(dots, axis=1)
            emit(keep, direct, wide, split, z, step % 4, rest)


def grad_call(name, idx, specs, args, jobs, piece, flops, got=None, direct=True):
    keep = got is not None
    n_jobs = len(jobs)
    rows, cols = piece
    block = pl.BlockSpec((1, 1, 4, 2, rows, cols), lambda i, idx: (i % 4, i // 4, 0, 0, 0, 0))
    half = (1, 1, 4, rows, cols)
    if keep and direct:
        specs = specs + [block]
        args = args + [got]
        out_specs = (pl.BlockSpec((1, 4, 2, rows, cols), lambda i, idx: (0, 0, 0, 0, 0)),) * 4
        out_shape = (SDS((1, 4, 2, rows, cols), BF),) * 4
    elif keep:
        along_y = (
            lambda i, idx: (jnp.minimum(i % 4, 1), i // 4, 0, 0, 0),
            lambda i, idx: (jnp.maximum(i % 4 - 2, 0), i // 4, 0, 0, 0),
        )
        along_x = (lambda i, idx: (i % 4 // 2, i // 4, 0, 0, 0),) * 2
        specs = specs + [block]
        args = args + [got]
        out_specs = tuple(pl.BlockSpec(half, m) for m in along_y + along_x)
        out_shape = (SDS((2, n_jobs, 4, rows, cols), BF),) * 4
    else:
        out_specs = block
        out_shape = SDS((4, n_jobs, 4, 2, rows, cols), BF)
    return pl.pallas_call(
        functools.partial(grad_kernel, keep, direct, jobs),
        grid_spec=pltpu.PrefetchScalarGridSpec(
            num_scalar_prefetch=1, grid=(4 * n_jobs,), in_specs=specs, out_specs=out_specs
        ),
        out_shape=out_shape,
        compiler_params=params(),
        cost_estimate=cost(flops, flops // 400),
        name=name + ("_keep" if keep else "_send"),
    )(idx, *args)


def chip_of(i, idx):
    return (idx[0] // 2) ^ (3 - i)


def core_of(keep, idx):
    return idx[0] & 1 if keep else (idx[0] & 1) ^ 1


def grad_down(idx, act, gffn, got=None):
    tokens, width = gffn.shape
    keep = got is not None
    rows = act.shape[1] // 32

    def act_spec(zz):
        def at(i, idx):
            return (0, zz * 8 + chip_of(i, idx) * 2 + core_of(keep, idx))

        return pl.BlockSpec((tokens, rows), at)

    specs = [act_spec(0), act_spec(1), act_spec(2), act_spec(3)]
    specs += [pl.BlockSpec((tokens, width), lambda i, idx: (0, 0))]
    args = [act, act, act, act, gffn]
    flops = act.shape[1] * width * tokens
    jobs = [([(4, 1)], split_down)]
    return grad_call("grad_down", idx, specs, args, jobs, (rows, width // 2), flops, got)


def grad_up(idx, two, ghid, got=None):
    tokens, width = two.shape
    keep = got is not None
    cols = ghid.shape[1] // 8
    specs = [
        pl.BlockSpec((tokens, width), lambda i, idx: (0, 0)),
        pl.BlockSpec((tokens, cols), lambda i, idx: (0, chip_of(i, idx) * 2 + core_of(keep, idx))),
    ]
    flops = ghid.shape[1] * width * tokens
    jobs = [([(1, 1)], split_up)]
    return grad_call("grad_up", idx, specs, [two, ghid], jobs, (width // 8, cols), flops, got)


def grad_out_kernel(idx_ref, att_ref, gmix_ref, send_ref, own_ref, wide):
    wide[...] = dot_tn(att_ref[...], gmix_ref[...])
    share_out(wide, idx_ref, send_ref, own_ref)


def grad_out(idx, att, gmix):
    tokens, width = att.shape
    cols = width // 4
    piece = (4, 2, width // 16, cols)
    block = pl.BlockSpec((1, 1) + piece, lambda i, idx: (i, 0, 0, 0, 0, 0))
    return pl.pallas_call(
        grad_out_kernel,
        grid_spec=pltpu.PrefetchScalarGridSpec(
            num_scalar_prefetch=1,
            grid=(4,),
            in_specs=[
                pl.BlockSpec((tokens, width), lambda i, idx: (0, 0)),
                pl.BlockSpec((tokens, cols), lambda i, idx: (0, chip_of(i, idx))),
            ],
            out_specs=(block, block),
            scratch_shapes=[pltpu.VMEM((width, cols), F32)],
        ),
        out_shape=(SDS((4, 1) + piece, BF),) * 2,
        compiler_params=params(),
        cost_estimate=cost(2 * tokens * width * width, 8 * tokens * width),
        name="grad_out",
    )(idx, att, gmix)


def head_sums_kernel(n, *refs):
    owns, gots, outs = refs[:n], refs[n : 2 * n], refs[2 * n :]
    for dst in range(4):

        @pl.when(pl.program_id(0) == dst)
        def _():
            for f in range(2):
                parts = [o[0, 0, :, f].astype(F32) + g[0, 0, :, f].astype(F32) for o, g in zip(owns, gots)]
                bit = dst // 2 if f == 0 else dst % 2
                outs[2 * f + bit][0, 0] = jnp.concatenate(parts, axis=-1).astype(BF)


def head_sums(owns, gots):
    _, _, slots, _, rows, _ = owns[0].shape
    cols = sum(o.shape[-1] for o in owns)
    half = (1, 1, slots, rows, cols)
    along_y = (lambda i: (jnp.minimum(i, 1), 0, 0, 0, 0), lambda i: (jnp.maximum(i - 2, 0), 0, 0, 0, 0))
    along_x = (lambda i: (i // 2, 0, 0, 0, 0),) * 2
    return pl.pallas_call(
        functools.partial(head_sums_kernel, len(owns)),
        grid=(4,),
        in_specs=[pl.BlockSpec((1,) + a.shape[1:], lambda i: (i, 0, 0, 0, 0, 0)) for a in owns + gots],
        out_specs=tuple(pl.BlockSpec(half, m) for m in along_y + along_x),
        out_shape=(SDS((2, 1, slots, rows, cols), BF),) * 4,
        compiler_params=params(),
        cost_estimate=cost(0, 48 * slots * rows * cols),
        name="head_sums",
    )(*owns, *gots)


def add_low(a, b):
    return (a.astype(F32) + b.astype(F32)).astype(BF)


def add_wide(a, b):
    return a.astype(F32) + b.astype(F32)


def plane_first(parts):
    return [swap(parts[2 * f], "dp", mask) for f, mask in enumerate((4, 2))]


def plane_adds(parts, got):
    send = [add_low(parts[2 * f + 1][0], got[f][0]) for f in range(2)]
    keep = [add_low(parts[2 * f + 1][1], got[f][1]) for f in range(2)]
    return keep, send


def plane_second(parts, got):
    keep, send = plane_adds(parts, got)
    return keep, [swap(s, "dp", mask) for s, mask in zip(send, (2, 4))]


def plane_direct(parts):
    return [swap(part, "dp", mask) for part, mask in zip(parts, (6, 4, 2))]


def plane_total(parts, got):
    return add_wide(parts[3], got[0]) + add_wide(got[1], got[2])


def across_first(both):
    return both[:, 0::2].astype(BF), both[:, 1::2].astype(BF)


def spread(piece):
    four = jnp.stack([piece] + [swap(piece, "dp", mask) for mask in (2, 4, 6)])
    return four


def spread_core(four):
    return [((0, 2, 4, 6), four), ((1, 3, 5, 7), swap(four, "dp", 1))]


def place_ffn(dp, piece, outs):
    up_grad, down_grad = outs
    rows, cols = piece.shape[2], piece.shape[3]
    at = pl.ds(pl.multiple_of(dp * rows, rows), rows)
    down_grad[at, :cols] = piece[0, 0].astype(F32)
    down_grad[at, cols:] = piece[0, 1].astype(F32)
    at = pl.ds(pl.multiple_of(dp * cols, cols), cols)
    up_grad[:rows, at] = piece[1, 0].astype(F32)
    up_grad[rows:, at] = piece[1, 1].astype(F32)


def place_heads(dp, piece, outs):
    qkv_grad, out_grad = outs
    width = out_grad.shape[1]
    rows, cols = out_grad.shape[0] // 2, width // 4
    chip, core = dp // 2, dp % 2
    at_rows = pl.ds(pl.multiple_of(core * rows, rows), rows)
    part_of = piece[:rows].astype(F32)
    for half, skip in ((0, 0), (1, 3 * PAIR + cols)):
        for part in range(3):
            at = pl.multiple_of(part * width + half * (width // 2) + chip * PAIR, PAIR)
            here = skip + part * PAIR
            qkv_grad[at_rows, pl.ds(at, PAIR)] = part_of[:, here : here + PAIR]
    at = pl.multiple_of(chip * cols, cols)
    out_grad[at_rows, pl.ds(at, cols)] = part_of[:, 3 * PAIR : 3 * PAIR + cols]


def finish_kernel(placer, masks, idx_ref, *refs):
    ins, outs = refs[: len(masks)], refs[len(masks) :]
    for group, ref in zip(masks, ins):
        for which, mask in enumerate(group):
            placer(idx_ref[0] ^ mask, ref[which], outs)


def finish(name, idx, placer, flow, shapes):
    masks = [m for m, _ in flow]
    arrays = [a for _, a in flow]
    vmem = pl.BlockSpec(memory_space=pltpu.VMEM)
    return pl.pallas_call(
        functools.partial(finish_kernel, placer, masks),
        in_specs=[SMEM] + [vmem] * len(arrays),
        out_specs=(vmem,) * len(shapes),
        out_shape=tuple(SDS(s, F32) for s in shapes),
        compiler_params=params(),
        cost_estimate=cost(0, sum(6 * math.prod(s) for s in shapes)),
        name=name,
    )(idx, *arrays)


def segment_starts(lengths, length):
    ends = jnp.cumsum(lengths)
    positions = jnp.arange(length, dtype=jnp.int32)
    begun = jnp.where(ends[None, :] <= positions[:, None], ends[None, :], 0)
    return jnp.max(begun, axis=1).astype(jnp.int32), positions < ends[-1]


def eighth(shard):
    rows = shard.shape[0] // 8
    return lax.dynamic_slice_in_dim(shard, lax.axis_index("dp") * rows, rows, axis=0)


SMALL_ROWS = 16


def pack_small(qv_bias, out_bias, up_bias, down_bias, gain, shift):
    flat = [a.reshape(-1) for a in (qv_bias, out_bias, up_bias, down_bias, gain, shift)]
    return jnp.concatenate(flat)


def unpack_small(shards):
    count, total = shards.shape
    unit = total // SMALL_ROWS
    sizes = ((2, unit), (1, unit), (1, 4 * unit), (1, unit), (4, unit), (4, unit))
    out, at = [], 0
    for lead, cols in sizes:
        block = shards[:, at : at + lead * cols].reshape(count, lead, cols)
        out.append(jnp.swapaxes(block, 0, 1).reshape(lead, count * cols))
        at += lead * cols
    return out


def by_shard(rows, count):
    flat = []
    for arr in rows:
        lead, cols = arr.shape
        flat.append(
            jnp.swapaxes(arr.reshape(lead, count, cols // count), 0, 1).reshape(count, -1)
        )
    return jnp.concatenate(flat, axis=1)


def gather_small(own, got):
    z = lax.axis_index("fsdp")
    slots = jnp.stack([own] + got)
    low, high = z % 2, z // 2
    slots = jnp.where(low == 0, slots, slots[jnp.array([1, 0, 3, 2])])
    return jnp.where(high == 0, slots, slots[jnp.array([2, 3, 0, 1])])


def on_device(
    layer_input,
    qkv_weight,
    query_value_bias,
    out_weight,
    out_bias,
    up_weight,
    up_bias,
    down_weight,
    down_bias,
    norm_gain,
    norm_shift,
    doc_lengths,
    cotangent,
):
    _, tokens, width = layer_input.shape
    shards = lax.axis_size("fsdp")
    halves = shards == 4 and lax.axis_size("dp") == 8
    idx = jnp.stack([lax.axis_index("dp"), lax.axis_index("fsdp")]).astype(jnp.int32)
    x = layer_input[0]
    cot = cotangent[0]
    start, live = segment_starts(doc_lengths[0], tokens)
    start_row = start[None, :]
    live_col = live.astype(F32)[:, None]
    small_own = pack_small(query_value_bias, out_bias, up_bias, down_bias, norm_gain, norm_shift)
    tie = lax.optimization_barrier
    both = (4, 2)
    if halves:
        piece = eighth(qkv_weight)
        cols = piece.shape[1]
        extra = small_own.reshape(piece.shape[0], -1)
        got = shard_swaps(jnp.concatenate([piece, extra], axis=1))
        small = gather_small(small_own, [g[:, cols:].reshape(-1) for g in got])
        half_q = cols // 2
        q_own = [jnp.stack([g[:, :half_q] for g in got]), jnp.stack([g[:, half_q:cols] for g in got])]
        q_own, piece_u = after(q_own, jnp.concatenate([eighth(out_weight), eighth(up_weight)], axis=1))
        q_got = [swap(o, "dp", m) for o, m in zip(q_own, both)]
        got_u = swap(piece_u, "fsdp", 2)
        q_two = [jnp.concatenate([o, g]) for o, g in zip(q_own, q_got)]
        q_four = [swap(t, "dp", 6 - m) for t, m in zip(q_two, both)]
        slots_q = plane_slots(q_two, q_four)
        q_four, got_u = after(q_four, got_u)
        half_u = piece_u.shape[1] // 2
        pair_u = shard_pair(piece_u, got_u)
        own_q, own_u, own_d, at, count = qkv_weight, [out_weight, up_weight], down_weight, idx, shards
    else:
        small = lax.all_gather(small_own, "fsdp", axis=0)
        own_q = lax.all_gather(qkv_weight, "fsdp", axis=0, tiled=True)
        own_u = [
            lax.all_gather(out_weight, "fsdp", axis=0, tiled=True),
            lax.all_gather(up_weight, "fsdp", axis=0, tiled=True),
        ]
        own_d = lax.all_gather(down_weight, "fsdp", axis=0, tiled=True)
        half_q, half_u, at, count = own_q.shape[1] // 2, 0, jnp.zeros_like(idx), 1
        slots_q = slots_u = slots_d = []
    qv_b, out_b, up_b, down_b, gain, shift = unpack_small(small.astype(F32))
    qkv_b = jnp.concatenate([qv_b[0:1], jnp.zeros((1, width), F32), qv_b[1:2]], axis=1)

    spec = (
        [(0, 0, half_q, 0), (0, half_q, half_q, 1)],
        plane_spec([[(0, 0, 0, half_q, 0)], [(0, half_q, 0, half_q, 1)]]) if halves else [],
    )
    normed_one, packed, w_qkv = qkv_forward(
        at, own_q, spec, slots_q, count, x, qkv_b, gain[0:1], shift[0:1]
    )
    if halves:
        packed, pair_u = after(packed, pair_u)
        slots = shard_slots(got_u, pair_u)
        u_own = [jnp.stack([g[:, :half_u] for g in slots]), jnp.stack([g[:, half_u:] for g in slots])]
        u_got = [swap(o, "dp", m) for o, m in zip(u_own, both)]
        u_own, piece_d = after(u_own, eighth(down_weight))
        got_d = swap(piece_d, "fsdp", 2)
        u_own, packed = after(u_own, packed)
    pairs = width // PAIR
    part = attend(packed, start_row, 0, pairs // 2)
    if halves:
        part, u_got, got_d = tie((part, u_got, got_d))
        u_two = [jnp.concatenate([o, g]) for o, g in zip(u_own, u_got)]
        u_four = [swap(t, "dp", 6 - m) for t, m in zip(u_two, both)]
        u_two, got_d, packed = tie((u_two, got_d, packed))
        pair_d = shard_pair(piece_d, got_d)
    attended, lse = attend(packed, start_row, pairs // 2, pairs // 2, part)
    if halves:
        attended, u_four, pair_d = tie((attended, u_four, pair_d))
        slots_u = plane_slots(u_two, u_four)
        slots = shard_slots(got_d, pair_d)
        half_d = width // 2
        d_own = [jnp.stack([g[:, :half_d] for g in slots]), jnp.stack([g[:, half_d:] for g in slots])]
        d_got = [swap(o, "dp", m) for o, m in zip(d_own, both)]
    spec = ([(0, 0, width, 0)], plane_spec([[(0, 0, 0, width, 0)], []])[:4] if halves else [])
    mixed, mid, two, w_out = out_forward(
        at, own_u[0], spec, slots_u[:4], count, attended, x, out_b, gain, shift
    )
    if halves:
        two, d_got = after(two, d_got)
        d_two = [jnp.concatenate([o, g]) for o, g in zip(d_own, d_got)]
        d_four = [swap(t, "dp", 6 - m) for t, m in zip(d_two, both)]
        two, d_two = after(two, d_two)
    up_cols = own_u[1].shape[1]
    rest = half_u - width
    spec = (
        [(0, 0, up_cols, 0)],
        plane_spec([[(0, 0, width, rest, 0)], [(0, rest, 0, half_u, 0)]]) if halves else [],
    )
    act, slope, w_up = up_forward(at, own_u[1], spec, slots_u, count, two, up_b)
    if halves:
        act, d_four = after(act, d_four)
        slots_d = plane_slots(d_two, d_four)
    half = width // 2
    spec = ([(0, 0, width, 0)], plane_spec([[(0, 0, 0, half, 0)], [(0, half, 0, half, 0)]]) if halves else [])
    layer_out, gffn, sums3, ghid, up_sum = down_both(
        at, own_d, spec, slots_d, count, act, slope, down_b, mid, cot, live_col, gain, shift
    )

    if halves:
        send = grad_down(idx, act, gffn)
        got_down = swap(send, "dp", 1)
        send, ghid = after(send, ghid)
        send = grad_up(idx, two, ghid)
        got_up = swap(send, "dp", 1)
        send, got_down, act = tie((send, got_down, act))
        down_parts = grad_down(idx, act, gffn, got_down)
        down_got = plane_direct(down_parts)
        down_parts, ghid = after(down_parts, ghid)
    gmid, gmix, gatt, sums21 = mid_backward(ghid, w_up, w_out, mid, mixed, cot, live_col, gain)
    if halves:
        got_up, ghid, gmix, down_got[1:] = tie((got_up, ghid, gmix, down_got[1:]))
        up_parts = grad_up(idx, two, ghid, got_up)
        up_got = plane_direct(up_parts)
        up_parts, gatt = after(up_parts, gatt)
    back = functools.partial(attend_back, packed)
    share = (idx, normed_one) if halves else ()
    gq0, gk0, gv0, sq0, sv0, *shared0 = back(gatt, attended, lse, start_row, 0, 2, *share)
    if halves:
        gq0, gmix, down_got[0] = tie((gq0, gmix, down_got[0]))
        got0 = swap(shared0[0], "dp", 1)
        out_send, out_own = grad_out(idx, attended, gmix)
        out_got = swap(out_send, "dp", 1)
        out_send, gatt, up_got[1:] = tie((out_send, gatt, up_got[1:]))
    gq1, gk1, gv1, sq1, sv1, *shared1 = back(gatt, attended, lse, start_row, 1, 2, *share)
    if halves:
        up_got[0], gq1 = after(up_got[0], gq1)
        got1 = swap(shared1[0], "dp", 1)
        total = jnp.concatenate([plane_total(down_parts, down_got), plane_total(up_parts, up_got)])
        ffn_keep, ffn_send = across_first(total)
        ffn_got = swap(ffn_send, "fsdp", 1)
        ffn_keep, ffn_send, gq1, got0, out_got, got1 = tie((ffn_keep, ffn_send, gq1, got0, out_got, got1))
        heads_parts = head_sums([shared0[1], out_own, shared1[1]], [got0, out_got, got1])
        heads_got = plane_first(heads_parts)
        _, _, gq1 = tie((heads_parts[0], heads_parts[2], gq1))
    grads = [gq0, gq1, gk0, gk1, gv0, gv1]
    grad_input, sums0 = input_backward(grads, w_qkv, x, gmid, gain, 0, tokens // BLOCK)
    if halves:
        sums0, ffn_got = after(sums0, ffn_got)
        ffn_send = add_low(ffn_keep[:, 1], ffn_got[:, 1])
        ffn_keep = add_low(ffn_keep[:, 0], ffn_got[:, 0])
        ffn_got = swap(ffn_send, "fsdp", 2)
        ffn_send, ffn_keep, heads_got = tie((ffn_send, ffn_keep, heads_got))
        heads_keep, heads_send = plane_adds(heads_parts, heads_got)
        heads_got = [swap(part, "dp", mask) for part, mask in zip(heads_send, (2, 4))]
    small_grads = by_shard(
        [
            jnp.concatenate([jnp.concatenate([sq0, sq1], axis=1), jnp.concatenate([sv0, sv1], axis=1)]),
            sums21[4:5],
            up_sum,
            sums3[2:3],
            jnp.concatenate([sums0[0:1], sums21[2:3], sums21[0:1], sums3[0:1]]),
            jnp.concatenate([sums0[1:2], sums21[3:4], sums21[1:2], sums3[1:2]]),
        ],
        shards,
    )
    if halves:
        pairs_of = list(zip(heads_keep, heads_got))
        keep = [add_low(k[:, 0::2], g[:, 0::2]) for k, g in pairs_of]
        send = [add_low(k[:, 1::2], g[:, 1::2]).reshape(-1, width) for k, g in pairs_of]
        tail = small_grads.reshape(-1, width)
        more = tail.shape[0]
        got = swap(jnp.concatenate(send + [tail.astype(BF)]), "fsdp", 1)
        keep, ffn_got = after(keep, ffn_got)
        ffn_four = spread(add_low(ffn_keep, ffn_got))

        keep, got = tie((keep, got))
        tail = tail + got[-more:].astype(F32)
        each = keep[0].size // width
        pairs_of = [(k, got[f * each : (f + 1) * each].reshape(k.shape)) for f, k in enumerate(keep)]
        send = [add_low(k[:, 1], g[:, 1]).reshape(-1, width) for k, g in pairs_of]
        keep = [add_low(k[:, 0], g[:, 0]).reshape(-1, width) for k, g in pairs_of]
        got = swap(jnp.concatenate(send + [tail.astype(BF)]), "fsdp", 2)

        keep, got, ffn_four = tie((keep, got, ffn_four))
        tail = (tail + got[-more:].astype(F32)).astype(BF)
        piece = add_low(jnp.concatenate(keep), got[:-more])
        piece = jnp.concatenate([piece, tail])
        heads_got = [swap(piece, "dp", mask) for mask in (2, 4, 6)]
        ffn_all = spread_core(ffn_four)
        up_grad, down_grad = finish(
            "finish_ffn", idx, place_ffn, ffn_all, [up_weight.shape, down_weight.shape]
        )

        up_grad, heads_got = after(up_grad, heads_got)
        heads_four = jnp.stack([piece] + heads_got)
        heads_all = spread_core(heads_four)
        heads_core = heads_all[1][1]
        heads_all = [heads_all[0], (heads_all[1][0], heads_core)]
        tail = jnp.sum(heads_four[:, -more:].astype(F32), axis=0) + jnp.sum(
            heads_core[:, -more:].astype(F32), axis=0
        )
        small_sum = lax.dynamic_index_in_dim(
            tail.reshape(small_grads.shape), lax.axis_index("fsdp"), 0, keepdims=False
        )
        qkv_grad, out_grad = finish(
            "finish_heads", idx, place_heads, heads_all, [qkv_weight.shape, out_weight.shape]
        )
    else:
        gpacked = jnp.concatenate([gq0, gq1, gk0, gk1, gv0, gv1], axis=1)

        def reduced(left, right):
            grad = dot_tn(left, right)
            return lax.psum(lax.psum_scatter(grad, "fsdp", scatter_dimension=0, tiled=True), "dp")

        qkv_grad = reduced(normed_one, gpacked)
        out_grad = reduced(attended, gmix)
        up_grad = reduced(two, ghid)
        down_grad = reduced(act, gffn)
        small_sum = lax.dynamic_index_in_dim(
            lax.psum(small_grads, ("dp", "fsdp")), lax.axis_index("fsdp"), 0, keepdims=False
        )
    qv_g, outb_g, upb_g, downb_g, gain_g, shift_g = unpack_small(small_sum[None])
    return (
        layer_out[None],
        grad_input[None],
        qkv_grad,
        qv_g,
        out_grad,
        outb_g[0],
        up_grad,
        upb_g[0],
        down_grad,
        downb_g[0],
        gain_g,
        shift_g,
    )


def solution(mesh):
    rows = P(("dp", "fsdp"), None, None)
    split = P("fsdp", None)
    placed = (
        rows,
        split,
        P(None, "fsdp"),
        split,
        P("fsdp"),
        split,
        P("fsdp"),
        split,
        P("fsdp"),
        P(None, "fsdp"),
        P(None, "fsdp"),
        P(("dp", "fsdp"), None),
        rows,
    )
    return jax.shard_map(
        on_device,
        mesh=mesh,
        in_specs=placed,
        out_specs=(
            rows,
            rows,
            split,
            P(None, "fsdp"),
            split,
            P("fsdp"),
            split,
            P("fsdp"),
            split,
            P("fsdp"),
            P(None, "fsdp"),
            P(None, "fsdp"),
        ),
        check_vma=False,
    )
```

```python
import functools
import math

import jax
import jax.numpy as jnp
from jax import lax
from jax.experimental import pallas as pl
from jax.experimental.pallas import tpu as pltpu
from jax.sharding import PartitionSpec as P

F32 = jnp.float32
BF = jnp.bfloat16
SDS = jax.ShapeDtypeStruct
HEAD_DIM = 64
PAIR = 2 * HEAD_DIM
EPS = 1e-05
MASKED = -1e30
QUERY_SCALE = math.log2(math.e) / math.sqrt(HEAD_DIM)
GRAD_SCALE = 1.0 / math.sqrt(HEAD_DIM)
BLOCK = 256
UP_COLS = 1024
HIDDEN_COLS = 1024
GELU_A = math.sqrt(2.0 / math.pi)
GELU_B = 0.044715 * GELU_A


def params(mebibytes=60):
    return pltpu.CompilerParams(vmem_limit_bytes=mebibytes * 1024 * 1024)


def cost(flops, nbytes, trans=0):
    return pl.CostEstimate(flops=int(flops) // 1, bytes_accessed=int(nbytes) // 1, transcendentals=int(trans))


def dot_nn(a, b):
    return lax.dot_general(a, b, (((1,), (0,)), ((), ())), preferred_element_type=F32)


def dot_nt(a, b):
    return lax.dot_general(a, b, (((1,), (1,)), ((), ())), preferred_element_type=F32)


def dot_tn(a, b):
    return lax.dot_general(a, b, (((0,), (0,)), ((), ())), preferred_element_type=F32)


def centred(values):
    centre = values - jnp.mean(values, axis=-1, keepdims=True)
    rstd = lax.rsqrt(jnp.mean(centre * centre, axis=-1, keepdims=True) + EPS)
    return centre * rstd, rstd


def norm_back(grad, vhat, rstd, gain):
    e = grad * gain
    mean_e = jnp.mean(e, axis=-1, keepdims=True)
    mean_ev = jnp.mean(e * vhat, axis=-1, keepdims=True)
    return (e - mean_e - vhat * mean_ev) * rstd


def col_sum(values):
    return jnp.sum(values, axis=0, keepdims=True)


def piece_copies(spec, idx_ref, own_refs, slot_refs, places, sems):
    own_spec, slot_spec = spec
    dp, z = idx_ref[0], idx_ref[1]
    copies = []

    def add(group, src, dst):
        copies.append((group, pltpu.make_async_copy(src, dst, sems.at[len(copies)])))

    for o, first, cols, group in own_spec:
        rows = own_refs[o].shape[0]
        dst = places[o].at[pl.ds(pl.multiple_of(z * rows, rows), rows), first : first + cols]
        add(group, own_refs[o].at[:, first : first + cols], dst)
    for (pair, parts), ref in zip(slot_spec, slot_refs):
        rows = ref.shape[1]
        others = ref.shape[0] // 2
        for which, mask in enumerate(pair):
            for k in range(1, others + 1):
                at = which * others + k - 1
                for o, there, here, cols, group in parts:
                    dst = pl.multiple_of((z ^ k) * own_refs[o].shape[0] + (dp ^ mask) * rows, rows)
                    add(
                        group,
                        ref.at[at, :, here : here + cols],
                        places[o].at[pl.ds(dst, rows), there : there + cols],
                    )
    return copies


def count_copies(spec, slots):
    own_spec, slot_spec = spec
    return len(own_spec) + sum(len(parts) * s.shape[0] for (_, parts), s in zip(slot_spec, slots))


def start_all(copies):
    for _, copy in copies:
        copy.start()


def wait_group(copies, group):
    for g, copy in copies:
        if g == group:
            copy.wait()


def whole_shapes(owns, shards):
    return [(o.shape[0] * shards, o.shape[1]) for o in owns]


ANY = pl.BlockSpec(memory_space=pl.ANY)
SMEM = pl.BlockSpec(memory_space=pltpu.SMEM)


def qkv_kernel(spec, n_slots, idx_ref, own_ref, *refs):
    slots = refs[:n_slots]
    x_ref, bias_ref, gain_ref, shift_ref, normed_ref, packed_ref, out_ref = refs[n_slots : n_slots + 7]
    weight, sems, out_sem = refs[n_slots + 7 :]
    step, steps = pl.program_id(0), pl.num_programs(0)
    copies = piece_copies(spec, idx_ref, [own_ref], slots, [weight], sems)
    bn = packed_ref.shape[1]

    @pl.when(step == 0)
    def _():
        start_all(copies)
        vhat, _ = centred(x_ref[...].astype(F32))
        normed_ref[...] = (vhat * gain_ref[...] + shift_ref[...]).astype(BF)
        wait_group(copies, 0)

    half = weight.shape[1] // 2

    @pl.when(step == half // bn)
    def _():
        wait_group(copies, 1)
        pltpu.make_async_copy(weight, out_ref, out_sem).start()

    block = weight[:, pl.ds(pl.multiple_of(step * bn, bn), bn)]
    out = dot_nn(normed_ref[...], block) + bias_ref[...]
    packed_ref[...] = (out * jnp.where(step < steps // 3, QUERY_SCALE, 1.0)).astype(BF)

    @pl.when(step == steps - 1)
    def _():
        pltpu.make_async_copy(weight, out_ref, out_sem).wait()


def qkv_forward(idx, own, spec, slots, shards, x, bias, gain, shift):
    tokens, width = x.shape
    ((rows, cols),) = whole_shapes([own], shards)
    bn = width // 2
    row = pl.BlockSpec((1, width), lambda j: (0, 0))
    full = pl.BlockSpec((tokens, width), lambda j: (0, 0))
    return pl.pallas_call(
        functools.partial(qkv_kernel, spec, len(slots)),
        grid=(cols // bn,),
        in_specs=[SMEM] + [ANY] * (1 + len(slots))
        + [full, pl.BlockSpec((1, bn), lambda j: (0, j)), row, row],
        out_specs=(full, pl.BlockSpec((tokens, bn), lambda j: (0, j)), ANY),
        out_shape=(SDS((tokens, width), BF), SDS((tokens, cols), BF), SDS((rows, cols), BF)),
        scratch_shapes=[
            pltpu.VMEM((rows, cols), BF),
            pltpu.SemaphoreType.DMA((count_copies(spec, slots),)),
            pltpu.SemaphoreType.DMA(()),
        ],
        compiler_params=params(),
        cost_estimate=cost(2 * tokens * width * cols, 2 * width * cols + 2 * tokens * cols),
        name="qkv_forward",
    )(idx, own, *slots, x, bias, gain, shift)


def gelu_and_slope(a):
    sq = a * a
    t = jnp.tanh(a * (sq * GELU_B + GELU_A))
    half = 0.5 * t + 0.5
    act = a * half
    slope = half + act * ((1.0 - half) * (sq * (6.0 * GELU_B) + 2.0 * GELU_A))
    return act.astype(BF), slope.astype(BF)


def out_kernel(spec, n_slots, idx_ref, own_ref, *refs):
    slots = refs[:n_slots]
    att_ref, x_ref, bias_ref, gain_ref, shift_ref = refs[n_slots : n_slots + 5]
    mixed_ref, mid_ref, two_ref, save_ref, weight, sems, save_sem = refs[n_slots + 5 :]
    step, steps = pl.program_id(0), pl.num_programs(0)
    copies = piece_copies(spec, idx_ref, [own_ref], slots, [weight], sems)
    save = pltpu.make_async_copy(weight, save_ref, save_sem)

    @pl.when(step == 0)
    def _():
        start_all(copies)
        wait_group(copies, 0)
        save.start()

    mixed = dot_nn(att_ref[...], weight[...]) + bias_ref[...]
    mixed_ref[...] = mixed
    vhat, _ = centred(mixed)
    mid = x_ref[...].astype(F32) + vhat * gain_ref[1:2, :] + shift_ref[1:2, :]
    mid_ref[...] = mid
    vhat, _ = centred(mid)
    two_ref[...] = (vhat * gain_ref[2:3, :] + shift_ref[2:3, :]).astype(BF)

    @pl.when(step == steps - 1)
    def _():
        save.wait()


def out_forward(idx, own, spec, slots, shards, attended, x, bias, gain, shift):
    tokens, width = x.shape
    (shape,) = whole_shapes([own], shards)
    tok = pl.BlockSpec((BLOCK, width), lambda i: (i, 0))

    def whole(arr):
        return pl.BlockSpec(arr.shape, lambda i: (0, 0))

    return pl.pallas_call(
        functools.partial(out_kernel, spec, len(slots)),
        grid=(tokens // BLOCK,),
        in_specs=[SMEM] + [ANY] * (1 + len(slots)) + [tok, tok, whole(bias), whole(gain), whole(shift)],
        out_specs=(tok, tok, tok, ANY),
        out_shape=(
            SDS((tokens, width), F32),
            SDS((tokens, width), F32),
            SDS((tokens, width), BF),
            SDS(shape, BF),
        ),
        scratch_shapes=[
            pltpu.VMEM(shape, BF),
            pltpu.SemaphoreType.DMA((count_copies(spec, slots),)),
            pltpu.SemaphoreType.DMA(()),
        ],
        compiler_params=params(),
        cost_estimate=cost(2 * tokens * width * width, 16 * tokens * width),
        name="out_forward",
    )(idx, own, *slots, attended, x, bias, gain, shift)


def up_kernel(spec, n_slots, idx_ref, own_ref, *refs):
    slots = refs[:n_slots]
    two_ref, bias_ref, act_ref, slope_ref, save_ref, weight, sems, save_sem = refs[n_slots:]
    step, steps = pl.program_id(0), pl.num_programs(0)
    copies = piece_copies(spec, idx_ref, [own_ref], slots, [weight], sems)
    save = pltpu.make_async_copy(weight, save_ref, save_sem)

    @pl.when(step == 0)
    def _():
        start_all(copies)
        wait_group(copies, 0)
        save.start()

    bn = act_ref.shape[1]
    at = pl.ds(pl.multiple_of(step * bn, bn), bn)
    a = dot_nn(two_ref[...], weight[:, at]) + bias_ref[...]
    act_ref[...], slope_ref[...] = gelu_and_slope(a)

    @pl.when(step == steps - 1)
    def _():
        save.wait()


def up_forward(idx, own, spec, slots, shards, two, bias):
    tokens, width = two.shape
    (shape,) = whole_shapes([own], shards)
    cols = shape[1]
    bn = UP_COLS
    col = pl.BlockSpec((tokens, bn), lambda i: (0, i))
    return pl.pallas_call(
        functools.partial(up_kernel, spec, len(slots)),
        grid=(cols // bn,),
        in_specs=[SMEM] + [ANY] * (1 + len(slots))
        + [pl.BlockSpec((tokens, width), lambda i: (0, 0)), pl.BlockSpec((1, bn), lambda i: (0, i))],
        out_specs=(col, col, ANY),
        out_shape=(SDS((tokens, cols), BF), SDS((tokens, cols), BF), SDS(shape, BF)),
        scratch_shapes=[
            pltpu.VMEM(shape, BF),
            pltpu.SemaphoreType.DMA((count_copies(spec, slots),)),
            pltpu.SemaphoreType.DMA(()),
        ],
        compiler_params=params(),
        cost_estimate=cost(2 * tokens * width * cols, 2 * width * cols + 4 * tokens * cols),
        name="up_forward",
    )(idx, own, *slots, two, bias)


def down_kernel(spec, n_slots, first, idx_ref, own_ref, *refs):
    slots = refs[:n_slots]
    act_ref, slope_ref, bias_ref, mid_ref, cot_ref, live_ref, gain_ref, shift_ref = refs[n_slots : n_slots + 8]
    out_ref, grad_ref, sums_ref, hid_ref, hsum_ref, weight, sems = refs[n_slots + 8 :]
    step = pl.program_id(0)
    copies = piece_copies(spec, idx_ref, [own_ref], slots, [weight], sems)

    @pl.when(step == 0)
    def _():
        start_all(copies)
        sums_ref[...] = jnp.zeros_like(sums_ref)
        wait_group(copies, 0)

    @pl.when(step < first)
    def _():
        ffn = dot_nn(act_ref[...], weight[...]) + bias_ref[...]
        vhat, rstd = centred(ffn)
        gain = gain_ref[3:4, :]
        out_ref[...] = (mid_ref[...] + vhat * gain + shift_ref[3:4, :]).astype(BF)
        grad = cot_ref[...].astype(F32) * live_ref[...]
        low = norm_back(grad, vhat, rstd, gain).astype(BF)
        grad_ref[pl.ds(pl.multiple_of(step * BLOCK, BLOCK), BLOCK), :] = low
        sums_ref[0:1, :] += col_sum(grad * vhat)
        sums_ref[1:2, :] += col_sum(grad)
        sums_ref[2:3, :] += col_sum(low.astype(F32))

    @pl.when(step >= first)
    def _():
        bn = hid_ref.shape[1]
        at = pl.ds(pl.multiple_of((step - first) * bn, bn), bn)
        low = (dot_nt(grad_ref[...], weight[at, :]) * slope_ref[...].astype(F32)).astype(BF)
        hid_ref[...] = low
        hsum_ref[...] = col_sum(low.astype(F32))


def down_both(idx, own, spec, slots, shards, act, slope, bias, mid, cot, live, gain, shift):
    tokens, width = mid.shape
    (shape,) = whole_shapes([own], shards)
    cols = shape[0]
    bn = HIDDEN_COLS
    first = tokens // BLOCK

    def at(i):
        return jnp.minimum(i, first - 1)

    tok = pl.BlockSpec((BLOCK, width), lambda i: (at(i), 0))
    col = pl.BlockSpec((tokens, bn), lambda i: (0, jnp.maximum(i - first, 0)))

    def whole(arr):
        return pl.BlockSpec(arr.shape, lambda i: (0, 0))

    return pl.pallas_call(
        functools.partial(down_kernel, spec, len(slots), first),
        grid=(first + cols // bn,),
        in_specs=[SMEM] + [ANY] * (1 + len(slots))
        + [
            pl.BlockSpec((BLOCK, cols), lambda i: (at(i), 0)),
            col,
            whole(bias),
            tok,
            tok,
            pl.BlockSpec((BLOCK, 1), lambda i: (at(i), 0)),
            whole(gain),
            whole(shift),
        ],
        out_specs=(
            tok,
            pl.BlockSpec((tokens, width), lambda i: (0, 0)),
            pl.BlockSpec((8, width), lambda i: (0, 0)),
            col,
            pl.BlockSpec((1, bn), lambda i: (0, jnp.maximum(i - first, 0))),
        ),
        out_shape=(
            SDS((tokens, width), BF),
            SDS((tokens, width), BF),
            SDS((8, width), F32),
            SDS((tokens, cols), BF),
            SDS((1, cols), F32),
        ),
        scratch_shapes=[pltpu.VMEM(shape, BF), pltpu.SemaphoreType.DMA((count_copies(spec, slots),))],
        compiler_params=params(),
        cost_estimate=cost(4 * tokens * width * cols, 2 * width * cols + 6 * tokens * cols),
        name="down_both",
    )(idx, own, *slots, act, slope, bias, mid, cot, live, gain, shift)


def mid_kernel(
    gh_ref, up_ref, out_w_ref, mid_ref, mixed_ref, cot_ref, live_ref, gain_ref,
    gmid_ref, gmix_ref, gatt_ref, sums_ref,
):
    @pl.when(pl.program_id(0) == 0)
    def _():
        sums_ref[...] = jnp.zeros_like(sums_ref)

    grad = dot_nt(gh_ref[...], up_ref[...])
    vhat, rstd = centred(mid_ref[...])
    sums_ref[0:1, :] += col_sum(grad * vhat)
    sums_ref[1:2, :] += col_sum(grad)
    gmid = cot_ref[...].astype(F32) * live_ref[...] + norm_back(grad, vhat, rstd, gain_ref[2:3, :])
    gmid_ref[...] = gmid
    vhat, rstd = centred(mixed_ref[...])
    sums_ref[2:3, :] += col_sum(gmid * vhat)
    sums_ref[3:4, :] += col_sum(gmid)
    low = norm_back(gmid, vhat, rstd, gain_ref[1:2, :]).astype(BF)
    gmix_ref[...] = low
    sums_ref[4:5, :] += col_sum(low.astype(F32))
    gatt_ref[...] = dot_nt(low, out_w_ref[...]).astype(BF)


def mid_backward(gh, up, out_w, mid, mixed, cot, live, gain):
    tokens, width = mid.shape
    cols = gh.shape[1]
    tok = pl.BlockSpec((BLOCK, width), lambda i: (i, 0))

    def whole(arr):
        return pl.BlockSpec(arr.shape, lambda i: (0, 0))

    return pl.pallas_call(
        mid_kernel,
        grid=(tokens // BLOCK,),
        in_specs=[
            pl.BlockSpec((BLOCK, cols), lambda i: (i, 0)),
            whole(up),
            whole(out_w),
            tok,
            tok,
            tok,
            pl.BlockSpec((BLOCK, 1), lambda i: (i, 0)),
            whole(gain),
        ],
        out_specs=(tok, tok, tok, pl.BlockSpec((8, width), lambda i: (0, 0))),
        out_shape=(
            SDS((tokens, width), F32),
            SDS((tokens, width), BF),
            SDS((tokens, width), BF),
            SDS((8, width), F32),
        ),
        compiler_params=params(),
        cost_estimate=cost(2 * tokens * width * (cols + width), 2 * width * cols + 2 * tokens * cols),
        name="mid_backward",
    )(gh, up, out_w, mid, mixed, cot, live, gain)


def input_kernel(n_grads, n_into, *refs):
    grad_refs, (w_ref, x_ref, gmid_ref, gain_ref) = refs[:n_grads], refs[n_grads : n_grads + 4]
    out_ref, sums_ref = refs[n_grads + 4 + n_into :]

    @pl.when(pl.program_id(0) == 0)
    def _():
        sums_ref[...] = jnp.zeros_like(sums_ref)

    grads = jnp.concatenate([ref[...] for ref in grad_refs], axis=1)
    grad = dot_nt(grads, w_ref[...])
    vhat, rstd = centred(x_ref[...].astype(F32))
    sums_ref[0:1, :] += col_sum(grad * vhat)
    sums_ref[1:2, :] += col_sum(grad)
    out_ref[...] = gmid_ref[...] + norm_back(grad, vhat, rstd, gain_ref[0:1, :])


def input_backward(grads, weight, x, gmid, gain, first, count, into=None):
    tokens, width = x.shape
    tok = pl.BlockSpec((BLOCK, width), lambda i: (first + i, 0))

    def whole(arr):
        return pl.BlockSpec(arr.shape, lambda i: (0, 0))

    in_specs = [pl.BlockSpec((BLOCK, g.shape[1]), lambda i: (first + i, 0)) for g in grads]
    in_specs += [whole(weight), tok, tok, whole(gain)]
    args = [*grads, weight, x, gmid, gain]
    aliases = {}
    if into is not None:
        aliases = {len(args): 0}
        in_specs.append(pl.BlockSpec(memory_space=pl.ANY))
        args.append(into)
    return pl.pallas_call(
        functools.partial(input_kernel, len(grads), len(aliases)),
        grid=(count,),
        in_specs=in_specs,
        out_specs=(tok, pl.BlockSpec((8, width), lambda i: (0, 0))),
        out_shape=(SDS((tokens, width), F32), SDS((8, width), F32)),
        input_output_aliases=aliases,
        compiler_params=params(),
        cost_estimate=cost(6 * count * BLOCK * width * width, 6 * width * width),
        name="input_backward",
    )(*args)


def fill_bias(bias, start_ref):
    length = bias.shape[0]
    for j in range(length // BLOCK):
        key = lax.broadcasted_iota(jnp.int32, (BLOCK, length), 0) + j * BLOCK
        query = lax.broadcasted_iota(jnp.int32, (BLOCK, length), 1)
        allowed = (key <= query) & (key >= start_ref[...])
        bias[j * BLOCK : (j + 1) * BLOCK, :] = jnp.where(allowed, 0.0, MASKED)


def one_head(low, arr, head):
    zero = jnp.zeros_like(arr)
    return jnp.where(low, arr, zero) if head == 0 else jnp.where(low, zero, arr)


def attend_kernel(q_ref, k_ref, v_ref, start_ref, out_ref, lse_ref, bias):
    length = q_ref.shape[0]

    @pl.when(pl.program_id(0) == 0)
    def _():
        fill_bias(bias, start_ref)

    low = lax.broadcasted_iota(jnp.int32, (1, PAIR), 1) < HEAD_DIM
    low_rows = lax.broadcasted_iota(jnp.int32, (PAIR, 1), 0) < HEAD_DIM
    keys = k_ref[...]
    values = jnp.concatenate([v_ref[...], jnp.ones((length, PAIR), BF)], axis=1)
    for i in range(length // BLOCK):
        reach = (i + 1) * BLOCK
        sl = slice(i * BLOCK, reach)
        queries = q_ref[sl, :]
        parts = []
        for head in range(2):
            scores = dot_nt(keys[:reach], one_head(low, queries, head)) + bias[:reach, sl]
            top = jnp.max(scores, axis=0, keepdims=True)
            probs = jnp.exp2(scores - top).astype(BF)
            mixed = dot_tn(values[:reach], probs)
            total = mixed[PAIR : PAIR + 1]
            parts.append(mixed[:PAIR] / total)
            lse_ref[0, head : head + 1, sl] = top + jnp.log2(total)
        out_ref[sl, :] = jnp.where(low_rows, parts[0], parts[1]).T.astype(BF)


def attend(packed, start_row, first, count, into=None):
    length = packed.shape[0]
    pairs = packed.shape[1] // (3 * PAIR)

    def blk(offset):
        return pl.BlockSpec((length, PAIR), lambda h: (0, offset + first + h))

    in_specs = [blk(0), blk(pairs), blk(2 * pairs), pl.BlockSpec((1, length), lambda h: (0, 0))]
    args = [packed, packed, packed, start_row]
    kernel, aliases = attend_kernel, {}
    if into is not None:
        in_specs = in_specs + [ANY] * len(into)
        aliases = {len(args) + i: i for i in range(len(into))}
        args = args + list(into)

        def kernel(*refs):
            attend_kernel(*refs[:4], *refs[4 + len(into) :])

    return pl.pallas_call(
        kernel,
        grid=(count,),
        in_specs=in_specs,
        out_specs=(blk(0), pl.BlockSpec((1, 2, length), lambda h: (first + h, 0, 0))),
        out_shape=(SDS((length, PAIR * pairs), BF), SDS((pairs, 2, length), F32)),
        input_output_aliases=aliases,
        scratch_shapes=[pltpu.VMEM((length, length), F32)],
        compiler_params=params(),
        cost_estimate=cost(8 * count * length * length * PAIR, 8 * length * count * PAIR),
        name="attend",
    )(*args)


def share_out(wide, idx_ref, send_ref, own_ref):
    core, z = idx_ref[0] & 1, idx_ref[1]
    rows = wide.shape[0] // 8
    for zz in range(4):
        for ref, c in ((send_ref, core ^ 1), (own_ref, core)):
            at = pl.ds(pl.multiple_of((2 * zz + c) * rows, rows), rows)
            part = wide[at, :].astype(BF)
            ref[0, 0, zz ^ z, 0] = part[: rows // 2]
            ref[0, 0, zz ^ z, 1] = part[rows // 2 :]


def attend_back_kernel(shared, *refs):
    if shared:
        idx_ref, one_ref, refs = refs[0], refs[1], refs[2:]
        send_ref, own_ref, wide = refs[12], refs[13], refs[16]
        refs = refs[:12] + refs[14:16]
    q_ref, k_ref, v_ref, g_ref, o_ref, lse_ref, start_ref = refs[:7]
    gq_ref, gk_ref, gv_ref, sq_ref, sv_ref, bias, acc = refs[7:]
    length = q_ref.shape[0]

    @pl.when(pl.program_id(0) == 0)
    def _():
        fill_bias(bias, start_ref)

    low = lax.broadcasted_iota(jnp.int32, (1, PAIR), 1) < HEAD_DIM
    queries, grads = q_ref[...], g_ref[...]
    q_of = [one_head(low, queries, head) for head in range(2)]
    g_of = [one_head(low, grads, head) for head in range(2)]
    inner = (grads.astype(F32) * o_ref[...].astype(F32)).T
    inner_of = [col_sum(inner[:HEAD_DIM]), col_sum(inner[HEAD_DIM:])]
    sum_v = jnp.zeros((1, PAIR), F32)
    for j in range(length // BLOCK):
        first = j * BLOCK
        sl = slice(first, first + BLOCK)
        keys, values = k_ref[sl, :], v_ref[sl, :]
        gk = gv = gq = 0.0
        for head in range(2):
            scores = dot_nt(keys, q_of[head][first:]) + bias[sl, first:]
            probs = jnp.exp2(scores - lse_ref[0, head : head + 1, first:])
            gprobs = dot_nt(values, g_of[head][first:])
            gscores = (probs * (gprobs - inner_of[head][:, first:]) * GRAD_SCALE).astype(BF)
            gv = gv + dot_nn(probs.astype(BF), g_of[head][first:])
            gk = gk + dot_nn(gscores, q_of[head][first:])
            gq = gq + dot_tn(gscores, one_head(low, keys, head))
        low_v = gv.astype(BF)
        gv_ref[sl, :] = low_v
        gk_ref[sl, :] = (gk * (1.0 / QUERY_SCALE)).astype(BF)
        sum_v = sum_v + col_sum(low_v.astype(F32))
        if j == 0:
            acc[...] = gq
        else:
            acc[first:, :] += gq
    low_q = acc[...].astype(BF)
    gq_ref[...] = low_q
    sq_ref[...] = col_sum(low_q.astype(F32))
    sv_ref[...] = sum_v
    if shared:
        grads = jnp.concatenate([low_q, gk_ref[...], gv_ref[...]], axis=1)
        wide[...] = dot_tn(one_ref[...], grads)
        share_out(wide, idx_ref, send_ref, own_ref)


def attend_back(packed, grads, attended, lse, start_row, part, parts, idx=None, one=None):
    length = packed.shape[0]
    total = packed.shape[1] // (3 * PAIR)
    count = total // parts
    first = part * count
    shared = one is not None

    def blk(offset):
        return pl.BlockSpec((length, PAIR), lambda h, *_: (0, offset + h))

    row = pl.BlockSpec((1, PAIR), lambda h, *_: (0, h))
    grad = SDS((length, PAIR * count), BF)
    sums = SDS((1, PAIR * count), F32)
    in_specs = [
        blk(first),
        blk(total + first),
        blk(2 * total + first),
        blk(first),
        blk(first),
        pl.BlockSpec((1, 2, length), lambda h, *_: (first + h, 0, 0)),
        pl.BlockSpec((1, length), lambda h, *_: (0, 0)),
    ]
    args = [packed, packed, packed, grads, attended, lse, start_row]
    out_specs = [blk(0), blk(0), blk(0), row, row]
    out_shape = [grad, grad, grad, sums, sums]
    scratch = [pltpu.VMEM((length, length), F32), pltpu.VMEM((length, PAIR), F32)]
    if shared:
        width = one.shape[1]
        piece = (4, 2, width // 16, 3 * PAIR)
        block = pl.BlockSpec((1, 1) + piece, lambda h, idx: (3 ^ h ^ (idx[0] // 2), 0, 0, 0, 0, 0))
        in_specs = [pl.BlockSpec(one.shape, lambda h, *_: (0, 0))] + in_specs
        args = [idx, one] + args
        out_specs = out_specs + [block, block]
        out_shape = out_shape + [SDS((4, 1) + piece, BF)] * 2
        scratch = scratch + [pltpu.VMEM((width, 3 * PAIR), F32)]
    return pl.pallas_call(
        functools.partial(attend_back_kernel, shared),
        grid_spec=pltpu.PrefetchScalarGridSpec(
            num_scalar_prefetch=int(shared),
            grid=(count,),
            in_specs=in_specs,
            out_specs=tuple(out_specs),
            scratch_shapes=scratch,
        ),
        out_shape=tuple(out_shape),
        compiler_params=params(),
        cost_estimate=cost(20 * count * length * length * PAIR, 16 * length * count * PAIR),
        name="attend_back",
    )(*args)


def swap(arr, axis, mask):
    size = lax.axis_size(axis)
    return lax.ppermute(arr, axis, [(i, i ^ mask) for i in range(size)])


def after(first, then):
    return lax.optimization_barrier((first, then))


def shard_swaps(piece):
    return [swap(piece, "fsdp", k) for k in range(1, lax.axis_size("fsdp"))]


def shard_pair(piece, got):
    return swap(jnp.stack([piece, got]), "fsdp", 1)


def shard_slots(got, pair):
    return [pair[0], got, pair[1]]


PLANE_MASKS = [
    (0, 4), (2, 6), (1, 5), (3, 7),
    (0, 2), (4, 6), (1, 3), (5, 7),
]


def plane_slots(two, four):
    return [a for t, f in zip(two, four) for a in (t, f, swap(t, "dp", 1), swap(f, "dp", 1))]


def plane_spec(parts):
    return [(pair, parts[i // 4]) for i, pair in enumerate(PLANE_MASKS)]


def split_down(wide, zz):
    rows, cols = wide.shape[0] // 4, wide.shape[1] // 2
    part = wide[zz * rows : (zz + 1) * rows]
    return part[:, :cols], part[:, cols:]


def split_up(wide, zz):
    rows = wide.shape[0] // 8
    return wide[2 * zz * rows : (2 * zz + 1) * rows], wide[(2 * zz + 1) * rows : (2 * zz + 2) * rows]


def side_by_side(refs):
    blocks = [r[...] for r in refs]
    return blocks[0] if len(blocks) == 1 else jnp.concatenate(blocks, axis=1)


def emit(keep, direct, wide, split, z, chip, rest):
    if not keep:
        for zz in range(4):
            for f, part in enumerate(split(wide, zz)):
                rest[0][0, 0, zz ^ z, f] = part.astype(BF)
        return
    got_ref, outs = rest[0], rest[1:]
    for dst in range(4):

        @pl.when(chip == dst)
        def _():
            for zz in range(4):
                slot = zz ^ z
                for f, part in enumerate(split(wide, zz)):
                    low = (part + got_ref[0, 0, slot, f].astype(F32)).astype(BF)
                    if direct:
                        outs[dst][0, slot, f] = low
                    else:
                        bit = dst // 2 if f == 0 else dst % 2
                        outs[2 * f + bit][0, 0, slot] = low


def grad_kernel(keep, direct, jobs, idx_ref, *refs):
    step, z = pl.program_id(0), idx_ref[1]
    at = 0
    n_in = sum(n for groups, _ in jobs for group in groups for n in group)
    rest = refs[n_in:]
    for number, (groups, split) in enumerate(jobs):
        blocks = []
        for n_left, n_right in groups:
            blocks.append((refs[at : at + n_left], refs[at + n_left : at + n_left + n_right]))
            at += n_left + n_right

        @pl.when(step // 4 == number)
        def _():
            dots = [dot_tn(side_by_side(left), side_by_side(right)) for left, right in blocks]
            wide = dots[0] if len(dots) == 1 else jnp.concatenate(dots, axis=1)
            emit(keep, direct, wide, split, z, step % 4, rest)


def grad_call(name, idx, specs, args, jobs, piece, flops, got=None, direct=True):
    keep = got is not None
    n_jobs = len(jobs)
    rows, cols = piece
    block = pl.BlockSpec((1, 1, 4, 2, rows, cols), lambda i, idx: (i % 4, i // 4, 0, 0, 0, 0))
    half = (1, 1, 4, rows, cols)
    if keep and direct:
        specs = specs + [block]
        args = args + [got]
        out_specs = (pl.BlockSpec((1, 4, 2, rows, cols), lambda i, idx: (0, 0, 0, 0, 0)),) * 4
        out_shape = (SDS((1, 4, 2, rows, cols), BF),) * 4
    elif keep:
        along_y = (
            lambda i, idx: (jnp.minimum(i % 4, 1), i // 4, 0, 0, 0),
            lambda i, idx: (jnp.maximum(i % 4 - 2, 0), i // 4, 0, 0, 0),
        )
        along_x = (lambda i, idx: (i % 4 // 2, i // 4, 0, 0, 0),) * 2
        specs = specs + [block]
        args = args + [got]
        out_specs = tuple(pl.BlockSpec(half, m) for m in along_y + along_x)
        out_shape = (SDS((2, n_jobs, 4, rows, cols), BF),) * 4
    else:
        out_specs = block
        out_shape = SDS((4, n_jobs, 4, 2, rows, cols), BF)
    return pl.pallas_call(
        functools.partial(grad_kernel, keep, direct, jobs),
        grid_spec=pltpu.PrefetchScalarGridSpec(
            num_scalar_prefetch=1, grid=(4 * n_jobs,), in_specs=specs, out_specs=out_specs
        ),
        out_shape=out_shape,
        compiler_params=params(),
        cost_estimate=cost(flops, flops // 400),
        name=name + ("_keep" if keep else "_send"),
    )(idx, *args)


def chip_of(i, idx):
    return (idx[0] // 2) ^ (3 - i)


def core_of(keep, idx):
    return idx[0] & 1 if keep else (idx[0] & 1) ^ 1


def grad_down(idx, act, gffn, got=None):
    tokens, width = gffn.shape
    keep = got is not None
    rows = act.shape[1] // 32

    def act_spec(zz):
        def at(i, idx):
            return (0, zz * 8 + chip_of(i, idx) * 2 + core_of(keep, idx))

        return pl.BlockSpec((tokens, rows), at)

    specs = [act_spec(0), act_spec(1), act_spec(2), act_spec(3)]
    specs += [pl.BlockSpec((tokens, width), lambda i, idx: (0, 0))]
    args = [act, act, act, act, gffn]
    flops = act.shape[1] * width * tokens
    jobs = [([(4, 1)], split_down)]
    return grad_call("grad_down", idx, specs, args, jobs, (rows, width // 2), flops, got)


def grad_up(idx, two, ghid, got=None):
    tokens, width = two.shape
    keep = got is not None
    cols = ghid.shape[1] // 8
    specs = [
        pl.BlockSpec((tokens, width), lambda i, idx: (0, 0)),
        pl.BlockSpec((tokens, cols), lambda i, idx: (0, chip_of(i, idx) * 2 + core_of(keep, idx))),
    ]
    flops = ghid.shape[1] * width * tokens
    jobs = [([(1, 1)], split_up)]
    return grad_call("grad_up", idx, specs, [two, ghid], jobs, (width // 8, cols), flops, got)


def grad_out_kernel(idx_ref, att_ref, gmix_ref, send_ref, own_ref, wide):
    wide[...] = dot_tn(att_ref[...], gmix_ref[...])
    share_out(wide, idx_ref, send_ref, own_ref)


def grad_out(idx, att, gmix):
    tokens, width = att.shape
    cols = width // 4
    piece = (4, 2, width // 16, cols)
    block = pl.BlockSpec((1, 1) + piece, lambda i, idx: (i, 0, 0, 0, 0, 0))
    return pl.pallas_call(
        grad_out_kernel,
        grid_spec=pltpu.PrefetchScalarGridSpec(
            num_scalar_prefetch=1,
            grid=(4,),
            in_specs=[
                pl.BlockSpec((tokens, width), lambda i, idx: (0, 0)),
                pl.BlockSpec((tokens, cols), lambda i, idx: (0, chip_of(i, idx))),
            ],
            out_specs=(block, block),
            scratch_shapes=[pltpu.VMEM((width, cols), F32)],
        ),
        out_shape=(SDS((4, 1) + piece, BF),) * 2,
        compiler_params=params(),
        cost_estimate=cost(2 * tokens * width * width, 8 * tokens * width),
        name="grad_out",
    )(idx, att, gmix)


def head_sums_kernel(n, *refs):
    owns, gots, outs = refs[:n], refs[n : 2 * n], refs[2 * n :]
    for dst in range(4):

        @pl.when(pl.program_id(0) == dst)
        def _():
            for f in range(2):
                parts = [o[0, 0, :, f].astype(F32) + g[0, 0, :, f].astype(F32) for o, g in zip(owns, gots)]
                bit = dst // 2 if f == 0 else dst % 2
                outs[2 * f + bit][0, 0] = jnp.concatenate(parts, axis=-1).astype(BF)


def head_sums(owns, gots):
    _, _, slots, _, rows, _ = owns[0].shape
    cols = sum(o.shape[-1] for o in owns)
    half = (1, 1, slots, rows, cols)
    along_y = (lambda i: (jnp.minimum(i, 1), 0, 0, 0, 0), lambda i: (jnp.maximum(i - 2, 0), 0, 0, 0, 0))
    along_x = (lambda i: (i // 2, 0, 0, 0, 0),) * 2
    return pl.pallas_call(
        functools.partial(head_sums_kernel, len(owns)),
        grid=(4,),
        in_specs=[pl.BlockSpec((1,) + a.shape[1:], lambda i: (i, 0, 0, 0, 0, 0)) for a in owns + gots],
        out_specs=tuple(pl.BlockSpec(half, m) for m in along_y + along_x),
        out_shape=(SDS((2, 1, slots, rows, cols), BF),) * 4,
        compiler_params=params(),
        cost_estimate=cost(0, 48 * slots * rows * cols),
        name="head_sums",
    )(*owns, *gots)


def add_low(a, b):
    return (a.astype(F32) + b.astype(F32)).astype(BF)


def add_wide(a, b):
    return a.astype(F32) + b.astype(F32)


def plane_first(parts):
    return [swap(parts[2 * f], "dp", mask) for f, mask in enumerate((4, 2))]


def plane_adds(parts, got):
    send = [add_low(parts[2 * f + 1][0], got[f][0]) for f in range(2)]
    keep = [add_low(parts[2 * f + 1][1], got[f][1]) for f in range(2)]
    return keep, send


def plane_second(parts, got):
    keep, send = plane_adds(parts, got)
    return keep, [swap(s, "dp", mask) for s, mask in zip(send, (2, 4))]


def plane_direct(parts):
    return [swap(part, "dp", mask) for part, mask in zip(parts, (6, 4, 2))]


def plane_total(parts, got):
    return add_wide(parts[3], got[0]) + add_wide(got[1], got[2])


def across_first(both):
    return both[:, 0::2].astype(BF), both[:, 1::2].astype(BF)


def spread(piece):
    four = jnp.stack([piece] + [swap(piece, "dp", mask) for mask in (2, 4, 6)])
    return four


def spread_core(four):
    return [((0, 2, 4, 6), four), ((1, 3, 5, 7), swap(four, "dp", 1))]


def place_ffn(dp, piece, outs):
    up_grad, down_grad = outs
    rows, cols = piece.shape[2], piece.shape[3]
    at = pl.ds(pl.multiple_of(dp * rows, rows), rows)
    down_grad[at, :cols] = piece[0, 0].astype(F32)
    down_grad[at, cols:] = piece[0, 1].astype(F32)
    at = pl.ds(pl.multiple_of(dp * cols, cols), cols)
    up_grad[:rows, at] = piece[1, 0].astype(F32)
    up_grad[rows:, at] = piece[1, 1].astype(F32)


def place_heads(dp, piece, outs):
    qkv_grad, out_grad = outs
    width = out_grad.shape[1]
    rows, cols = out_grad.shape[0] // 2, width // 4
    chip, core = dp // 2, dp % 2
    at_rows = pl.ds(pl.multiple_of(core * rows, rows), rows)
    part_of = piece[:rows].astype(F32)
    for half, skip in ((0, 0), (1, 3 * PAIR + cols)):
        for part in range(3):
            at = pl.multiple_of(part * width + half * (width // 2) + chip * PAIR, PAIR)
            here = skip + part * PAIR
            qkv_grad[at_rows, pl.ds(at, PAIR)] = part_of[:, here : here + PAIR]
    at = pl.multiple_of(chip * cols, cols)
    out_grad[at_rows, pl.ds(at, cols)] = part_of[:, 3 * PAIR : 3 * PAIR + cols]


def finish_kernel(placer, masks, idx_ref, *refs):
    ins, outs = refs[: len(masks)], refs[len(masks) :]
    for group, ref in zip(masks, ins):
        for which, mask in enumerate(group):
            placer(idx_ref[0] ^ mask, ref[which], outs)


def finish(name, idx, placer, flow, shapes):
    masks = [m for m, _ in flow]
    arrays = [a for _, a in flow]
    vmem = pl.BlockSpec(memory_space=pltpu.VMEM)
    return pl.pallas_call(
        functools.partial(finish_kernel, placer, masks),
        in_specs=[SMEM] + [vmem] * len(arrays),
        out_specs=(vmem,) * len(shapes),
        out_shape=tuple(SDS(s, F32) for s in shapes),
        compiler_params=params(32),
        cost_estimate=cost(0, sum(6 * math.prod(s) for s in shapes)),
        name=name,
    )(idx, *arrays)


def segment_starts(lengths, length):
    ends = jnp.cumsum(lengths)
    positions = jnp.arange(length, dtype=jnp.int32)
    begun = jnp.where(ends[None, :] <= positions[:, None], ends[None, :], 0)
    return jnp.max(begun, axis=1).astype(jnp.int32), positions < ends[-1]


def eighth(shard):
    rows = shard.shape[0] // 8
    return lax.dynamic_slice_in_dim(shard, lax.axis_index("dp") * rows, rows, axis=0)


SMALL_ROWS = 16


def pack_small(qv_bias, out_bias, up_bias, down_bias, gain, shift):
    flat = [a.reshape(-1) for a in (qv_bias, out_bias, up_bias, down_bias, gain, shift)]
    return jnp.concatenate(flat)


def unpack_small(shards):
    count, total = shards.shape
    unit = total // SMALL_ROWS
    sizes = ((2, unit), (1, unit), (1, 4 * unit), (1, unit), (4, unit), (4, unit))
    out, at = [], 0
    for lead, cols in sizes:
        block = shards[:, at : at + lead * cols].reshape(count, lead, cols)
        out.append(jnp.swapaxes(block, 0, 1).reshape(lead, count * cols))
        at += lead * cols
    return out


def by_shard(rows, count):
    flat = []
    for arr in rows:
        lead, cols = arr.shape
        flat.append(
            jnp.swapaxes(arr.reshape(lead, count, cols // count), 0, 1).reshape(count, -1)
        )
    return jnp.concatenate(flat, axis=1)


def gather_small(own, got):
    z = lax.axis_index("fsdp")
    slots = jnp.stack([own] + got)
    low, high = z % 2, z // 2
    slots = jnp.where(low == 0, slots, slots[jnp.array([1, 0, 3, 2])])
    return jnp.where(high == 0, slots, slots[jnp.array([2, 3, 0, 1])])


def on_device(
    layer_input,
    qkv_weight,
    query_value_bias,
    out_weight,
    out_bias,
    up_weight,
    up_bias,
    down_weight,
    down_bias,
    norm_gain,
    norm_shift,
    doc_lengths,
    cotangent,
):
    _, tokens, width = layer_input.shape
    shards = lax.axis_size("fsdp")
    halves = shards == 4 and lax.axis_size("dp") == 8
    idx = jnp.stack([lax.axis_index("dp"), lax.axis_index("fsdp")]).astype(jnp.int32)
    x = layer_input[0]
    cot = cotangent[0]
    start, live = segment_starts(doc_lengths[0], tokens)
    start_row = start[None, :]
    live_col = live.astype(F32)[:, None]
    small_own = pack_small(query_value_bias, out_bias, up_bias, down_bias, norm_gain, norm_shift)
    tie = lax.optimization_barrier
    both = (4, 2)
    if halves:
        piece = eighth(qkv_weight)
        cols = piece.shape[1]
        extra = small_own.reshape(piece.shape[0], -1)
        got = shard_swaps(jnp.concatenate([piece, extra], axis=1))
        small = gather_small(small_own, [g[:, cols:].reshape(-1) for g in got])
        half_q = cols // 2
        q_own = [jnp.stack([g[:, :half_q] for g in got]), jnp.stack([g[:, half_q:cols] for g in got])]
        q_own, piece_u = after(q_own, jnp.concatenate([eighth(out_weight), eighth(up_weight)], axis=1))
        q_got = [swap(o, "dp", m) for o, m in zip(q_own, both)]
        got_u = swap(piece_u, "fsdp", 2)
        q_two = [jnp.concatenate([o, g]) for o, g in zip(q_own, q_got)]
        q_four = [swap(t, "dp", 6 - m) for t, m in zip(q_two, both)]
        slots_q = plane_slots(q_two, q_four)
        q_four, got_u = after(q_four, got_u)
        half_u = piece_u.shape[1] // 2
        pair_u = shard_pair(piece_u, got_u)
        own_q, own_u, own_d, at, count = qkv_weight, [out_weight, up_weight], down_weight, idx, shards
    else:
        small = lax.all_gather(small_own, "fsdp", axis=0)
        own_q = lax.all_gather(qkv_weight, "fsdp", axis=0, tiled=True)
        own_u = [
            lax.all_gather(out_weight, "fsdp", axis=0, tiled=True),
            lax.all_gather(up_weight, "fsdp", axis=0, tiled=True),
        ]
        own_d = lax.all_gather(down_weight, "fsdp", axis=0, tiled=True)
        half_q, half_u, at, count = own_q.shape[1] // 2, 0, jnp.zeros_like(idx), 1
        slots_q = slots_u = slots_d = []
    qv_b, out_b, up_b, down_b, gain, shift = unpack_small(small.astype(F32))
    qkv_b = jnp.concatenate([qv_b[0:1], jnp.zeros((1, width), F32), qv_b[1:2]], axis=1)

    spec = (
        [(0, 0, half_q, 0), (0, half_q, half_q, 1)],
        plane_spec([[(0, 0, 0, half_q, 0)], [(0, half_q, 0, half_q, 1)]]) if halves else [],
    )
    normed_one, packed, w_qkv = qkv_forward(
        at, own_q, spec, slots_q, count, x, qkv_b, gain[0:1], shift[0:1]
    )
    if halves:
        packed, pair_u = after(packed, pair_u)
        slots = shard_slots(got_u, pair_u)
        u_own = [jnp.stack([g[:, :half_u] for g in slots]), jnp.stack([g[:, half_u:] for g in slots])]
        u_got = [swap(o, "dp", m) for o, m in zip(u_own, both)]
        u_own, piece_d = after(u_own, eighth(down_weight))
        got_d = swap(piece_d, "fsdp", 2)
        u_own, packed = after(u_own, packed)
    pairs = width // PAIR
    part = attend(packed, start_row, 0, pairs // 2)
    if halves:
        part, u_got, got_d = tie((part, u_got, got_d))
        u_two = [jnp.concatenate([o, g]) for o, g in zip(u_own, u_got)]
        u_four = [swap(t, "dp", 6 - m) for t, m in zip(u_two, both)]
        u_two, got_d, packed = tie((u_two, got_d, packed))
        pair_d = shard_pair(piece_d, got_d)
    attended, lse = attend(packed, start_row, pairs // 2, pairs // 2, part)
    if halves:
        attended, u_four, pair_d = tie((attended, u_four, pair_d))
        slots_u = plane_slots(u_two, u_four)
        slots = shard_slots(got_d, pair_d)
        half_d = width // 2
        d_own = [jnp.stack([g[:, :half_d] for g in slots]), jnp.stack([g[:, half_d:] for g in slots])]
        d_got = [swap(o, "dp", m) for o, m in zip(d_own, both)]
    spec = ([(0, 0, width, 0)], plane_spec([[(0, 0, 0, width, 0)], []])[:4] if halves else [])
    mixed, mid, two, w_out = out_forward(
        at, own_u[0], spec, slots_u[:4], count, attended, x, out_b, gain, shift
    )
    if halves:
        two, d_got = after(two, d_got)
        d_two = [jnp.concatenate([o, g]) for o, g in zip(d_own, d_got)]
        d_four = [swap(t, "dp", 6 - m) for t, m in zip(d_two, both)]
        two, d_two = after(two, d_two)
    up_cols = own_u[1].shape[1]
    rest = half_u - width
    spec = (
        [(0, 0, up_cols, 0)],
        plane_spec([[(0, 0, width, rest, 0)], [(0, rest, 0, half_u, 0)]]) if halves else [],
    )
    act, slope, w_up = up_forward(at, own_u[1], spec, slots_u, count, two, up_b)
    if halves:
        act, d_four = after(act, d_four)
        slots_d = plane_slots(d_two, d_four)
    half = width // 2
    spec = ([(0, 0, width, 0)], plane_spec([[(0, 0, 0, half, 0)], [(0, half, 0, half, 0)]]) if halves else [])
    layer_out, gffn, sums3, ghid, up_sum = down_both(
        at, own_d, spec, slots_d, count, act, slope, down_b, mid, cot, live_col, gain, shift
    )

    if halves:
        send = grad_down(idx, act, gffn)
        got_down = swap(send, "dp", 1)
        send, ghid = after(send, ghid)
        send = grad_up(idx, two, ghid)
        got_up = swap(send, "dp", 1)
        send, got_down, act = tie((send, got_down, act))
        down_parts = grad_down(idx, act, gffn, got_down)
        down_got = plane_direct(down_parts)
        down_parts, ghid = after(down_parts, ghid)
    gmid, gmix, gatt, sums21 = mid_backward(ghid, w_up, w_out, mid, mixed, cot, live_col, gain)
    if halves:
        got_up, ghid, gmix, down_got[1:] = tie((got_up, ghid, gmix, down_got[1:]))
        up_parts = grad_up(idx, two, ghid, got_up)
        up_got = plane_direct(up_parts)
        up_parts, gatt = after(up_parts, gatt)
    back = functools.partial(attend_back, packed)
    share = (idx, normed_one) if halves else ()
    gq0, gk0, gv0, sq0, sv0, *shared0 = back(gatt, attended, lse, start_row, 0, 2, *share)
    if halves:
        gq0, gmix, down_got[0] = tie((gq0, gmix, down_got[0]))
        got0 = swap(shared0[0], "dp", 1)
        out_send, out_own = grad_out(idx, attended, gmix)
        out_got = swap(out_send, "dp", 1)
        out_send, gatt, up_got[1:] = tie((out_send, gatt, up_got[1:]))
    gq1, gk1, gv1, sq1, sv1, *shared1 = back(gatt, attended, lse, start_row, 1, 2, *share)
    if halves:
        up_got[0], gq1 = after(up_got[0], gq1)
        got1 = swap(shared1[0], "dp", 1)
        total = jnp.concatenate([plane_total(down_parts, down_got), plane_total(up_parts, up_got)])
        ffn_keep, ffn_send = across_first(total)
        ffn_got = swap(ffn_send, "fsdp", 1)
        ffn_keep, ffn_send, gq1, got0, out_got, got1 = tie((ffn_keep, ffn_send, gq1, got0, out_got, got1))
        heads_parts = head_sums([shared0[1], out_own, shared1[1]], [got0, out_got, got1])
        heads_got = plane_first(heads_parts)
        _, _, gq1 = tie((heads_parts[0], heads_parts[2], gq1))
    grads = [gq0, gq1, gk0, gk1, gv0, gv1]
    grad_input, sums0 = input_backward(grads, w_qkv, x, gmid, gain, 0, tokens // BLOCK)
    if halves:
        sums0, ffn_got = after(sums0, ffn_got)
        ffn_send = add_low(ffn_keep[:, 1], ffn_got[:, 1])
        ffn_keep = add_low(ffn_keep[:, 0], ffn_got[:, 0])
        ffn_got = swap(ffn_send, "fsdp", 2)
        ffn_send, ffn_keep, heads_got = tie((ffn_send, ffn_keep, heads_got))
        heads_send = [add_low(heads_parts[2 * f + 1][0], heads_got[f][0]) for f in range(2)]
        more_got = [swap(part, "dp", mask) for part, mask in zip(heads_send, (2, 4))]
        heads_send, heads_got = after(heads_send, heads_got)
        heads_keep = [add_low(heads_parts[2 * f + 1][1], heads_got[f][1]) for f in range(2)]
        heads_got = more_got
    small_grads = by_shard(
        [
            jnp.concatenate([jnp.concatenate([sq0, sq1], axis=1), jnp.concatenate([sv0, sv1], axis=1)]),
            sums21[4:5],
            up_sum,
            sums3[2:3],
            jnp.concatenate([sums0[0:1], sums21[2:3], sums21[0:1], sums3[0:1]]),
            jnp.concatenate([sums0[1:2], sums21[3:4], sums21[1:2], sums3[1:2]]),
        ],
        shards,
    )
    if halves:
        pairs_of = list(zip(heads_keep, heads_got))
        keep = [add_low(k[:, 0::2], g[:, 0::2]) for k, g in pairs_of]
        send = [add_low(k[:, 1::2], g[:, 1::2]).reshape(-1, width) for k, g in pairs_of]
        tail = small_grads.reshape(-1, width)
        more = tail.shape[0]
        got = swap(jnp.concatenate(send + [tail.astype(BF)]), "fsdp", 1)
        keep, ffn_got = after(keep, ffn_got)
        ffn_four = spread(add_low(ffn_keep, ffn_got))

        keep, got = tie((keep, got))
        tail = tail + got[-more:].astype(F32)
        each = keep[0].size // width
        pairs_of = [(k, got[f * each : (f + 1) * each].reshape(k.shape)) for f, k in enumerate(keep)]
        send = [add_low(k[:, 1], g[:, 1]).reshape(-1, width) for k, g in pairs_of]
        keep = [add_low(k[:, 0], g[:, 0]).reshape(-1, width) for k, g in pairs_of]
        got = swap(jnp.concatenate(send + [tail.astype(BF)]), "fsdp", 2)

        keep, got, ffn_four = tie((keep, got, ffn_four))
        tail = (tail + got[-more:].astype(F32)).astype(BF)
        piece = add_low(jnp.concatenate(keep), got[:-more])
        piece = jnp.concatenate([piece, tail])
        heads_got = [swap(piece, "dp", mask) for mask in (2, 4, 6)]
        ffn_all = spread_core(ffn_four)
        up_grad, down_grad = finish(
            "finish_ffn", idx, place_ffn, ffn_all, [up_weight.shape, down_weight.shape]
        )

        up_grad, heads_got = after(up_grad, heads_got)
        heads_four = jnp.stack([piece] + heads_got)
        heads_all = spread_core(heads_four)
        heads_core = heads_all[1][1]
        heads_all = [heads_all[0], (heads_all[1][0], heads_core)]
        tail = jnp.sum(heads_four[:, -more:].astype(F32), axis=0) + jnp.sum(
            heads_core[:, -more:].astype(F32), axis=0
        )
        small_sum = lax.dynamic_index_in_dim(
            tail.reshape(small_grads.shape), lax.axis_index("fsdp"), 0, keepdims=False
        )
        qkv_grad, out_grad = finish(
            "finish_heads", idx, place_heads, heads_all, [qkv_weight.shape, out_weight.shape]
        )
    else:
        gpacked = jnp.concatenate([gq0, gq1, gk0, gk1, gv0, gv1], axis=1)

        def reduced(left, right):
            grad = dot_tn(left, right)
            return lax.psum(lax.psum_scatter(grad, "fsdp", scatter_dimension=0, tiled=True), "dp")

        qkv_grad = reduced(normed_one, gpacked)
        out_grad = reduced(attended, gmix)
        up_grad = reduced(two, ghid)
        down_grad = reduced(act, gffn)
        small_sum = lax.dynamic_index_in_dim(
            lax.psum(small_grads, ("dp", "fsdp")), lax.axis_index("fsdp"), 0, keepdims=False
        )
    qv_g, outb_g, upb_g, downb_g, gain_g, shift_g = unpack_small(small_sum[None])
    return (
        layer_out[None],
        grad_input[None],
        qkv_grad,
        qv_g,
        out_grad,
        outb_g[0],
        up_grad,
        upb_g[0],
        down_grad,
        downb_g[0],
        gain_g,
        shift_g,
    )


def solution(mesh):
    rows = P(("dp", "fsdp"), None, None)
    split = P("fsdp", None)
    placed = (
        rows,
        split,
        P(None, "fsdp"),
        split,
        P("fsdp"),
        split,
        P("fsdp"),
        split,
        P("fsdp"),
        P(None, "fsdp"),
        P(None, "fsdp"),
        P(("dp", "fsdp"), None),
        rows,
    )
    return jax.shard_map(
        on_device,
        mesh=mesh,
        in_specs=placed,
        out_specs=(
            rows,
            rows,
            split,
            P(None, "fsdp"),
            split,
            P("fsdp"),
            split,
            P("fsdp"),
            split,
            P("fsdp"),
            P(None, "fsdp"),
            P(None, "fsdp"),
        ),
        check_vma=False,
    )
```

```python
import functools
import math

import jax
import jax.numpy as jnp
from jax import lax
from jax.experimental import pallas as pl
from jax.experimental.pallas import tpu as pltpu
from jax.sharding import PartitionSpec as P

F32 = jnp.float32
BF = jnp.bfloat16
SDS = jax.ShapeDtypeStruct
HEAD_DIM = 64
PAIR = 2 * HEAD_DIM
EPS = 1e-05
MASKED = -1e30
QUERY_SCALE = math.log2(math.e) / math.sqrt(HEAD_DIM)
GRAD_SCALE = 1.0 / math.sqrt(HEAD_DIM)
BLOCK = 256
UP_COLS = 1024
HIDDEN_COLS = 1024
GELU_A = math.sqrt(2.0 / math.pi)
GELU_B = 0.044715 * GELU_A


def params(mebibytes=60):
    return pltpu.CompilerParams(vmem_limit_bytes=mebibytes * 1024 * 1024)


def cost(flops, nbytes, trans=0):
    return pl.CostEstimate(flops=int(flops) // 1, bytes_accessed=int(nbytes) // 1, transcendentals=int(trans))


def dot_nn(a, b):
    return lax.dot_general(a, b, (((1,), (0,)), ((), ())), preferred_element_type=F32)


def dot_nt(a, b):
    return lax.dot_general(a, b, (((1,), (1,)), ((), ())), preferred_element_type=F32)


def dot_tn(a, b):
    return lax.dot_general(a, b, (((0,), (0,)), ((), ())), preferred_element_type=F32)


def centred(values):
    centre = values - jnp.mean(values, axis=-1, keepdims=True)
    rstd = lax.rsqrt(jnp.mean(centre * centre, axis=-1, keepdims=True) + EPS)
    return centre * rstd, rstd


def norm_back(grad, vhat, rstd, gain):
    e = grad * gain
    mean_e = jnp.mean(e, axis=-1, keepdims=True)
    mean_ev = jnp.mean(e * vhat, axis=-1, keepdims=True)
    return (e - mean_e - vhat * mean_ev) * rstd


def col_sum(values):
    return jnp.sum(values, axis=0, keepdims=True)


def piece_copies(spec, idx_ref, own_refs, slot_refs, places, sems):
    own_spec, slot_spec = spec
    dp, z = idx_ref[0], idx_ref[1]
    copies = []

    def add(group, src, dst):
        copies.append((group, pltpu.make_async_copy(src, dst, sems.at[len(copies)])))

    for o, first, cols, group in own_spec:
        rows = own_refs[o].shape[0]
        dst = places[o].at[pl.ds(pl.multiple_of(z * rows, rows), rows), first : first + cols]
        add(group, own_refs[o].at[:, first : first + cols], dst)
    for (pair, parts), ref in zip(slot_spec, slot_refs):
        rows = ref.shape[1]
        others = ref.shape[0] // 2
        for which, mask in enumerate(pair):
            for k in range(1, others + 1):
                at = which * others + k - 1
                for o, there, here, cols, group in parts:
                    dst = pl.multiple_of((z ^ k) * own_refs[o].shape[0] + (dp ^ mask) * rows, rows)
                    add(
                        group,
                        ref.at[at, :, here : here + cols],
                        places[o].at[pl.ds(dst, rows), there : there + cols],
                    )
    return copies


def count_copies(spec, slots):
    own_spec, slot_spec = spec
    return len(own_spec) + sum(len(parts) * s.shape[0] for (_, parts), s in zip(slot_spec, slots))


def start_all(copies):
    for _, copy in copies:
        copy.start()


def wait_group(copies, group):
    for g, copy in copies:
        if g == group:
            copy.wait()


def whole_shapes(owns, shards):
    return [(o.shape[0] * shards, o.shape[1]) for o in owns]


ANY = pl.BlockSpec(memory_space=pl.ANY)
SMEM = pl.BlockSpec(memory_space=pltpu.SMEM)


def qkv_kernel(spec, n_slots, idx_ref, own_ref, *refs):
    slots = refs[:n_slots]
    x_ref, bias_ref, gain_ref, shift_ref, normed_ref, packed_ref, out_ref = refs[n_slots : n_slots + 7]
    weight, sems, out_sem = refs[n_slots + 7 :]
    step, steps = pl.program_id(0), pl.num_programs(0)
    copies = piece_copies(spec, idx_ref, [own_ref], slots, [weight], sems)
    bn = packed_ref.shape[1]

    @pl.when(step == 0)
    def _():
        start_all(copies)
        vhat, _ = centred(x_ref[...].astype(F32))
        normed_ref[...] = (vhat * gain_ref[...] + shift_ref[...]).astype(BF)
        wait_group(copies, 0)

    half = weight.shape[1] // 2

    @pl.when(step == half // bn)
    def _():
        wait_group(copies, 1)
        pltpu.make_async_copy(weight, out_ref, out_sem).start()

    block = weight[:, pl.ds(pl.multiple_of(step * bn, bn), bn)]
    out = dot_nn(normed_ref[...], block) + bias_ref[...]
    packed_ref[...] = (out * jnp.where(step < steps // 3, QUERY_SCALE, 1.0)).astype(BF)

    @pl.when(step == steps - 1)
    def _():
        pltpu.make_async_copy(weight, out_ref, out_sem).wait()


def qkv_forward(idx, own, spec, slots, shards, x, bias, gain, shift):
    tokens, width = x.shape
    ((rows, cols),) = whole_shapes([own], shards)
    bn = width // 2
    row = pl.BlockSpec((1, width), lambda j: (0, 0))
    full = pl.BlockSpec((tokens, width), lambda j: (0, 0))
    return pl.pallas_call(
        functools.partial(qkv_kernel, spec, len(slots)),
        grid=(cols // bn,),
        in_specs=[SMEM] + [ANY] * (1 + len(slots))
        + [full, pl.BlockSpec((1, bn), lambda j: (0, j)), row, row],
        out_specs=(full, pl.BlockSpec((tokens, bn), lambda j: (0, j)), ANY),
        out_shape=(SDS((tokens, width), BF), SDS((tokens, cols), BF), SDS((rows, cols), BF)),
        scratch_shapes=[
            pltpu.VMEM((rows, cols), BF),
            pltpu.SemaphoreType.DMA((count_copies(spec, slots),)),
            pltpu.SemaphoreType.DMA(()),
        ],
        compiler_params=params(36),
        cost_estimate=cost(2 * tokens * width * cols, 2 * width * cols + 2 * tokens * cols),
        name="qkv_forward",
    )(idx, own, *slots, x, bias, gain, shift)


def gelu_and_slope(a):
    sq = a * a
    t = jnp.tanh(a * (sq * GELU_B + GELU_A))
    half = 0.5 * t + 0.5
    act = a * half
    slope = half + act * ((1.0 - half) * (sq * (6.0 * GELU_B) + 2.0 * GELU_A))
    return act.astype(BF), slope.astype(BF)


def out_kernel(spec, n_slots, idx_ref, own_ref, *refs):
    slots = refs[:n_slots]
    att_ref, x_ref, bias_ref, gain_ref, shift_ref = refs[n_slots : n_slots + 5]
    mixed_ref, mid_ref, two_ref, save_ref, weight, sems, save_sem = refs[n_slots + 5 :]
    step, steps = pl.program_id(0), pl.num_programs(0)
    copies = piece_copies(spec, idx_ref, [own_ref], slots, [weight], sems)
    save = pltpu.make_async_copy(weight, save_ref, save_sem)

    @pl.when(step == 0)
    def _():
        start_all(copies)
        wait_group(copies, 0)
        save.start()

    mixed = dot_nn(att_ref[...], weight[...]) + bias_ref[...]
    mixed_ref[...] = mixed
    vhat, _ = centred(mixed)
    mid = x_ref[...].astype(F32) + vhat * gain_ref[1:2, :] + shift_ref[1:2, :]
    mid_ref[...] = mid
    vhat, _ = centred(mid)
    two_ref[...] = (vhat * gain_ref[2:3, :] + shift_ref[2:3, :]).astype(BF)

    @pl.when(step == steps - 1)
    def _():
        save.wait()


def out_forward(idx, own, spec, slots, shards, attended, x, bias, gain, shift):
    tokens, width = x.shape
    (shape,) = whole_shapes([own], shards)
    tok = pl.BlockSpec((BLOCK, width), lambda i: (i, 0))

    def whole(arr):
        return pl.BlockSpec(arr.shape, lambda i: (0, 0))

    return pl.pallas_call(
        functools.partial(out_kernel, spec, len(slots)),
        grid=(tokens // BLOCK,),
        in_specs=[SMEM] + [ANY] * (1 + len(slots)) + [tok, tok, whole(bias), whole(gain), whole(shift)],
        out_specs=(tok, tok, tok, ANY),
        out_shape=(
            SDS((tokens, width), F32),
            SDS((tokens, width), F32),
            SDS((tokens, width), BF),
            SDS(shape, BF),
        ),
        scratch_shapes=[
            pltpu.VMEM(shape, BF),
            pltpu.SemaphoreType.DMA((count_copies(spec, slots),)),
            pltpu.SemaphoreType.DMA(()),
        ],
        compiler_params=params(30),
        cost_estimate=cost(2 * tokens * width * width, 16 * tokens * width),
        name="out_forward",
    )(idx, own, *slots, attended, x, bias, gain, shift)


def up_kernel(spec, n_slots, idx_ref, own_ref, *refs):
    slots = refs[:n_slots]
    two_ref, bias_ref, act_ref, slope_ref, save_ref, weight, sems, save_sem = refs[n_slots:]
    step, steps = pl.program_id(0), pl.num_programs(0)
    copies = piece_copies(spec, idx_ref, [own_ref], slots, [weight], sems)
    save = pltpu.make_async_copy(weight, save_ref, save_sem)

    @pl.when(step == 0)
    def _():
        start_all(copies)
        wait_group(copies, 0)
        save.start()

    bn = act_ref.shape[1]
    at = pl.ds(pl.multiple_of(step * bn, bn), bn)
    a = dot_nn(two_ref[...], weight[:, at]) + bias_ref[...]
    act_ref[...], slope_ref[...] = gelu_and_slope(a)

    @pl.when(step == steps - 1)
    def _():
        save.wait()


def up_forward(idx, own, spec, slots, shards, two, bias):
    tokens, width = two.shape
    (shape,) = whole_shapes([own], shards)
    cols = shape[1]
    bn = UP_COLS
    col = pl.BlockSpec((tokens, bn), lambda i: (0, i))
    return pl.pallas_call(
        functools.partial(up_kernel, spec, len(slots)),
        grid=(cols // bn,),
        in_specs=[SMEM] + [ANY] * (1 + len(slots))
        + [pl.BlockSpec((tokens, width), lambda i: (0, 0)), pl.BlockSpec((1, bn), lambda i: (0, i))],
        out_specs=(col, col, ANY),
        out_shape=(SDS((tokens, cols), BF), SDS((tokens, cols), BF), SDS(shape, BF)),
        scratch_shapes=[
            pltpu.VMEM(shape, BF),
            pltpu.SemaphoreType.DMA((count_copies(spec, slots),)),
            pltpu.SemaphoreType.DMA(()),
        ],
        compiler_params=params(48),
        cost_estimate=cost(2 * tokens * width * cols, 2 * width * cols + 4 * tokens * cols),
        name="up_forward",
    )(idx, own, *slots, two, bias)


def down_kernel(spec, n_slots, first, idx_ref, own_ref, *refs):
    slots = refs[:n_slots]
    act_ref, slope_ref, bias_ref, mid_ref, cot_ref, live_ref, gain_ref, shift_ref = refs[n_slots : n_slots + 8]
    out_ref, grad_ref, sums_ref, hid_ref, hsum_ref, weight, sems = refs[n_slots + 8 :]
    step = pl.program_id(0)
    copies = piece_copies(spec, idx_ref, [own_ref], slots, [weight], sems)

    @pl.when(step == 0)
    def _():
        start_all(copies)
        sums_ref[...] = jnp.zeros_like(sums_ref)
        wait_group(copies, 0)

    @pl.when(step < first)
    def _():
        ffn = dot_nn(act_ref[...], weight[...]) + bias_ref[...]
        vhat, rstd = centred(ffn)
        gain = gain_ref[3:4, :]
        out_ref[...] = (mid_ref[...] + vhat * gain + shift_ref[3:4, :]).astype(BF)
        grad = cot_ref[...].astype(F32) * live_ref[...]
        low = norm_back(grad, vhat, rstd, gain).astype(BF)
        grad_ref[pl.ds(pl.multiple_of(step * BLOCK, BLOCK), BLOCK), :] = low
        sums_ref[0:1, :] += col_sum(grad * vhat)
        sums_ref[1:2, :] += col_sum(grad)
        sums_ref[2:3, :] += col_sum(low.astype(F32))

    @pl.when(step >= first)
    def _():
        bn = hid_ref.shape[1]
        at = pl.ds(pl.multiple_of((step - first) * bn, bn), bn)
        low = (dot_nt(grad_ref[...], weight[at, :]) * slope_ref[...].astype(F32)).astype(BF)
        hid_ref[...] = low
        hsum_ref[...] = col_sum(low.astype(F32))


def down_both(idx, own, spec, slots, shards, act, slope, bias, mid, cot, live, gain, shift):
    tokens, width = mid.shape
    (shape,) = whole_shapes([own], shards)
    cols = shape[0]
    bn = HIDDEN_COLS
    first = tokens // BLOCK

    def at(i):
        return jnp.minimum(i, first - 1)

    tok = pl.BlockSpec((BLOCK, width), lambda i: (at(i), 0))
    col = pl.BlockSpec((tokens, bn), lambda i: (0, jnp.maximum(i - first, 0)))

    def whole(arr):
        return pl.BlockSpec(arr.shape, lambda i: (0, 0))

    return pl.pallas_call(
        functools.partial(down_kernel, spec, len(slots), first),
        grid=(first + cols // bn,),
        in_specs=[SMEM] + [ANY] * (1 + len(slots))
        + [
            pl.BlockSpec((BLOCK, cols), lambda i: (at(i), 0)),
            col,
            whole(bias),
            tok,
            tok,
            pl.BlockSpec((BLOCK, 1), lambda i: (at(i), 0)),
            whole(gain),
            whole(shift),
        ],
        out_specs=(
            tok,
            pl.BlockSpec((tokens, width), lambda i: (0, 0)),
            pl.BlockSpec((8, width), lambda i: (0, 0)),
            col,
            pl.BlockSpec((1, bn), lambda i: (0, jnp.maximum(i - first, 0))),
        ),
        out_shape=(
            SDS((tokens, width), BF),
            SDS((tokens, width), BF),
            SDS((8, width), F32),
            SDS((tokens, cols), BF),
            SDS((1, cols), F32),
        ),
        scratch_shapes=[pltpu.VMEM(shape, BF), pltpu.SemaphoreType.DMA((count_copies(spec, slots),))],
        compiler_params=params(),
        cost_estimate=cost(4 * tokens * width * cols, 2 * width * cols + 6 * tokens * cols),
        name="down_both",
    )(idx, own, *slots, act, slope, bias, mid, cot, live, gain, shift)


def mid_kernel(
    gh_ref, up_ref, out_w_ref, mid_ref, mixed_ref, cot_ref, live_ref, gain_ref,
    gmid_ref, gmix_ref, gatt_ref, sums_ref,
):
    @pl.when(pl.program_id(0) == 0)
    def _():
        sums_ref[...] = jnp.zeros_like(sums_ref)

    grad = dot_nt(gh_ref[...], up_ref[...])
    vhat, rstd = centred(mid_ref[...])
    sums_ref[0:1, :] += col_sum(grad * vhat)
    sums_ref[1:2, :] += col_sum(grad)
    gmid = cot_ref[...].astype(F32) * live_ref[...] + norm_back(grad, vhat, rstd, gain_ref[2:3, :])
    gmid_ref[...] = gmid
    vhat, rstd = centred(mixed_ref[...])
    sums_ref[2:3, :] += col_sum(gmid * vhat)
    sums_ref[3:4, :] += col_sum(gmid)
    low = norm_back(gmid, vhat, rstd, gain_ref[1:2, :]).astype(BF)
    gmix_ref[...] = low
    sums_ref[4:5, :] += col_sum(low.astype(F32))
    gatt_ref[...] = dot_nt(low, out_w_ref[...]).astype(BF)


def mid_backward(gh, up, out_w, mid, mixed, cot, live, gain):
    tokens, width = mid.shape
    cols = gh.shape[1]
    tok = pl.BlockSpec((BLOCK, width), lambda i: (i, 0))

    def whole(arr):
        return pl.BlockSpec(arr.shape, lambda i: (0, 0))

    return pl.pallas_call(
        mid_kernel,
        grid=(tokens // BLOCK,),
        in_specs=[
            pl.BlockSpec((BLOCK, cols), lambda i: (i, 0)),
            whole(up),
            whole(out_w),
            tok,
            tok,
            tok,
            pl.BlockSpec((BLOCK, 1), lambda i: (i, 0)),
            whole(gain),
        ],
        out_specs=(tok, tok, tok, pl.BlockSpec((8, width), lambda i: (0, 0))),
        out_shape=(
            SDS((tokens, width), F32),
            SDS((tokens, width), BF),
            SDS((tokens, width), BF),
            SDS((8, width), F32),
        ),
        compiler_params=params(),
        cost_estimate=cost(2 * tokens * width * (cols + width), 2 * width * cols + 2 * tokens * cols),
        name="mid_backward",
    )(gh, up, out_w, mid, mixed, cot, live, gain)


def input_kernel(n_grads, n_into, *refs):
    grad_refs, (w_ref, x_ref, gmid_ref, gain_ref) = refs[:n_grads], refs[n_grads : n_grads + 4]
    out_ref, sums_ref = refs[n_grads + 4 + n_into :]

    @pl.when(pl.program_id(0) == 0)
    def _():
        sums_ref[...] = jnp.zeros_like(sums_ref)

    grads = jnp.concatenate([ref[...] for ref in grad_refs], axis=1)
    grad = dot_nt(grads, w_ref[...])
    vhat, rstd = centred(x_ref[...].astype(F32))
    sums_ref[0:1, :] += col_sum(grad * vhat)
    sums_ref[1:2, :] += col_sum(grad)
    out_ref[...] = gmid_ref[...] + norm_back(grad, vhat, rstd, gain_ref[0:1, :])


def input_backward(grads, weight, x, gmid, gain, first, count, into=None):
    tokens, width = x.shape
    tok = pl.BlockSpec((BLOCK, width), lambda i: (first + i, 0))

    def whole(arr):
        return pl.BlockSpec(arr.shape, lambda i: (0, 0))

    in_specs = [pl.BlockSpec((BLOCK, g.shape[1]), lambda i: (first + i, 0)) for g in grads]
    in_specs += [whole(weight), tok, tok, whole(gain)]
    args = [*grads, weight, x, gmid, gain]
    aliases = {}
    if into is not None:
        aliases = {len(args): 0}
        in_specs.append(pl.BlockSpec(memory_space=pl.ANY))
        args.append(into)
    return pl.pallas_call(
        functools.partial(input_kernel, len(grads), len(aliases)),
        grid=(count,),
        in_specs=in_specs,
        out_specs=(tok, pl.BlockSpec((8, width), lambda i: (0, 0))),
        out_shape=(SDS((tokens, width), F32), SDS((8, width), F32)),
        input_output_aliases=aliases,
        compiler_params=params(),
        cost_estimate=cost(6 * count * BLOCK * width * width, 6 * width * width),
        name="input_backward",
    )(*args)


def fill_bias(bias, start_ref):
    length = bias.shape[0]
    for j in range(length // BLOCK):
        key = lax.broadcasted_iota(jnp.int32, (BLOCK, length), 0) + j * BLOCK
        query = lax.broadcasted_iota(jnp.int32, (BLOCK, length), 1)
        allowed = (key <= query) & (key >= start_ref[...])
        bias[j * BLOCK : (j + 1) * BLOCK, :] = jnp.where(allowed, 0.0, MASKED)


def one_head(low, arr, head):
    zero = jnp.zeros_like(arr)
    return jnp.where(low, arr, zero) if head == 0 else jnp.where(low, zero, arr)


def attend_kernel(q_ref, k_ref, v_ref, start_ref, out_ref, lse_ref, bias):
    length = q_ref.shape[0]

    @pl.when(pl.program_id(0) == 0)
    def _():
        fill_bias(bias, start_ref)

    low = lax.broadcasted_iota(jnp.int32, (1, PAIR), 1) < HEAD_DIM
    low_rows = lax.broadcasted_iota(jnp.int32, (PAIR, 1), 0) < HEAD_DIM
    keys = k_ref[...]
    values = jnp.concatenate([v_ref[...], jnp.ones((length, PAIR), BF)], axis=1)
    for i in range(length // BLOCK):
        reach = (i + 1) * BLOCK
        sl = slice(i * BLOCK, reach)
        queries = q_ref[sl, :]
        parts = []
        for head in range(2):
            scores = dot_nt(keys[:reach], one_head(low, queries, head)) + bias[:reach, sl]
            top = jnp.max(scores, axis=0, keepdims=True)
            probs = jnp.exp2(scores - top).astype(BF)
            mixed = dot_tn(values[:reach], probs)
            total = mixed[PAIR : PAIR + 1]
            parts.append(mixed[:PAIR] / total)
            lse_ref[0, head : head + 1, sl] = top + jnp.log2(total)
        out_ref[sl, :] = jnp.where(low_rows, parts[0], parts[1]).T.astype(BF)


def attend(packed, start_row, first, count, into=None):
    length = packed.shape[0]
    pairs = packed.shape[1] // (3 * PAIR)

    def blk(offset):
        return pl.BlockSpec((length, PAIR), lambda h: (0, offset + first + h))

    in_specs = [blk(0), blk(pairs), blk(2 * pairs), pl.BlockSpec((1, length), lambda h: (0, 0))]
    args = [packed, packed, packed, start_row]
    kernel, aliases = attend_kernel, {}
    if into is not None:
        in_specs = in_specs + [ANY] * len(into)
        aliases = {len(args) + i: i for i in range(len(into))}
        args = args + list(into)

        def kernel(*refs):
            attend_kernel(*refs[:4], *refs[4 + len(into) :])

    return pl.pallas_call(
        kernel,
        grid=(count,),
        in_specs=in_specs,
        out_specs=(blk(0), pl.BlockSpec((1, 2, length), lambda h: (first + h, 0, 0))),
        out_shape=(SDS((length, PAIR * pairs), BF), SDS((pairs, 2, length), F32)),
        input_output_aliases=aliases,
        scratch_shapes=[pltpu.VMEM((length, length), F32)],
        compiler_params=params(),
        cost_estimate=cost(8 * count * length * length * PAIR, 8 * length * count * PAIR),
        name="attend",
    )(*args)


def share_out(wide, idx_ref, send_ref, own_ref):
    core, z = idx_ref[0] & 1, idx_ref[1]
    rows = wide.shape[0] // 8
    for zz in range(4):
        for ref, c in ((send_ref, core ^ 1), (own_ref, core)):
            at = pl.ds(pl.multiple_of((2 * zz + c) * rows, rows), rows)
            part = wide[at, :].astype(BF)
            ref[0, 0, zz ^ z, 0] = part[: rows // 2]
            ref[0, 0, zz ^ z, 1] = part[rows // 2 :]


def attend_back_kernel(shared, *refs):
    if shared:
        idx_ref, one_ref, refs = refs[0], refs[1], refs[2:]
        send_ref, own_ref, wide = refs[12], refs[13], refs[16]
        refs = refs[:12] + refs[14:16]
    q_ref, k_ref, v_ref, g_ref, o_ref, lse_ref, start_ref = refs[:7]
    gq_ref, gk_ref, gv_ref, sq_ref, sv_ref, bias, acc = refs[7:]
    length = q_ref.shape[0]

    @pl.when(pl.program_id(0) == 0)
    def _():
        fill_bias(bias, start_ref)

    low = lax.broadcasted_iota(jnp.int32, (1, PAIR), 1) < HEAD_DIM
    queries, grads = q_ref[...], g_ref[...]
    q_of = [one_head(low, queries, head) for head in range(2)]
    g_of = [one_head(low, grads, head) for head in range(2)]
    inner = (grads.astype(F32) * o_ref[...].astype(F32)).T
    inner_of = [col_sum(inner[:HEAD_DIM]), col_sum(inner[HEAD_DIM:])]
    sum_v = jnp.zeros((1, PAIR), F32)
    for j in range(length // BLOCK):
        first = j * BLOCK
        sl = slice(first, first + BLOCK)
        keys, values = k_ref[sl, :], v_ref[sl, :]
        gk = gv = gq = 0.0
        for head in range(2):
            scores = dot_nt(keys, q_of[head][first:]) + bias[sl, first:]
            probs = jnp.exp2(scores - lse_ref[0, head : head + 1, first:])
            gprobs = dot_nt(values, g_of[head][first:])
            gscores = (probs * (gprobs - inner_of[head][:, first:]) * GRAD_SCALE).astype(BF)
            gv = gv + dot_nn(probs.astype(BF), g_of[head][first:])
            gk = gk + dot_nn(gscores, q_of[head][first:])
            gq = gq + dot_tn(gscores, one_head(low, keys, head))
        low_v = gv.astype(BF)
        gv_ref[sl, :] = low_v
        gk_ref[sl, :] = (gk * (1.0 / QUERY_SCALE)).astype(BF)
        sum_v = sum_v + col_sum(low_v.astype(F32))
        if j == 0:
            acc[...] = gq
        else:
            acc[first:, :] += gq
    low_q = acc[...].astype(BF)
    gq_ref[...] = low_q
    sq_ref[...] = col_sum(low_q.astype(F32))
    sv_ref[...] = sum_v
    if shared:
        grads = jnp.concatenate([low_q, gk_ref[...], gv_ref[...]], axis=1)
        wide[...] = dot_tn(one_ref[...], grads)
        share_out(wide, idx_ref, send_ref, own_ref)


def attend_back(packed, grads, attended, lse, start_row, part, parts, idx=None, one=None):
    length = packed.shape[0]
    total = packed.shape[1] // (3 * PAIR)
    count = total // parts
    first = part * count
    shared = one is not None

    def blk(offset):
        return pl.BlockSpec((length, PAIR), lambda h, *_: (0, offset + h))

    row = pl.BlockSpec((1, PAIR), lambda h, *_: (0, h))
    grad = SDS((length, PAIR * count), BF)
    sums = SDS((1, PAIR * count), F32)
    in_specs = [
        blk(first),
        blk(total + first),
        blk(2 * total + first),
        blk(first),
        blk(first),
        pl.BlockSpec((1, 2, length), lambda h, *_: (first + h, 0, 0)),
        pl.BlockSpec((1, length), lambda h, *_: (0, 0)),
    ]
    args = [packed, packed, packed, grads, attended, lse, start_row]
    out_specs = [blk(0), blk(0), blk(0), row, row]
    out_shape = [grad, grad, grad, sums, sums]
    scratch = [pltpu.VMEM((length, length), F32), pltpu.VMEM((length, PAIR), F32)]
    if shared:
        width = one.shape[1]
        piece = (4, 2, width // 16, 3 * PAIR)
        block = pl.BlockSpec((1, 1) + piece, lambda h, idx: (3 ^ h ^ (idx[0] // 2), 0, 0, 0, 0, 0))
        in_specs = [pl.BlockSpec(one.shape, lambda h, *_: (0, 0))] + in_specs
        args = [idx, one] + args
        out_specs = out_specs + [block, block]
        out_shape = out_shape + [SDS((4, 1) + piece, BF)] * 2
        scratch = scratch + [pltpu.VMEM((width, 3 * PAIR), F32)]
    return pl.pallas_call(
        functools.partial(attend_back_kernel, shared),
        grid_spec=pltpu.PrefetchScalarGridSpec(
            num_scalar_prefetch=int(shared),
            grid=(count,),
            in_specs=in_specs,
            out_specs=tuple(out_specs),
            scratch_shapes=scratch,
        ),
        out_shape=tuple(out_shape),
        compiler_params=params(),
        cost_estimate=cost(20 * count * length * length * PAIR, 16 * length * count * PAIR),
        name="attend_back",
    )(*args)


def swap(arr, axis, mask):
    size = lax.axis_size(axis)
    return lax.ppermute(arr, axis, [(i, i ^ mask) for i in range(size)])


def after(first, then):
    return lax.optimization_barrier((first, then))


def shard_swaps(piece):
    return [swap(piece, "fsdp", k) for k in range(1, lax.axis_size("fsdp"))]


def shard_pair(piece, got):
    return swap(jnp.stack([piece, got]), "fsdp", 1)


def shard_slots(got, pair):
    return [pair[0], got, pair[1]]


PLANE_MASKS = [
    (0, 4), (2, 6), (1, 5), (3, 7),
    (0, 2), (4, 6), (1, 3), (5, 7),
]


def plane_slots(two, four):
    return [a for t, f in zip(two, four) for a in (t, f, swap(t, "dp", 1), swap(f, "dp", 1))]


def plane_spec(parts):
    return [(pair, parts[i // 4]) for i, pair in enumerate(PLANE_MASKS)]


def split_down(wide, zz):
    rows, cols = wide.shape[0] // 4, wide.shape[1] // 2
    part = wide[zz * rows : (zz + 1) * rows]
    return part[:, :cols], part[:, cols:]


def split_up(wide, zz):
    rows = wide.shape[0] // 8
    return wide[2 * zz * rows : (2 * zz + 1) * rows], wide[(2 * zz + 1) * rows : (2 * zz + 2) * rows]


def side_by_side(refs):
    blocks = [r[...] for r in refs]
    return blocks[0] if len(blocks) == 1 else jnp.concatenate(blocks, axis=1)


def emit(keep, direct, wide, split, z, chip, rest):
    if not keep:
        for zz in range(4):
            for f, part in enumerate(split(wide, zz)):
                rest[0][0, 0, zz ^ z, f] = part.astype(BF)
        return
    got_ref, outs = rest[0], rest[1:]
    for dst in range(4):

        @pl.when(chip == dst)
        def _():
            for zz in range(4):
                slot = zz ^ z
                for f, part in enumerate(split(wide, zz)):
                    low = (part + got_ref[0, 0, slot, f].astype(F32)).astype(BF)
                    if direct:
                        outs[dst][0, slot, f] = low
                    else:
                        bit = dst // 2 if f == 0 else dst % 2
                        outs[2 * f + bit][0, 0, slot] = low


def grad_kernel(keep, direct, jobs, idx_ref, *refs):
    step, z = pl.program_id(0), idx_ref[1]
    at = 0
    n_in = sum(n for groups, _ in jobs for group in groups for n in group)
    rest = refs[n_in:]
    for number, (groups, split) in enumerate(jobs):
        blocks = []
        for n_left, n_right in groups:
            blocks.append((refs[at : at + n_left], refs[at + n_left : at + n_left + n_right]))
            at += n_left + n_right

        @pl.when(step // 4 == number)
        def _():
            dots = [dot_tn(side_by_side(left), side_by_side(right)) for left, right in blocks]
            wide = dots[0] if len(dots) == 1 else jnp.concatenate(dots, axis=1)
            emit(keep, direct, wide, split, z, step % 4, rest)


def grad_call(name, idx, specs, args, jobs, piece, flops, got=None, direct=True):
    keep = got is not None
    n_jobs = len(jobs)
    rows, cols = piece
    block = pl.BlockSpec((1, 1, 4, 2, rows, cols), lambda i, idx: (i % 4, i // 4, 0, 0, 0, 0))
    half = (1, 1, 4, rows, cols)
    if keep and direct:
        specs = specs + [block]
        args = args + [got]
        out_specs = (pl.BlockSpec((1, 4, 2, rows, cols), lambda i, idx: (0, 0, 0, 0, 0)),) * 4
        out_shape = (SDS((1, 4, 2, rows, cols), BF),) * 4
    elif keep:
        along_y = (
            lambda i, idx: (jnp.minimum(i % 4, 1), i // 4, 0, 0, 0),
            lambda i, idx: (jnp.maximum(i % 4 - 2, 0), i // 4, 0, 0, 0),
        )
        along_x = (lambda i, idx: (i % 4 // 2, i // 4, 0, 0, 0),) * 2
        specs = specs + [block]
        args = args + [got]
        out_specs = tuple(pl.BlockSpec(half, m) for m in along_y + along_x)
        out_shape = (SDS((2, n_jobs, 4, rows, cols), BF),) * 4
    else:
        out_specs = block
        out_shape = SDS((4, n_jobs, 4, 2, rows, cols), BF)
    return pl.pallas_call(
        functools.partial(grad_kernel, keep, direct, jobs),
        grid_spec=pltpu.PrefetchScalarGridSpec(
            num_scalar_prefetch=1, grid=(4 * n_jobs,), in_specs=specs, out_specs=out_specs
        ),
        out_shape=out_shape,
        compiler_params=params(),
        cost_estimate=cost(flops, flops // 400),
        name=name + ("_keep" if keep else "_send"),
    )(idx, *args)


def chip_of(i, idx):
    return (idx[0] // 2) ^ (3 - i)


def core_of(keep, idx):
    return idx[0] & 1 if keep else (idx[0] & 1) ^ 1


def grad_down(idx, act, gffn, got=None):
    tokens, width = gffn.shape
    keep = got is not None
    rows = act.shape[1] // 32

    def act_spec(zz):
        def at(i, idx):
            return (0, zz * 8 + chip_of(i, idx) * 2 + core_of(keep, idx))

        return pl.BlockSpec((tokens, rows), at)

    specs = [act_spec(0), act_spec(1), act_spec(2), act_spec(3)]
    specs += [pl.BlockSpec((tokens, width), lambda i, idx: (0, 0))]
    args = [act, act, act, act, gffn]
    flops = act.shape[1] * width * tokens
    jobs = [([(4, 1)], split_down)]
    return grad_call("grad_down", idx, specs, args, jobs, (rows, width // 2), flops, got)


def grad_up(idx, two, ghid, got=None):
    tokens, width = two.shape
    keep = got is not None
    cols = ghid.shape[1] // 8
    specs = [
        pl.BlockSpec((tokens, width), lambda i, idx: (0, 0)),
        pl.BlockSpec((tokens, cols), lambda i, idx: (0, chip_of(i, idx) * 2 + core_of(keep, idx))),
    ]
    flops = ghid.shape[1] * width * tokens
    jobs = [([(1, 1)], split_up)]
    return grad_call("grad_up", idx, specs, [two, ghid], jobs, (width // 8, cols), flops, got)


def grad_out_kernel(idx_ref, att_ref, gmix_ref, send_ref, own_ref, wide):
    wide[...] = dot_tn(att_ref[...], gmix_ref[...])
    share_out(wide, idx_ref, send_ref, own_ref)


def grad_out(idx, att, gmix):
    tokens, width = att.shape
    cols = width // 4
    piece = (4, 2, width // 16, cols)
    block = pl.BlockSpec((1, 1) + piece, lambda i, idx: (i, 0, 0, 0, 0, 0))
    return pl.pallas_call(
        grad_out_kernel,
        grid_spec=pltpu.PrefetchScalarGridSpec(
            num_scalar_prefetch=1,
            grid=(4,),
            in_specs=[
                pl.BlockSpec((tokens, width), lambda i, idx: (0, 0)),
                pl.BlockSpec((tokens, cols), lambda i, idx: (0, chip_of(i, idx))),
            ],
            out_specs=(block, block),
            scratch_shapes=[pltpu.VMEM((width, cols), F32)],
        ),
        out_shape=(SDS((4, 1) + piece, BF),) * 2,
        compiler_params=params(),
        cost_estimate=cost(2 * tokens * width * width, 8 * tokens * width),
        name="grad_out",
    )(idx, att, gmix)


def head_sums_kernel(n, *refs):
    owns, gots, outs = refs[:n], refs[n : 2 * n], refs[2 * n :]
    for dst in range(4):

        @pl.when(pl.program_id(0) == dst)
        def _():
            for f in range(2):
                parts = [o[0, 0, :, f].astype(F32) + g[0, 0, :, f].astype(F32) for o, g in zip(owns, gots)]
                bit = dst // 2 if f == 0 else dst % 2
                outs[2 * f + bit][0, 0] = jnp.concatenate(parts, axis=-1).astype(BF)


def head_sums(owns, gots):
    _, _, slots, _, rows, _ = owns[0].shape
    cols = sum(o.shape[-1] for o in owns)
    half = (1, 1, slots, rows, cols)
    along_y = (lambda i: (jnp.minimum(i, 1), 0, 0, 0, 0), lambda i: (jnp.maximum(i - 2, 0), 0, 0, 0, 0))
    along_x = (lambda i: (i // 2, 0, 0, 0, 0),) * 2
    return pl.pallas_call(
        functools.partial(head_sums_kernel, len(owns)),
        grid=(4,),
        in_specs=[pl.BlockSpec((1,) + a.shape[1:], lambda i: (i, 0, 0, 0, 0, 0)) for a in owns + gots],
        out_specs=tuple(pl.BlockSpec(half, m) for m in along_y + along_x),
        out_shape=(SDS((2, 1, slots, rows, cols), BF),) * 4,
        compiler_params=params(),
        cost_estimate=cost(0, 48 * slots * rows * cols),
        name="head_sums",
    )(*owns, *gots)


def add_low(a, b):
    return (a.astype(F32) + b.astype(F32)).astype(BF)


def add_wide(a, b):
    return a.astype(F32) + b.astype(F32)


def plane_first(parts):
    return [swap(parts[2 * f], "dp", mask) for f, mask in enumerate((4, 2))]


def plane_adds(parts, got):
    send = [add_low(parts[2 * f + 1][0], got[f][0]) for f in range(2)]
    keep = [add_low(parts[2 * f + 1][1], got[f][1]) for f in range(2)]
    return keep, send


def plane_second(parts, got):
    keep, send = plane_adds(parts, got)
    return keep, [swap(s, "dp", mask) for s, mask in zip(send, (2, 4))]


def plane_direct(parts):
    return [swap(part, "dp", mask) for part, mask in zip(parts, (6, 4, 2))]


def plane_total(parts, got):
    return add_wide(parts[3], got[0]) + add_wide(got[1], got[2])


def across_first(both):
    return both[:, 0::2].astype(BF), both[:, 1::2].astype(BF)


def spread(piece):
    four = jnp.stack([piece] + [swap(piece, "dp", mask) for mask in (2, 4, 6)])
    return four


def spread_core(four):
    return [((0, 2, 4, 6), four), ((1, 3, 5, 7), swap(four, "dp", 1))]


def place_ffn(dp, piece, outs):
    up_grad, down_grad = outs
    rows, cols = piece.shape[2], piece.shape[3]
    at = pl.ds(pl.multiple_of(dp * rows, rows), rows)
    down_grad[at, :cols] = piece[0, 0].astype(F32)
    down_grad[at, cols:] = piece[0, 1].astype(F32)
    at = pl.ds(pl.multiple_of(dp * cols, cols), cols)
    up_grad[:rows, at] = piece[1, 0].astype(F32)
    up_grad[rows:, at] = piece[1, 1].astype(F32)


def place_heads(dp, piece, outs):
    qkv_grad, out_grad = outs
    width = out_grad.shape[1]
    rows, cols = out_grad.shape[0] // 2, width // 4
    chip, core = dp // 2, dp % 2
    at_rows = pl.ds(pl.multiple_of(core * rows, rows), rows)
    part_of = piece[:rows].astype(F32)
    for half, skip in ((0, 0), (1, 3 * PAIR + cols)):
        for part in range(3):
            at = pl.multiple_of(part * width + half * (width // 2) + chip * PAIR, PAIR)
            here = skip + part * PAIR
            qkv_grad[at_rows, pl.ds(at, PAIR)] = part_of[:, here : here + PAIR]
    at = pl.multiple_of(chip * cols, cols)
    out_grad[at_rows, pl.ds(at, cols)] = part_of[:, 3 * PAIR : 3 * PAIR + cols]


def finish_kernel(placer, masks, idx_ref, *refs):
    ins, outs = refs[: len(masks)], refs[len(masks) :]
    for group, ref in zip(masks, ins):
        for which, mask in enumerate(group):
            placer(idx_ref[0] ^ mask, ref[which], outs)


def finish(name, idx, placer, flow, shapes):
    masks = [m for m, _ in flow]
    arrays = [a for _, a in flow]
    vmem = pl.BlockSpec(memory_space=pltpu.VMEM)
    return pl.pallas_call(
        functools.partial(finish_kernel, placer, masks),
        in_specs=[SMEM] + [vmem] * len(arrays),
        out_specs=(vmem,) * len(shapes),
        out_shape=tuple(SDS(s, F32) for s in shapes),
        compiler_params=params(32),
        cost_estimate=cost(0, sum(6 * math.prod(s) for s in shapes)),
        name=name,
    )(idx, *arrays)


def segment_starts(lengths, length):
    ends = jnp.cumsum(lengths)
    positions = jnp.arange(length, dtype=jnp.int32)
    begun = jnp.where(ends[None, :] <= positions[:, None], ends[None, :], 0)
    return jnp.max(begun, axis=1).astype(jnp.int32), positions < ends[-1]


def eighth(shard):
    rows = shard.shape[0] // 8
    return lax.dynamic_slice_in_dim(shard, lax.axis_index("dp") * rows, rows, axis=0)


SMALL_ROWS = 16


def pack_small(qv_bias, out_bias, up_bias, down_bias, gain, shift):
    flat = [a.reshape(-1) for a in (qv_bias, out_bias, up_bias, down_bias, gain, shift)]
    return jnp.concatenate(flat)


def unpack_small(shards):
    count, total = shards.shape
    unit = total // SMALL_ROWS
    sizes = ((2, unit), (1, unit), (1, 4 * unit), (1, unit), (4, unit), (4, unit))
    out, at = [], 0
    for lead, cols in sizes:
        block = shards[:, at : at + lead * cols].reshape(count, lead, cols)
        out.append(jnp.swapaxes(block, 0, 1).reshape(lead, count * cols))
        at += lead * cols
    return out


def by_shard(rows, count):
    flat = []
    for arr in rows:
        lead, cols = arr.shape
        flat.append(
            jnp.swapaxes(arr.reshape(lead, count, cols // count), 0, 1).reshape(count, -1)
        )
    return jnp.concatenate(flat, axis=1)


def gather_small(own, got):
    z = lax.axis_index("fsdp")
    slots = jnp.stack([own] + got)
    low, high = z % 2, z // 2
    slots = jnp.where(low == 0, slots, slots[jnp.array([1, 0, 3, 2])])
    return jnp.where(high == 0, slots, slots[jnp.array([2, 3, 0, 1])])


def on_device(
    layer_input,
    qkv_weight,
    query_value_bias,
    out_weight,
    out_bias,
    up_weight,
    up_bias,
    down_weight,
    down_bias,
    norm_gain,
    norm_shift,
    doc_lengths,
    cotangent,
):
    _, tokens, width = layer_input.shape
    shards = lax.axis_size("fsdp")
    halves = shards == 4 and lax.axis_size("dp") == 8
    idx = jnp.stack([lax.axis_index("dp"), lax.axis_index("fsdp")]).astype(jnp.int32)
    x = layer_input[0]
    cot = cotangent[0]
    start, live = segment_starts(doc_lengths[0], tokens)
    start_row = start[None, :]
    live_col = live.astype(F32)[:, None]
    small_own = pack_small(query_value_bias, out_bias, up_bias, down_bias, norm_gain, norm_shift)
    tie = lax.optimization_barrier
    both = (4, 2)
    if halves:
        piece = eighth(qkv_weight)
        cols = piece.shape[1]
        extra = small_own.reshape(piece.shape[0], -1)
        got = shard_swaps(jnp.concatenate([piece, extra], axis=1))
        small = gather_small(small_own, [g[:, cols:].reshape(-1) for g in got])
        half_q = cols // 2
        q_own = [jnp.stack([g[:, :half_q] for g in got]), jnp.stack([g[:, half_q:cols] for g in got])]
        q_own, piece_u = after(q_own, jnp.concatenate([eighth(out_weight), eighth(up_weight)], axis=1))
        q_got = [swap(o, "dp", m) for o, m in zip(q_own, both)]
        got_u = swap(piece_u, "fsdp", 2)
        q_two = [jnp.concatenate([o, g]) for o, g in zip(q_own, q_got)]
        q_four = [swap(t, "dp", 6 - m) for t, m in zip(q_two, both)]
        slots_q = plane_slots(q_two, q_four)
        q_four, got_u = after(q_four, got_u)
        half_u = piece_u.shape[1] // 2
        pair_u = shard_pair(piece_u, got_u)
        own_q, own_u, own_d, at, count = qkv_weight, [out_weight, up_weight], down_weight, idx, shards
    else:
        small = lax.all_gather(small_own, "fsdp", axis=0)
        own_q = lax.all_gather(qkv_weight, "fsdp", axis=0, tiled=True)
        own_u = [
            lax.all_gather(out_weight, "fsdp", axis=0, tiled=True),
            lax.all_gather(up_weight, "fsdp", axis=0, tiled=True),
        ]
        own_d = lax.all_gather(down_weight, "fsdp", axis=0, tiled=True)
        half_q, half_u, at, count = own_q.shape[1] // 2, 0, jnp.zeros_like(idx), 1
        slots_q = slots_u = slots_d = []
    qv_b, out_b, up_b, down_b, gain, shift = unpack_small(small.astype(F32))
    qkv_b = jnp.concatenate([qv_b[0:1], jnp.zeros((1, width), F32), qv_b[1:2]], axis=1)

    spec = (
        [(0, 0, half_q, 0), (0, half_q, half_q, 1)],
        plane_spec([[(0, 0, 0, half_q, 0)], [(0, half_q, 0, half_q, 1)]]) if halves else [],
    )
    normed_one, packed, w_qkv = qkv_forward(
        at, own_q, spec, slots_q, count, x, qkv_b, gain[0:1], shift[0:1]
    )
    if halves:
        packed, pair_u = after(packed, pair_u)
        slots = shard_slots(got_u, pair_u)
        u_own = [jnp.stack([g[:, :half_u] for g in slots]), jnp.stack([g[:, half_u:] for g in slots])]
        u_got = [swap(o, "dp", m) for o, m in zip(u_own, both)]
        u_own, piece_d = after(u_own, eighth(down_weight))
        got_d = swap(piece_d, "fsdp", 2)
        u_own, packed = after(u_own, packed)
    pairs = width // PAIR
    part = attend(packed, start_row, 0, pairs // 2)
    if halves:
        part, u_got, got_d = tie((part, u_got, got_d))
        u_two = [jnp.concatenate([o, g]) for o, g in zip(u_own, u_got)]
        u_four = [swap(t, "dp", 6 - m) for t, m in zip(u_two, both)]
        u_two, got_d, packed = tie((u_two, got_d, packed))
        pair_d = shard_pair(piece_d, got_d)
    attended, lse = attend(packed, start_row, pairs // 2, pairs // 2, part)
    if halves:
        attended, u_four, pair_d = tie((attended, u_four, pair_d))
        slots_u = plane_slots(u_two, u_four)
        slots = shard_slots(got_d, pair_d)
        half_d = width // 2
        d_own = [jnp.stack([g[:, :half_d] for g in slots]), jnp.stack([g[:, half_d:] for g in slots])]
        d_got = [swap(o, "dp", m) for o, m in zip(d_own, both)]
    spec = ([(0, 0, width, 0)], plane_spec([[(0, 0, 0, width, 0)], []])[:4] if halves else [])
    mixed, mid, two, w_out = out_forward(
        at, own_u[0], spec, slots_u[:4], count, attended, x, out_b, gain, shift
    )
    if halves:
        two, d_got = after(two, d_got)
        d_two = [jnp.concatenate([o, g]) for o, g in zip(d_own, d_got)]
        d_four = [swap(t, "dp", 6 - m) for t, m in zip(d_two, both)]
        two, d_two = after(two, d_two)
    up_cols = own_u[1].shape[1]
    rest = half_u - width
    spec = (
        [(0, 0, up_cols, 0)],
        plane_spec([[(0, 0, width, rest, 0)], [(0, rest, 0, half_u, 0)]]) if halves else [],
    )
    act, slope, w_up = up_forward(at, own_u[1], spec, slots_u, count, two, up_b)
    if halves:
        act, d_four = after(act, d_four)
        slots_d = plane_slots(d_two, d_four)
    half = width // 2
    spec = ([(0, 0, width, 0)], plane_spec([[(0, 0, 0, half, 0)], [(0, half, 0, half, 0)]]) if halves else [])
    layer_out, gffn, sums3, ghid, up_sum = down_both(
        at, own_d, spec, slots_d, count, act, slope, down_b, mid, cot, live_col, gain, shift
    )

    if halves:
        send = grad_down(idx, act, gffn)
        got_down = swap(send, "dp", 1)
        send, ghid = after(send, ghid)
        send = grad_up(idx, two, ghid)
        got_up = swap(send, "dp", 1)
        send, got_down, act = tie((send, got_down, act))
        down_parts = grad_down(idx, act, gffn, got_down)
        down_got = plane_direct(down_parts)
        down_parts, ghid = after(down_parts, ghid)
    gmid, gmix, gatt, sums21 = mid_backward(ghid, w_up, w_out, mid, mixed, cot, live_col, gain)
    if halves:
        got_up, ghid, gmix, down_got[1:] = tie((got_up, ghid, gmix, down_got[1:]))
        up_parts = grad_up(idx, two, ghid, got_up)
        up_got = plane_direct(up_parts)
        up_parts, gatt = after(up_parts, gatt)
    back = functools.partial(attend_back, packed)
    share = (idx, normed_one) if halves else ()
    gq0, gk0, gv0, sq0, sv0, *shared0 = back(gatt, attended, lse, start_row, 0, 2, *share)
    if halves:
        gq0, gmix, down_got[0] = tie((gq0, gmix, down_got[0]))
        got0 = swap(shared0[0], "dp", 1)
        out_send, out_own = grad_out(idx, attended, gmix)
        out_got = swap(out_send, "dp", 1)
        out_send, gatt, up_got[1:] = tie((out_send, gatt, up_got[1:]))
    gq1, gk1, gv1, sq1, sv1, *shared1 = back(gatt, attended, lse, start_row, 1, 2, *share)
    if halves:
        up_got[0], gq1 = after(up_got[0], gq1)
        got1 = swap(shared1[0], "dp", 1)
        total = jnp.concatenate([plane_total(down_parts, down_got), plane_total(up_parts, up_got)])
        ffn_keep, ffn_send = across_first(total)
        ffn_got = swap(ffn_send, "fsdp", 1)
        ffn_keep, ffn_send, gq1, got0, out_got, got1 = tie((ffn_keep, ffn_send, gq1, got0, out_got, got1))
        heads_parts = head_sums([shared0[1], out_own, shared1[1]], [got0, out_got, got1])
        heads_got = plane_first(heads_parts)
        _, _, gq1 = tie((heads_parts[0], heads_parts[2], gq1))
    grads = [gq0, gq1, gk0, gk1, gv0, gv1]
    grad_input, sums0 = input_backward(grads, w_qkv, x, gmid, gain, 0, tokens // BLOCK)
    if halves:
        sums0, ffn_got = after(sums0, ffn_got)
        ffn_send = add_low(ffn_keep[:, 1], ffn_got[:, 1])
        ffn_keep = add_low(ffn_keep[:, 0], ffn_got[:, 0])
        ffn_got = swap(ffn_send, "fsdp", 2)
        ffn_send, ffn_keep, heads_got = tie((ffn_send, ffn_keep, heads_got))
        heads_send = [add_low(heads_parts[2 * f + 1][0], heads_got[f][0]) for f in range(2)]
        more_got = [swap(part, "dp", mask) for part, mask in zip(heads_send, (2, 4))]
        heads_send, heads_got = after(heads_send, heads_got)
        heads_keep = [add_low(heads_parts[2 * f + 1][1], heads_got[f][1]) for f in range(2)]
        heads_got = more_got
    small_grads = by_shard(
        [
            jnp.concatenate([jnp.concatenate([sq0, sq1], axis=1), jnp.concatenate([sv0, sv1], axis=1)]),
            sums21[4:5],
            up_sum,
            sums3[2:3],
            jnp.concatenate([sums0[0:1], sums21[2:3], sums21[0:1], sums3[0:1]]),
            jnp.concatenate([sums0[1:2], sums21[3:4], sums21[1:2], sums3[1:2]]),
        ],
        shards,
    )
    if halves:
        pairs_of = list(zip(heads_keep, heads_got))
        keep = [add_low(k[:, 0::2], g[:, 0::2]) for k, g in pairs_of]
        send = [add_low(k[:, 1::2], g[:, 1::2]).reshape(-1, width) for k, g in pairs_of]
        tail = small_grads.reshape(-1, width)
        more = tail.shape[0]
        got = swap(jnp.concatenate(send + [tail.astype(BF)]), "fsdp", 1)
        keep, ffn_got = after(keep, ffn_got)
        ffn_four = spread(add_low(ffn_keep, ffn_got))

        keep, got = tie((keep, got))
        tail = tail + got[-more:].astype(F32)
        each = keep[0].size // width
        pairs_of = [(k, got[f * each : (f + 1) * each].reshape(k.shape)) for f, k in enumerate(keep)]
        send = [add_low(k[:, 1], g[:, 1]).reshape(-1, width) for k, g in pairs_of]
        keep = [add_low(k[:, 0], g[:, 0]).reshape(-1, width) for k, g in pairs_of]
        got = swap(jnp.concatenate(send + [tail.astype(BF)]), "fsdp", 2)

        keep, got, ffn_four = tie((keep, got, ffn_four))
        tail = (tail + got[-more:].astype(F32)).astype(BF)
        piece = add_low(jnp.concatenate(keep), got[:-more])
        piece = jnp.concatenate([piece, tail])
        heads_got = [swap(piece, "dp", mask) for mask in (2, 4, 6)]
        ffn_all = spread_core(ffn_four)
        up_grad, down_grad = finish(
            "finish_ffn", idx, place_ffn, ffn_all, [up_weight.shape, down_weight.shape]
        )

        up_grad, heads_got = after(up_grad, heads_got)
        heads_four = jnp.stack([piece] + heads_got)
        heads_all = spread_core(heads_four)
        heads_core = heads_all[1][1]
        heads_all = [heads_all[0], (heads_all[1][0], heads_core)]
        tail = jnp.sum(heads_four[:, -more:].astype(F32), axis=0) + jnp.sum(
            heads_core[:, -more:].astype(F32), axis=0
        )
        small_sum = lax.dynamic_index_in_dim(
            tail.reshape(small_grads.shape), lax.axis_index("fsdp"), 0, keepdims=False
        )
        qkv_grad, out_grad = finish(
            "finish_heads", idx, place_heads, heads_all, [qkv_weight.shape, out_weight.shape]
        )
    else:
        gpacked = jnp.concatenate([gq0, gq1, gk0, gk1, gv0, gv1], axis=1)

        def reduced(left, right):
            grad = dot_tn(left, right)
            return lax.psum(lax.psum_scatter(grad, "fsdp", scatter_dimension=0, tiled=True), "dp")

        qkv_grad = reduced(normed_one, gpacked)
        out_grad = reduced(attended, gmix)
        up_grad = reduced(two, ghid)
        down_grad = reduced(act, gffn)
        small_sum = lax.dynamic_index_in_dim(
            lax.psum(small_grads, ("dp", "fsdp")), lax.axis_index("fsdp"), 0, keepdims=False
        )
    qv_g, outb_g, upb_g, downb_g, gain_g, shift_g = unpack_small(small_sum[None])
    return (
        layer_out[None],
        grad_input[None],
        qkv_grad,
        qv_g,
        out_grad,
        outb_g[0],
        up_grad,
        upb_g[0],
        down_grad,
        downb_g[0],
        gain_g,
        shift_g,
    )


def solution(mesh):
    rows = P(("dp", "fsdp"), None, None)
    split = P("fsdp", None)
    placed = (
        rows,
        split,
        P(None, "fsdp"),
        split,
        P("fsdp"),
        split,
        P("fsdp"),
        split,
        P("fsdp"),
        P(None, "fsdp"),
        P(None, "fsdp"),
        P(("dp", "fsdp"), None),
        rows,
    )
    return jax.shard_map(
        on_device,
        mesh=mesh,
        in_specs=placed,
        out_specs=(
            rows,
            rows,
            split,
            P(None, "fsdp"),
            split,
            P("fsdp"),
            split,
            P("fsdp"),
            split,
            P("fsdp"),
            P(None, "fsdp"),
            P(None, "fsdp"),
        ),
        check_vma=False,
    )
```

```python
import functools
import math

import jax
import jax.numpy as jnp
from jax import lax
from jax.experimental import pallas as pl
from jax.experimental.pallas import tpu as pltpu
from jax.sharding import PartitionSpec as P

F32 = jnp.float32
BF = jnp.bfloat16
SDS = jax.ShapeDtypeStruct
HEAD_DIM = 64
PAIR = 2 * HEAD_DIM
EPS = 1e-05
MASKED = -1e30
QUERY_SCALE = math.log2(math.e) / math.sqrt(HEAD_DIM)
GRAD_SCALE = 1.0 / math.sqrt(HEAD_DIM)
BLOCK = 256
UP_COLS = 1024
HIDDEN_COLS = 1024
GELU_A = math.sqrt(2.0 / math.pi)
GELU_B = 0.044715 * GELU_A


def params(mebibytes=60):
    return pltpu.CompilerParams(vmem_limit_bytes=mebibytes * 1024 * 1024)


def cost(flops, nbytes, trans=0):
    return pl.CostEstimate(flops=int(flops) // 1, bytes_accessed=int(nbytes) // 1, transcendentals=int(trans))


def dot_nn(a, b):
    return lax.dot_general(a, b, (((1,), (0,)), ((), ())), preferred_element_type=F32)


def dot_nt(a, b):
    return lax.dot_general(a, b, (((1,), (1,)), ((), ())), preferred_element_type=F32)


def dot_tn(a, b):
    return lax.dot_general(a, b, (((0,), (0,)), ((), ())), preferred_element_type=F32)


def centred(values):
    centre = values - jnp.mean(values, axis=-1, keepdims=True)
    rstd = lax.rsqrt(jnp.mean(centre * centre, axis=-1, keepdims=True) + EPS)
    return centre * rstd, rstd


def norm_back(grad, vhat, rstd, gain):
    e = grad * gain
    mean_e = jnp.mean(e, axis=-1, keepdims=True)
    mean_ev = jnp.mean(e * vhat, axis=-1, keepdims=True)
    return (e - mean_e - vhat * mean_ev) * rstd


def col_sum(values):
    return jnp.sum(values, axis=0, keepdims=True)


def piece_copies(spec, idx_ref, own_refs, slot_refs, places, sems):
    own_spec, slot_spec = spec
    dp, z = idx_ref[0], idx_ref[1]
    copies = []

    def add(group, src, dst):
        copies.append((group, pltpu.make_async_copy(src, dst, sems.at[len(copies)])))

    for o, first, cols, group in own_spec:
        rows = own_refs[o].shape[0]
        dst = places[o].at[pl.ds(pl.multiple_of(z * rows, rows), rows), first : first + cols]
        add(group, own_refs[o].at[:, first : first + cols], dst)
    for (pair, parts), ref in zip(slot_spec, slot_refs):
        rows = ref.shape[1]
        others = ref.shape[0] // 2
        for which, mask in enumerate(pair):
            for k in range(1, others + 1):
                at = which * others + k - 1
                for o, there, here, cols, group in parts:
                    dst = pl.multiple_of((z ^ k) * own_refs[o].shape[0] + (dp ^ mask) * rows, rows)
                    add(
                        group,
                        ref.at[at, :, here : here + cols],
                        places[o].at[pl.ds(dst, rows), there : there + cols],
                    )
    return copies


def count_copies(spec, slots):
    own_spec, slot_spec = spec
    return len(own_spec) + sum(len(parts) * s.shape[0] for (_, parts), s in zip(slot_spec, slots))


def start_all(copies):
    for _, copy in copies:
        copy.start()


def wait_group(copies, group):
    for g, copy in copies:
        if g == group:
            copy.wait()


def whole_shapes(owns, shards):
    return [(o.shape[0] * shards, o.shape[1]) for o in owns]


ANY = pl.BlockSpec(memory_space=pl.ANY)
SMEM = pl.BlockSpec(memory_space=pltpu.SMEM)


def qkv_kernel(spec, n_slots, idx_ref, own_ref, *refs):
    slots = refs[:n_slots]
    x_ref, bias_ref, gain_ref, shift_ref, normed_ref, packed_ref, out_ref = refs[n_slots : n_slots + 7]
    weight, sems, out_sem = refs[n_slots + 7 :]
    step, steps = pl.program_id(0), pl.num_programs(0)
    copies = piece_copies(spec, idx_ref, [own_ref], slots, [weight], sems)
    bn = packed_ref.shape[1]

    @pl.when(step == 0)
    def _():
        start_all(copies)
        vhat, _ = centred(x_ref[...].astype(F32))
        normed_ref[...] = (vhat * gain_ref[...] + shift_ref[...]).astype(BF)
        wait_group(copies, 0)

    half = weight.shape[1] // 2

    @pl.when(step == half // bn)
    def _():
        wait_group(copies, 1)
        pltpu.make_async_copy(weight, out_ref, out_sem).start()

    block = weight[:, pl.ds(pl.multiple_of(step * bn, bn), bn)]
    out = dot_nn(normed_ref[...], block) + bias_ref[...]
    packed_ref[...] = (out * jnp.where(step < steps // 3, QUERY_SCALE, 1.0)).astype(BF)

    @pl.when(step == steps - 1)
    def _():
        pltpu.make_async_copy(weight, out_ref, out_sem).wait()


def qkv_forward(idx, own, spec, slots, shards, x, bias, gain, shift):
    tokens, width = x.shape
    ((rows, cols),) = whole_shapes([own], shards)
    bn = width // 2
    row = pl.BlockSpec((1, width), lambda j: (0, 0))
    full = pl.BlockSpec((tokens, width), lambda j: (0, 0))
    return pl.pallas_call(
        functools.partial(qkv_kernel, spec, len(slots)),
        grid=(cols // bn,),
        in_specs=[SMEM] + [ANY] * (1 + len(slots))
        + [full, pl.BlockSpec((1, bn), lambda j: (0, j)), row, row],
        out_specs=(full, pl.BlockSpec((tokens, bn), lambda j: (0, j)), ANY),
        out_shape=(SDS((tokens, width), BF), SDS((tokens, cols), BF), SDS((rows, cols), BF)),
        scratch_shapes=[
            pltpu.VMEM((rows, cols), BF),
            pltpu.SemaphoreType.DMA((count_copies(spec, slots),)),
            pltpu.SemaphoreType.DMA(()),
        ],
        compiler_params=params(),
        cost_estimate=cost(2 * tokens * width * cols, 2 * width * cols + 2 * tokens * cols),
        name="qkv_forward",
    )(idx, own, *slots, x, bias, gain, shift)


def gelu_and_slope(a):
    sq = a * a
    t = jnp.tanh(a * (sq * GELU_B + GELU_A))
    half = 0.5 * t + 0.5
    act = a * half
    slope = half + act * ((1.0 - half) * (sq * (6.0 * GELU_B) + 2.0 * GELU_A))
    return act.astype(BF), slope.astype(BF)


def out_kernel(spec, n_slots, idx_ref, own_ref, *refs):
    slots = refs[:n_slots]
    att_ref, x_ref, bias_ref, gain_ref, shift_ref = refs[n_slots : n_slots + 5]
    mixed_ref, mid_ref, two_ref, save_ref, weight, sems, save_sem = refs[n_slots + 5 :]
    step, steps = pl.program_id(0), pl.num_programs(0)
    copies = piece_copies(spec, idx_ref, [own_ref], slots, [weight], sems)
    save = pltpu.make_async_copy(weight, save_ref, save_sem)

    @pl.when(step == 0)
    def _():
        start_all(copies)
        wait_group(copies, 0)
        save.start()

    mixed = dot_nn(att_ref[...], weight[...]) + bias_ref[...]
    mixed_ref[...] = mixed
    vhat, _ = centred(mixed)
    mid = x_ref[...].astype(F32) + vhat * gain_ref[1:2, :] + shift_ref[1:2, :]
    mid_ref[...] = mid
    vhat, _ = centred(mid)
    two_ref[...] = (vhat * gain_ref[2:3, :] + shift_ref[2:3, :]).astype(BF)

    @pl.when(step == steps - 1)
    def _():
        save.wait()


def out_forward(idx, own, spec, slots, shards, attended, x, bias, gain, shift):
    tokens, width = x.shape
    (shape,) = whole_shapes([own], shards)
    tok = pl.BlockSpec((BLOCK, width), lambda i: (i, 0))

    def whole(arr):
        return pl.BlockSpec(arr.shape, lambda i: (0, 0))

    return pl.pallas_call(
        functools.partial(out_kernel, spec, len(slots)),
        grid=(tokens // BLOCK,),
        in_specs=[SMEM] + [ANY] * (1 + len(slots)) + [tok, tok, whole(bias), whole(gain), whole(shift)],
        out_specs=(tok, tok, tok, ANY),
        out_shape=(
            SDS((tokens, width), F32),
            SDS((tokens, width), F32),
            SDS((tokens, width), BF),
            SDS(shape, BF),
        ),
        scratch_shapes=[
            pltpu.VMEM(shape, BF),
            pltpu.SemaphoreType.DMA((count_copies(spec, slots),)),
            pltpu.SemaphoreType.DMA(()),
        ],
        compiler_params=params(),
        cost_estimate=cost(2 * tokens * width * width, 16 * tokens * width),
        name="out_forward",
    )(idx, own, *slots, attended, x, bias, gain, shift)


def up_kernel(spec, n_slots, idx_ref, own_ref, *refs):
    slots = refs[:n_slots]
    two_ref, bias_ref, act_ref, slope_ref, save_ref, weight, sems, save_sem = refs[n_slots:]
    step, steps = pl.program_id(0), pl.num_programs(0)
    copies = piece_copies(spec, idx_ref, [own_ref], slots, [weight], sems)
    save = pltpu.make_async_copy(weight, save_ref, save_sem)

    @pl.when(step == 0)
    def _():
        start_all(copies)
        wait_group(copies, 0)
        save.start()

    bn = act_ref.shape[1]
    at = pl.ds(pl.multiple_of(step * bn, bn), bn)
    a = dot_nn(two_ref[...], weight[:, at]) + bias_ref[...]
    act_ref[...], slope_ref[...] = gelu_and_slope(a)

    @pl.when(step == steps - 1)
    def _():
        save.wait()


def up_forward(idx, own, spec, slots, shards, two, bias):
    tokens, width = two.shape
    (shape,) = whole_shapes([own], shards)
    cols = shape[1]
    bn = UP_COLS
    col = pl.BlockSpec((tokens, bn), lambda i: (0, i))
    return pl.pallas_call(
        functools.partial(up_kernel, spec, len(slots)),
        grid=(cols // bn,),
        in_specs=[SMEM] + [ANY] * (1 + len(slots))
        + [pl.BlockSpec((tokens, width), lambda i: (0, 0)), pl.BlockSpec((1, bn), lambda i: (0, i))],
        out_specs=(col, col, ANY),
        out_shape=(SDS((tokens, cols), BF), SDS((tokens, cols), BF), SDS(shape, BF)),
        scratch_shapes=[
            pltpu.VMEM(shape, BF),
            pltpu.SemaphoreType.DMA((count_copies(spec, slots),)),
            pltpu.SemaphoreType.DMA(()),
        ],
        compiler_params=params(),
        cost_estimate=cost(2 * tokens * width * cols, 2 * width * cols + 4 * tokens * cols),
        name="up_forward",
    )(idx, own, *slots, two, bias)


def down_kernel(spec, n_slots, first, idx_ref, own_ref, *refs):
    slots = refs[:n_slots]
    act_ref, slope_ref, bias_ref, mid_ref, cot_ref, live_ref, gain_ref, shift_ref = refs[n_slots : n_slots + 8]
    out_ref, grad_ref, sums_ref, hid_ref, hsum_ref, weight, sems = refs[n_slots + 8 :]
    step = pl.program_id(0)
    copies = piece_copies(spec, idx_ref, [own_ref], slots, [weight], sems)

    @pl.when(step == 0)
    def _():
        start_all(copies)
        sums_ref[...] = jnp.zeros_like(sums_ref)
        wait_group(copies, 0)

    @pl.when(step < first)
    def _():
        ffn = dot_nn(act_ref[...], weight[...]) + bias_ref[...]
        vhat, rstd = centred(ffn)
        gain = gain_ref[3:4, :]
        out_ref[...] = (mid_ref[...] + vhat * gain + shift_ref[3:4, :]).astype(BF)
        grad = cot_ref[...].astype(F32) * live_ref[...]
        low = norm_back(grad, vhat, rstd, gain).astype(BF)
        grad_ref[pl.ds(pl.multiple_of(step * BLOCK, BLOCK), BLOCK), :] = low
        sums_ref[0:1, :] += col_sum(grad * vhat)
        sums_ref[1:2, :] += col_sum(grad)
        sums_ref[2:3, :] += col_sum(low.astype(F32))

    @pl.when(step >= first)
    def _():
        bn = hid_ref.shape[1]
        at = pl.ds(pl.multiple_of((step - first) * bn, bn), bn)
        low = (dot_nt(grad_ref[...], weight[at, :]) * slope_ref[...].astype(F32)).astype(BF)
        hid_ref[...] = low
        hsum_ref[...] = col_sum(low.astype(F32))


def down_both(idx, own, spec, slots, shards, act, slope, bias, mid, cot, live, gain, shift):
    tokens, width = mid.shape
    (shape,) = whole_shapes([own], shards)
    cols = shape[0]
    bn = HIDDEN_COLS
    first = tokens // BLOCK

    def at(i):
        return jnp.minimum(i, first - 1)

    tok = pl.BlockSpec((BLOCK, width), lambda i: (at(i), 0))
    col = pl.BlockSpec((tokens, bn), lambda i: (0, jnp.maximum(i - first, 0)))

    def whole(arr):
        return pl.BlockSpec(arr.shape, lambda i: (0, 0))

    return pl.pallas_call(
        functools.partial(down_kernel, spec, len(slots), first),
        grid=(first + cols // bn,),
        in_specs=[SMEM] + [ANY] * (1 + len(slots))
        + [
            pl.BlockSpec((BLOCK, cols), lambda i: (at(i), 0)),
            col,
            whole(bias),
            tok,
            tok,
            pl.BlockSpec((BLOCK, 1), lambda i: (at(i), 0)),
            whole(gain),
            whole(shift),
        ],
        out_specs=(
            tok,
            pl.BlockSpec((tokens, width), lambda i: (0, 0)),
            pl.BlockSpec((8, width), lambda i: (0, 0)),
            col,
            pl.BlockSpec((1, bn), lambda i: (0, jnp.maximum(i - first, 0))),
        ),
        out_shape=(
            SDS((tokens, width), BF),
            SDS((tokens, width), BF),
            SDS((8, width), F32),
            SDS((tokens, cols), BF),
            SDS((1, cols), F32),
        ),
        scratch_shapes=[pltpu.VMEM(shape, BF), pltpu.SemaphoreType.DMA((count_copies(spec, slots),))],
        compiler_params=params(),
        cost_estimate=cost(4 * tokens * width * cols, 2 * width * cols + 6 * tokens * cols),
        name="down_both",
    )(idx, own, *slots, act, slope, bias, mid, cot, live, gain, shift)


def mid_kernel(
    gh_ref, up_ref, out_w_ref, mid_ref, mixed_ref, cot_ref, live_ref, gain_ref,
    gmid_ref, gmix_ref, gatt_ref, sums_ref,
):
    @pl.when(pl.program_id(0) == 0)
    def _():
        sums_ref[...] = jnp.zeros_like(sums_ref)

    grad = dot_nt(gh_ref[...], up_ref[...])
    vhat, rstd = centred(mid_ref[...])
    sums_ref[0:1, :] += col_sum(grad * vhat)
    sums_ref[1:2, :] += col_sum(grad)
    gmid = cot_ref[...].astype(F32) * live_ref[...] + norm_back(grad, vhat, rstd, gain_ref[2:3, :])
    gmid_ref[...] = gmid
    vhat, rstd = centred(mixed_ref[...])
    sums_ref[2:3, :] += col_sum(gmid * vhat)
    sums_ref[3:4, :] += col_sum(gmid)
    low = norm_back(gmid, vhat, rstd, gain_ref[1:2, :]).astype(BF)
    gmix_ref[...] = low
    sums_ref[4:5, :] += col_sum(low.astype(F32))
    gatt_ref[...] = dot_nt(low, out_w_ref[...]).astype(BF)


def mid_backward(gh, up, out_w, mid, mixed, cot, live, gain):
    tokens, width = mid.shape
    cols = gh.shape[1]
    tok = pl.BlockSpec((BLOCK, width), lambda i: (i, 0))

    def whole(arr):
        return pl.BlockSpec(arr.shape, lambda i: (0, 0))

    return pl.pallas_call(
        mid_kernel,
        grid=(tokens // BLOCK,),
        in_specs=[
            pl.BlockSpec((BLOCK, cols), lambda i: (i, 0)),
            whole(up),
            whole(out_w),
            tok,
            tok,
            tok,
            pl.BlockSpec((BLOCK, 1), lambda i: (i, 0)),
            whole(gain),
        ],
        out_specs=(tok, tok, tok, pl.BlockSpec((8, width), lambda i: (0, 0))),
        out_shape=(
            SDS((tokens, width), F32),
            SDS((tokens, width), BF),
            SDS((tokens, width), BF),
            SDS((8, width), F32),
        ),
        compiler_params=params(),
        cost_estimate=cost(2 * tokens * width * (cols + width), 2 * width * cols + 2 * tokens * cols),
        name="mid_backward",
    )(gh, up, out_w, mid, mixed, cot, live, gain)


def input_kernel(n_grads, n_into, *refs):
    grad_refs, (w_ref, x_ref, gmid_ref, gain_ref) = refs[:n_grads], refs[n_grads : n_grads + 4]
    out_ref, sums_ref = refs[n_grads + 4 + n_into :]

    @pl.when(pl.program_id(0) == 0)
    def _():
        sums_ref[...] = jnp.zeros_like(sums_ref)

    grads = jnp.concatenate([ref[...] for ref in grad_refs], axis=1)
    grad = dot_nt(grads, w_ref[...])
    vhat, rstd = centred(x_ref[...].astype(F32))
    sums_ref[0:1, :] += col_sum(grad * vhat)
    sums_ref[1:2, :] += col_sum(grad)
    out_ref[...] = gmid_ref[...] + norm_back(grad, vhat, rstd, gain_ref[0:1, :])


def input_backward(grads, weight, x, gmid, gain, first, count, into=None):
    tokens, width = x.shape
    tok = pl.BlockSpec((BLOCK, width), lambda i: (first + i, 0))

    def whole(arr):
        return pl.BlockSpec(arr.shape, lambda i: (0, 0))

    in_specs = [pl.BlockSpec((BLOCK, g.shape[1]), lambda i: (first + i, 0)) for g in grads]
    in_specs += [whole(weight), tok, tok, whole(gain)]
    args = [*grads, weight, x, gmid, gain]
    aliases = {}
    if into is not None:
        aliases = {len(args): 0}
        in_specs.append(pl.BlockSpec(memory_space=pl.ANY))
        args.append(into)
    return pl.pallas_call(
        functools.partial(input_kernel, len(grads), len(aliases)),
        grid=(count,),
        in_specs=in_specs,
        out_specs=(tok, pl.BlockSpec((8, width), lambda i: (0, 0))),
        out_shape=(SDS((tokens, width), F32), SDS((8, width), F32)),
        input_output_aliases=aliases,
        compiler_params=params(),
        cost_estimate=cost(6 * count * BLOCK * width * width, 6 * width * width),
        name="input_backward",
    )(*args)


def fill_bias(bias, start_ref):
    length = bias.shape[0]
    for j in range(length // BLOCK):
        key = lax.broadcasted_iota(jnp.int32, (BLOCK, length), 0) + j * BLOCK
        query = lax.broadcasted_iota(jnp.int32, (BLOCK, length), 1)
        allowed = (key <= query) & (key >= start_ref[...])
        bias[j * BLOCK : (j + 1) * BLOCK, :] = jnp.where(allowed, 0.0, MASKED)


def one_head(low, arr, head):
    zero = jnp.zeros_like(arr)
    return jnp.where(low, arr, zero) if head == 0 else jnp.where(low, zero, arr)


def attend_kernel(q_ref, k_ref, v_ref, start_ref, out_ref, lse_ref, bias):
    length = q_ref.shape[0]

    @pl.when(pl.program_id(0) == 0)
    def _():
        fill_bias(bias, start_ref)

    low = lax.broadcasted_iota(jnp.int32, (1, PAIR), 1) < HEAD_DIM
    low_rows = lax.broadcasted_iota(jnp.int32, (PAIR, 1), 0) < HEAD_DIM
    keys = k_ref[...]
    values = jnp.concatenate([v_ref[...], jnp.ones((length, PAIR), BF)], axis=1)
    for i in range(length // BLOCK):
        reach = (i + 1) * BLOCK
        sl = slice(i * BLOCK, reach)
        queries = q_ref[sl, :]
        parts = []
        for head in range(2):
            scores = dot_nt(keys[:reach], one_head(low, queries, head)) + bias[:reach, sl]
            top = jnp.max(scores, axis=0, keepdims=True)
            probs = jnp.exp2(scores - top).astype(BF)
            mixed = dot_tn(values[:reach], probs)
            total = mixed[PAIR : PAIR + 1]
            parts.append(mixed[:PAIR] / total)
            lse_ref[0, head : head + 1, sl] = top + jnp.log2(total)
        out_ref[sl, :] = jnp.where(low_rows, parts[0], parts[1]).T.astype(BF)


def attend(packed, start_row, first, count, into=None):
    length = packed.shape[0]
    pairs = packed.shape[1] // (3 * PAIR)

    def blk(offset):
        return pl.BlockSpec((length, PAIR), lambda h: (0, offset + first + h))

    in_specs = [blk(0), blk(pairs), blk(2 * pairs), pl.BlockSpec((1, length), lambda h: (0, 0))]
    args = [packed, packed, packed, start_row]
    kernel, aliases = attend_kernel, {}
    if into is not None:
        in_specs = in_specs + [ANY] * len(into)
        aliases = {len(args) + i: i for i in range(len(into))}
        args = args + list(into)

        def kernel(*refs):
            attend_kernel(*refs[:4], *refs[4 + len(into) :])

    return pl.pallas_call(
        kernel,
        grid=(count,),
        in_specs=in_specs,
        out_specs=(blk(0), pl.BlockSpec((1, 2, length), lambda h: (first + h, 0, 0))),
        out_shape=(SDS((length, PAIR * pairs), BF), SDS((pairs, 2, length), F32)),
        input_output_aliases=aliases,
        scratch_shapes=[pltpu.VMEM((length, length), F32)],
        compiler_params=params(),
        cost_estimate=cost(8 * count * length * length * PAIR, 8 * length * count * PAIR),
        name="attend",
    )(*args)


def share_out(wide, idx_ref, send_ref, own_ref):
    core, z = idx_ref[0] & 1, idx_ref[1]
    rows = wide.shape[0] // 8
    for zz in range(4):
        for ref, c in ((send_ref, core ^ 1), (own_ref, core)):
            at = pl.ds(pl.multiple_of((2 * zz + c) * rows, rows), rows)
            part = wide[at, :].astype(BF)
            ref[0, 0, zz ^ z, 0] = part[: rows // 2]
            ref[0, 0, zz ^ z, 1] = part[rows // 2 :]


def attend_back_kernel(shared, *refs):
    if shared:
        idx_ref, one_ref, refs = refs[0], refs[1], refs[2:]
        send_ref, own_ref, wide = refs[12], refs[13], refs[16]
        refs = refs[:12] + refs[14:16]
    q_ref, k_ref, v_ref, g_ref, o_ref, lse_ref, start_ref = refs[:7]
    gq_ref, gk_ref, gv_ref, sq_ref, sv_ref, bias, acc = refs[7:]
    length = q_ref.shape[0]

    @pl.when(pl.program_id(0) == 0)
    def _():
        fill_bias(bias, start_ref)

    low = lax.broadcasted_iota(jnp.int32, (1, PAIR), 1) < HEAD_DIM
    queries, grads = q_ref[...], g_ref[...]
    q_of = [one_head(low, queries, head) for head in range(2)]
    g_of = [one_head(low, grads, head) for head in range(2)]
    inner = (grads.astype(F32) * o_ref[...].astype(F32)).T
    inner_of = [col_sum(inner[:HEAD_DIM]), col_sum(inner[HEAD_DIM:])]
    sum_v = jnp.zeros((1, PAIR), F32)
    for j in range(length // BLOCK):
        first = j * BLOCK
        sl = slice(first, first + BLOCK)
        keys, values = k_ref[sl, :], v_ref[sl, :]
        gk = gv = gq = 0.0
        for head in range(2):
            scores = dot_nt(keys, q_of[head][first:]) + bias[sl, first:]
            probs = jnp.exp2(scores - lse_ref[0, head : head + 1, first:])
            gprobs = dot_nt(values, g_of[head][first:])
            gscores = (probs * (gprobs - inner_of[head][:, first:]) * GRAD_SCALE).astype(BF)
            gv = gv + dot_nn(probs.astype(BF), g_of[head][first:])
            gk = gk + dot_nn(gscores, q_of[head][first:])
            gq = gq + dot_tn(gscores, one_head(low, keys, head))
        low_v = gv.astype(BF)
        gv_ref[sl, :] = low_v
        gk_ref[sl, :] = (gk * (1.0 / QUERY_SCALE)).astype(BF)
        sum_v = sum_v + col_sum(low_v.astype(F32))
        if j == 0:
            acc[...] = gq
        else:
            acc[first:, :] += gq
    low_q = acc[...].astype(BF)
    gq_ref[...] = low_q
    sq_ref[...] = col_sum(low_q.astype(F32))
    sv_ref[...] = sum_v
    if shared:
        grads = jnp.concatenate([low_q, gk_ref[...], gv_ref[...]], axis=1)
        wide[...] = dot_tn(one_ref[...], grads)
        share_out(wide, idx_ref, send_ref, own_ref)


def attend_back(packed, grads, attended, lse, start_row, part, parts, idx=None, one=None):
    length = packed.shape[0]
    total = packed.shape[1] // (3 * PAIR)
    count = total // parts
    first = part * count
    shared = one is not None

    def blk(offset):
        return pl.BlockSpec((length, PAIR), lambda h, *_: (0, offset + h))

    row = pl.BlockSpec((1, PAIR), lambda h, *_: (0, h))
    grad = SDS((length, PAIR * count), BF)
    sums = SDS((1, PAIR * count), F32)
    in_specs = [
        blk(first),
        blk(total + first),
        blk(2 * total + first),
        blk(first),
        blk(first),
        pl.BlockSpec((1, 2, length), lambda h, *_: (first + h, 0, 0)),
        pl.BlockSpec((1, length), lambda h, *_: (0, 0)),
    ]
    args = [packed, packed, packed, grads, attended, lse, start_row]
    out_specs = [blk(0), blk(0), blk(0), row, row]
    out_shape = [grad, grad, grad, sums, sums]
    scratch = [pltpu.VMEM((length, length), F32), pltpu.VMEM((length, PAIR), F32)]
    if shared:
        width = one.shape[1]
        piece = (4, 2, width // 16, 3 * PAIR)
        block = pl.BlockSpec((1, 1) + piece, lambda h, idx: (3 ^ h ^ (idx[0] // 2), 0, 0, 0, 0, 0))
        in_specs = [pl.BlockSpec(one.shape, lambda h, *_: (0, 0))] + in_specs
        args = [idx, one] + args
        out_specs = out_specs + [block, block]
        out_shape = out_shape + [SDS((4, 1) + piece, BF)] * 2
        scratch = scratch + [pltpu.VMEM((width, 3 * PAIR), F32)]
    return pl.pallas_call(
        functools.partial(attend_back_kernel, shared),
        grid_spec=pltpu.PrefetchScalarGridSpec(
            num_scalar_prefetch=int(shared),
            grid=(count,),
            in_specs=in_specs,
            out_specs=tuple(out_specs),
            scratch_shapes=scratch,
        ),
        out_shape=tuple(out_shape),
        compiler_params=params(),
        cost_estimate=cost(20 * count * length * length * PAIR, 16 * length * count * PAIR),
        name="attend_back",
    )(*args)


def swap(arr, axis, mask):
    size = lax.axis_size(axis)
    return lax.ppermute(arr, axis, [(i, i ^ mask) for i in range(size)])


def after(first, then):
    return lax.optimization_barrier((first, then))


def shard_swaps(piece):
    return [swap(piece, "fsdp", k) for k in range(1, lax.axis_size("fsdp"))]


def shard_pair(piece, got):
    return swap(jnp.stack([piece, got]), "fsdp", 1)


def shard_slots(got, pair):
    return [pair[0], got, pair[1]]


PLANE_MASKS = [
    (0, 4), (2, 6), (1, 5), (3, 7),
    (0, 2), (4, 6), (1, 3), (5, 7),
]


def plane_slots(two, four):
    return [a for t, f in zip(two, four) for a in (t, f, swap(t, "dp", 1), swap(f, "dp", 1))]


def plane_spec(parts):
    return [(pair, parts[i // 4]) for i, pair in enumerate(PLANE_MASKS)]


def split_down(wide, zz):
    rows, cols = wide.shape[0] // 4, wide.shape[1] // 2
    part = wide[zz * rows : (zz + 1) * rows]
    return part[:, :cols], part[:, cols:]


def split_up(wide, zz):
    rows = wide.shape[0] // 8
    return wide[2 * zz * rows : (2 * zz + 1) * rows], wide[(2 * zz + 1) * rows : (2 * zz + 2) * rows]


def side_by_side(refs):
    blocks = [r[...] for r in refs]
    return blocks[0] if len(blocks) == 1 else jnp.concatenate(blocks, axis=1)


def emit(keep, direct, wide, split, z, chip, rest):
    if not keep:
        for zz in range(4):
            for f, part in enumerate(split(wide, zz)):
                rest[0][0, 0, zz ^ z, f] = part.astype(BF)
        return
    got_ref, outs = rest[0], rest[1:]
    for dst in range(4):

        @pl.when(chip == dst)
        def _():
            for zz in range(4):
                slot = zz ^ z
                for f, part in enumerate(split(wide, zz)):
                    low = (part + got_ref[0, 0, slot, f].astype(F32)).astype(BF)
                    if direct:
                        outs[dst][0, slot, f] = low
                    else:
                        bit = dst // 2 if f == 0 else dst % 2
                        outs[2 * f + bit][0, 0, slot] = low


def grad_kernel(keep, direct, jobs, idx_ref, *refs):
    step, z = pl.program_id(0), idx_ref[1]
    at = 0
    n_in = sum(n for groups, _ in jobs for group in groups for n in group)
    rest = refs[n_in:]
    for number, (groups, split) in enumerate(jobs):
        blocks = []
        for n_left, n_right in groups:
            blocks.append((refs[at : at + n_left], refs[at + n_left : at + n_left + n_right]))
            at += n_left + n_right

        @pl.when(step // 4 == number)
        def _():
            dots = [dot_tn(side_by_side(left), side_by_side(right)) for left, right in blocks]
            wide = dots[0] if len(dots) == 1 else jnp.concatenate(dots, axis=1)
            emit(keep, direct, wide, split, z, step % 4, rest)


def grad_call(name, idx, specs, args, jobs, piece, flops, got=None, direct=True):
    keep = got is not None
    n_jobs = len(jobs)
    rows, cols = piece
    block = pl.BlockSpec((1, 1, 4, 2, rows, cols), lambda i, idx: (i % 4, i // 4, 0, 0, 0, 0))
    half = (1, 1, 4, rows, cols)
    if keep and direct:
        specs = specs + [block]
        args = args + [got]
        out_specs = (pl.BlockSpec((1, 4, 2, rows, cols), lambda i, idx: (0, 0, 0, 0, 0)),) * 4
        out_shape = (SDS((1, 4, 2, rows, cols), BF),) * 4
    elif keep:
        along_y = (
            lambda i, idx: (jnp.minimum(i % 4, 1), i // 4, 0, 0, 0),
            lambda i, idx: (jnp.maximum(i % 4 - 2, 0), i // 4, 0, 0, 0),
        )
        along_x = (lambda i, idx: (i % 4 // 2, i // 4, 0, 0, 0),) * 2
        specs = specs + [block]
        args = args + [got]
        out_specs = tuple(pl.BlockSpec(half, m) for m in along_y + along_x)
        out_shape = (SDS((2, n_jobs, 4, rows, cols), BF),) * 4
    else:
        out_specs = block
        out_shape = SDS((4, n_jobs, 4, 2, rows, cols), BF)
    return pl.pallas_call(
        functools.partial(grad_kernel, keep, direct, jobs),
        grid_spec=pltpu.PrefetchScalarGridSpec(
            num_scalar_prefetch=1, grid=(4 * n_jobs,), in_specs=specs, out_specs=out_specs
        ),
        out_shape=out_shape,
        compiler_params=params(),
        cost_estimate=cost(flops, flops // 400),
        name=name + ("_keep" if keep else "_send"),
    )(idx, *args)


def chip_of(i, idx):
    return (idx[0] // 2) ^ (3 - i)


def core_of(keep, idx):
    return idx[0] & 1 if keep else (idx[0] & 1) ^ 1


def grad_down(idx, act, gffn, got=None):
    tokens, width = gffn.shape
    keep = got is not None
    rows = act.shape[1] // 32

    def act_spec(zz):
        def at(i, idx):
            return (0, zz * 8 + chip_of(i, idx) * 2 + core_of(keep, idx))

        return pl.BlockSpec((tokens, rows), at)

    specs = [act_spec(0), act_spec(1), act_spec(2), act_spec(3)]
    specs += [pl.BlockSpec((tokens, width), lambda i, idx: (0, 0))]
    args = [act, act, act, act, gffn]
    flops = act.shape[1] * width * tokens
    jobs = [([(4, 1)], split_down)]
    return grad_call("grad_down", idx, specs, args, jobs, (rows, width // 2), flops, got)


def grad_up(idx, two, ghid, got=None):
    tokens, width = two.shape
    keep = got is not None
    cols = ghid.shape[1] // 8
    specs = [
        pl.BlockSpec((tokens, width), lambda i, idx: (0, 0)),
        pl.BlockSpec((tokens, cols), lambda i, idx: (0, chip_of(i, idx) * 2 + core_of(keep, idx))),
    ]
    flops = ghid.shape[1] * width * tokens
    jobs = [([(1, 1)], split_up)]
    return grad_call("grad_up", idx, specs, [two, ghid], jobs, (width // 8, cols), flops, got)


def grad_out_kernel(idx_ref, att_ref, gmix_ref, send_ref, own_ref, wide):
    wide[...] = dot_tn(att_ref[...], gmix_ref[...])
    share_out(wide, idx_ref, send_ref, own_ref)


def grad_out(idx, att, gmix):
    tokens, width = att.shape
    cols = width // 4
    piece = (4, 2, width // 16, cols)
    block = pl.BlockSpec((1, 1) + piece, lambda i, idx: (i, 0, 0, 0, 0, 0))
    return pl.pallas_call(
        grad_out_kernel,
        grid_spec=pltpu.PrefetchScalarGridSpec(
            num_scalar_prefetch=1,
            grid=(4,),
            in_specs=[
                pl.BlockSpec((tokens, width), lambda i, idx: (0, 0)),
                pl.BlockSpec((tokens, cols), lambda i, idx: (0, chip_of(i, idx))),
            ],
            out_specs=(block, block),
            scratch_shapes=[pltpu.VMEM((width, cols), F32)],
        ),
        out_shape=(SDS((4, 1) + piece, BF),) * 2,
        compiler_params=params(),
        cost_estimate=cost(2 * tokens * width * width, 8 * tokens * width),
        name="grad_out",
    )(idx, att, gmix)


def head_sums_kernel(n, *refs):
    owns, gots, outs = refs[:n], refs[n : 2 * n], refs[2 * n :]
    for dst in range(4):

        @pl.when(pl.program_id(0) == dst)
        def _():
            for f in range(2):
                parts = [o[0, 0, :, f].astype(F32) + g[0, 0, :, f].astype(F32) for o, g in zip(owns, gots)]
                bit = dst // 2 if f == 0 else dst % 2
                outs[2 * f + bit][0, 0] = jnp.concatenate(parts, axis=-1).astype(BF)


def head_sums(owns, gots):
    _, _, slots, _, rows, _ = owns[0].shape
    cols = sum(o.shape[-1] for o in owns)
    half = (1, 1, slots, rows, cols)
    along_y = (lambda i: (jnp.minimum(i, 1), 0, 0, 0, 0), lambda i: (jnp.maximum(i - 2, 0), 0, 0, 0, 0))
    along_x = (lambda i: (i // 2, 0, 0, 0, 0),) * 2
    return pl.pallas_call(
        functools.partial(head_sums_kernel, len(owns)),
        grid=(4,),
        in_specs=[pl.BlockSpec((1,) + a.shape[1:], lambda i: (i, 0, 0, 0, 0, 0)) for a in owns + gots],
        out_specs=tuple(pl.BlockSpec(half, m) for m in along_y + along_x),
        out_shape=(SDS((2, 1, slots, rows, cols), BF),) * 4,
        compiler_params=params(32),
        cost_estimate=cost(0, 48 * slots * rows * cols),
        name="head_sums",
    )(*owns, *gots)


def add_low(a, b):
    return (a.astype(F32) + b.astype(F32)).astype(BF)


def add_wide(a, b):
    return a.astype(F32) + b.astype(F32)


def plane_first(parts):
    return [swap(parts[2 * f], "dp", mask) for f, mask in enumerate((4, 2))]


def plane_adds(parts, got):
    send = [add_low(parts[2 * f + 1][0], got[f][0]) for f in range(2)]
    keep = [add_low(parts[2 * f + 1][1], got[f][1]) for f in range(2)]
    return keep, send


def plane_second(parts, got):
    keep, send = plane_adds(parts, got)
    return keep, [swap(s, "dp", mask) for s, mask in zip(send, (2, 4))]


def plane_direct(parts):
    return [swap(part, "dp", mask) for part, mask in zip(parts, (6, 4, 2))]


def plane_total(parts, got):
    return add_wide(parts[3], got[0]) + add_wide(got[1], got[2])


def across_first(both):
    return both[:, 0::2].astype(BF), both[:, 1::2].astype(BF)


def spread(piece):
    four = jnp.stack([piece] + [swap(piece, "dp", mask) for mask in (2, 4, 6)])
    return four


def spread_core(four):
    return [((0, 2, 4, 6), four), ((1, 3, 5, 7), swap(four, "dp", 1))]


def place_ffn(dp, piece, outs):
    up_grad, down_grad = outs
    rows, cols = piece.shape[2], piece.shape[3]
    at = pl.ds(pl.multiple_of(dp * rows, rows), rows)
    down_grad[at, :cols] = piece[0, 0].astype(F32)
    down_grad[at, cols:] = piece[0, 1].astype(F32)
    at = pl.ds(pl.multiple_of(dp * cols, cols), cols)
    up_grad[:rows, at] = piece[1, 0].astype(F32)
    up_grad[rows:, at] = piece[1, 1].astype(F32)


def place_heads(dp, piece, outs):
    qkv_grad, out_grad = outs
    width = out_grad.shape[1]
    rows, cols = out_grad.shape[0] // 2, width // 4
    chip, core = dp // 2, dp % 2
    at_rows = pl.ds(pl.multiple_of(core * rows, rows), rows)
    part_of = piece[:rows].astype(F32)
    for half, skip in ((0, 0), (1, 3 * PAIR + cols)):
        for part in range(3):
            at = pl.multiple_of(part * width + half * (width // 2) + chip * PAIR, PAIR)
            here = skip + part * PAIR
            qkv_grad[at_rows, pl.ds(at, PAIR)] = part_of[:, here : here + PAIR]
    at = pl.multiple_of(chip * cols, cols)
    out_grad[at_rows, pl.ds(at, cols)] = part_of[:, 3 * PAIR : 3 * PAIR + cols]


def finish_kernel(placer, masks, idx_ref, *refs):
    ins, outs = refs[: len(masks)], refs[len(masks) :]
    for group, ref in zip(masks, ins):
        for which, mask in enumerate(group):
            placer(idx_ref[0] ^ mask, ref[which], outs)


def finish(name, idx, placer, flow, shapes):
    masks = [m for m, _ in flow]
    arrays = [a for _, a in flow]
    vmem = pl.BlockSpec(memory_space=pltpu.VMEM)
    return pl.pallas_call(
        functools.partial(finish_kernel, placer, masks),
        in_specs=[SMEM] + [vmem] * len(arrays),
        out_specs=(vmem,) * len(shapes),
        out_shape=tuple(SDS(s, F32) for s in shapes),
        compiler_params=params(32),
        cost_estimate=cost(0, sum(6 * math.prod(s) for s in shapes)),
        name=name,
    )(idx, *arrays)


def segment_starts(lengths, length):
    ends = jnp.cumsum(lengths)
    positions = jnp.arange(length, dtype=jnp.int32)
    begun = jnp.where(ends[None, :] <= positions[:, None], ends[None, :], 0)
    return jnp.max(begun, axis=1).astype(jnp.int32), positions < ends[-1]


def eighth(shard):
    rows = shard.shape[0] // 8
    return lax.dynamic_slice_in_dim(shard, lax.axis_index("dp") * rows, rows, axis=0)


SMALL_ROWS = 16


def pack_small(qv_bias, out_bias, up_bias, down_bias, gain, shift):
    flat = [a.reshape(-1) for a in (qv_bias, out_bias, up_bias, down_bias, gain, shift)]
    return jnp.concatenate(flat)


def unpack_small(shards):
    count, total = shards.shape
    unit = total // SMALL_ROWS
    sizes = ((2, unit), (1, unit), (1, 4 * unit), (1, unit), (4, unit), (4, unit))
    out, at = [], 0
    for lead, cols in sizes:
        block = shards[:, at : at + lead * cols].reshape(count, lead, cols)
        out.append(jnp.swapaxes(block, 0, 1).reshape(lead, count * cols))
        at += lead * cols
    return out


def by_shard(rows, count):
    flat = []
    for arr in rows:
        lead, cols = arr.shape
        flat.append(
            jnp.swapaxes(arr.reshape(lead, count, cols // count), 0, 1).reshape(count, -1)
        )
    return jnp.concatenate(flat, axis=1)


def gather_small(own, got):
    z = lax.axis_index("fsdp")
    slots = jnp.stack([own] + got)
    low, high = z % 2, z // 2
    slots = jnp.where(low == 0, slots, slots[jnp.array([1, 0, 3, 2])])
    return jnp.where(high == 0, slots, slots[jnp.array([2, 3, 0, 1])])


def on_device(
    layer_input,
    qkv_weight,
    query_value_bias,
    out_weight,
    out_bias,
    up_weight,
    up_bias,
    down_weight,
    down_bias,
    norm_gain,
    norm_shift,
    doc_lengths,
    cotangent,
):
    _, tokens, width = layer_input.shape
    shards = lax.axis_size("fsdp")
    halves = shards == 4 and lax.axis_size("dp") == 8
    idx = jnp.stack([lax.axis_index("dp"), lax.axis_index("fsdp")]).astype(jnp.int32)
    x = layer_input[0]
    cot = cotangent[0]
    start, live = segment_starts(doc_lengths[0], tokens)
    start_row = start[None, :]
    live_col = live.astype(F32)[:, None]
    small_own = pack_small(query_value_bias, out_bias, up_bias, down_bias, norm_gain, norm_shift)
    tie = lax.optimization_barrier
    both = (4, 2)
    if halves:
        piece = eighth(qkv_weight)
        cols = piece.shape[1]
        extra = small_own.reshape(piece.shape[0], -1)
        got = shard_swaps(jnp.concatenate([piece, extra], axis=1))
        small = gather_small(small_own, [g[:, cols:].reshape(-1) for g in got])
        half_q = cols // 2
        q_own = [jnp.stack([g[:, :half_q] for g in got]), jnp.stack([g[:, half_q:cols] for g in got])]
        q_own, piece_u = after(q_own, jnp.concatenate([eighth(out_weight), eighth(up_weight)], axis=1))
        q_got = [swap(o, "dp", m) for o, m in zip(q_own, both)]
        got_u = swap(piece_u, "fsdp", 2)
        q_two = [jnp.concatenate([o, g]) for o, g in zip(q_own, q_got)]
        q_four = [swap(t, "dp", 6 - m) for t, m in zip(q_two, both)]
        slots_q = plane_slots(q_two, q_four)
        q_four, got_u = after(q_four, got_u)
        half_u = piece_u.shape[1] // 2
        pair_u = shard_pair(piece_u, got_u)
        own_q, own_u, own_d, at, count = qkv_weight, [out_weight, up_weight], down_weight, idx, shards
    else:
        small = lax.all_gather(small_own, "fsdp", axis=0)
        own_q = lax.all_gather(qkv_weight, "fsdp", axis=0, tiled=True)
        own_u = [
            lax.all_gather(out_weight, "fsdp", axis=0, tiled=True),
            lax.all_gather(up_weight, "fsdp", axis=0, tiled=True),
        ]
        own_d = lax.all_gather(down_weight, "fsdp", axis=0, tiled=True)
        half_q, half_u, at, count = own_q.shape[1] // 2, 0, jnp.zeros_like(idx), 1
        slots_q = slots_u = slots_d = []
    qv_b, out_b, up_b, down_b, gain, shift = unpack_small(small.astype(F32))
    qkv_b = jnp.concatenate([qv_b[0:1], jnp.zeros((1, width), F32), qv_b[1:2]], axis=1)

    spec = (
        [(0, 0, half_q, 0), (0, half_q, half_q, 1)],
        plane_spec([[(0, 0, 0, half_q, 0)], [(0, half_q, 0, half_q, 1)]]) if halves else [],
    )
    normed_one, packed, w_qkv = qkv_forward(
        at, own_q, spec, slots_q, count, x, qkv_b, gain[0:1], shift[0:1]
    )
    if halves:
        packed, pair_u = after(packed, pair_u)
        slots = shard_slots(got_u, pair_u)
        u_own = [jnp.stack([g[:, :half_u] for g in slots]), jnp.stack([g[:, half_u:] for g in slots])]
        u_got = [swap(o, "dp", m) for o, m in zip(u_own, both)]
        u_own, piece_d = after(u_own, eighth(down_weight))
        got_d = swap(piece_d, "fsdp", 2)
        u_own, packed = after(u_own, packed)
    pairs = width // PAIR
    part = attend(packed, start_row, 0, pairs // 2)
    if halves:
        part, u_got, got_d = tie((part, u_got, got_d))
        u_two = [jnp.concatenate([o, g]) for o, g in zip(u_own, u_got)]
        u_four = [swap(t, "dp", 6 - m) for t, m in zip(u_two, both)]
        u_two, got_d, packed = tie((u_two, got_d, packed))
        pair_d = shard_pair(piece_d, got_d)
    attended, lse = attend(packed, start_row, pairs // 2, pairs // 2, part)
    if halves:
        attended, u_four, pair_d = tie((attended, u_four, pair_d))
        slots_u = plane_slots(u_two, u_four)
        slots = shard_slots(got_d, pair_d)
        half_d = width // 2
        d_own = [jnp.stack([g[:, :half_d] for g in slots]), jnp.stack([g[:, half_d:] for g in slots])]
        d_got = [swap(o, "dp", m) for o, m in zip(d_own, both)]
    spec = ([(0, 0, width, 0)], plane_spec([[(0, 0, 0, width, 0)], []])[:4] if halves else [])
    mixed, mid, two, w_out = out_forward(
        at, own_u[0], spec, slots_u[:4], count, attended, x, out_b, gain, shift
    )
    if halves:
        two, d_got = after(two, d_got)
        d_two = [jnp.concatenate([o, g]) for o, g in zip(d_own, d_got)]
        d_four = [swap(t, "dp", 6 - m) for t, m in zip(d_two, both)]
        two, d_two = after(two, d_two)
    up_cols = own_u[1].shape[1]
    rest = half_u - width
    spec = (
        [(0, 0, up_cols, 0)],
        plane_spec([[(0, 0, width, rest, 0)], [(0, rest, 0, half_u, 0)]]) if halves else [],
    )
    act, slope, w_up = up_forward(at, own_u[1], spec, slots_u, count, two, up_b)
    if halves:
        act, d_four = after(act, d_four)
        slots_d = plane_slots(d_two, d_four)
    half = width // 2
    spec = ([(0, 0, width, 0)], plane_spec([[(0, 0, 0, half, 0)], [(0, half, 0, half, 0)]]) if halves else [])
    layer_out, gffn, sums3, ghid, up_sum = down_both(
        at, own_d, spec, slots_d, count, act, slope, down_b, mid, cot, live_col, gain, shift
    )

    if halves:
        send = grad_down(idx, act, gffn)
        got_down = swap(send, "dp", 1)
        send, ghid = after(send, ghid)
        send = grad_up(idx, two, ghid)
        got_up = swap(send, "dp", 1)
        send, got_down, act = tie((send, got_down, act))
        down_parts = grad_down(idx, act, gffn, got_down)
        down_got = plane_direct(down_parts)
        down_parts, ghid = after(down_parts, ghid)
    gmid, gmix, gatt, sums21 = mid_backward(ghid, w_up, w_out, mid, mixed, cot, live_col, gain)
    if halves:
        got_up, ghid, gmix, down_got[1:] = tie((got_up, ghid, gmix, down_got[1:]))
        up_parts = grad_up(idx, two, ghid, got_up)
        up_got = plane_direct(up_parts)
        up_parts, gatt = after(up_parts, gatt)
    back = functools.partial(attend_back, packed)
    share = (idx, normed_one) if halves else ()
    gq0, gk0, gv0, sq0, sv0, *shared0 = back(gatt, attended, lse, start_row, 0, 2, *share)
    if halves:
        gq0, gmix, down_got[0] = tie((gq0, gmix, down_got[0]))
        got0 = swap(shared0[0], "dp", 1)
        out_send, out_own = grad_out(idx, attended, gmix)
        out_got = swap(out_send, "dp", 1)
        out_send, gatt, up_got[1:] = tie((out_send, gatt, up_got[1:]))
    gq1, gk1, gv1, sq1, sv1, *shared1 = back(gatt, attended, lse, start_row, 1, 2, *share)
    if halves:
        up_got[0], gq1 = after(up_got[0], gq1)
        got1 = swap(shared1[0], "dp", 1)
        total = jnp.concatenate([plane_total(down_parts, down_got), plane_total(up_parts, up_got)])
        ffn_keep, ffn_send = across_first(total)
        ffn_got = swap(ffn_send, "fsdp", 1)
        ffn_keep, ffn_send, gq1, got0, out_got, got1 = tie((ffn_keep, ffn_send, gq1, got0, out_got, got1))
        heads_parts = head_sums([shared0[1], out_own, shared1[1]], [got0, out_got, got1])
        heads_got = plane_first(heads_parts)
        _, _, gq1 = tie((heads_parts[0], heads_parts[2], gq1))
    grads = [gq0, gq1, gk0, gk1, gv0, gv1]
    grad_input, sums0 = input_backward(grads, w_qkv, x, gmid, gain, 0, tokens // BLOCK)
    if halves:
        sums0, ffn_got = after(sums0, ffn_got)
        ffn_send = add_low(ffn_keep[:, 1], ffn_got[:, 1])
        ffn_keep = add_low(ffn_keep[:, 0], ffn_got[:, 0])
        ffn_got = swap(ffn_send, "fsdp", 2)
        ffn_send, ffn_keep, heads_got = tie((ffn_send, ffn_keep, heads_got))
        heads_send = [add_low(heads_parts[2 * f + 1][0], heads_got[f][0]) for f in range(2)]
        more_got = [swap(part, "dp", mask) for part, mask in zip(heads_send, (2, 4))]
        heads_send, heads_got = after(heads_send, heads_got)
        heads_keep = [add_low(heads_parts[2 * f + 1][1], heads_got[f][1]) for f in range(2)]
        heads_got = more_got
    small_grads = by_shard(
        [
            jnp.concatenate([jnp.concatenate([sq0, sq1], axis=1), jnp.concatenate([sv0, sv1], axis=1)]),
            sums21[4:5],
            up_sum,
            sums3[2:3],
            jnp.concatenate([sums0[0:1], sums21[2:3], sums21[0:1], sums3[0:1]]),
            jnp.concatenate([sums0[1:2], sums21[3:4], sums21[1:2], sums3[1:2]]),
        ],
        shards,
    )
    if halves:
        pairs_of = list(zip(heads_keep, heads_got))
        keep = [add_low(k[:, 0::2], g[:, 0::2]) for k, g in pairs_of]
        send = [add_low(k[:, 1::2], g[:, 1::2]).reshape(-1, width) for k, g in pairs_of]
        tail = small_grads.reshape(-1, width)
        more = tail.shape[0]
        got = swap(jnp.concatenate(send + [tail.astype(BF)]), "fsdp", 1)
        keep, ffn_got = after(keep, ffn_got)
        ffn_four = spread(add_low(ffn_keep, ffn_got))

        keep, got = tie((keep, got))
        tail = tail + got[-more:].astype(F32)
        each = keep[0].size // width
        pairs_of = [(k, got[f * each : (f + 1) * each].reshape(k.shape)) for f, k in enumerate(keep)]
        send = [add_low(k[:, 1], g[:, 1]).reshape(-1, width) for k, g in pairs_of]
        keep = [add_low(k[:, 0], g[:, 0]).reshape(-1, width) for k, g in pairs_of]
        got = swap(jnp.concatenate(send + [tail.astype(BF)]), "fsdp", 2)

        keep, got, ffn_four = tie((keep, got, ffn_four))
        tail = (tail + got[-more:].astype(F32)).astype(BF)
        piece = add_low(jnp.concatenate(keep), got[:-more])
        piece = jnp.concatenate([piece, tail])
        heads_got = [swap(piece, "dp", mask) for mask in (2, 4, 6)]
        ffn_all = spread_core(ffn_four)
        up_grad, down_grad = finish(
            "finish_ffn", idx, place_ffn, ffn_all, [up_weight.shape, down_weight.shape]
        )

        up_grad, heads_got = after(up_grad, heads_got)
        heads_four = jnp.stack([piece] + heads_got)
        heads_all = spread_core(heads_four)
        heads_core = heads_all[1][1]
        heads_all = [heads_all[0], (heads_all[1][0], heads_core)]
        tail = jnp.sum(heads_four[:, -more:].astype(F32), axis=0) + jnp.sum(
            heads_core[:, -more:].astype(F32), axis=0
        )
        small_sum = lax.dynamic_index_in_dim(
            tail.reshape(small_grads.shape), lax.axis_index("fsdp"), 0, keepdims=False
        )
        qkv_grad, out_grad = finish(
            "finish_heads", idx, place_heads, heads_all, [qkv_weight.shape, out_weight.shape]
        )
    else:
        gpacked = jnp.concatenate([gq0, gq1, gk0, gk1, gv0, gv1], axis=1)

        def reduced(left, right):
            grad = dot_tn(left, right)
            return lax.psum(lax.psum_scatter(grad, "fsdp", scatter_dimension=0, tiled=True), "dp")

        qkv_grad = reduced(normed_one, gpacked)
        out_grad = reduced(attended, gmix)
        up_grad = reduced(two, ghid)
        down_grad = reduced(act, gffn)
        small_sum = lax.dynamic_index_in_dim(
            lax.psum(small_grads, ("dp", "fsdp")), lax.axis_index("fsdp"), 0, keepdims=False
        )
    qv_g, outb_g, upb_g, downb_g, gain_g, shift_g = unpack_small(small_sum[None])
    return (
        layer_out[None],
        grad_input[None],
        qkv_grad,
        qv_g,
        out_grad,
        outb_g[0],
        up_grad,
        upb_g[0],
        down_grad,
        downb_g[0],
        gain_g,
        shift_g,
    )


def solution(mesh):
    rows = P(("dp", "fsdp"), None, None)
    split = P("fsdp", None)
    placed = (
        rows,
        split,
        P(None, "fsdp"),
        split,
        P("fsdp"),
        split,
        P("fsdp"),
        split,
        P("fsdp"),
        P(None, "fsdp"),
        P(None, "fsdp"),
        P(("dp", "fsdp"), None),
        rows,
    )
    return jax.shard_map(
        on_device,
        mesh=mesh,
        in_specs=placed,
        out_specs=(
            rows,
            rows,
            split,
            P(None, "fsdp"),
            split,
            P("fsdp"),
            split,
            P("fsdp"),
            split,
            P("fsdp"),
            P(None, "fsdp"),
            P(None, "fsdp"),
        ),
        check_vma=False,
    )
```
